256 devices in a mesh: dp: 32 (over z, y_hi, core), mp: 8 (over y_lo, x).
Axes of the slice: x: 4, y: 4 (y_hi: 2, y_lo: 2; y = y_hi * 2 + y_lo), z: 8, core: 2. Of those that a mesh axis runs over, the one named last changes fastest.
Arguments:
- audio: bfloat16 [64, 4096, 512], P('dp', 'mp'), may hold values from -6 to 6
- lengths: int32 [64], replicated, may hold values from 1 to 2048, as said below
- moved_slots: int32 [16, 1], replicated, may hold values from 0 to 1, as said below
- conv_weight: bfloat16 [1024, 512], replicated, may hold values from -0.1875 to 0.1875
- channel_params: float32 [512, 5], replicated, may hold values from 0.5 to 1.5
- proj_weight: bfloat16 [512, 120], replicated, may hold values from -0.25 to 0.25
- pos_weight: bfloat16 [128, 120, 120], replicated, may hold values from -0.046875 to 0.046875
- cotangent: bfloat16 [64, 2048, 120], P('dp', 'mp'), may hold values from -6 to 6
Outputs:
- hidden: bfloat16 [64, 2048, 120], P('dp', 'mp')
- grad_features: bfloat16 [64, 4096, 512], P('dp', 'mp')
- grad_pos: float32 [128, 120, 120], P('dp')
- grad_conv: float32 [1024, 512], P('dp')
- grad_proj: float32 [512, 120], P('dp')
- grad_channels: float32 [512, 5], P('dp')
The draws below stay inside these ranges and needn't reach their ends.
Inputs may be any that keep to these rules, and one draw needn't show every extreme that they name: `lengths`: some utterance has all 2048 frames in every draw. `moved_slots`: each row holds one slot number, 0 or 1.
All inputs are finite; a program needn't handle non-finite values.
Results may differ from the reference program's by a relative error of at most 0.025.
Values may be sent and summed in bfloat16 or wider, within the bound.
No kernel may reach another device: no remote copies, remote signals or barrier semaphores. Data moves between devices by JAX's collectives and lax.ppermute only.
A program may use at most 128 MiB of HBM per device.

```python
import jax
import jax.numpy as jnp
from jax import lax

C = 512
GC = 120
K = 128
U_DEV = 2
MOVE = 1
PAIRS = 16
UTT = 64
FRAMES = 2048
N_DP = 32


def draw_lengths(key, part):
    key = jax.random.fold_in(key, 11)
    ranking = jax.random.permutation(jax.random.fold_in(key, 1), N_DP)
    heavy_rank = ranking < max(1, N_DP // 4)
    light_len = jax.random.randint(jax.random.fold_in(key, 2), (N_DP, U_DEV), 1, FRAMES // 4 + 1)
    heavy_len = jax.random.randint(jax.random.fold_in(key, 3), (N_DP, U_DEV), FRAMES // 2, FRAMES + 1)
    is_first = jnp.arange(U_DEV)[None, :] == 0
    heavy_len = jnp.where(is_first, FRAMES, heavy_len)
    return jnp.where(heavy_rank[:, None], heavy_len, light_len).reshape(UTT).astype(jnp.int32)


def draw_moved_slots(key, part):
    key = jax.random.fold_in(key, 23)
    scores = jax.random.randint(key, (PAIRS, U_DEV), 0, 1048576) * U_DEV + jnp.arange(U_DEV)[None, :]
    ranking = jnp.argsort(scores, axis=1)
    return ranking[:, :MOVE].astype(jnp.int32)


def shard_levels(own_key, dims, cuts, least, top_value):
    level, own = 1.0, jax.random.fold_in(own_key, 6)
    for axis_at, blocks in cuts:
        draws = jnp.exp(jax.random.uniform(jax.random.fold_in(own, axis_at), (blocks,), jnp.float32, least / len(cuts), top_value / len(cuts)))
        level = level * jnp.repeat(draws, dims[axis_at] // blocks).reshape([-1 if axis == axis_at else 1 for axis in range(len(dims))])
    return level


def noise(key, dims, width, limit, cuts=(), kind=jnp.bfloat16):
    entries = jax.random.normal(key, dims, jnp.float32) * width
    if len(cuts) > 0:
        entries = shard_levels(key, dims, cuts, -0.22, 0.18) * entries
    return jnp.clip(entries, min=-limit, max=limit).astype(kind)


def setup_inputs(seed: int = 0) -> dict:
    splits = jax.random.split(jax.random.key(seed), 9)
    audio = noise(splits[0], (UTT, 2 * FRAMES, C), 1.0, 6.0, ((0, 32), (1, 8)))
    lengths = draw_lengths(jax.random.fold_in(splits[8], 71), 0)
    moved_slots = draw_moved_slots(jax.random.fold_in(splits[8], 71), 0)
    conv_weight = noise(splits[3], (2 * C, C), (2 * C) ** -0.5, 0.1875)
    channel_params = jnp.clip(jax.random.uniform(splits[4], (C, 5), jnp.float32, 0.5, 1.5), 0.5, 1.5)
    proj_weight = noise(splits[5], (C, GC), C ** -0.5, 0.25)
    pos_weight = noise(splits[6], (K, GC, GC), (K * GC) ** -0.5, 0.046875)
    cotangent = noise(splits[7], (UTT, FRAMES, GC), 1.0, 6.0, ((0, 32), (1, 8)))
    return dict(audio=audio, lengths=lengths, moved_slots=moved_slots, conv_weight=conv_weight, channel_params=channel_params, proj_weight=proj_weight, pos_weight=pos_weight, cotangent=cotangent)


epsilon = 1e-05
root_half = 0.7071067811865476
density = 0.3989422804014327

def gelu_exact(values):
    return 0.5 * values * (1.0 + lax.erf(values * root_half))

def gelu_slope(values):
    return 0.5 * (1.0 + lax.erf(values * root_half)) + values * jnp.exp(-0.5 * values * values) * density

def layer_norm(values, gain_row, shift_row):
    centre = lax.optimization_barrier(jnp.mean(values, axis=-1, keepdims=True))
    offset = values - centre
    inverse = lax.rsqrt(lax.optimization_barrier(jnp.mean(offset * offset, axis=-1, keepdims=True)) + epsilon)
    normed = offset * inverse
    return (normed, inverse, normed * gain_row + shift_row)

def norm_backward(grad_out, normed, inverse, gain_row):
    scaled = grad_out * gain_row
    first_mean = lax.optimization_barrier(jnp.mean(scaled, axis=-1, keepdims=True))
    second = lax.optimization_barrier(jnp.mean(scaled * normed, axis=-1, keepdims=True))
    return inverse * (scaled - first_mean - normed * second)

def encode_forward(audio_rows, frame_mask, conv_weight, channel_params, proj_weight):
    paired = audio_rows.reshape(audio_rows.shape[0] // 2, 2 * audio_rows.shape[1])
    conv_out = jnp.dot(paired, conv_weight, preferred_element_type=jnp.float32) + channel_params[:, 0]
    normed_one, inverse_one, affine = layer_norm(conv_out, channel_params[:, 1], channel_params[:, 2])
    encoded = gelu_exact(affine).astype(jnp.bfloat16)
    normed_two, inverse_two, projected_in = layer_norm(encoded.astype(jnp.float32), channel_params[:, 3], channel_params[:, 4])
    projected_in = projected_in.astype(jnp.bfloat16)
    projected = jnp.dot(projected_in, proj_weight, preferred_element_type=jnp.float32)
    features = (projected * frame_mask[:, None]).astype(jnp.bfloat16)
    return (features, (normed_one, inverse_one, affine, normed_two, inverse_two, projected_in))

def encode_backward(audio_rows, stored, feature_grad, conv_weight, channel_params, proj_weight):
    normed_one, inverse_one, affine, normed_two, inverse_two, projected_in = stored
    paired = audio_rows.reshape(audio_rows.shape[0] // 2, 2 * audio_rows.shape[1])
    proj_grad = lax.dot_general(projected_in, feature_grad, (((0,), (0,)), ((), ())), preferred_element_type=jnp.float32)
    normed_grad = lax.dot_general(feature_grad, proj_weight, (((1,), (1,)), ((), ())), preferred_element_type=jnp.float32)
    encoded_grad = norm_backward(normed_grad, normed_two, inverse_two, channel_params[:, 3])
    affine_grad = encoded_grad * gelu_slope(affine)
    conv_grad = norm_backward(affine_grad, normed_one, inverse_one, channel_params[:, 1])
    conv_operand = conv_grad.astype(jnp.bfloat16)
    weight_grad = lax.dot_general(paired, conv_operand, (((0,), (0,)), ((), ())), preferred_element_type=jnp.float32)
    audio_grad = lax.dot_general(conv_operand, conv_weight, (((1,), (1,)), ((), ())), preferred_element_type=jnp.float32)
    audio_grad = audio_grad.astype(jnp.bfloat16).reshape(audio_rows.shape)
    vector_grad = jnp.stack([lax.optimization_barrier(jnp.sum(conv_grad, axis=0)), lax.optimization_barrier(jnp.sum(affine_grad * normed_one, axis=0)), lax.optimization_barrier(jnp.sum(affine_grad, axis=0)), lax.optimization_barrier(jnp.sum(normed_grad * normed_two, axis=0)), lax.optimization_barrier(jnp.sum(normed_grad, axis=0))], axis=1)
    return (weight_grad, proj_grad, vector_grad, audio_grad)

def mix_forward(padded, features, frame_mask, pos_weight):
    mixed_pre = lax.conv_general_dilated(padded[None], pos_weight, (1,), 'VALID', dimension_numbers=('NWC', 'WIO', 'NWC'), preferred_element_type=jnp.float32)[0]
    hidden = ((features.astype(jnp.float32) + gelu_exact(mixed_pre)) * frame_mask[:, None]).astype(jnp.bfloat16)
    return (mixed_pre, hidden)

def mix_backward(padded, slope_pad, slope_rows, back_rows, frame_mask, flipped):
    kernel_grad = lax.conv_general_dilated(padded[:, :, None], slope_rows[:, None, :], (1,), 'VALID', dimension_numbers=('WNC', 'WIO', 'WNC'), preferred_element_type=jnp.float32)
    spread = lax.conv_general_dilated(slope_pad[None], flipped, (1,), 'VALID', dimension_numbers=('NWC', 'WIO', 'NWC'), preferred_element_type=jnp.float32)[0]
    feature_grad = ((back_rows.astype(jnp.float32) + spread) * frame_mask[:, None]).astype(jnp.bfloat16)
    return (kernel_grad, feature_grad)

def reference(audio, lengths, moved_slots, conv_weight, channel_params, proj_weight, pos_weight, cotangent):
    half_axis = N_DP // 2
    slot_ids = jnp.arange(UTT, dtype=jnp.int32)
    data_ranks = slot_ids // U_DEV
    within = slot_ids % U_DEV
    chosen = moved_slots[data_ranks % half_axis]
    is_moved = jnp.any(chosen == within[:, None], axis=1)
    source = jnp.where(is_moved, jnp.bitwise_xor(data_ranks, half_axis) * U_DEV + within, slot_ids).astype(jnp.int32)
    back = cotangent[source]
    frames = jnp.arange(FRAMES, dtype=jnp.int32)
    flipped = jnp.flip(pos_weight, 0).transpose(0, 2, 1)
    reach = K // 2

    def one_utterance(totals, members):
        audio_rows, length, back_rows = members
        frame_mask = (frames < length).astype(jnp.float32)
        features, stored = encode_forward(audio_rows, frame_mask, conv_weight, channel_params, proj_weight)
        padded = jnp.pad(features, ((reach, reach - 1), (0, 0)))
        mixed_pre, states = mix_forward(padded, features, frame_mask, pos_weight)
        slope_rows = (back_rows.astype(jnp.float32) * gelu_slope(mixed_pre) * frame_mask[:, None]).astype(jnp.bfloat16)
        slope_pad = jnp.pad(slope_rows, ((reach - 1, reach), (0, 0)))
        kernel_grad, feature_grad = mix_backward(padded, slope_pad, slope_rows, back_rows, frame_mask, flipped)
        weight_grad, proj_grad, vector_grad, audio_grad = encode_backward(audio_rows, stored, feature_grad, conv_weight, channel_params, proj_weight)
        totals = (totals[0] + kernel_grad, totals[1] + weight_grad, totals[2] + proj_grad, totals[3] + vector_grad)
        return (totals, (states, audio_grad))
    initial = (jnp.zeros(pos_weight.shape, jnp.float32), jnp.zeros(conv_weight.shape, jnp.float32), jnp.zeros(proj_weight.shape, jnp.float32), jnp.zeros(channel_params.shape, jnp.float32))
    totals, outputs = lax.scan(one_utterance, initial, (audio, lengths, back))
    states, grad_features = outputs
    grad_scale = (UTT * FRAMES) ** (-0.5)
    return (states[source], grad_features, totals[0] * grad_scale, totals[1] * grad_scale, totals[2] * grad_scale, totals[3] * grad_scale)
```

```python
import functools

import jax
import jax.numpy as jnp
from jax import lax
from jax.experimental import pallas as pl
from jax.experimental.pallas import tpu as pltpu
from jax.sharding import PartitionSpec as P

epsilon = 1e-05
root_half = 0.7071067811865476
density = 0.3989422804014327

SLOTS = 2
T = 256
C = 512
GC = 120
LANES = 128
K = 128
REACH = 64
EXT = T + 2 * REACH
NEAR = 16
GROUPS = 2
PER_GROUP = 4
SPAN = T + NEAR * (PER_GROUP - 1)
CHUNK = 32
VMEM_LIMIT = 56 * 1024 * 1024

f32 = jnp.float32
bf16 = jnp.bfloat16

VMEM = pl.BlockSpec(memory_space=pltpu.VMEM)
SMEM = pl.BlockSpec(memory_space=pltpu.SMEM)


def params(**more):
    return pltpu.CompilerParams(vmem_limit_bytes=VMEM_LIMIT, **more)


def cost(flops, moved, trans=0):
    return pl.CostEstimate(flops=flops, bytes_accessed=moved, transcendentals=trans)


def phi(values):
    return 0.5 * (1.0 + lax.erf(values * root_half))


def bell(values):
    return jnp.exp(-0.5 * values * values) * density


def row_mask(info_ref, slot, first, rows):
    ids = info_ref[0] + first + lax.broadcasted_iota(jnp.int32, (rows, 1), 0)
    return ids < info_ref[2 + slot]


def alive(info_ref, slot):
    return info_ref[0] < info_ref[2 + slot]


def nt(a, b):
    return lax.dot_general(a, b, (((1,), (1,)), ((), ())), preferred_element_type=f32)


def tn(a, b):
    return lax.dot_general(a, b, (((0,), (0,)), ((), ())), preferred_element_type=f32)


def nn(a, b):
    return jnp.dot(a, b, preferred_element_type=f32)


def arrange_body(pos_ref, fwd_ref, bwd_ref):
    fwd_ref[...] = jnp.zeros_like(fwd_ref)
    bwd_ref[...] = jnp.zeros_like(bwd_ref)
    for q in range(K // NEAR):
        for r in range(NEAR):
            fwd_ref[r * LANES : r * LANES + GC, q * LANES : q * LANES + GC] = pos_ref[q * NEAR + r]
            bwd_ref[q * LANES : q * LANES + GC, r * LANES : r * LANES + GC] = pos_ref[
                K - 1 - q * NEAR - r
            ]


def arrange(pos_weight):
    deep, wide = NEAR * LANES, K // NEAR * LANES
    return pl.pallas_call(
        arrange_body,
        out_shape=(
            jax.ShapeDtypeStruct((deep, wide), bf16),
            jax.ShapeDtypeStruct((wide, deep), bf16),
        ),
        in_specs=[VMEM],
        out_specs=(VMEM, VMEM),
        compiler_params=params(),
        cost_estimate=cost(0, 12 << 20),
        name="arrange",
    )(pos_weight)


def encode_body(
    info_ref,
    audio_ref,
    conv_ref,
    chan_ref,
    proj_ref,
    feat_ref,
    tail_ref,
    head_ref,
    pair_ref,
    q_ref,
    slope_ref,
    m_ref,
    inv_ref,
    wide,
    proj,
    mid,
):
    slot = pl.program_id(0)

    @pl.when(slot == 0)
    def _():
        proj[...] = jnp.zeros_like(proj)
        proj[:, :GC] = proj_ref[...]

    living = alive(info_ref, slot)

    @pl.when(living)
    def _():
        for c in range(C // LANES):
            wide[c] = audio_ref[0, :, c * LANES : (c + 1) * LANES].astype(f32)
            for tap in range(2):
                at = tap * C + c * LANES
                pair_ref[0, :, at : at + LANES] = wide[c, pl.ds(tap, T, stride=2), :].astype(bf16)
        mid[...] = nn(pair_ref[0], conv_ref[...])
        bias, gain, shift = chan_ref[0:1, :], chan_ref[1:2, :], chan_ref[2:3, :]
        gain_two, shift_two = chan_ref[3:4, :], chan_ref[4:5, :]
        for at in range(0, T, CHUNK):
            rows = slice(at, at + CHUNK)
            conv = mid[rows, :] + bias
            offset = conv - jnp.mean(conv, axis=-1, keepdims=True)
            inverse = lax.rsqrt(jnp.mean(offset * offset, axis=-1, keepdims=True) + epsilon)
            q = offset * inverse
            pre = q * gain + shift
            below = phi(pre)
            encoded = (pre * below).astype(bf16).astype(f32)
            slope_ref[0, rows, :] = below + pre * bell(pre)
            q_ref[0, rows, :] = q
            offset = encoded - jnp.mean(encoded, axis=-1, keepdims=True)
            inverse_two = lax.rsqrt(jnp.mean(offset * offset, axis=-1, keepdims=True) + epsilon)
            m = offset * inverse_two
            m_ref[0, rows, :] = m
            inv_ref[0, rows, :] = jnp.concatenate(
                [
                    jnp.broadcast_to(inverse, (CHUNK, LANES)),
                    jnp.broadcast_to(inverse_two, (CHUNK, LANES)),
                ],
                axis=1,
            )
            normed = (m * gain_two + shift_two).astype(bf16)
            projected = nn(normed, proj[...])
            mask = row_mask(info_ref, slot, at, CHUNK)
            feat_ref[0, rows, :] = jnp.where(mask, projected, 0.0).astype(bf16)

    @pl.when(jnp.logical_not(living))
    def _():
        feat_ref[...] = jnp.zeros_like(feat_ref)

    tail_ref[0] = feat_ref[0, T - REACH :, :]
    head_ref[0] = feat_ref[0, :REACH, :]


def by_slot(*dims):
    return pl.BlockSpec((1,) + dims, lambda s: (s,) + (0,) * len(dims))


def whole(*dims):
    return pl.BlockSpec(dims, lambda s: (0,) * len(dims))


def encode(info, audio, conv_weight, channels, proj_weight):
    return pl.pallas_call(
        encode_body,
        grid=(SLOTS,),
        out_shape=(
            jax.ShapeDtypeStruct((SLOTS, T, LANES), bf16),
            jax.ShapeDtypeStruct((SLOTS, REACH, LANES), bf16),
            jax.ShapeDtypeStruct((SLOTS, REACH, LANES), bf16),
            jax.ShapeDtypeStruct((SLOTS, T, 2 * C), bf16),
            jax.ShapeDtypeStruct((SLOTS, T, C), f32),
            jax.ShapeDtypeStruct((SLOTS, T, C), f32),
            jax.ShapeDtypeStruct((SLOTS, T, C), f32),
            jax.ShapeDtypeStruct((SLOTS, T, 2 * LANES), f32),
        ),
        in_specs=[
            SMEM,
            by_slot(2 * T, C),
            whole(2 * C, C),
            whole(8, C),
            whole(C, GC),
        ],
        out_specs=(
            by_slot(T, LANES),
            by_slot(REACH, LANES),
            by_slot(REACH, LANES),
            by_slot(T, 2 * C),
            by_slot(T, C),
            by_slot(T, C),
            by_slot(T, C),
            by_slot(T, 2 * LANES),
        ),
        scratch_shapes=[
            pltpu.VMEM((C // LANES, 2 * T, LANES), f32),
            pltpu.VMEM((C, LANES), bf16),
            pltpu.VMEM((T, C), f32),
        ],
        compiler_params=params(),
        cost_estimate=cost(2 * SLOTS * T * C * (2 * C + LANES), 8 << 20, SLOTS * T * C * 2),
        name="encode",
    )(info, audio, conv_weight, channels, proj_weight)


def fill_ext(ext, low, own, high):
    ext[:REACH, :] = low.astype(f32)
    ext[REACH : REACH + T, :] = own.astype(f32)
    ext[REACH + T :, :] = high.astype(f32)


def fill_windows(windows, ext, first):
    rows = T + NEAR * (K // NEAR - 1)
    for r in range(NEAR):
        take = min(rows, EXT - first - r)
        windows[:take, r * LANES : (r + 1) * LANES] = ext[
            first + r : first + r + take, :
        ].astype(bf16)


def gathered(group):
    total = group[:T, :LANES]
    for p in range(1, PER_GROUP):
        total += group[NEAR * p : NEAR * p + T, p * LANES : (p + 1) * LANES]
    return total


def mix_body(
    info_ref,
    feat_ref,
    low_ref,
    high_ref,
    weight_ref,
    cot_ref,
    recv_ref,
    states_ref,
    slopes_ref,
    tail_ref,
    head_ref,
    ext,
    windows,
    back,
):
    slot = pl.program_id(0)
    living = alive(info_ref, slot)
    wide = PER_GROUP * LANES

    @pl.when(living)
    def _():
        own = feat_ref[0]
        fill_ext(ext, low_ref[0], own, high_ref[0])
        fill_windows(windows, ext, 0)
        back[...] = jnp.zeros_like(back)
        picked = info_ref[1] == slot
        back[:, :GC] = jnp.where(
            picked, recv_ref[...].astype(f32), cot_ref[0].astype(f32)
        )
        group = jnp.zeros((SPAN, wide), f32)
        for g in range(GROUPS):
            at = g * NEAR * PER_GROUP
            group += nn(windows[at : at + SPAN, :], weight_ref[:, g * wide : (g + 1) * wide])
        mixed = gathered(group)
        below = phi(mixed)
        mask = row_mask(info_ref, slot, 0, T)
        states = jnp.where(mask, own.astype(f32) + mixed * below, 0.0)
        states_ref[0] = states[:, :GC].astype(bf16)
        slopes = jnp.where(mask, back[...] * (below + mixed * bell(mixed)), 0.0)
        slopes_ref[0] = slopes.astype(bf16)

    @pl.when(jnp.logical_not(living))
    def _():
        states_ref[...] = jnp.zeros_like(states_ref)
        slopes_ref[...] = jnp.zeros_like(slopes_ref)

    tail_ref[0] = slopes_ref[0, T - REACH :, :]
    head_ref[0] = slopes_ref[0, :REACH, :]


def mix(info, features, low, high, weight, cotangent, received):
    return pl.pallas_call(
        mix_body,
        grid=(SLOTS,),
        out_shape=(
            jax.ShapeDtypeStruct((SLOTS, T, GC), bf16),
            jax.ShapeDtypeStruct((SLOTS, T, LANES), bf16),
            jax.ShapeDtypeStruct((SLOTS, REACH, LANES), bf16),
            jax.ShapeDtypeStruct((SLOTS, REACH, LANES), bf16),
        ),
        in_specs=[
            SMEM,
            by_slot(T, LANES),
            by_slot(REACH, LANES),
            by_slot(REACH, LANES),
            whole(*weight.shape),
            by_slot(T, GC),
            whole(T, GC),
        ],
        out_specs=(
            by_slot(T, GC),
            by_slot(T, LANES),
            by_slot(REACH, LANES),
            by_slot(REACH, LANES),
        ),
        scratch_shapes=[
            pltpu.VMEM((EXT, LANES), f32),
            pltpu.VMEM((T + NEAR * (K // NEAR - 1), NEAR * LANES), bf16),
            pltpu.VMEM((T, LANES), f32),
        ],
        compiler_params=params(),
        cost_estimate=cost(2 * SLOTS * SPAN * K * LANES * LANES, 6 << 20, SLOTS * T * LANES * 2),
        name="mix",
    )(info, features, low, high, weight, cotangent, received)


def taps_body(scale, info_ref, feat_ref, low_ref, high_ref, slopes_ref, keep_ref, send_ref, ext, stack, spread):
    living = jnp.logical_or(alive(info_ref, 0), alive(info_ref, 1))
    first_core = info_ref[4] == 0

    @pl.when(living)
    def _():
        for slot in range(SLOTS):
            fill_ext(ext, low_ref[slot], feat_ref[slot], high_ref[slot])
            for g in range(GROUPS):
                at = g * NEAR * PER_GROUP
                for r in range(NEAR):
                    stack[
                        g, slot * SPAN : (slot + 1) * SPAN, r * LANES : (r + 1) * LANES
                    ] = ext[at + r : at + r + SPAN, :].astype(bf16)
        spread[...] = jnp.zeros_like(spread)
        for slot in range(SLOTS):
            for p in range(PER_GROUP):
                at = slot * SPAN + NEAR * p
                spread[at : at + T, p * LANES : (p + 1) * LANES] = slopes_ref[slot]
        turned = spread[...].T
        half = 8 * LANES
        for g in range(GROUPS):
            for far in range(2):
                sums = nn(turned, stack[g, :, far * half : (far + 1) * half]) * scale
                for p in range(PER_GROUP):
                    cell = 2 * (g * PER_GROUP + p) + far
                    for x in range(4):
                        rows = slice(p * LANES, (p + 1) * LANES)
                        even = sums[rows, x * LANES : (x + 1) * LANES]
                        odd = sums[rows, (x + 4) * LANES : (x + 5) * LANES]
                        keep = jnp.where(first_core, even, odd).astype(bf16)
                        send = jnp.where(first_core, odd, even).astype(bf16)
                        for y in range(2):
                            part = slice(y * REACH, (y + 1) * REACH)
                            keep_ref[y * 4 + x, cell] = keep[part, :]
                            send_ref[y * 4 + x, cell] = send[part, :]

    @pl.when(jnp.logical_not(living))
    def _():
        keep_ref[...] = jnp.zeros_like(keep_ref)
        send_ref[...] = jnp.zeros_like(send_ref)


def taps(scale, info, features, low, high, slopes):
    shape = jax.ShapeDtypeStruct((8, 16, REACH, LANES), bf16)
    return pl.pallas_call(
        functools.partial(taps_body, scale),
        out_shape=(shape, shape),
        in_specs=[SMEM] + [VMEM] * 4,
        out_specs=(VMEM, VMEM),
        scratch_shapes=[
            pltpu.VMEM((EXT, LANES), f32),
            pltpu.VMEM((GROUPS, SLOTS * SPAN, NEAR * LANES), bf16),
            pltpu.VMEM((SLOTS * SPAN, PER_GROUP * LANES), bf16),
        ],
        compiler_params=params(),
        cost_estimate=cost(2 * SLOTS * SPAN * K * LANES * LANES, 6 << 20),
        name="taps",
    )(info, features, low, high, slopes)


def backward_body(
    scale,
    info_ref,
    slopes_ref,
    low_ref,
    high_ref,
    cot_ref,
    recv_ref,
    weight_ref,
    pair_ref,
    q_ref,
    slope_ref,
    m_ref,
    inv_ref,
    conv_ref,
    chan_ref,
    proj_ref,
    audio_grad_ref,
    keep_ref,
    send_ref,
    ext,
    windows,
    proj,
    feat_grad,
    normed,
    mid,
    wide,
    conv_sum,
    proj_sum,
    chan_sum,
):
    slot = pl.program_id(0)
    living = alive(info_ref, slot)
    span = PER_GROUP * LANES

    @pl.when(slot == 0)
    def _():
        proj[...] = jnp.zeros_like(proj)
        proj[:, :GC] = proj_ref[...]
        conv_sum[...] = jnp.zeros_like(conv_sum)
        proj_sum[...] = jnp.zeros_like(proj_sum)
        chan_sum[...] = jnp.zeros_like(chan_sum)

    @pl.when(living)
    def _():
        fill_ext(ext, low_ref[0], slopes_ref[0], high_ref[0])
        fill_windows(windows, ext, 1)
        group = jnp.zeros((SPAN, span), f32)
        for g in range(GROUPS):
            at = g * NEAR * PER_GROUP
            group += nt(windows[at : at + SPAN, :], weight_ref[g * span : (g + 1) * span, :])
        spread = gathered(group)
        wide[0, :T, :] = jnp.zeros((T, LANES), f32)
        picked = info_ref[1] == slot
        wide[0, :T, :GC] = jnp.where(picked, recv_ref[...].astype(f32), cot_ref[0].astype(f32))
        mask = row_mask(info_ref, slot, 0, T)
        feat_grad[...] = jnp.where(mask, wide[0, :T, :] + spread, 0.0).astype(bf16)
        gain = chan_ref[1:2, :]
        gain_two, shift_two = chan_ref[3:4, :], chan_ref[4:5, :]
        mid[...] = nt(feat_grad[...], proj[...])
        for at in range(0, T, CHUNK):
            rows = slice(at, at + CHUNK)
            m = m_ref[0, rows, :]
            normed[rows, :] = (m * gain_two + shift_two).astype(bf16)
            normed_grad = mid[rows, :]
            chan_sum[24:32, :] += jnp.sum((normed_grad * m).reshape(-1, 8, C), axis=0)
            chan_sum[32:40, :] += jnp.sum(normed_grad.reshape(-1, 8, C), axis=0)
            scaled = normed_grad * gain_two
            first = jnp.mean(scaled, axis=-1, keepdims=True)
            second = jnp.mean(scaled * m, axis=-1, keepdims=True)
            inverse_two = inv_ref[0, rows, LANES : LANES + 1]
            pre_grad = inverse_two * (scaled - first - m * second) * slope_ref[0, rows, :]
            q = q_ref[0, rows, :]
            chan_sum[8:16, :] += jnp.sum((pre_grad * q).reshape(-1, 8, C), axis=0)
            chan_sum[16:24, :] += jnp.sum(pre_grad.reshape(-1, 8, C), axis=0)
            scaled = pre_grad * gain
            first = jnp.mean(scaled, axis=-1, keepdims=True)
            second = jnp.mean(scaled * q, axis=-1, keepdims=True)
            inverse = inv_ref[0, rows, 0:1]
            conv_grad = inverse * (scaled - first - q * second)
            chan_sum[0:8, :] += jnp.sum(conv_grad.reshape(-1, 8, C), axis=0)
            mid[rows, :] = conv_grad
        operand = mid[...].astype(bf16)
        for tap in range(2):
            rows = slice(tap * C, (tap + 1) * C)
            audio_grad = nt(operand, conv_ref[rows, :])
            for c in range(C // LANES):
                wide[c, pl.ds(tap, T, stride=2), :] = audio_grad[:, c * LANES : (c + 1) * LANES]
            conv_sum[rows, :] += tn(pair_ref[0, :, rows], operand)
        for c in range(C // LANES):
            audio_grad_ref[0, :, c * LANES : (c + 1) * LANES] = wide[c].astype(bf16)
        proj_sum[...] += tn(normed[...], feat_grad[...])

    @pl.when(jnp.logical_not(living))
    def _():
        audio_grad_ref[...] = jnp.zeros_like(audio_grad_ref)

    @pl.when(slot == SLOTS - 1)
    def _():
        first_core = info_ref[4] == 0
        for cell in range(16):
            for y in range(2):
                for x in range(4):
                    parts = []
                    for odd in range(2):
                        at = (2 * cell + odd) * 32 + y * 16
                        parts.append(conv_sum[at : at + 16, x * LANES : (x + 1) * LANES] * scale)
                    even, odd = parts
                    keep_ref[y * 4 + x, cell, :16, :] = jnp.where(first_core, even, odd).astype(bf16)
                    send_ref[y * 4 + x, cell, :16, :] = jnp.where(first_core, odd, even).astype(bf16)
            even = proj_sum[cell * 32 : cell * 32 + 16, :] * scale
            odd = proj_sum[cell * 32 + 16 : cell * 32 + 32, :] * scale
            keep_ref[0, cell, 16:, :] = jnp.where(first_core, even, odd).astype(bf16)
            send_ref[0, cell, 16:, :] = jnp.where(first_core, odd, even).astype(bf16)
            tile = slice(cell // 4 * LANES, (cell // 4 + 1) * LANES)
            lines = [
                jnp.sum(chan_sum[8 * n : 8 * n + 8, tile], axis=0, keepdims=True) * scale
                for n in range(5)
            ]
            block = jnp.concatenate(lines + [jnp.zeros((11, LANES), f32)], axis=0).astype(bf16)
            keep_ref[1, cell, 16:, :] = block
            send_ref[1, cell, 16:, :] = block
            for rest in range(2, 8):
                keep_ref[rest, cell, 16:, :] = jnp.zeros((16, LANES), bf16)
                send_ref[rest, cell, 16:, :] = jnp.zeros((16, LANES), bf16)


def backward(
    scale, info, slopes, low, high, cotangent, received, weight, stored, conv_weight, channels, proj_weight
):
    pair, q, slope, m, inv = stored
    shape = jax.ShapeDtypeStruct((8, 16, 32, LANES), bf16)
    return pl.pallas_call(
        functools.partial(backward_body, scale),
        grid=(SLOTS,),
        out_shape=(jax.ShapeDtypeStruct((SLOTS, 2 * T, C), bf16), shape, shape),
        in_specs=[
            SMEM,
            by_slot(T, LANES),
            by_slot(REACH, LANES),
            by_slot(REACH, LANES),
            by_slot(T, GC),
            whole(T, GC),
            whole(*weight.shape),
            by_slot(T, 2 * C),
            by_slot(T, C),
            by_slot(T, C),
            by_slot(T, C),
            by_slot(T, 2 * LANES),
            whole(2 * C, C),
            whole(8, C),
            whole(C, GC),
        ],
        out_specs=(by_slot(2 * T, C), whole(*shape.shape), whole(*shape.shape)),
        scratch_shapes=[
            pltpu.VMEM((EXT, LANES), f32),
            pltpu.VMEM((T + NEAR * (K // NEAR - 1), NEAR * LANES), bf16),
            pltpu.VMEM((C, LANES), bf16),
            pltpu.VMEM((T, LANES), bf16),
            pltpu.VMEM((T, C), bf16),
            pltpu.VMEM((T, C), f32),
            pltpu.VMEM((C // LANES, 2 * T, LANES), f32),
            pltpu.VMEM((2 * C, C), f32),
            pltpu.VMEM((C, LANES), f32),
            pltpu.VMEM((40, C), f32),
        ],
        compiler_params=params(),
        cost_estimate=cost(
            2 * SLOTS * (SPAN * K * LANES * LANES + T * C * (4 * C + 2 * LANES)), 14 << 20
        ),
        name="backward",
    )(
        info,
        slopes,
        low,
        high,
        cotangent,
        received,
        weight,
        pair,
        q,
        slope,
        m,
        inv,
        conv_weight,
        channels,
        proj_weight,
    )


def join_body(a_ref, b_ref, c_ref, d_ref, out_ref):
    out_ref[0, :, :REACH, :] = (a_ref[0].astype(f32) + b_ref[0].astype(f32)).astype(bf16)
    out_ref[0, :, REACH:, :] = (c_ref[0].astype(f32) + d_ref[0].astype(f32)).astype(bf16)


def join(a, b, c, d):
    rows = REACH + 32
    return pl.pallas_call(
        join_body,
        grid=(8,),
        out_shape=jax.ShapeDtypeStruct((8, 16, rows, LANES), bf16),
        in_specs=[by_slot(16, REACH, LANES)] * 2 + [by_slot(16, 32, LANES)] * 2,
        out_specs=by_slot(16, rows, LANES),
        compiler_params=params(),
        cost_estimate=cost(0, 10 << 20),
        name="join",
    )(a, b, c, d)


def total_body(in_ref, out_ref):
    total = in_ref[0].astype(f32)
    for n in range(1, in_ref.shape[0]):
        total += in_ref[n].astype(f32)
    out_ref[...] = total.astype(bf16)


def total(parts):
    return pl.pallas_call(
        total_body,
        out_shape=jax.ShapeDtypeStruct(parts.shape[1:], bf16),
        in_specs=[VMEM],
        out_specs=VMEM,
        compiler_params=params(),
        cost_estimate=cost(0, 2 * parts.size),
        name="total",
    )(parts)


def finish_body(info_ref, in_ref, pos_ref, conv_ref, proj_ref, chan_ref, turned):
    for x in range(4):
        block = jnp.concatenate(
            [in_ref[x, :REACH, :].astype(f32), in_ref[4 + x, :REACH, :].astype(f32)], axis=0
        ).T
        pos_ref[x] = block[:GC, :GC]
        for y in range(2):
            conv_ref[y * 16 : (y + 1) * 16, x * LANES : (x + 1) * LANES] = in_ref[
                y * 4 + x, REACH : REACH + 16, :
            ].astype(f32)
    proj_ref[...] = in_ref[0, REACH + 16 :, :].astype(f32)[:, :GC]
    lines = in_ref[1, REACH + 16 :, :].astype(f32)
    turned[...] = jnp.concatenate([lines] * 8, axis=0).T
    at = pl.multiple_of(lax.rem(info_ref[5], 8) * 16, 16)
    chan_ref[...] = turned[pl.ds(at, 16), :][:, :5]


def finish(info, cells):
    return pl.pallas_call(
        finish_body,
        out_shape=(
            jax.ShapeDtypeStruct((4, GC, GC), f32),
            jax.ShapeDtypeStruct((32, C), f32),
            jax.ShapeDtypeStruct((16, GC), f32),
            jax.ShapeDtypeStruct((16, 5), f32),
        ),
        in_specs=[SMEM, VMEM],
        out_specs=(VMEM,) * 4,
        scratch_shapes=[pltpu.VMEM((LANES, LANES), f32)],
        compiler_params=params(),
        name="finish",
    )(info, cells)


def neighbours(tail, head):
    count = lax.axis_size("mp")
    forward = [(i, i + 1) for i in range(count - 1)]
    backward_route = [(i + 1, i) for i in range(count - 1)]
    return lax.ppermute(tail, "mp", forward), lax.ppermute(head, "mp", backward_route)


def per_device(
    audio, lengths, moved_slots, conv_weight, channel_params, proj_weight, pos_weight, cotangent
):
    data_size = lax.axis_size("dp")
    model_size = lax.axis_size("mp")
    half = data_size // 2
    data_index = lax.axis_index("dp")
    model_index = lax.axis_index("mp")
    scale = (SLOTS * data_size * T * model_size) ** -0.5
    chosen = lax.dynamic_index_in_dim(moved_slots[:, 0], data_index % half, 0, keepdims=False)
    own = lax.dynamic_slice_in_dim(lengths, data_index * SLOTS, SLOTS)
    info = jnp.stack(
        [model_index * T, chosen, own[0], own[1], data_index % 2, data_index, 0, 0]
    ).astype(jnp.int32)
    swap = [(i, i ^ half) for i in range(data_size)]
    core_swap = [(i, i ^ 1) for i in range(data_size)]
    channels = jnp.pad(channel_params.T, ((0, 3), (0, 0)))

    def picked(rows):
        return lax.dynamic_index_in_dim(rows, chosen, 0, keepdims=False)

    received = lax.ppermute(picked(cotangent), "dp", swap)
    features, tail, head, *stored = encode(info, audio, conv_weight, channels, proj_weight)
    low, high = neighbours(tail, head)
    forward_weight, backward_weight = arrange(pos_weight)
    states, slopes, tail, head = mix(
        info, features, low, high, forward_weight, cotangent, received
    )
    slope_low, slope_high = neighbours(tail, head)
    other = lax.ppermute(picked(states), "dp", swap)
    pos_keep, pos_send = taps(scale, info, features, low, high, slopes)
    pos_recv = lax.ppermute(pos_send, "dp", core_swap)
    audio_grad, keep, send = backward(
        scale,
        info,
        slopes,
        slope_low,
        slope_high,
        cotangent,
        received,
        backward_weight,
        stored,
        conv_weight,
        channels,
        proj_weight,
    )
    recv = lax.ppermute(send, "dp", core_swap)
    moved = (jnp.arange(SLOTS) == chosen)[:, None, None]
    hidden = jnp.where(moved, other[None], states)
    cells = join(pos_keep, pos_recv, keep, recv)
    cells = total(lax.all_to_all(cells, "mp", 0, 0, tiled=True))
    groups = [list(range(bit, data_size, 2)) for bit in range(2)]
    cells = total(
        lax.all_to_all(cells, "dp", 0, 0, axis_index_groups=groups, tiled=True)
    )
    copies = jnp.broadcast_to(cells[None], (model_size,) + cells.shape)
    cells = lax.all_to_all(copies, "mp", 0, 0, tiled=True)
    return (hidden, audio_grad) + tuple(finish(info, cells))


def solution(mesh):
    return jax.shard_map(
        per_device,
        mesh=mesh,
        in_specs=(P("dp", "mp", None), P(), P(), P(), P(), P(), P(), P("dp", "mp", None)),
        out_specs=(
            P("dp", "mp", None),
            P("dp", "mp", None),
            P("dp", None, None),
            P("dp", None),
            P("dp", None),
            P("dp", None),
        ),
        check_vma=False,
    )
```

```python
import functools

import jax
import jax.numpy as jnp
from jax import lax
from jax.experimental import pallas as pl
from jax.experimental.pallas import tpu as pltpu
from jax.sharding import PartitionSpec as P

epsilon = 1e-05
root_half = 0.7071067811865476
density = 0.3989422804014327

SLOTS = 2
T = 256
C = 512
GC = 120
LANES = 128
K = 128
REACH = 64
EXT = T + 2 * REACH
NEAR = 16
GROUPS = 2
PER_GROUP = 4
SPAN = T + NEAR * (PER_GROUP - 1)
CHUNK = 32
MP = 8
DP = 32
X = 4
CELLS = 16
PIECE = 2 * T + REACH
REST = CELLS + 2
VMEM_LIMIT = 56 * 1024 * 1024

f32 = jnp.float32
bf16 = jnp.bfloat16

VMEM = pl.BlockSpec(memory_space=pltpu.VMEM)
SMEM = pl.BlockSpec(memory_space=pltpu.SMEM)


def params(**more):
    return pltpu.CompilerParams(vmem_limit_bytes=VMEM_LIMIT, **more)


def cost(flops, moved, trans=0):
    return pl.CostEstimate(flops=flops, bytes_accessed=moved, transcendentals=trans)


def phi(values):
    return 0.5 * (1.0 + lax.erf(values * root_half))


def bell(values):
    return jnp.exp(-0.5 * values * values) * density


def nt(a, b):
    return lax.dot_general(a, b, (((1,), (1,)), ((), ())), preferred_element_type=f32)


def tn(a, b):
    return lax.dot_general(a, b, (((0,), (0,)), ((), ())), preferred_element_type=f32)


def nn(a, b):
    return jnp.dot(a, b, preferred_element_type=f32)


class Place:
    def __init__(self, dev_ref, len_ref, mov_ref):
        self.data = dev_ref[0] // MP
        self.model = lax.rem(dev_ref[0], MP)
        self.x = lax.rem(self.model, X)
        self.y = self.model // X
        self.core = lax.rem(self.data, 2)
        self.cell = self.data // 2
        self.first = self.model * T
        self.lengths = len_ref
        self.chosen = mov_ref[lax.rem(self.data, DP // 2)]

    def length(self, slot):
        return self.lengths[self.data * SLOTS + slot]

    def alive(self, slot):
        return self.first < self.length(slot)

    def mask(self, slot):
        ids = self.first + lax.broadcasted_iota(jnp.int32, (T, 1), 0)
        return ids < self.length(slot)


def by_slot(*dims):
    return pl.BlockSpec((1,) + dims, lambda s: (s,) + (0,) * len(dims))


def whole(*dims):
    return pl.BlockSpec(dims, lambda s: (0,) * len(dims))


def encode_body(
    dev_ref,
    len_ref,
    mov_ref,
    audio_ref,
    conv_ref,
    chan_ref,
    proj_ref,
    feat_ref,
    tail_ref,
    head_ref,
    pair_ref,
    q_ref,
    slope_ref,
    m_ref,
    inv_ref,
    wide,
    proj,
    mid,
    normed,
):
    place = Place(dev_ref, len_ref, mov_ref)
    slot = pl.program_id(0)

    @pl.when(slot == 0)
    def _():
        proj[...] = jnp.zeros_like(proj)
        proj[:GC, :] = proj_ref[...]

    living = place.alive(slot)

    @pl.when(living)
    def _():
        for c in range(C // LANES):
            wide[c] = audio_ref[0, :, c * LANES : (c + 1) * LANES].astype(f32)
            for tap in range(2):
                at = tap * C + c * LANES
                pair_ref[0, :, at : at + LANES] = wide[c, pl.ds(tap, T, stride=2), :].astype(bf16)
        mid[...] = nn(pair_ref[0], conv_ref[...])
        bias, gain, shift = chan_ref[0:1, :], chan_ref[1:2, :], chan_ref[2:3, :]
        gain_two, shift_two = chan_ref[3:4, :], chan_ref[4:5, :]
        for at in range(0, T, CHUNK):
            rows = slice(at, at + CHUNK)
            conv = mid[rows, :] + bias
            offset = conv - jnp.mean(conv, axis=-1, keepdims=True)
            inverse = lax.rsqrt(jnp.mean(offset * offset, axis=-1, keepdims=True) + epsilon)
            q = offset * inverse
            pre = q * gain + shift
            below = phi(pre)
            encoded = (pre * below).astype(bf16).astype(f32)
            slope_ref[0, rows, :] = below + pre * bell(pre)
            q_ref[0, rows, :] = q
            offset = encoded - jnp.mean(encoded, axis=-1, keepdims=True)
            inverse_two = lax.rsqrt(jnp.mean(offset * offset, axis=-1, keepdims=True) + epsilon)
            m = offset * inverse_two
            m_ref[0, rows, :] = m
            inv_ref[0, rows, :] = jnp.concatenate(
                [
                    jnp.broadcast_to(inverse, (CHUNK, LANES)),
                    jnp.broadcast_to(inverse_two, (CHUNK, LANES)),
                ],
                axis=1,
            )
            normed[rows, :] = (m * gain_two + shift_two).astype(bf16)
        projected = nt(normed[...], proj[...])
        feat_ref[0] = jnp.where(place.mask(slot), projected, 0.0).astype(bf16)

    @pl.when(jnp.logical_not(living))
    def _():
        feat_ref[...] = jnp.zeros_like(feat_ref)

    tail_ref[0] = feat_ref[0, T - REACH :, :]
    head_ref[0] = feat_ref[0, :REACH, :]


def encode(place, audio, conv_weight, channels, proj):
    return pl.pallas_call(
        encode_body,
        grid=(SLOTS,),
        out_shape=(
            jax.ShapeDtypeStruct((SLOTS, T, LANES), bf16),
            jax.ShapeDtypeStruct((SLOTS, REACH, LANES), bf16),
            jax.ShapeDtypeStruct((SLOTS, REACH, LANES), bf16),
            jax.ShapeDtypeStruct((SLOTS, T, 2 * C), bf16),
            jax.ShapeDtypeStruct((SLOTS, T, C), f32),
            jax.ShapeDtypeStruct((SLOTS, T, C), f32),
            jax.ShapeDtypeStruct((SLOTS, T, C), f32),
            jax.ShapeDtypeStruct((SLOTS, T, 2 * LANES), f32),
        ),
        in_specs=[SMEM] * 3
        + [
            by_slot(2 * T, C),
            whole(2 * C, C),
            whole(5, C),
            whole(GC, C),
        ],
        out_specs=(
            by_slot(T, LANES),
            by_slot(REACH, LANES),
            by_slot(REACH, LANES),
            by_slot(T, 2 * C),
            by_slot(T, C),
            by_slot(T, C),
            by_slot(T, C),
            by_slot(T, 2 * LANES),
        ),
        scratch_shapes=[
            pltpu.VMEM((C // LANES, 2 * T, LANES), f32),
            pltpu.VMEM((LANES, C), bf16),
            pltpu.VMEM((T, C), f32),
            pltpu.VMEM((T, C), bf16),
        ],
        compiler_params=params(),
        cost_estimate=cost(2 * SLOTS * T * C * (2 * C + LANES), 8 << 20, SLOTS * T * C * 2),
        name="encode",
    )(*place, audio, conv_weight, channels, proj)


def fill_ext(ext, low, own, high):
    ext[:REACH, :] = low.astype(f32)
    ext[REACH : REACH + T, :] = own.astype(f32)
    ext[REACH + T :, :] = high.astype(f32)


def fill_windows(windows, ext, first):
    rows = T + NEAR * (K // NEAR - 1)
    for r in range(NEAR):
        windows[:, r * LANES : (r + 1) * LANES] = ext[first + r : first + r + rows, :].astype(bf16)


def gathered(group):
    total = group[:T, :LANES]
    for p in range(1, PER_GROUP):
        total += group[NEAR * p : NEAR * p + T, p * LANES : (p + 1) * LANES]
    return total


def fill_back(turned, place, slot, cot_ref, recv_ref):
    turned[GC:, :] = jnp.zeros((LANES - GC, T), f32)
    turned[:GC, :] = jnp.where(
        place.chosen == slot, recv_ref[0].astype(f32), cot_ref[0].astype(f32)
    )


def mix_body(
    dev_ref,
    len_ref,
    mov_ref,
    feat_ref,
    low_ref,
    high_ref,
    pos_ref,
    cot_ref,
    recv_ref,
    states_ref,
    sent_ref,
    slopes_ref,
    tail_ref,
    head_ref,
    piece_ref,
    ext,
    windows,
    turned,
    weight,
):
    place = Place(dev_ref, len_ref, mov_ref)
    slot = pl.program_id(0)
    living = place.alive(slot)
    wide = PER_GROUP * LANES

    @pl.when(slot == 0)
    def _():
        fill_weight(weight, pos_ref, True)

    @pl.when(living)
    def _():
        own = feat_ref[0]
        fill_ext(ext, low_ref[0], own, high_ref[0])
        fill_windows(windows, ext, 0)
        fill_back(turned, place, slot, cot_ref, recv_ref)
        back = turned[...].T
        group = jnp.zeros((SPAN, wide), f32)
        for g in range(GROUPS):
            at = g * NEAR * PER_GROUP
            group += nn(windows[at : at + SPAN, :], weight[:, g * wide : (g + 1) * wide])
        mixed = gathered(group)
        below = phi(mixed)
        mask = place.mask(slot)
        states = jnp.where(mask, own.astype(f32) + mixed * below, 0.0)
        states_ref[0] = states.T[:GC, :].astype(bf16)
        slopes = jnp.where(mask, back * (below + mixed * bell(mixed)), 0.0)
        slopes_ref[0] = slopes.astype(bf16)
        edge = jnp.where(place.x < X // 2, low_ref[0].astype(f32), high_ref[0].astype(f32))
        for copy in range(X):
            piece_ref[copy, 0, :T, :] = own
            piece_ref[copy, 0, T : T + REACH, :] = edge.astype(bf16)
            piece_ref[copy, 0, T + REACH :, :] = slopes.astype(bf16)

    @pl.when(jnp.logical_not(living))
    def _():
        states_ref[...] = jnp.zeros_like(states_ref)
        slopes_ref[...] = jnp.zeros_like(slopes_ref)
        piece_ref[...] = jnp.zeros_like(piece_ref)

    @pl.when(place.chosen == slot)
    def _():
        sent_ref[...] = states_ref[0]

    tail_ref[0] = slopes_ref[0, T - REACH :, :]
    head_ref[0] = slopes_ref[0, :REACH, :]


def fill_weight(weight, pos_ref, ahead):
    size = LANES
    for q in range(K // NEAR):
        for r in range(NEAR):
            tap = q * NEAR + r
            if ahead:
                weight[r * size : (r + 1) * size, q * size : (q + 1) * size] = pos_ref[tap]
            else:
                weight[q * size : (q + 1) * size, r * size : (r + 1) * size] = pos_ref[K - 1 - tap]


def mix(place, features, low, high, pos, cotangent, received):
    return pl.pallas_call(
        mix_body,
        grid=(SLOTS,),
        out_shape=(
            jax.ShapeDtypeStruct((SLOTS, GC, T), bf16),
            jax.ShapeDtypeStruct((GC, T), bf16),
            jax.ShapeDtypeStruct((SLOTS, T, LANES), bf16),
            jax.ShapeDtypeStruct((SLOTS, REACH, LANES), bf16),
            jax.ShapeDtypeStruct((SLOTS, REACH, LANES), bf16),
            jax.ShapeDtypeStruct((X, SLOTS, PIECE, LANES), bf16),
        ),
        in_specs=[SMEM] * 3
        + [
            by_slot(T, LANES),
            by_slot(REACH, LANES),
            by_slot(REACH, LANES),
            whole(K, LANES, LANES),
            by_slot(GC, T),
            by_slot(GC, T),
        ],
        out_specs=(
            by_slot(GC, T),
            whole(GC, T),
            by_slot(T, LANES),
            by_slot(REACH, LANES),
            by_slot(REACH, LANES),
            pl.BlockSpec((X, 1, PIECE, LANES), lambda s: (0, s, 0, 0)),
        ),
        scratch_shapes=[
            pltpu.VMEM((EXT, LANES), f32),
            pltpu.VMEM((T + NEAR * (K // NEAR - 1), NEAR * LANES), bf16),
            pltpu.VMEM((LANES, T), f32),
            pltpu.VMEM((NEAR * LANES, K // NEAR * LANES), bf16),
        ],
        compiler_params=params(),
        cost_estimate=cost(2 * SLOTS * SPAN * K * LANES * LANES, 7 << 20, SLOTS * T * LANES * 2),
        name="mix",
    )(*place, features, low, high, pos, cotangent, received)


def taps_body(
    scale, dev_ref, len_ref, mov_ref, piece_ref, keep_ref, send_ref, ext, windows, turned, sums
):
    place = Place(dev_ref, len_ref, mov_ref)
    slot = pl.program_id(0)
    spread = X * T
    rows = spread + NEAR * (K // NEAR - 1)

    @pl.when(slot == 0)
    def _():
        sums[...] = jnp.zeros_like(sums)

    @pl.when(place.y * spread < place.length(slot))
    def _():
        ext[:REACH, :] = piece_ref[0, 0, T : T + REACH, :].astype(f32)
        ext[REACH + spread :, :] = piece_ref[X - 1, 0, T : T + REACH, :].astype(f32)
        for x in range(X):
            ext[REACH + x * T : REACH + (x + 1) * T, :] = piece_ref[x, 0, :T, :].astype(f32)
            turned[:, x * T : (x + 1) * T] = (
                piece_ref[x, 0, T + REACH :, :].astype(f32).T.astype(bf16)
            )
        for j in range(4):
            windows[:, j * LANES : (j + 1) * LANES] = ext[
                pl.ds(place.x + 4 * j, rows), :
            ].astype(bf16)
        for q in range(K // NEAR):
            sums[q] += nn(turned[...], windows[q * NEAR : q * NEAR + spread, :])

    @pl.when(slot == SLOTS - 1)
    def _():
        first_core = place.core == 0
        for q in range(K // NEAR):
            for far in range(2):
                even = sums[q, :, (2 * far) * LANES : (2 * far + 1) * LANES] * scale
                odd = sums[q, :, (2 * far + 1) * LANES : (2 * far + 2) * LANES] * scale
                keep = jnp.where(first_core, even, odd).astype(bf16)
                send = jnp.where(first_core, odd, even).astype(bf16)
                for y in range(2):
                    keep_ref[y, 2 * q + far] = keep[y * REACH : (y + 1) * REACH, :]
                    send_ref[y, 2 * q + far] = send[y * REACH : (y + 1) * REACH, :]


def taps(scale, place, pieces):
    shape = jax.ShapeDtypeStruct((2, CELLS, REACH, LANES), bf16)
    spread = X * T
    return pl.pallas_call(
        functools.partial(taps_body, scale),
        grid=(SLOTS,),
        out_shape=(shape, shape),
        in_specs=[SMEM] * 3 + [pl.BlockSpec((X, 1, PIECE, LANES), lambda s: (0, s, 0, 0))],
        out_specs=(whole(*shape.shape), whole(*shape.shape)),
        scratch_shapes=[
            pltpu.VMEM((spread + 2 * REACH, LANES), f32),
            pltpu.VMEM((spread + NEAR * (K // NEAR - 1), 4 * LANES), bf16),
            pltpu.VMEM((LANES, spread), bf16),
            pltpu.VMEM((K // NEAR, LANES, 4 * LANES), f32),
        ],
        compiler_params=params(),
        cost_estimate=cost(2 * SLOTS * SPAN * K * LANES * LANES, 4 << 20),
        name="taps",
    )(*place, pieces)


def backward_body(
    scale,
    dev_ref,
    len_ref,
    mov_ref,
    slopes_ref,
    low_ref,
    high_ref,
    cot_ref,
    recv_ref,
    pos_ref,
    pair_ref,
    q_ref,
    slope_ref,
    m_ref,
    inv_ref,
    conv_ref,
    chan_ref,
    proj_ref,
    audio_grad_ref,
    keep_ref,
    send_ref,
    ext,
    windows,
    turned,
    weight,
    proj,
    feat_grad,
    normed,
    mid,
    wide,
    conv_sum,
    proj_sum,
    chan_sum,
    columns,
):
    place = Place(dev_ref, len_ref, mov_ref)
    slot = pl.program_id(0)
    living = place.alive(slot)
    span = PER_GROUP * LANES

    @pl.when(slot == 0)
    def _():
        fill_weight(weight, pos_ref, False)
        proj[...] = jnp.zeros_like(proj)
        proj[:GC, :] = proj_ref[...]
        conv_sum[...] = jnp.zeros_like(conv_sum)
        proj_sum[...] = jnp.zeros_like(proj_sum)
        chan_sum[...] = jnp.zeros_like(chan_sum)

    @pl.when(living)
    def _():
        fill_ext(ext, low_ref[0], slopes_ref[0], high_ref[0])
        fill_windows(windows, ext, 1)
        fill_back(turned, place, slot, cot_ref, recv_ref)
        group = jnp.zeros((SPAN, span), f32)
        for g in range(GROUPS):
            at = g * NEAR * PER_GROUP
            group += nt(windows[at : at + SPAN, :], weight[g * span : (g + 1) * span, :])
        spread = gathered(group)
        feat_grad[...] = jnp.where(place.mask(slot), turned[...].T + spread, 0.0).astype(bf16)
        gain = chan_ref[1:2, :]
        gain_two, shift_two = chan_ref[3:4, :], chan_ref[4:5, :]
        mid[...] = nn(feat_grad[...], proj[...])
        for at in range(0, T, CHUNK):
            rows = slice(at, at + CHUNK)
            m = m_ref[0, rows, :]
            normed[rows, :] = (m * gain_two + shift_two).astype(bf16)
            normed_grad = mid[rows, :]
            chan_sum[24:32, :] += jnp.sum((normed_grad * m).reshape(-1, 8, C), axis=0)
            chan_sum[32:40, :] += jnp.sum(normed_grad.reshape(-1, 8, C), axis=0)
            scaled = normed_grad * gain_two
            first = jnp.mean(scaled, axis=-1, keepdims=True)
            second = jnp.mean(scaled * m, axis=-1, keepdims=True)
            inverse_two = inv_ref[0, rows, LANES : LANES + 1]
            pre_grad = inverse_two * (scaled - first - m * second) * slope_ref[0, rows, :]
            q = q_ref[0, rows, :]
            chan_sum[8:16, :] += jnp.sum((pre_grad * q).reshape(-1, 8, C), axis=0)
            chan_sum[16:24, :] += jnp.sum(pre_grad.reshape(-1, 8, C), axis=0)
            scaled = pre_grad * gain
            first = jnp.mean(scaled, axis=-1, keepdims=True)
            second = jnp.mean(scaled * q, axis=-1, keepdims=True)
            inverse = inv_ref[0, rows, 0:1]
            conv_grad = inverse * (scaled - first - q * second)
            chan_sum[0:8, :] += jnp.sum(conv_grad.reshape(-1, 8, C), axis=0)
            mid[rows, :] = conv_grad
        operand = mid[...].astype(bf16)
        for tap in range(2):
            rows = slice(tap * C, (tap + 1) * C)
            audio_grad = nt(operand, conv_ref[rows, :])
            for c in range(C // LANES):
                wide[c, pl.ds(tap, T, stride=2), :] = audio_grad[:, c * LANES : (c + 1) * LANES]
            conv_sum[rows, :] += tn(pair_ref[0, :, rows], operand)
        for c in range(C // LANES):
            audio_grad_ref[0, :, c * LANES : (c + 1) * LANES] = wide[c].astype(bf16)
        proj_sum[...] += tn(normed[...], feat_grad[...])

    @pl.when(jnp.logical_not(living))
    def _():
        audio_grad_ref[...] = jnp.zeros_like(audio_grad_ref)

    @pl.when(slot == SLOTS - 1)
    def _():
        first_core = place.core == 0
        columns[...] = jnp.zeros_like(columns)
        for n in range(5):
            columns[GC + n : GC + n + 1, :] = jnp.sum(
                chan_sum[8 * n : 8 * n + 8, :], axis=0, keepdims=True
            )
        proj_sum[...] += columns[...].T
        keep_ref[:, CELLS:, :, :] = jnp.zeros((MP, 2, 16, LANES), bf16)
        send_ref[:, CELLS:, :, :] = jnp.zeros((MP, 2, 16, LANES), bf16)

        def put(at, cell, even, odd):
            keep_ref[at, cell] = (jnp.where(first_core, even, odd) * scale).astype(bf16)
            send_ref[at, cell] = (jnp.where(first_core, odd, even) * scale).astype(bf16)

        for cell in range(CELLS):
            for y in range(2):
                for x in range(X):
                    at = 2 * cell * 32 + y * 16
                    lanes = slice(x * LANES, (x + 1) * LANES)
                    put(
                        y * X + x,
                        cell,
                        conv_sum[at : at + 16, lanes],
                        conv_sum[at + 32 : at + 48, lanes],
                    )
            at = cell * 32
            put(
                cell // 2,
                CELLS + cell % 2,
                proj_sum[at : at + 16, :],
                proj_sum[at + 16 : at + 32, :],
            )


def backward(
    scale, place, slopes, low, high, cotangent, received, pos, stored, conv_weight, channels, proj
):
    shape = jax.ShapeDtypeStruct((MP, REST, 16, LANES), bf16)
    return pl.pallas_call(
        functools.partial(backward_body, scale),
        grid=(SLOTS,),
        out_shape=(jax.ShapeDtypeStruct((SLOTS, 2 * T, C), bf16), shape, shape),
        in_specs=[SMEM] * 3
        + [
            by_slot(T, LANES),
            by_slot(REACH, LANES),
            by_slot(REACH, LANES),
            by_slot(GC, T),
            by_slot(GC, T),
            whole(K, LANES, LANES),
            by_slot(T, 2 * C),
            by_slot(T, C),
            by_slot(T, C),
            by_slot(T, C),
            by_slot(T, 2 * LANES),
            whole(2 * C, C),
            whole(5, C),
            whole(GC, C),
        ],
        out_specs=(by_slot(2 * T, C), whole(*shape.shape), whole(*shape.shape)),
        scratch_shapes=[
            pltpu.VMEM((EXT, LANES), f32),
            pltpu.VMEM((T + NEAR * (K // NEAR - 1), NEAR * LANES), bf16),
            pltpu.VMEM((LANES, T), f32),
            pltpu.VMEM((K // NEAR * LANES, NEAR * LANES), bf16),
            pltpu.VMEM((LANES, C), bf16),
            pltpu.VMEM((T, LANES), bf16),
            pltpu.VMEM((T, C), bf16),
            pltpu.VMEM((T, C), f32),
            pltpu.VMEM((C // LANES, 2 * T, LANES), f32),
            pltpu.VMEM((2 * C, C), f32),
            pltpu.VMEM((C, LANES), f32),
            pltpu.VMEM((40, C), f32),
            pltpu.VMEM((LANES, C), f32),
        ],
        compiler_params=params(),
        cost_estimate=cost(
            2 * SLOTS * (SPAN * K * LANES * LANES + T * C * (4 * C + 2 * LANES)), 14 << 20
        ),
        name="backward",
    )(
        *place,
        slopes,
        low,
        high,
        cotangent,
        received,
        pos,
        *stored,
        conv_weight,
        channels,
        proj,
    )


def cells_body(dev_ref, kept_ref, recv_ref, rest_ref, out_ref):
    model = lax.rem(dev_ref[0], MP)
    out_ref[:, :REACH, :] = (kept_ref[...].astype(f32) + recv_ref[...].astype(f32)).astype(bf16)
    rest = rest_ref[0].astype(f32)
    for n in range(1, MP):
        rest += rest_ref[n].astype(f32)
    out_ref[:, REACH : REACH + 16, :] = rest[:CELLS].astype(bf16)
    for cell in range(CELLS):
        small = jnp.where(model == cell // 2, rest[CELLS + cell % 2], 0.0)
        out_ref[cell, REACH + 16 :, :] = small.astype(bf16)


def make_cells(dev, kept, received, rest):
    return pl.pallas_call(
        cells_body,
        out_shape=jax.ShapeDtypeStruct((CELLS, REACH + 32, LANES), bf16),
        in_specs=[SMEM] + [VMEM] * 3,
        out_specs=VMEM,
        compiler_params=params(),
        cost_estimate=cost(0, 2 << 20),
        name="cells",
    )(dev, kept, received, rest)


def total_body(in_ref, out_ref):
    total = in_ref[0].astype(f32)
    for n in range(1, in_ref.shape[0]):
        total += in_ref[n].astype(f32)
    for copy in range(MP):
        out_ref[copy] = total.astype(bf16)


def total(parts):
    return pl.pallas_call(
        total_body,
        out_shape=jax.ShapeDtypeStruct((MP,) + parts.shape[1:], bf16),
        in_specs=[VMEM],
        out_specs=VMEM,
        compiler_params=params(),
        cost_estimate=cost(0, 2 * parts.size),
        name="total",
    )(parts)


def finish_body(
    dev_ref,
    len_ref,
    mov_ref,
    in_ref,
    states_ref,
    other_ref,
    hidden_ref,
    pos_ref,
    conv_ref,
    proj_ref,
    chan_ref,
):
    place = Place(dev_ref, len_ref, mov_ref)
    for slot in range(SLOTS):
        hidden_ref[slot] = jnp.where(
            place.chosen == slot, other_ref[...].astype(f32), states_ref[slot].astype(f32)
        ).astype(bf16)
    for x in range(X):
        block = jnp.concatenate(
            [in_ref[x, :REACH, :].astype(f32), in_ref[X + x, :REACH, :].astype(f32)], axis=0
        ).T
        pos_ref[x] = block[:GC, :GC]
        for y in range(2):
            conv_ref[y * 16 : (y + 1) * 16, x * LANES : (x + 1) * LANES] = in_ref[
                y * X + x, REACH : REACH + 16, :
            ].astype(f32)
    small = in_ref[place.cell // 2, REACH + 16 :, :].astype(f32)
    proj_ref[...] = small[:, :GC]
    chan_ref[...] = jnp.concatenate([small] * 8, axis=0).T[GC : GC + 5, :16]


def finish(place, cells, states, other):
    return pl.pallas_call(
        finish_body,
        out_shape=(
            jax.ShapeDtypeStruct((SLOTS, GC, T), bf16),
            jax.ShapeDtypeStruct((4, GC, GC), f32),
            jax.ShapeDtypeStruct((32, C), f32),
            jax.ShapeDtypeStruct((16, GC), f32),
            jax.ShapeDtypeStruct((5, 16), f32),
        ),
        in_specs=[SMEM] * 3 + [VMEM] * 3,
        out_specs=(VMEM,) * 5,
        compiler_params=params(),
        name="finish",
    )(*place, cells, states, other)


def neighbours(tail, head):
    count = lax.axis_size("mp")
    forward = [(i, i + 1) for i in range(count - 1)]
    backward_route = [(i + 1, i) for i in range(count - 1)]
    return lax.ppermute(tail, "mp", forward), lax.ppermute(head, "mp", backward_route)


def added(a, b):
    return (a.astype(f32) + b.astype(f32)).astype(bf16)


def per_device(
    audio, lengths, moved_slots, conv_weight, channel_params, proj_weight, pos_weight, cotangent
):
    data_index = lax.axis_index("dp")
    model_index = lax.axis_index("mp")
    scale = (SLOTS * DP * T * MP) ** -0.5
    dev = (data_index * MP + model_index).astype(jnp.int32).reshape(1)
    place = (dev, lengths, moved_slots.reshape(-1))
    swap = [(i, i ^ (DP // 2)) for i in range(DP)]
    core_swap = [(i, i ^ 1) for i in range(DP)]
    channels = channel_params.T
    proj = proj_weight.T
    cot = cotangent.transpose(0, 2, 1)
    pos = jnp.pad(pos_weight, ((0, 0), (0, LANES - GC), (0, LANES - GC)))

    received = lax.ppermute(cot, "dp", swap)
    features, tail, head, *stored = encode(place, audio, conv_weight, channels, proj)
    low, high = neighbours(tail, head)
    states, sent, slopes, tail, head, pieces = mix(
        place, features, low, high, pos, cot, received
    )
    slope_low, slope_high = neighbours(tail, head)
    rows = [list(range(X)), list(range(X, 2 * X))]
    pieces = lax.all_to_all(pieces, "mp", 0, 0, axis_index_groups=rows, tiled=True)
    other = lax.ppermute(sent, "dp", swap)
    audio_grad, keep, send = backward(
        scale,
        place,
        slopes,
        slope_low,
        slope_high,
        cot,
        received,
        pos,
        stored,
        conv_weight,
        channels,
        proj,
    )
    rest = added(keep, lax.ppermute(send, "dp", core_swap))
    pos_keep, pos_send = taps(scale, place, pieces)
    rest = lax.all_to_all(rest, "mp", 0, 0, tiled=True)
    pos_sum = added(pos_keep, lax.ppermute(pos_send, "dp", core_swap))
    low_half = model_index < X
    kept = jnp.where(low_half, pos_sum[0], pos_sum[1])
    leaving = jnp.where(low_half, pos_sum[1], pos_sum[0])
    coming = lax.ppermute(leaving, "mp", [(i, i ^ X) for i in range(MP)])
    cells = make_cells(dev, kept, coming, rest)
    groups = [list(range(bit, DP, 2)) for bit in range(2)]
    cells = lax.all_to_all(cells, "dp", 0, 0, axis_index_groups=groups, tiled=True)
    cells = lax.all_to_all(total(cells), "mp", 0, 0, tiled=True)
    hidden, grad_pos, grad_conv, grad_proj, grad_channels = finish(place, cells, states, other)
    return (
        hidden.transpose(0, 2, 1),
        audio_grad,
        grad_pos,
        grad_conv,
        grad_proj,
        grad_channels.T,
    )


def solution(mesh):
    return jax.shard_map(
        per_device,
        mesh=mesh,
        in_specs=(P("dp", "mp", None), P(), P(), P(), P(), P(), P(), P("dp", "mp", None)),
        out_specs=(
            P("dp", "mp", None),
            P("dp", "mp", None),
            P("dp", None, None),
            P("dp", None),
            P("dp", None),
            P("dp", None),
        ),
        check_vma=False,
    )
```

```python
import functools

import jax
import jax.numpy as jnp
from jax import lax
from jax.experimental import pallas as pl
from jax.experimental.pallas import tpu as pltpu
from jax.sharding import PartitionSpec as P

epsilon = 1e-05
root_half = 0.7071067811865476
density = 0.3989422804014327

SLOTS = 2
T = 256
C = 512
GC = 120
LANES = 128
K = 128
REACH = 64
EXT = T + 2 * REACH
NEAR = 16
GROUPS = 2
PER_GROUP = 4
SPAN = T + NEAR * (PER_GROUP - 1)
CHUNK = 32
MP = 8
DP = 32
X = 4
CELLS = 16
PIECE = 2 * T + REACH
REST = CELLS + 2

f32 = jnp.float32
bf16 = jnp.bfloat16

VMEM = pl.BlockSpec(memory_space=pltpu.VMEM)
SMEM = pl.BlockSpec(memory_space=pltpu.SMEM)


def params(mebibytes):
    return pltpu.CompilerParams(vmem_limit_bytes=mebibytes << 20)


def cost(flops, moved, trans=0):
    return pl.CostEstimate(flops=flops, bytes_accessed=moved, transcendentals=trans)


def phi(values):
    return 0.5 * (1.0 + lax.erf(values * root_half))


def bell(values):
    return jnp.exp(-0.5 * values * values) * density


def nt(a, b):
    return lax.dot_general(a, b, (((1,), (1,)), ((), ())), preferred_element_type=f32)


def tn(a, b):
    return lax.dot_general(a, b, (((0,), (0,)), ((), ())), preferred_element_type=f32)


def nn(a, b):
    return jnp.dot(a, b, preferred_element_type=f32)


class Place:
    def __init__(self, dev_ref, len_ref, mov_ref):
        self.data = dev_ref[0] // MP
        self.model = lax.rem(dev_ref[0], MP)
        self.x = lax.rem(self.model, X)
        self.y = self.model // X
        self.core = lax.rem(self.data, 2)
        self.cell = self.data // 2
        self.first = self.model * T
        self.lengths = len_ref
        self.chosen = mov_ref[lax.rem(self.data, DP // 2)]

    def length(self, slot):
        return self.lengths[self.data * SLOTS + slot]

    def alive(self, slot):
        return self.first < self.length(slot)

    def mask(self, slot):
        ids = self.first + lax.broadcasted_iota(jnp.int32, (T, 1), 0)
        return ids < self.length(slot)


def by_slot(*dims):
    return pl.BlockSpec((1,) + dims, lambda s: (s,) + (0,) * len(dims))


def whole(*dims):
    return pl.BlockSpec(dims, lambda s: (0,) * len(dims))


def once(*dims):
    return pl.BlockSpec(dims, lambda s: (0,) * len(dims), pipeline_mode=pl.Buffered(1))


def turn_body(in_ref, ahead_ref, behind_ref, rows):
    block = pl.program_id(0)
    blocks = pl.num_programs(0)
    for n in range(NEAR):
        tile = jnp.concatenate(
            [in_ref[n].astype(f32), jnp.zeros((LANES - GC, K), f32)], axis=0
        ).T
        if n >= GC % NEAR:
            tile = jnp.where(block == blocks - 1, 0.0, tile)
        rows[pl.ds(n, K, stride=NEAR), :] = tile
    far = K // NEAR
    for q in range(far):
        for r in range(NEAR):
            at = (q * NEAR + r) * NEAR
            tile = rows[at : at + NEAR, :].astype(bf16)
            ahead_ref[r, :, q * LANES : (q + 1) * LANES] = tile
            r_back = NEAR - 1 - r
            behind_ref[far - 1 - q, :, r_back * LANES : (r_back + 1) * LANES] = tile


def turn(pos):
    far = K // NEAR
    ahead, behind = pl.pallas_call(
        turn_body,
        grid=(LANES // NEAR,),
        out_shape=(
            jax.ShapeDtypeStruct((NEAR, LANES, far * LANES), bf16),
            jax.ShapeDtypeStruct((far, LANES, NEAR * LANES), bf16),
        ),
        in_specs=[pl.BlockSpec((NEAR, GC, K), lambda b: (b, 0, 0))],
        out_specs=(
            pl.BlockSpec((NEAR, NEAR, far * LANES), lambda b: (0, b, 0)),
            pl.BlockSpec((far, NEAR, NEAR * LANES), lambda b: (0, b, 0)),
        ),
        scratch_shapes=[pltpu.VMEM((K * NEAR, LANES), f32)],
        compiler_params=params(10),
        cost_estimate=cost(0, 12 << 20),
        name="turn",
    )(pos)
    return ahead.reshape(NEAR * LANES, -1), behind.reshape(far * LANES, -1)


def encode_body(
    dev_ref,
    len_ref,
    mov_ref,
    audio_ref,
    conv_ref,
    chan_ref,
    proj_ref,
    feat_ref,
    tail_ref,
    head_ref,
    pair_ref,
    q_ref,
    slope_ref,
    m_ref,
    inv_ref,
    wide,
    proj,
    mid,
    normed,
):
    place = Place(dev_ref, len_ref, mov_ref)
    slot = pl.program_id(0)

    @pl.when(slot == 0)
    def _():
        proj[...] = jnp.zeros_like(proj)
        proj[:GC, :] = proj_ref[...]

    living = place.alive(slot)

    @pl.when(living)
    def _():
        for c in range(C // LANES):
            wide[c] = audio_ref[0, :, c * LANES : (c + 1) * LANES].astype(f32)
            for tap in range(2):
                at = tap * C + c * LANES
                pair_ref[0, :, at : at + LANES] = wide[c, pl.ds(tap, T, stride=2), :].astype(bf16)
        mid[...] = nn(pair_ref[0], conv_ref[...])
        bias, gain, shift = chan_ref[0:1, :], chan_ref[1:2, :], chan_ref[2:3, :]
        gain_two, shift_two = chan_ref[3:4, :], chan_ref[4:5, :]
        for at in range(0, T, CHUNK):
            rows = slice(at, at + CHUNK)
            conv = mid[rows, :] + bias
            offset = conv - jnp.mean(conv, axis=-1, keepdims=True)
            inverse = lax.rsqrt(jnp.mean(offset * offset, axis=-1, keepdims=True) + epsilon)
            q = offset * inverse
            pre = q * gain + shift
            below = phi(pre)
            encoded = (pre * below).astype(bf16).astype(f32)
            slope_ref[0, rows, :] = (below + pre * bell(pre)).astype(bf16)
            q_ref[0, rows, :] = q.astype(bf16)
            offset = encoded - jnp.mean(encoded, axis=-1, keepdims=True)
            inverse_two = lax.rsqrt(jnp.mean(offset * offset, axis=-1, keepdims=True) + epsilon)
            m = offset * inverse_two
            m_ref[0, rows, :] = m.astype(bf16)
            inv_ref[0, rows, :] = jnp.concatenate(
                [
                    jnp.broadcast_to(inverse, (CHUNK, LANES)),
                    jnp.broadcast_to(inverse_two, (CHUNK, LANES)),
                ],
                axis=1,
            )
            normed[rows, :] = (m * gain_two + shift_two).astype(bf16)
        projected = nt(normed[...], proj[...])
        feat_ref[0] = jnp.where(place.mask(slot), projected, 0.0).astype(bf16)

    @pl.when(jnp.logical_not(living))
    def _():
        feat_ref[...] = jnp.zeros_like(feat_ref)

    tail_ref[0] = feat_ref[0, T - REACH :, :]
    head_ref[0] = feat_ref[0, :REACH, :]


def encode(place, audio, conv_weight, channels, proj):
    return pl.pallas_call(
        encode_body,
        grid=(SLOTS,),
        out_shape=(
            jax.ShapeDtypeStruct((SLOTS, T, LANES), bf16),
            jax.ShapeDtypeStruct((SLOTS, REACH, LANES), bf16),
            jax.ShapeDtypeStruct((SLOTS, REACH, LANES), bf16),
            jax.ShapeDtypeStruct((SLOTS, T, 2 * C), bf16),
            jax.ShapeDtypeStruct((SLOTS, T, C), bf16),
            jax.ShapeDtypeStruct((SLOTS, T, C), bf16),
            jax.ShapeDtypeStruct((SLOTS, T, C), bf16),
            jax.ShapeDtypeStruct((SLOTS, T, 2 * LANES), f32),
        ),
        in_specs=[SMEM] * 3
        + [
            by_slot(2 * T, C),
            once(2 * C, C),
            whole(5, C),
            whole(GC, C),
        ],
        out_specs=(
            by_slot(T, LANES),
            by_slot(REACH, LANES),
            by_slot(REACH, LANES),
            by_slot(T, 2 * C),
            by_slot(T, C),
            by_slot(T, C),
            by_slot(T, C),
            by_slot(T, 2 * LANES),
        ),
        scratch_shapes=[
            pltpu.VMEM((C // LANES, 2 * T, LANES), f32),
            pltpu.VMEM((LANES, C), bf16),
            pltpu.VMEM((T, C), f32),
            pltpu.VMEM((T, C), bf16),
        ],
        compiler_params=params(14),
        cost_estimate=cost(2 * SLOTS * T * C * (2 * C + LANES), 8 << 20, SLOTS * T * C * 2),
        name="encode",
    )(*place, audio, conv_weight, channels, proj)


def fill_ext(ext, low, own, high):
    ext[:REACH, :] = low.astype(f32)
    ext[REACH : REACH + T, :] = own.astype(f32)
    ext[REACH + T :, :] = high.astype(f32)


def fill_windows(windows, ext, first):
    rows = T + NEAR * (K // NEAR - 1)
    for r in range(NEAR):
        windows[:, r * LANES : (r + 1) * LANES] = ext[first + r : first + r + rows, :].astype(bf16)


def gathered(group):
    total = group[:T, :LANES]
    for p in range(1, PER_GROUP):
        total += group[NEAR * p : NEAR * p + T, p * LANES : (p + 1) * LANES]
    return total


def fill_back(turned, place, slot, cot_ref, recv_ref):
    turned[GC:, :] = jnp.zeros((LANES - GC, T), f32)
    turned[:GC, :] = jnp.where(
        place.chosen == slot, recv_ref[0].astype(f32), cot_ref[0].astype(f32)
    )


def mix_body(
    dev_ref,
    len_ref,
    mov_ref,
    feat_ref,
    low_ref,
    high_ref,
    weight,
    cot_ref,
    recv_ref,
    states_ref,
    sent_ref,
    slopes_ref,
    tail_ref,
    head_ref,
    piece_ref,
    ext,
    windows,
    turned,
):
    place = Place(dev_ref, len_ref, mov_ref)
    slot = pl.program_id(0)
    living = place.alive(slot)
    wide = PER_GROUP * LANES

    @pl.when(living)
    def _():
        own = feat_ref[0]
        fill_ext(ext, low_ref[0], own, high_ref[0])
        fill_windows(windows, ext, 0)
        fill_back(turned, place, slot, cot_ref, recv_ref)
        back = turned[...].T
        group = jnp.zeros((SPAN, wide), f32)
        for g in range(GROUPS):
            at = g * NEAR * PER_GROUP
            group += nn(windows[at : at + SPAN, :], weight[:, g * wide : (g + 1) * wide])
        mixed = gathered(group)
        below = phi(mixed)
        mask = place.mask(slot)
        states = jnp.where(mask, own.astype(f32) + mixed * below, 0.0)
        states_ref[0] = states.T[:GC, :].astype(bf16)
        slopes = jnp.where(mask, back * (below + mixed * bell(mixed)), 0.0)
        slopes_ref[0] = slopes.astype(bf16)
        edge = jnp.where(place.x < X // 2, low_ref[0].astype(f32), high_ref[0].astype(f32))
        for copy in range(X):
            piece_ref[copy, 0, :T, :] = own
            piece_ref[copy, 0, T : T + REACH, :] = edge.astype(bf16)
            piece_ref[copy, 0, T + REACH :, :] = slopes.astype(bf16)

    @pl.when(jnp.logical_not(living))
    def _():
        states_ref[...] = jnp.zeros_like(states_ref)
        slopes_ref[...] = jnp.zeros_like(slopes_ref)
        piece_ref[...] = jnp.zeros_like(piece_ref)

    @pl.when(place.chosen == slot)
    def _():
        sent_ref[...] = states_ref[0]

    tail_ref[0] = slopes_ref[0, T - REACH :, :]
    head_ref[0] = slopes_ref[0, :REACH, :]


def mix(place, features, low, high, weight, cotangent, received):
    return pl.pallas_call(
        mix_body,
        grid=(SLOTS,),
        out_shape=(
            jax.ShapeDtypeStruct((SLOTS, GC, T), bf16),
            jax.ShapeDtypeStruct((GC, T), bf16),
            jax.ShapeDtypeStruct((SLOTS, T, LANES), bf16),
            jax.ShapeDtypeStruct((SLOTS, REACH, LANES), bf16),
            jax.ShapeDtypeStruct((SLOTS, REACH, LANES), bf16),
            jax.ShapeDtypeStruct((X, SLOTS, PIECE, LANES), bf16),
        ),
        in_specs=[SMEM] * 3
        + [
            by_slot(T, LANES),
            by_slot(REACH, LANES),
            by_slot(REACH, LANES),
            once(*weight.shape),
            by_slot(GC, T),
            by_slot(GC, T),
        ],
        out_specs=(
            by_slot(GC, T),
            whole(GC, T),
            by_slot(T, LANES),
            by_slot(REACH, LANES),
            by_slot(REACH, LANES),
            pl.BlockSpec((X, 1, PIECE, LANES), lambda s: (0, s, 0, 0)),
        ),
        scratch_shapes=[
            pltpu.VMEM((EXT, LANES), f32),
            pltpu.VMEM((T + NEAR * (K // NEAR - 1), NEAR * LANES), bf16),
            pltpu.VMEM((LANES, T), f32),
        ],
        compiler_params=params(20),
        cost_estimate=cost(2 * SLOTS * SPAN * K * LANES * LANES, 7 << 20, SLOTS * T * LANES * 2),
        name="mix",
    )(*place, features, low, high, weight, cotangent, received)


def taps_body(
    scale, dev_ref, len_ref, mov_ref, piece_ref, keep_ref, send_ref, ext, windows, turned, sums
):
    place = Place(dev_ref, len_ref, mov_ref)
    slot = pl.program_id(0)
    spread = X * T
    rows = spread + NEAR * (K // NEAR - 1)

    @pl.when(slot == 0)
    def _():
        sums[...] = jnp.zeros_like(sums)

    @pl.when(place.y * spread < place.length(slot))
    def _():
        ext[:REACH, :] = piece_ref[0, 0, T : T + REACH, :].astype(f32)
        ext[REACH + spread :, :] = piece_ref[X - 1, 0, T : T + REACH, :].astype(f32)
        for x in range(X):
            ext[REACH + x * T : REACH + (x + 1) * T, :] = piece_ref[x, 0, :T, :].astype(f32)
            turned[:, x * T : (x + 1) * T] = (
                piece_ref[x, 0, T + REACH :, :].astype(f32).T.astype(bf16)
            )
        for j in range(4):
            windows[:, j * LANES : (j + 1) * LANES] = ext[
                pl.ds(place.x + 4 * j, rows), :
            ].astype(bf16)
        for q in range(K // NEAR):
            sums[q] += nn(turned[...], windows[q * NEAR : q * NEAR + spread, :])

    @pl.when(slot == SLOTS - 1)
    def _():
        first_core = place.core == 0
        for q in range(K // NEAR):
            for far in range(2):
                even = sums[q, :, (2 * far) * LANES : (2 * far + 1) * LANES] * scale
                odd = sums[q, :, (2 * far + 1) * LANES : (2 * far + 2) * LANES] * scale
                keep = jnp.where(first_core, even, odd).astype(bf16)
                send = jnp.where(first_core, odd, even).astype(bf16)
                for y in range(2):
                    keep_ref[2 * (2 * q + far) + y] = keep[y * REACH : (y + 1) * REACH, :]
                    send_ref[2 * (2 * q + far) + y] = send[y * REACH : (y + 1) * REACH, :]


def taps(scale, place, pieces):
    shape = jax.ShapeDtypeStruct((2 * CELLS, REACH, LANES), bf16)
    spread = X * T
    return pl.pallas_call(
        functools.partial(taps_body, scale),
        grid=(SLOTS,),
        out_shape=(shape, shape),
        in_specs=[SMEM] * 3 + [pl.BlockSpec((X, 1, PIECE, LANES), lambda s: (0, s, 0, 0))],
        out_specs=(whole(*shape.shape), whole(*shape.shape)),
        scratch_shapes=[
            pltpu.VMEM((spread + 2 * REACH, LANES), f32),
            pltpu.VMEM((spread + NEAR * (K // NEAR - 1), 4 * LANES), bf16),
            pltpu.VMEM((LANES, spread), bf16),
            pltpu.VMEM((K // NEAR, LANES, 4 * LANES), f32),
        ],
        compiler_params=params(16),
        cost_estimate=cost(2 * SLOTS * SPAN * K * LANES * LANES, 4 << 20),
        name="taps",
    )(*place, pieces)


def backward_body(
    scale,
    dev_ref,
    len_ref,
    mov_ref,
    slopes_ref,
    low_ref,
    high_ref,
    cot_ref,
    recv_ref,
    weight,
    pair_ref,
    q_ref,
    slope_ref,
    m_ref,
    inv_ref,
    conv_ref,
    chan_ref,
    proj_ref,
    audio_grad_ref,
    keep_ref,
    send_ref,
    ext,
    windows,
    turned,
    proj,
    feat_grad,
    normed,
    mid,
    wide,
    conv_sum,
    proj_sum,
    chan_sum,
    columns,
):
    place = Place(dev_ref, len_ref, mov_ref)
    slot = pl.program_id(0)
    living = place.alive(slot)
    span = PER_GROUP * LANES

    @pl.when(slot == 0)
    def _():
        proj[...] = jnp.zeros_like(proj)
        proj[:GC, :] = proj_ref[...]
        conv_sum[...] = jnp.zeros_like(conv_sum)
        proj_sum[...] = jnp.zeros_like(proj_sum)
        chan_sum[...] = jnp.zeros_like(chan_sum)

    @pl.when(living)
    def _():
        fill_ext(ext, low_ref[0], slopes_ref[0], high_ref[0])
        fill_windows(windows, ext, 1)
        fill_back(turned, place, slot, cot_ref, recv_ref)
        group = jnp.zeros((SPAN, span), f32)
        for g in range(GROUPS):
            at = g * NEAR * PER_GROUP
            group += nt(windows[at : at + SPAN, :], weight[g * span : (g + 1) * span, :])
        spread = gathered(group)
        feat_grad[...] = jnp.where(place.mask(slot), turned[...].T + spread, 0.0).astype(bf16)
        gain = chan_ref[1:2, :]
        gain_two, shift_two = chan_ref[3:4, :], chan_ref[4:5, :]
        mid[...] = nn(feat_grad[...], proj[...])
        for at in range(0, T, CHUNK):
            rows = slice(at, at + CHUNK)
            m = m_ref[0, rows, :].astype(f32)
            normed[rows, :] = (m * gain_two + shift_two).astype(bf16)
            normed_grad = mid[rows, :]
            chan_sum[24:32, :] += jnp.sum((normed_grad * m).reshape(-1, 8, C), axis=0)
            chan_sum[32:40, :] += jnp.sum(normed_grad.reshape(-1, 8, C), axis=0)
            scaled = normed_grad * gain_two
            first = jnp.mean(scaled, axis=-1, keepdims=True)
            second = jnp.mean(scaled * m, axis=-1, keepdims=True)
            inverse_two = inv_ref[0, rows, LANES : LANES + 1]
            pre_grad = inverse_two * (scaled - first - m * second) * slope_ref[
                0, rows, :
            ].astype(f32)
            q = q_ref[0, rows, :].astype(f32)
            chan_sum[8:16, :] += jnp.sum((pre_grad * q).reshape(-1, 8, C), axis=0)
            chan_sum[16:24, :] += jnp.sum(pre_grad.reshape(-1, 8, C), axis=0)
            scaled = pre_grad * gain
            first = jnp.mean(scaled, axis=-1, keepdims=True)
            second = jnp.mean(scaled * q, axis=-1, keepdims=True)
            inverse = inv_ref[0, rows, 0:1]
            conv_grad = inverse * (scaled - first - q * second)
            chan_sum[0:8, :] += jnp.sum(conv_grad.reshape(-1, 8, C), axis=0)
            mid[rows, :] = conv_grad
        operand = mid[...].astype(bf16)
        for tap in range(2):
            rows = slice(tap * C, (tap + 1) * C)
            audio_grad = nt(operand, conv_ref[rows, :])
            for c in range(C // LANES):
                wide[c, pl.ds(tap, T, stride=2), :] = audio_grad[:, c * LANES : (c + 1) * LANES]
            conv_sum[rows, :] += tn(pair_ref[0, :, rows], operand)
        for c in range(C // LANES):
            audio_grad_ref[0, :, c * LANES : (c + 1) * LANES] = wide[c].astype(bf16)
        proj_sum[...] += tn(normed[...], feat_grad[...])

    @pl.when(jnp.logical_not(living))
    def _():
        audio_grad_ref[...] = jnp.zeros_like(audio_grad_ref)

    @pl.when(slot == SLOTS - 1)
    def _():
        first_core = place.core == 0
        columns[...] = jnp.zeros_like(columns)
        for n in range(5):
            columns[GC + n : GC + n + 1, :] = jnp.sum(
                chan_sum[8 * n : 8 * n + 8, :], axis=0, keepdims=True
            )
        proj_sum[...] += columns[...].T
        keep_ref[:, CELLS:, :, :] = jnp.zeros((MP, 2, 16, LANES), bf16)
        send_ref[:, CELLS:, :, :] = jnp.zeros((MP, 2, 16, LANES), bf16)

        def put(at, cell, even, odd):
            keep_ref[at, cell] = (jnp.where(first_core, even, odd) * scale).astype(bf16)
            send_ref[at, cell] = (jnp.where(first_core, odd, even) * scale).astype(bf16)

        for cell in range(CELLS):
            for y in range(2):
                for x in range(X):
                    at = 2 * cell * 32 + y * 16
                    lanes = slice(x * LANES, (x + 1) * LANES)
                    put(
                        y * X + x,
                        cell,
                        conv_sum[at : at + 16, lanes],
                        conv_sum[at + 32 : at + 48, lanes],
                    )
            at = cell * 32
            put(
                cell // 2,
                CELLS + cell % 2,
                proj_sum[at : at + 16, :],
                proj_sum[at + 16 : at + 32, :],
            )


def backward(
    scale, place, slopes, low, high, cotangent, received, weight, stored, conv_weight, channels, proj
):
    shape = jax.ShapeDtypeStruct((MP, REST, 16, LANES), bf16)
    return pl.pallas_call(
        functools.partial(backward_body, scale),
        grid=(SLOTS,),
        out_shape=(jax.ShapeDtypeStruct((SLOTS, 2 * T, C), bf16), shape, shape),
        in_specs=[SMEM] * 3
        + [
            by_slot(T, LANES),
            by_slot(REACH, LANES),
            by_slot(REACH, LANES),
            by_slot(GC, T),
            by_slot(GC, T),
            once(*weight.shape),
            by_slot(T, 2 * C),
            by_slot(T, C),
            by_slot(T, C),
            by_slot(T, C),
            by_slot(T, 2 * LANES),
            once(2 * C, C),
            whole(5, C),
            whole(GC, C),
        ],
        out_specs=(by_slot(2 * T, C), whole(*shape.shape), whole(*shape.shape)),
        scratch_shapes=[
            pltpu.VMEM((EXT, LANES), f32),
            pltpu.VMEM((T + NEAR * (K // NEAR - 1), NEAR * LANES), bf16),
            pltpu.VMEM((LANES, T), f32),
            pltpu.VMEM((LANES, C), bf16),
            pltpu.VMEM((T, LANES), bf16),
            pltpu.VMEM((T, C), bf16),
            pltpu.VMEM((T, C), f32),
            pltpu.VMEM((C // LANES, 2 * T, LANES), f32),
            pltpu.VMEM((2 * C, C), f32),
            pltpu.VMEM((C, LANES), f32),
            pltpu.VMEM((40, C), f32),
            pltpu.VMEM((LANES, C), f32),
        ],
        compiler_params=params(30),
        cost_estimate=cost(
            2 * SLOTS * (SPAN * K * LANES * LANES + T * C * (4 * C + 2 * LANES)), 14 << 20
        ),
        name="backward",
    )(
        *place,
        slopes,
        low,
        high,
        cotangent,
        received,
        weight,
        *stored,
        conv_weight,
        channels,
        proj,
    )


def cells_body(dev_ref, rest_ref, out_ref):
    model = lax.rem(dev_ref[0], MP)
    rest = rest_ref[0].astype(f32)
    for n in range(1, MP):
        rest += rest_ref[n].astype(f32)
    out_ref[:, :16, :] = rest[:CELLS].astype(bf16)
    for cell in range(CELLS):
        small = jnp.where(model == cell // 2, rest[CELLS + cell % 2], 0.0)
        out_ref[cell, 16:, :] = small.astype(bf16)


def make_cells(dev, rest):
    return pl.pallas_call(
        cells_body,
        out_shape=jax.ShapeDtypeStruct((CELLS, 32, LANES), bf16),
        in_specs=[SMEM, VMEM],
        out_specs=VMEM,
        compiler_params=params(8),
        cost_estimate=cost(0, 1 << 20),
        name="cells",
    )(dev, rest)


def total_body(pos_ref, rest_ref, out_ref):
    for at, parts_ref in ((0, pos_ref), (REACH, rest_ref)):
        total = parts_ref[0].astype(f32)
        for n in range(1, parts_ref.shape[0]):
            total += parts_ref[n].astype(f32)
        for copy in range(MP):
            out_ref[copy, at : at + total.shape[0], :] = total.astype(bf16)


def total(pos, rest):
    return pl.pallas_call(
        total_body,
        out_shape=jax.ShapeDtypeStruct((MP, REACH + 32, LANES), bf16),
        in_specs=[VMEM] * 2,
        out_specs=VMEM,
        compiler_params=params(8),
        cost_estimate=cost(0, 2 << 20),
        name="total",
    )(pos, rest)


def finish_body(
    dev_ref,
    len_ref,
    mov_ref,
    in_ref,
    states_ref,
    other_ref,
    hidden_ref,
    pos_ref,
    conv_ref,
    proj_ref,
    chan_ref,
):
    place = Place(dev_ref, len_ref, mov_ref)
    for slot in range(SLOTS):
        hidden_ref[slot] = jnp.where(
            place.chosen == slot, other_ref[...].astype(f32), states_ref[slot].astype(f32)
        ).astype(bf16)
    for x in range(X):
        block = jnp.concatenate(
            [in_ref[x, :REACH, :].astype(f32), in_ref[X + x, :REACH, :].astype(f32)], axis=0
        ).T
        pos_ref[x] = block[:GC, :GC]
        for y in range(2):
            conv_ref[y * 16 : (y + 1) * 16, x * LANES : (x + 1) * LANES] = in_ref[
                y * X + x, REACH : REACH + 16, :
            ].astype(f32)
    small = in_ref[place.cell // 2, REACH + 16 :, :].astype(f32)
    proj_ref[...] = small[:, :GC]
    chan_ref[...] = jnp.concatenate([small] * 8, axis=0).T[GC : GC + 5, :16]


def finish(place, cells, states, other):
    return pl.pallas_call(
        finish_body,
        out_shape=(
            jax.ShapeDtypeStruct((SLOTS, GC, T), bf16),
            jax.ShapeDtypeStruct((4, GC, GC), f32),
            jax.ShapeDtypeStruct((32, C), f32),
            jax.ShapeDtypeStruct((16, GC), f32),
            jax.ShapeDtypeStruct((5, 16), f32),
        ),
        in_specs=[SMEM] * 3 + [VMEM] * 3,
        out_specs=(VMEM,) * 5,
        compiler_params=params(8),
        name="finish",
    )(*place, cells, states, other)


def neighbours(tail, head):
    count = lax.axis_size("mp")
    forward = [(i, i + 1) for i in range(count - 1)]
    backward_route = [(i + 1, i) for i in range(count - 1)]
    return lax.ppermute(tail, "mp", forward), lax.ppermute(head, "mp", backward_route)


def added(a, b):
    return (a.astype(f32) + b.astype(f32)).astype(bf16)


def per_device(
    audio, lengths, moved_slots, conv_weight, channel_params, proj_weight, pos_weight, cotangent
):
    data_index = lax.axis_index("dp")
    model_index = lax.axis_index("mp")
    scale = (SLOTS * DP * T * MP) ** -0.5
    dev = (data_index * MP + model_index).astype(jnp.int32).reshape(1)
    place = (dev, lengths, moved_slots.reshape(-1))
    swap = [(i, i ^ (DP // 2)) for i in range(DP)]
    core_swap = [(i, i ^ 1) for i in range(DP)]
    channels = channel_params.T
    proj = proj_weight.T
    cot = cotangent.transpose(0, 2, 1)

    received = lax.ppermute(cot, "dp", swap)
    features, tail, head, *stored = encode(place, audio, conv_weight, channels, proj)
    low, high = neighbours(tail, head)
    ahead, behind = turn(pos_weight.transpose(1, 2, 0))
    states, sent, slopes, tail, head, pieces = mix(
        place, features, low, high, ahead, cot, received
    )
    slope_low, slope_high = neighbours(tail, head)
    pieces, slope_low, slope_high = lax.optimization_barrier((pieces, slope_low, slope_high))
    rows = [list(range(X)), list(range(X, 2 * X))]
    pieces = lax.all_to_all(pieces, "mp", 0, 0, axis_index_groups=rows, tiled=True)
    other = lax.ppermute(sent, "dp", swap)
    audio_grad, keep, send = backward(
        scale,
        place,
        slopes,
        slope_low,
        slope_high,
        cot,
        received,
        behind,
        stored,
        conv_weight,
        channels,
        proj,
    )
    rest = added(keep, lax.ppermute(send, "dp", core_swap))
    pos_keep, pos_send = taps(scale, place, pieces)
    rest = lax.all_to_all(rest, "mp", 0, 0, tiled=True)
    pos_sum = added(pos_keep, lax.ppermute(pos_send, "dp", core_swap))
    links = [
        [MP * (2 * cell + core) + X * y + x for cell in range(CELLS) for y in range(2)]
        for core in range(2)
        for x in range(X)
    ]
    pos_sum = lax.all_to_all(
        pos_sum,
        ("dp", "mp"),
        0,
        0,
        axis_index_groups=links,
        tiled=True,
    )
    rest, other = lax.optimization_barrier((rest, other))
    groups = [list(range(bit, DP, 2)) for bit in range(2)]
    rest = lax.all_to_all(
        make_cells(dev, rest), "dp", 0, 0, axis_index_groups=groups, tiled=True
    )
    cells = lax.all_to_all(total(pos_sum, rest), "mp", 0, 0, tiled=True)
    hidden, grad_pos, grad_conv, grad_proj, grad_channels = finish(place, cells, states, other)
    return (
        hidden.transpose(0, 2, 1),
        audio_grad,
        grad_pos,
        grad_conv,
        grad_proj,
        grad_channels.T,
    )


def solution(mesh):
    return jax.shard_map(
        per_device,
        mesh=mesh,
        in_specs=(P("dp", "mp", None), P(), P(), P(), P(), P(), P(), P("dp", "mp", None)),
        out_specs=(
            P("dp", "mp", None),
            P("dp", "mp", None),
            P("dp", None, None),
            P("dp", None),
            P("dp", None),
            P("dp", None),
        ),
        check_vma=False,
    )
```

```python
import functools

import jax
import jax.numpy as jnp
from jax import lax
from jax.experimental import pallas as pl
from jax.experimental.pallas import tpu as pltpu
from jax.sharding import PartitionSpec as P

epsilon = 1e-05
root_half = 0.7071067811865476
density = 0.3989422804014327

SLOTS = 2
T = 256
C = 512
GC = 120
LANES = 128
K = 128
REACH = 64
EXT = T + 2 * REACH
NEAR = 16
GROUPS = 2
PER_GROUP = 4
SPAN = T + NEAR * (PER_GROUP - 1)
CHUNK = 32
MP = 8
DP = 32
X = 4
CELLS = 16
PIECE = T + REACH
REST = CELLS + 2

f32 = jnp.float32
bf16 = jnp.bfloat16

VMEM = pl.BlockSpec(memory_space=pltpu.VMEM)
SMEM = pl.BlockSpec(memory_space=pltpu.SMEM)


def params(mebibytes):
    return pltpu.CompilerParams(vmem_limit_bytes=mebibytes << 20)


def cost(flops, moved, trans=0):
    return pl.CostEstimate(flops=flops, bytes_accessed=moved, transcendentals=trans)


def phi(values):
    return 0.5 * (1.0 + lax.erf(values * root_half))


def bell(values):
    return jnp.exp(-0.5 * values * values) * density


def nt(a, b):
    return lax.dot_general(a, b, (((1,), (1,)), ((), ())), preferred_element_type=f32)


def tn(a, b):
    return lax.dot_general(a, b, (((0,), (0,)), ((), ())), preferred_element_type=f32)


def nn(a, b):
    return jnp.dot(a, b, preferred_element_type=f32)


class Place:
    def __init__(self, dev_ref, len_ref, mov_ref):
        self.data = dev_ref[0] // MP
        self.model = lax.rem(dev_ref[0], MP)
        self.x = lax.rem(self.model, X)
        self.y = self.model // X
        self.core = lax.rem(self.data, 2)
        self.cell = self.data // 2
        self.first = self.model * T
        self.lengths = len_ref
        self.chosen = mov_ref[lax.rem(self.data, DP // 2)]

    def length(self, slot):
        return self.lengths[self.data * SLOTS + slot]

    def alive(self, slot):
        return self.first < self.length(slot)

    def seam(self, rows):
        return jnp.where(self.x == 0, rows[:REACH, :], rows[T - REACH :, :]).astype(bf16)

    def extended(self, ext, edge, pieces):
        own = pieces[self.x, 0, :T, :].astype(f32)
        before = pieces[jnp.maximum(self.x - 1, 0), 0, T - REACH : T, :].astype(f32)
        after = pieces[jnp.minimum(self.x + 1, X - 1), 0, :REACH, :].astype(f32)
        ext[:REACH, :] = jnp.where(self.x == 0, edge, before)
        ext[REACH : REACH + T, :] = own
        ext[REACH + T :, :] = jnp.where(self.x == X - 1, edge, after)
        return own

    def mask(self, slot):
        ids = self.first + lax.broadcasted_iota(jnp.int32, (T, 1), 0)
        return ids < self.length(slot)


def by_slot(*dims):
    return pl.BlockSpec((1,) + dims, lambda s: (s,) + (0,) * len(dims))


def whole(*dims):
    return pl.BlockSpec(dims, lambda s: (0,) * len(dims))


def all_x(rows):
    return pl.BlockSpec((X, 1, rows, LANES), lambda s: (0, s, 0, 0))


def once(*dims):
    return pl.BlockSpec(dims, lambda s: (0,) * len(dims), pipeline_mode=pl.Buffered(1))


def turn_body(in_ref, ahead_ref, behind_ref, rows):
    block = pl.program_id(0)
    blocks = pl.num_programs(0)
    for n in range(NEAR):
        tile = jnp.concatenate(
            [in_ref[n].astype(f32), jnp.zeros((LANES - GC, K), f32)], axis=0
        ).T
        if n >= GC % NEAR:
            tile = jnp.where(block == blocks - 1, 0.0, tile)
        rows[pl.ds(n, K, stride=NEAR), :] = tile
    far = K // NEAR
    for q in range(far):
        for r in range(NEAR):
            at = (q * NEAR + r) * NEAR
            tile = rows[at : at + NEAR, :].astype(bf16)
            ahead_ref[r, :, q * LANES : (q + 1) * LANES] = tile
            r_back = NEAR - 1 - r
            behind_ref[far - 1 - q, :, r_back * LANES : (r_back + 1) * LANES] = tile


def turn(pos):
    far = K // NEAR
    ahead, behind = pl.pallas_call(
        turn_body,
        grid=(LANES // NEAR,),
        out_shape=(
            jax.ShapeDtypeStruct((NEAR, LANES, far * LANES), bf16),
            jax.ShapeDtypeStruct((far, LANES, NEAR * LANES), bf16),
        ),
        in_specs=[pl.BlockSpec((NEAR, GC, K), lambda b: (b, 0, 0))],
        out_specs=(
            pl.BlockSpec((NEAR, NEAR, far * LANES), lambda b: (0, b, 0)),
            pl.BlockSpec((far, NEAR, NEAR * LANES), lambda b: (0, b, 0)),
        ),
        scratch_shapes=[pltpu.VMEM((K * NEAR, LANES), f32)],
        compiler_params=params(56),
        cost_estimate=cost(0, 12 << 20),
        name="turn",
    )(pos)
    return ahead.reshape(NEAR * LANES, -1), behind.reshape(far * LANES, -1)


def encode_body(
    dev_ref,
    len_ref,
    mov_ref,
    audio_ref,
    conv_ref,
    chan_ref,
    proj_ref,
    feat_ref,
    edge_ref,
    pair_ref,
    q_ref,
    slope_ref,
    m_ref,
    inv_ref,
    wide,
    proj,
    mid,
    normed,
):
    place = Place(dev_ref, len_ref, mov_ref)
    slot = pl.program_id(0)

    @pl.when(slot == 0)
    def _():
        proj[...] = jnp.zeros_like(proj)
        proj[:GC, :] = proj_ref[...]

    living = place.alive(slot)

    @pl.when(living)
    def _():
        for c in range(C // LANES):
            wide[c] = audio_ref[0, :, c * LANES : (c + 1) * LANES].astype(f32)
            for tap in range(2):
                at = tap * C + c * LANES
                pair_ref[0, :, at : at + LANES] = wide[c, pl.ds(tap, T, stride=2), :].astype(bf16)
        mid[...] = nn(pair_ref[0], conv_ref[...])
        bias, gain, shift = chan_ref[0:1, :], chan_ref[1:2, :], chan_ref[2:3, :]
        gain_two, shift_two = chan_ref[3:4, :], chan_ref[4:5, :]
        for at in range(0, T, CHUNK):
            rows = slice(at, at + CHUNK)
            conv = mid[rows, :] + bias
            offset = conv - jnp.mean(conv, axis=-1, keepdims=True)
            inverse = lax.rsqrt(jnp.mean(offset * offset, axis=-1, keepdims=True) + epsilon)
            q = offset * inverse
            pre = q * gain + shift
            below = phi(pre)
            encoded = (pre * below).astype(bf16).astype(f32)
            slope_ref[0, rows, :] = (below + pre * bell(pre)).astype(bf16)
            q_ref[0, rows, :] = q.astype(bf16)
            offset = encoded - jnp.mean(encoded, axis=-1, keepdims=True)
            inverse_two = lax.rsqrt(jnp.mean(offset * offset, axis=-1, keepdims=True) + epsilon)
            m = offset * inverse_two
            m_ref[0, rows, :] = m.astype(bf16)
            inv_ref[0, rows, :] = jnp.concatenate(
                [
                    jnp.broadcast_to(inverse, (CHUNK, LANES)),
                    jnp.broadcast_to(inverse_two, (CHUNK, LANES)),
                ],
                axis=1,
            )
            normed[rows, :] = (m * gain_two + shift_two).astype(bf16)
        projected = nt(normed[...], proj[...])
        features = jnp.where(place.mask(slot), projected, 0.0)
        for copy in range(X):
            feat_ref[copy, 0] = features.astype(bf16)
        edge_ref[0] = place.seam(features)

    @pl.when(jnp.logical_not(living))
    def _():
        feat_ref[...] = jnp.zeros_like(feat_ref)
        edge_ref[...] = jnp.zeros_like(edge_ref)


def encode(place, audio, conv_weight, channels, proj):
    return pl.pallas_call(
        encode_body,
        grid=(SLOTS,),
        out_shape=(
            jax.ShapeDtypeStruct((X, SLOTS, T, LANES), bf16),
            jax.ShapeDtypeStruct((SLOTS, REACH, LANES), bf16),
            jax.ShapeDtypeStruct((SLOTS, T, 2 * C), bf16),
            jax.ShapeDtypeStruct((SLOTS, T, C), bf16),
            jax.ShapeDtypeStruct((SLOTS, T, C), bf16),
            jax.ShapeDtypeStruct((SLOTS, T, C), bf16),
            jax.ShapeDtypeStruct((SLOTS, T, 2 * LANES), f32),
        ),
        in_specs=[SMEM] * 3
        + [
            by_slot(2 * T, C),
            once(2 * C, C),
            whole(5, C),
            whole(GC, C),
        ],
        out_specs=(
            all_x(T),
            by_slot(REACH, LANES),
            by_slot(T, 2 * C),
            by_slot(T, C),
            by_slot(T, C),
            by_slot(T, C),
            by_slot(T, 2 * LANES),
        ),
        scratch_shapes=[
            pltpu.VMEM((C // LANES, 2 * T, LANES), f32),
            pltpu.VMEM((LANES, C), bf16),
            pltpu.VMEM((T, C), f32),
            pltpu.VMEM((T, C), bf16),
        ],
        compiler_params=params(56),
        cost_estimate=cost(2 * SLOTS * T * C * (2 * C + LANES), 8 << 20, SLOTS * T * C * 2),
        name="encode",
    )(*place, audio, conv_weight, channels, proj)


def fill_windows(windows, ext, first):
    rows = T + NEAR * (K // NEAR - 1)
    for r in range(NEAR):
        windows[:, r * LANES : (r + 1) * LANES] = ext[first + r : first + r + rows, :].astype(bf16)


def gathered(group):
    total = group[:T, :LANES]
    for p in range(1, PER_GROUP):
        total += group[NEAR * p : NEAR * p + T, p * LANES : (p + 1) * LANES]
    return total


def fill_back(turned, place, slot, cot_ref, recv_ref):
    turned[GC:, :] = jnp.zeros((LANES - GC, T), f32)
    turned[:GC, :] = jnp.where(
        place.chosen == slot, recv_ref[0].astype(f32), cot_ref[0].astype(f32)
    )


def mix_body(
    dev_ref,
    len_ref,
    mov_ref,
    feat_ref,
    edge_ref,
    weight,
    cot_ref,
    recv_ref,
    states_ref,
    sent_ref,
    piece_ref,
    seam_ref,
    ext,
    windows,
    turned,
):
    place = Place(dev_ref, len_ref, mov_ref)
    slot = pl.program_id(0)
    living = place.alive(slot)
    wide = PER_GROUP * LANES

    @pl.when(living)
    def _():
        edge = edge_ref[0].astype(f32)
        own = place.extended(ext, edge, feat_ref)
        fill_windows(windows, ext, 0)
        fill_back(turned, place, slot, cot_ref, recv_ref)
        back = turned[...].T
        group = jnp.zeros((SPAN, wide), f32)
        for g in range(GROUPS):
            at = g * NEAR * PER_GROUP
            group += nn(windows[at : at + SPAN, :], weight[:, g * wide : (g + 1) * wide])
        mixed = gathered(group)
        below = phi(mixed)
        mask = place.mask(slot)
        states = jnp.where(mask, own + mixed * below, 0.0)
        states_ref[0] = states.T[:GC, :].astype(bf16)
        slopes = jnp.where(mask, back * (below + mixed * bell(mixed)), 0.0)
        for copy in range(X):
            piece_ref[copy, 0, :T, :] = slopes.astype(bf16)
            piece_ref[copy, 0, T:, :] = edge.astype(bf16)
        seam_ref[0] = place.seam(slopes)

    @pl.when(jnp.logical_not(living))
    def _():
        states_ref[...] = jnp.zeros_like(states_ref)
        piece_ref[...] = jnp.zeros_like(piece_ref)
        seam_ref[...] = jnp.zeros_like(seam_ref)

    @pl.when(place.chosen == slot)
    def _():
        sent_ref[...] = states_ref[0]


def mix(place, features, edge, weight, cotangent, received):
    return pl.pallas_call(
        mix_body,
        grid=(SLOTS,),
        out_shape=(
            jax.ShapeDtypeStruct((SLOTS, GC, T), bf16),
            jax.ShapeDtypeStruct((GC, T), bf16),
            jax.ShapeDtypeStruct((X, SLOTS, PIECE, LANES), bf16),
            jax.ShapeDtypeStruct((SLOTS, REACH, LANES), bf16),
        ),
        in_specs=[SMEM] * 3
        + [
            all_x(T),
            by_slot(REACH, LANES),
            once(*weight.shape),
            by_slot(GC, T),
            by_slot(GC, T),
        ],
        out_specs=(
            by_slot(GC, T),
            whole(GC, T),
            all_x(PIECE),
            by_slot(REACH, LANES),
        ),
        scratch_shapes=[
            pltpu.VMEM((EXT, LANES), f32),
            pltpu.VMEM((T + NEAR * (K // NEAR - 1), NEAR * LANES), bf16),
            pltpu.VMEM((LANES, T), f32),
        ],
        compiler_params=params(56),
        cost_estimate=cost(2 * SLOTS * SPAN * K * LANES * LANES, 7 << 20, SLOTS * T * LANES * 2),
        name="mix",
    )(*place, features, edge, weight, cotangent, received)


def taps_body(
    scale, dev_ref, len_ref, mov_ref, feat_ref, piece_ref, keep_ref, send_ref, ext, windows, turned, sums
):
    place = Place(dev_ref, len_ref, mov_ref)
    slot = pl.program_id(0)
    spread = X * T
    rows = spread + NEAR * (K // NEAR - 1)

    @pl.when(slot == 0)
    def _():
        sums[...] = jnp.zeros_like(sums)

    @pl.when(place.y * spread < place.length(slot))
    def _():
        ext[:REACH, :] = piece_ref[0, 0, T:, :].astype(f32)
        ext[REACH + spread :, :] = piece_ref[X - 1, 0, T:, :].astype(f32)
        for x in range(X):
            ext[REACH + x * T : REACH + (x + 1) * T, :] = feat_ref[x, 0].astype(f32)
            turned[:, x * T : (x + 1) * T] = (
                piece_ref[x, 0, :T, :].astype(f32).T.astype(bf16)
            )
        for j in range(4):
            windows[:, j * LANES : (j + 1) * LANES] = ext[
                pl.ds(place.x + 4 * j, rows), :
            ].astype(bf16)
        for q in range(K // NEAR):
            sums[q] += nn(turned[...], windows[q * NEAR : q * NEAR + spread, :])

    @pl.when(slot == SLOTS - 1)
    def _():
        first_core = place.core == 0
        for q in range(K // NEAR):
            for far in range(2):
                even = sums[q, :, (2 * far) * LANES : (2 * far + 1) * LANES] * scale
                odd = sums[q, :, (2 * far + 1) * LANES : (2 * far + 2) * LANES] * scale
                keep = jnp.where(first_core, even, odd).astype(bf16)
                send = jnp.where(first_core, odd, even).astype(bf16)
                for y in range(2):
                    keep_ref[y, 2 * q + far] = keep[y * REACH : (y + 1) * REACH, :]
                    send_ref[y, 2 * q + far] = send[y * REACH : (y + 1) * REACH, :]


def taps(scale, place, features, pieces):
    shape = jax.ShapeDtypeStruct((2, CELLS, REACH, LANES), bf16)
    spread = X * T
    return pl.pallas_call(
        functools.partial(taps_body, scale),
        grid=(SLOTS,),
        out_shape=(shape, shape),
        in_specs=[SMEM] * 3 + [all_x(T), all_x(PIECE)],
        out_specs=(whole(*shape.shape), whole(*shape.shape)),
        scratch_shapes=[
            pltpu.VMEM((spread + 2 * REACH, LANES), f32),
            pltpu.VMEM((spread + NEAR * (K // NEAR - 1), 4 * LANES), bf16),
            pltpu.VMEM((LANES, spread), bf16),
            pltpu.VMEM((K // NEAR, LANES, 4 * LANES), f32),
        ],
        compiler_params=params(16),
        cost_estimate=cost(2 * SLOTS * SPAN * K * LANES * LANES, 4 << 20),
        name="taps",
    )(*place, features, pieces)


def backward_body(
    scale,
    dev_ref,
    len_ref,
    mov_ref,
    piece_ref,
    edge_ref,
    cot_ref,
    recv_ref,
    weight,
    pair_ref,
    q_ref,
    slope_ref,
    m_ref,
    inv_ref,
    conv_ref,
    chan_ref,
    proj_ref,
    audio_grad_ref,
    keep_ref,
    send_ref,
    ext,
    windows,
    turned,
    proj,
    feat_grad,
    normed,
    mid,
    wide,
    conv_sum,
    proj_sum,
    chan_sum,
    columns,
):
    place = Place(dev_ref, len_ref, mov_ref)
    slot = pl.program_id(0)
    living = place.alive(slot)
    span = PER_GROUP * LANES

    @pl.when(slot == 0)
    def _():
        proj[...] = jnp.zeros_like(proj)
        proj[:GC, :] = proj_ref[...]
        conv_sum[...] = jnp.zeros_like(conv_sum)
        proj_sum[...] = jnp.zeros_like(proj_sum)
        chan_sum[...] = jnp.zeros_like(chan_sum)

    @pl.when(living)
    def _():
        place.extended(ext, edge_ref[0].astype(f32), piece_ref)
        fill_windows(windows, ext, 1)
        fill_back(turned, place, slot, cot_ref, recv_ref)
        group = jnp.zeros((SPAN, span), f32)
        for g in range(GROUPS):
            at = g * NEAR * PER_GROUP
            group += nt(windows[at : at + SPAN, :], weight[g * span : (g + 1) * span, :])
        spread = gathered(group)
        feat_grad[...] = jnp.where(place.mask(slot), turned[...].T + spread, 0.0).astype(bf16)
        gain = chan_ref[1:2, :]
        gain_two, shift_two = chan_ref[3:4, :], chan_ref[4:5, :]
        mid[...] = nn(feat_grad[...], proj[...])
        for at in range(0, T, CHUNK):
            rows = slice(at, at + CHUNK)
            m = m_ref[0, rows, :].astype(f32)
            normed[rows, :] = (m * gain_two + shift_two).astype(bf16)
            normed_grad = mid[rows, :]
            chan_sum[24:32, :] += jnp.sum((normed_grad * m).reshape(-1, 8, C), axis=0)
            chan_sum[32:40, :] += jnp.sum(normed_grad.reshape(-1, 8, C), axis=0)
            scaled = normed_grad * gain_two
            first = jnp.mean(scaled, axis=-1, keepdims=True)
            second = jnp.mean(scaled * m, axis=-1, keepdims=True)
            inverse_two = inv_ref[0, rows, LANES : LANES + 1]
            pre_grad = inverse_two * (scaled - first - m * second) * slope_ref[
                0, rows, :
            ].astype(f32)
            q = q_ref[0, rows, :].astype(f32)
            chan_sum[8:16, :] += jnp.sum((pre_grad * q).reshape(-1, 8, C), axis=0)
            chan_sum[16:24, :] += jnp.sum(pre_grad.reshape(-1, 8, C), axis=0)
            scaled = pre_grad * gain
            first = jnp.mean(scaled, axis=-1, keepdims=True)
            second = jnp.mean(scaled * q, axis=-1, keepdims=True)
            inverse = inv_ref[0, rows, 0:1]
            conv_grad = inverse * (scaled - first - q * second)
            chan_sum[0:8, :] += jnp.sum(conv_grad.reshape(-1, 8, C), axis=0)
            mid[rows, :] = conv_grad
        operand = mid[...].astype(bf16)
        for tap in range(2):
            rows = slice(tap * C, (tap + 1) * C)
            audio_grad = nt(operand, conv_ref[rows, :])
            for c in range(C // LANES):
                wide[c, pl.ds(tap, T, stride=2), :] = audio_grad[:, c * LANES : (c + 1) * LANES]
            conv_sum[rows, :] += tn(pair_ref[0, :, rows], operand)
        for c in range(C // LANES):
            audio_grad_ref[0, :, c * LANES : (c + 1) * LANES] = wide[c].astype(bf16)
        proj_sum[...] += tn(normed[...], feat_grad[...])

    @pl.when(jnp.logical_not(living))
    def _():
        audio_grad_ref[...] = jnp.zeros_like(audio_grad_ref)

    @pl.when(slot == SLOTS - 1)
    def _():
        first_core = place.core == 0
        columns[...] = jnp.zeros_like(columns)
        for n in range(5):
            columns[GC + n : GC + n + 1, :] = jnp.sum(
                chan_sum[8 * n : 8 * n + 8, :], axis=0, keepdims=True
            )
        proj_sum[...] += columns[...].T
        keep_ref[:, CELLS:, :, :] = jnp.zeros((MP, 2, 16, LANES), bf16)
        send_ref[:, CELLS:, :, :] = jnp.zeros((MP, 2, 16, LANES), bf16)

        def put(at, cell, even, odd):
            keep_ref[at, cell] = (jnp.where(first_core, even, odd) * scale).astype(bf16)
            send_ref[at, cell] = (jnp.where(first_core, odd, even) * scale).astype(bf16)

        for cell in range(CELLS):
            for y in range(2):
                for x in range(X):
                    at = 2 * cell * 32 + y * 16
                    lanes = slice(x * LANES, (x + 1) * LANES)
                    put(
                        y * X + x,
                        cell,
                        conv_sum[at : at + 16, lanes],
                        conv_sum[at + 32 : at + 48, lanes],
                    )
            at = cell * 32
            put(
                cell // 2,
                CELLS + cell % 2,
                proj_sum[at : at + 16, :],
                proj_sum[at + 16 : at + 32, :],
            )


def backward(
    scale, place, pieces, edge, cotangent, received, weight, stored, conv_weight, channels, proj
):
    shape = jax.ShapeDtypeStruct((MP, REST, 16, LANES), bf16)
    return pl.pallas_call(
        functools.partial(backward_body, scale),
        grid=(SLOTS,),
        out_shape=(jax.ShapeDtypeStruct((SLOTS, 2 * T, C), bf16), shape, shape),
        in_specs=[SMEM] * 3
        + [
            all_x(PIECE),
            by_slot(REACH, LANES),
            by_slot(GC, T),
            by_slot(GC, T),
            once(*weight.shape),
            by_slot(T, 2 * C),
            by_slot(T, C),
            by_slot(T, C),
            by_slot(T, C),
            by_slot(T, 2 * LANES),
            once(2 * C, C),
            whole(5, C),
            whole(GC, C),
        ],
        out_specs=(by_slot(2 * T, C), whole(*shape.shape), whole(*shape.shape)),
        scratch_shapes=[
            pltpu.VMEM((EXT, LANES), f32),
            pltpu.VMEM((T + NEAR * (K // NEAR - 1), NEAR * LANES), bf16),
            pltpu.VMEM((LANES, T), f32),
            pltpu.VMEM((LANES, C), bf16),
            pltpu.VMEM((T, LANES), bf16),
            pltpu.VMEM((T, C), bf16),
            pltpu.VMEM((T, C), f32),
            pltpu.VMEM((C // LANES, 2 * T, LANES), f32),
            pltpu.VMEM((2 * C, C), f32),
            pltpu.VMEM((C, LANES), f32),
            pltpu.VMEM((40, C), f32),
            pltpu.VMEM((LANES, C), f32),
        ],
        compiler_params=params(56),
        cost_estimate=cost(
            2 * SLOTS * (SPAN * K * LANES * LANES + T * C * (4 * C + 2 * LANES)), 14 << 20
        ),
        name="backward",
    )(
        *place,
        pieces,
        edge,
        cotangent,
        received,
        weight,
        *stored,
        conv_weight,
        channels,
        proj,
    )


def cells_body(dev_ref, kept_ref, recv_ref, rest_ref, out_ref):
    model = lax.rem(dev_ref[0], MP)
    out_ref[:, :REACH, :] = (kept_ref[...].astype(f32) + recv_ref[...].astype(f32)).astype(bf16)
    rest = rest_ref[0].astype(f32)
    for n in range(1, MP):
        rest += rest_ref[n].astype(f32)
    out_ref[:, REACH : REACH + 16, :] = rest[:CELLS].astype(bf16)
    for cell in range(CELLS):
        small = jnp.where(model == cell // 2, rest[CELLS + cell % 2], 0.0)
        out_ref[cell, REACH + 16 :, :] = small.astype(bf16)


def make_cells(dev, kept, received, rest):
    return pl.pallas_call(
        cells_body,
        out_shape=jax.ShapeDtypeStruct((CELLS, REACH + 32, LANES), bf16),
        in_specs=[SMEM] + [VMEM] * 3,
        out_specs=VMEM,
        compiler_params=params(10),
        cost_estimate=cost(0, 2 << 20),
        name="cells",
    )(dev, kept, received, rest)


def total_body(in_ref, out_ref):
    total = in_ref[0].astype(f32)
    for n in range(1, in_ref.shape[0]):
        total += in_ref[n].astype(f32)
    for copy in range(MP):
        out_ref[copy] = total.astype(bf16)


def total(parts):
    return pl.pallas_call(
        total_body,
        out_shape=jax.ShapeDtypeStruct((MP,) + parts.shape[1:], bf16),
        in_specs=[VMEM],
        out_specs=VMEM,
        compiler_params=params(10),
        cost_estimate=cost(0, 2 * parts.size),
        name="total",
    )(parts)


def finish_body(
    dev_ref,
    len_ref,
    mov_ref,
    in_ref,
    states_ref,
    other_ref,
    hidden_ref,
    pos_ref,
    conv_ref,
    proj_ref,
    chan_ref,
):
    place = Place(dev_ref, len_ref, mov_ref)
    for slot in range(SLOTS):
        hidden_ref[slot] = jnp.where(
            place.chosen == slot, other_ref[...].astype(f32), states_ref[slot].astype(f32)
        ).astype(bf16)
    for x in range(X):
        block = jnp.concatenate(
            [in_ref[x, :REACH, :].astype(f32), in_ref[X + x, :REACH, :].astype(f32)], axis=0
        ).T
        pos_ref[x] = block[:GC, :GC]
        for y in range(2):
            conv_ref[y * 16 : (y + 1) * 16, x * LANES : (x + 1) * LANES] = in_ref[
                y * X + x, REACH : REACH + 16, :
            ].astype(f32)
    small = in_ref[place.cell // 2, REACH + 16 :, :].astype(f32)
    proj_ref[...] = small[:, :GC]
    chan_ref[...] = jnp.concatenate([small] * 8, axis=0).T[GC : GC + 5, :16]


def finish(place, cells, states, other):
    return pl.pallas_call(
        finish_body,
        out_shape=(
            jax.ShapeDtypeStruct((SLOTS, GC, T), bf16),
            jax.ShapeDtypeStruct((4, GC, GC), f32),
            jax.ShapeDtypeStruct((32, C), f32),
            jax.ShapeDtypeStruct((16, GC), f32),
            jax.ShapeDtypeStruct((5, 16), f32),
        ),
        in_specs=[SMEM] * 3 + [VMEM] * 3,
        out_specs=(VMEM,) * 5,
        compiler_params=params(8),
        name="finish",
    )(*place, cells, states, other)


def added(a, b):
    return (a.astype(f32) + b.astype(f32)).astype(bf16)


def per_device(
    audio, lengths, moved_slots, conv_weight, channel_params, proj_weight, pos_weight, cotangent
):
    data_index = lax.axis_index("dp")
    model_index = lax.axis_index("mp")
    scale = (SLOTS * DP * T * MP) ** -0.5
    dev = (data_index * MP + model_index).astype(jnp.int32).reshape(1)
    place = (dev, lengths, moved_slots.reshape(-1))
    swap = [(i, i ^ (DP // 2)) for i in range(DP)]
    core_swap = [(i, i ^ 1) for i in range(DP)]
    channels = channel_params.T
    proj = proj_weight.T
    cot = cotangent.transpose(0, 2, 1)

    rows = [list(range(X)), list(range(X, 2 * X))]
    seam = [(X - 1, X), (X, X - 1)]

    def over_x(copies):
        return lax.all_to_all(copies, "mp", 0, 0, axis_index_groups=rows, tiled=True)

    received = lax.ppermute(cot, "dp", swap)
    features, edge, *stored = encode(place, audio, conv_weight, channels, proj)
    features = over_x(features)
    edge = lax.ppermute(edge, "mp", seam)
    ahead, behind = turn(pos_weight.transpose(1, 2, 0))
    states, sent, pieces, edge = mix(place, features, edge, ahead, cot, received)
    pieces = over_x(pieces)
    edge = lax.ppermute(edge, "mp", seam)
    other = lax.ppermute(sent, "dp", swap)
    pos_keep, pos_send = taps(scale, place, features, pieces)
    pos_send, edge = lax.optimization_barrier((pos_send, edge))
    pos_recv = lax.ppermute(pos_send, "dp", core_swap)
    audio_grad, keep, send = backward(
        scale,
        place,
        pieces,
        edge,
        cot,
        received,
        behind,
        stored,
        conv_weight,
        channels,
        proj,
    )
    rest = added(keep, lax.ppermute(send, "dp", core_swap))
    rest = lax.all_to_all(rest, "mp", 0, 0, tiled=True)
    pos_sum = added(pos_keep, pos_recv)
    low_half = model_index < X
    kept = jnp.where(low_half, pos_sum[0], pos_sum[1])
    leaving = jnp.where(low_half, pos_sum[1], pos_sum[0])
    coming = lax.ppermute(leaving, "mp", [(i, i ^ X) for i in range(MP)])
    rest, other = lax.optimization_barrier((rest, other))
    cells = make_cells(dev, kept, coming, rest)
    groups = [list(range(bit, DP, 2)) for bit in range(2)]
    cells = lax.all_to_all(cells, "dp", 0, 0, axis_index_groups=groups, tiled=True)
    cells = lax.all_to_all(total(cells), "mp", 0, 0, tiled=True)
    hidden, grad_pos, grad_conv, grad_proj, grad_channels = finish(place, cells, states, other)
    return (
        hidden.transpose(0, 2, 1),
        audio_grad,
        grad_pos,
        grad_conv,
        grad_proj,
        grad_channels.T,
    )


def solution(mesh):
    return jax.shard_map(
        per_device,
        mesh=mesh,
        in_specs=(P("dp", "mp", None), P(), P(), P(), P(), P(), P(), P("dp", "mp", None)),
        out_specs=(
            P("dp", "mp", None),
            P("dp", "mp", None),
            P("dp", None, None),
            P("dp", None),
            P("dp", None),
            P("dp", None),
        ),
        check_vma=False,
    )
```

```python
import functools

import jax
import jax.numpy as jnp
from jax import lax
from jax.experimental import pallas as pl
from jax.experimental.pallas import tpu as pltpu
from jax.sharding import PartitionSpec as P

epsilon = 1e-05
root_half = 0.7071067811865476
density = 0.3989422804014327

SLOTS = 2
T = 256
C = 512
GC = 120
LANES = 128
K = 128
REACH = 64
EXT = T + 2 * REACH
NEAR = 16
GROUPS = 2
PER_GROUP = 4
SPAN = T + NEAR * (PER_GROUP - 1)
CHUNK = 32
MP = 8
DP = 32
X = 4
CELLS = 16
PIECE = T + REACH
HALF = GC // 2
SPARE = REACH - HALF
CONV_ROWS = CELLS * 32
REST = CONV_ROWS + CELLS * SPARE

f32 = jnp.float32
bf16 = jnp.bfloat16

VMEM = pl.BlockSpec(memory_space=pltpu.VMEM)
SMEM = pl.BlockSpec(memory_space=pltpu.SMEM)


def params(mebibytes):
    return pltpu.CompilerParams(vmem_limit_bytes=mebibytes << 20)


def cost(flops, moved, trans=0):
    return pl.CostEstimate(flops=flops, bytes_accessed=moved, transcendentals=trans)


def phi(values):
    return 0.5 * (1.0 + lax.erf(values * root_half))


def bell(values):
    return jnp.exp(-0.5 * values * values) * density


def nt(a, b):
    return lax.dot_general(a, b, (((1,), (1,)), ((), ())), preferred_element_type=f32)


def tn(a, b):
    return lax.dot_general(a, b, (((0,), (0,)), ((), ())), preferred_element_type=f32)


def nn(a, b):
    return jnp.dot(a, b, preferred_element_type=f32)


class Place:
    def __init__(self, dev_ref, len_ref, mov_ref):
        self.data = dev_ref[0] // MP
        self.model = lax.rem(dev_ref[0], MP)
        self.x = lax.rem(self.model, X)
        self.y = self.model // X
        self.core = lax.rem(self.data, 2)
        self.cell = self.data // 2
        self.first = self.model * T
        self.lengths = len_ref
        self.chosen = mov_ref[lax.rem(self.data, DP // 2)]

    def length(self, slot):
        return self.lengths[self.data * SLOTS + slot]

    def alive(self, slot):
        return self.first < self.length(slot)

    def seam(self, rows):
        return jnp.where(self.x == 0, rows[:REACH, :], rows[T - REACH :, :]).astype(bf16)

    def extended(self, ext, edge, pieces):
        own = pieces[self.x, 0, :T, :].astype(f32)
        before = pieces[jnp.maximum(self.x - 1, 0), 0, T - REACH : T, :].astype(f32)
        after = pieces[jnp.minimum(self.x + 1, X - 1), 0, :REACH, :].astype(f32)
        ext[:REACH, :] = jnp.where(self.x == 0, edge, before)
        ext[REACH : REACH + T, :] = own
        ext[REACH + T :, :] = jnp.where(self.x == X - 1, edge, after)
        return own

    def mask(self, slot):
        ids = self.first + lax.broadcasted_iota(jnp.int32, (T, 1), 0)
        return ids < self.length(slot)


def by_slot(*dims):
    return pl.BlockSpec((1,) + dims, lambda s: (s,) + (0,) * len(dims))


def whole(*dims):
    return pl.BlockSpec(dims, lambda s: (0,) * len(dims))


def all_x(rows):
    return pl.BlockSpec((X, 1, rows, LANES), lambda s: (0, s, 0, 0))


def once(*dims):
    return pl.BlockSpec(dims, lambda s: (0,) * len(dims), pipeline_mode=pl.Buffered(1))


def turn_body(in_ref, ahead_ref, rows):
    block = pl.program_id(0)
    blocks = pl.num_programs(0)
    for n in range(NEAR):
        tile = jnp.concatenate(
            [in_ref[n].astype(f32), jnp.zeros((LANES - GC, K), f32)], axis=0
        ).T
        if n >= GC % NEAR:
            tile = jnp.where(block == blocks - 1, 0.0, tile)
        rows[pl.ds(n, K, stride=NEAR), :] = tile
    far = K // NEAR
    for q in range(far):
        for r in range(NEAR):
            at = (q * NEAR + r) * NEAR
            ahead_ref[r, :, q * LANES : (q + 1) * LANES] = rows[at : at + NEAR, :].astype(bf16)


def turn(pos):
    far = K // NEAR
    ahead = pl.pallas_call(
        turn_body,
        grid=(LANES // NEAR,),
        out_shape=jax.ShapeDtypeStruct((NEAR, LANES, far * LANES), bf16),
        in_specs=[pl.BlockSpec((NEAR, GC, K), lambda b: (b, 0, 0))],
        out_specs=pl.BlockSpec((NEAR, NEAR, far * LANES), lambda b: (0, b, 0)),
        scratch_shapes=[pltpu.VMEM((K * NEAR, LANES), f32)],
        compiler_params=params(10),
        cost_estimate=cost(0, 8 << 20),
        name="turn",
    )(pos)
    return ahead.reshape(NEAR * LANES, -1)


def flip_body(in_ref, out_ref):
    for r in range(NEAR):
        out_ref[:, r * LANES : (r + 1) * LANES] = in_ref[
            (NEAR - 1 - r) * LANES : (NEAR - r) * LANES, :
        ]


def flip(ahead):
    far = K // NEAR
    return pl.pallas_call(
        flip_body,
        grid=(far,),
        out_shape=jax.ShapeDtypeStruct((far * LANES, NEAR * LANES), bf16),
        in_specs=[pl.BlockSpec((NEAR * LANES, LANES), lambda q: (0, far - 1 - q))],
        out_specs=pl.BlockSpec((LANES, NEAR * LANES), lambda q: (q, 0)),
        compiler_params=params(8),
        cost_estimate=cost(0, 8 << 20),
        name="flip",
    )(ahead)


def encode_body(
    dev_ref,
    len_ref,
    mov_ref,
    audio_ref,
    conv_ref,
    chan_ref,
    proj_ref,
    feat_ref,
    edge_ref,
    pair_ref,
    q_ref,
    slope_ref,
    m_ref,
    inv_ref,
    wide,
    proj,
    mid,
    normed,
):
    place = Place(dev_ref, len_ref, mov_ref)
    slot = pl.program_id(0)

    @pl.when(slot == 0)
    def _():
        proj[...] = jnp.zeros_like(proj)
        proj[:GC, :] = proj_ref[...]

    living = place.alive(slot)

    @pl.when(living)
    def _():
        for c in range(C // LANES):
            wide[c] = audio_ref[0, :, c * LANES : (c + 1) * LANES].astype(f32)
            for tap in range(2):
                at = tap * C + c * LANES
                pair_ref[0, :, at : at + LANES] = wide[c, pl.ds(tap, T, stride=2), :].astype(bf16)
        mid[...] = nn(pair_ref[0], conv_ref[...])
        bias, gain, shift = chan_ref[0:1, :], chan_ref[1:2, :], chan_ref[2:3, :]
        gain_two, shift_two = chan_ref[3:4, :], chan_ref[4:5, :]
        for at in range(0, T, CHUNK):
            rows = slice(at, at + CHUNK)
            conv = mid[rows, :] + bias
            offset = conv - jnp.mean(conv, axis=-1, keepdims=True)
            inverse = lax.rsqrt(jnp.mean(offset * offset, axis=-1, keepdims=True) + epsilon)
            q = offset * inverse
            pre = q * gain + shift
            below = phi(pre)
            encoded = (pre * below).astype(bf16).astype(f32)
            slope_ref[0, rows, :] = (below + pre * bell(pre)).astype(bf16)
            q_ref[0, rows, :] = q.astype(bf16)
            offset = encoded - jnp.mean(encoded, axis=-1, keepdims=True)
            inverse_two = lax.rsqrt(jnp.mean(offset * offset, axis=-1, keepdims=True) + epsilon)
            m = offset * inverse_two
            m_ref[0, rows, :] = m.astype(bf16)
            inv_ref[0, rows, :] = jnp.concatenate(
                [
                    jnp.broadcast_to(inverse, (CHUNK, LANES)),
                    jnp.broadcast_to(inverse_two, (CHUNK, LANES)),
                ],
                axis=1,
            )
            normed[rows, :] = (m * gain_two + shift_two).astype(bf16)
        projected = nt(normed[...], proj[...])
        features = jnp.where(place.mask(slot), projected, 0.0)
        for copy in range(X):
            feat_ref[copy, 0] = features.astype(bf16)
        edge_ref[0] = place.seam(features)

    @pl.when(jnp.logical_not(living))
    def _():
        feat_ref[...] = jnp.zeros_like(feat_ref)
        edge_ref[...] = jnp.zeros_like(edge_ref)


def encode(place, audio, conv_weight, channels, proj):
    return pl.pallas_call(
        encode_body,
        grid=(SLOTS,),
        out_shape=(
            jax.ShapeDtypeStruct((X, SLOTS, T, LANES), bf16),
            jax.ShapeDtypeStruct((SLOTS, REACH, LANES), bf16),
            jax.ShapeDtypeStruct((SLOTS, T, 2 * C), bf16),
            jax.ShapeDtypeStruct((SLOTS, T, C), bf16),
            jax.ShapeDtypeStruct((SLOTS, T, C), bf16),
            jax.ShapeDtypeStruct((SLOTS, T, C), bf16),
            jax.ShapeDtypeStruct((SLOTS, T, 2 * LANES), f32),
        ),
        in_specs=[SMEM] * 3
        + [
            by_slot(2 * T, C),
            once(2 * C, C),
            whole(5, C),
            whole(GC, C),
        ],
        out_specs=(
            all_x(T),
            by_slot(REACH, LANES),
            by_slot(T, 2 * C),
            by_slot(T, C),
            by_slot(T, C),
            by_slot(T, C),
            by_slot(T, 2 * LANES),
        ),
        scratch_shapes=[
            pltpu.VMEM((C // LANES, 2 * T, LANES), f32),
            pltpu.VMEM((LANES, C), bf16),
            pltpu.VMEM((T, C), f32),
            pltpu.VMEM((T, C), bf16),
        ],
        compiler_params=params(56),
        cost_estimate=cost(2 * SLOTS * T * C * (2 * C + LANES), 8 << 20, SLOTS * T * C * 2),
        name="encode",
    )(*place, audio, conv_weight, channels, proj)


def fill_windows(windows, ext, first):
    rows = T + NEAR * (K // NEAR - 1)
    for r in range(NEAR):
        windows[:, r * LANES : (r + 1) * LANES] = ext[first + r : first + r + rows, :].astype(bf16)


def gathered(group):
    total = group[:T, :LANES]
    for p in range(1, PER_GROUP):
        total += group[NEAR * p : NEAR * p + T, p * LANES : (p + 1) * LANES]
    return total


def fill_back(turned, place, slot, cot_ref, recv_ref):
    turned[GC:, :] = jnp.zeros((LANES - GC, T), f32)
    turned[:GC, :] = jnp.where(
        place.chosen == slot, recv_ref[0].astype(f32), cot_ref[0].astype(f32)
    )


def mix_body(
    dev_ref,
    len_ref,
    mov_ref,
    feat_ref,
    edge_ref,
    weight,
    cot_ref,
    recv_ref,
    states_ref,
    sent_ref,
    piece_ref,
    seam_ref,
    ext,
    windows,
    turned,
):
    place = Place(dev_ref, len_ref, mov_ref)
    slot = pl.program_id(0)
    living = place.alive(slot)
    wide = PER_GROUP * LANES

    @pl.when(living)
    def _():
        edge = edge_ref[0].astype(f32)
        own = place.extended(ext, edge, feat_ref)
        fill_windows(windows, ext, 0)
        fill_back(turned, place, slot, cot_ref, recv_ref)
        back = turned[...].T
        group = jnp.zeros((SPAN, wide), f32)
        for g in range(GROUPS):
            at = g * NEAR * PER_GROUP
            group += nn(windows[at : at + SPAN, :], weight[:, g * wide : (g + 1) * wide])
        mixed = gathered(group)
        below = phi(mixed)
        mask = place.mask(slot)
        states = jnp.where(mask, own + mixed * below, 0.0)
        states_ref[0] = states.T[:GC, :].astype(bf16)
        slopes = jnp.where(mask, back * (below + mixed * bell(mixed)), 0.0)
        for copy in range(X):
            piece_ref[copy, 0, :T, :] = slopes.astype(bf16)
            piece_ref[copy, 0, T:, :] = edge.astype(bf16)
        seam_ref[0] = place.seam(slopes)

    @pl.when(jnp.logical_not(living))
    def _():
        states_ref[...] = jnp.zeros_like(states_ref)
        piece_ref[...] = jnp.zeros_like(piece_ref)
        seam_ref[...] = jnp.zeros_like(seam_ref)

    @pl.when(place.chosen == slot)
    def _():
        sent_ref[...] = states_ref[0]


def mix(place, features, edge, weight, cotangent, received):
    return pl.pallas_call(
        mix_body,
        grid=(SLOTS,),
        out_shape=(
            jax.ShapeDtypeStruct((SLOTS, GC, T), bf16),
            jax.ShapeDtypeStruct((GC, T), bf16),
            jax.ShapeDtypeStruct((X, SLOTS, PIECE, LANES), bf16),
            jax.ShapeDtypeStruct((SLOTS, REACH, LANES), bf16),
        ),
        in_specs=[SMEM] * 3
        + [
            all_x(T),
            by_slot(REACH, LANES),
            once(*weight.shape),
            by_slot(GC, T),
            by_slot(GC, T),
        ],
        out_specs=(
            by_slot(GC, T),
            whole(GC, T),
            all_x(PIECE),
            by_slot(REACH, LANES),
        ),
        scratch_shapes=[
            pltpu.VMEM((EXT, LANES), f32),
            pltpu.VMEM((T + NEAR * (K // NEAR - 1), NEAR * LANES), bf16),
            pltpu.VMEM((LANES, T), f32),
        ],
        compiler_params=params(20),
        cost_estimate=cost(2 * SLOTS * SPAN * K * LANES * LANES, 7 << 20, SLOTS * T * LANES * 2),
        name="mix",
    )(*place, features, edge, weight, cotangent, received)


def taps_body(
    scale, dev_ref, len_ref, mov_ref, feat_ref, piece_ref, own_ref, core_ref, low_ref, both_ref, ext, windows, turned, sums
):
    place = Place(dev_ref, len_ref, mov_ref)
    slot = pl.program_id(0)
    spread = X * T
    rows = spread + NEAR * (K // NEAR - 1)

    @pl.when(slot == 0)
    def _():
        sums[...] = jnp.zeros_like(sums)

    @pl.when(place.y * spread < place.length(slot))
    def _():
        ext[:REACH, :] = piece_ref[0, 0, T:, :].astype(f32)
        ext[REACH + spread :, :] = piece_ref[X - 1, 0, T:, :].astype(f32)
        for x in range(X):
            ext[REACH + x * T : REACH + (x + 1) * T, :] = feat_ref[x, 0].astype(f32)
            turned[:, x * T : (x + 1) * T] = (
                piece_ref[x, 0, :T, :].astype(f32).T.astype(bf16)
            )
        for j in range(4):
            windows[:, j * LANES : (j + 1) * LANES] = ext[
                pl.ds(place.x + 4 * j, rows), :
            ].astype(bf16)
        for q in range(K // NEAR):
            sums[q] += nn(turned[...], windows[q * NEAR : q * NEAR + spread, :])

    @pl.when(slot == SLOTS - 1)
    def _():
        first_core = place.core == 0
        first_half = place.y == 0
        for q in range(K // NEAR):
            for far in range(2):
                at = 2 * far * LANES
                even = sums[q, :, at : at + LANES] * scale
                odd = sums[q, :, at + LANES : at + 2 * LANES] * scale
                keep = jnp.where(first_core, even, odd)
                send = jnp.where(first_core, odd, even)
                cell = 2 * q + far
                for mine, other, rows in ((own_ref, low_ref, keep), (core_ref, both_ref, send)):
                    one, two = rows[:REACH, :], rows[HALF : HALF + REACH, :]
                    mine[cell] = jnp.where(first_half, one, two).astype(bf16)
                    other[cell] = jnp.where(first_half, two, one).astype(bf16)


def taps(scale, place, features, pieces):
    shape = jax.ShapeDtypeStruct((CELLS, REACH, LANES), bf16)
    spread = X * T
    return pl.pallas_call(
        functools.partial(taps_body, scale),
        grid=(SLOTS,),
        out_shape=(shape,) * 4,
        in_specs=[SMEM] * 3 + [all_x(T), all_x(PIECE)],
        out_specs=(whole(*shape.shape),) * 4,
        scratch_shapes=[
            pltpu.VMEM((spread + 2 * REACH, LANES), f32),
            pltpu.VMEM((spread + NEAR * (K // NEAR - 1), 4 * LANES), bf16),
            pltpu.VMEM((LANES, spread), bf16),
            pltpu.VMEM((K // NEAR, LANES, 4 * LANES), f32),
        ],
        compiler_params=params(16),
        cost_estimate=cost(2 * SLOTS * SPAN * K * LANES * LANES, 4 << 20),
        name="taps",
    )(*place, features, pieces)


def backward_body(
    scale,
    dev_ref,
    len_ref,
    mov_ref,
    piece_ref,
    edge_ref,
    cot_ref,
    recv_ref,
    weight,
    pair_ref,
    q_ref,
    slope_ref,
    m_ref,
    inv_ref,
    conv_ref,
    chan_ref,
    proj_ref,
    audio_grad_ref,
    keep_ref,
    send_ref,
    ext,
    windows,
    turned,
    proj,
    feat_grad,
    normed,
    mid,
    wide,
    conv_sum,
    proj_sum,
    chan_sum,
    columns,
):
    place = Place(dev_ref, len_ref, mov_ref)
    slot = pl.program_id(0)
    living = place.alive(slot)
    span = PER_GROUP * LANES

    @pl.when(slot == 0)
    def _():
        proj[...] = jnp.zeros_like(proj)
        proj[:GC, :] = proj_ref[...]
        conv_sum[...] = jnp.zeros_like(conv_sum)
        proj_sum[...] = jnp.zeros_like(proj_sum)
        chan_sum[...] = jnp.zeros_like(chan_sum)

    @pl.when(living)
    def _():
        place.extended(ext, edge_ref[0].astype(f32), piece_ref)
        fill_windows(windows, ext, 1)
        fill_back(turned, place, slot, cot_ref, recv_ref)
        group = jnp.zeros((SPAN, span), f32)
        for g in range(GROUPS):
            at = g * NEAR * PER_GROUP
            group += nt(windows[at : at + SPAN, :], weight[g * span : (g + 1) * span, :])
        spread = gathered(group)
        feat_grad[...] = jnp.where(place.mask(slot), turned[...].T + spread, 0.0).astype(bf16)
        gain = chan_ref[1:2, :]
        gain_two, shift_two = chan_ref[3:4, :], chan_ref[4:5, :]
        mid[...] = nn(feat_grad[...], proj[...])
        for at in range(0, T, CHUNK):
            rows = slice(at, at + CHUNK)
            m = m_ref[0, rows, :].astype(f32)
            normed[rows, :] = (m * gain_two + shift_two).astype(bf16)
            normed_grad = mid[rows, :]
            chan_sum[24:32, :] += jnp.sum((normed_grad * m).reshape(-1, 8, C), axis=0)
            chan_sum[32:40, :] += jnp.sum(normed_grad.reshape(-1, 8, C), axis=0)
            scaled = normed_grad * gain_two
            first = jnp.mean(scaled, axis=-1, keepdims=True)
            second = jnp.mean(scaled * m, axis=-1, keepdims=True)
            inverse_two = inv_ref[0, rows, LANES : LANES + 1]
            pre_grad = inverse_two * (scaled - first - m * second) * slope_ref[
                0, rows, :
            ].astype(f32)
            q = q_ref[0, rows, :].astype(f32)
            chan_sum[8:16, :] += jnp.sum((pre_grad * q).reshape(-1, 8, C), axis=0)
            chan_sum[16:24, :] += jnp.sum(pre_grad.reshape(-1, 8, C), axis=0)
            scaled = pre_grad * gain
            first = jnp.mean(scaled, axis=-1, keepdims=True)
            second = jnp.mean(scaled * q, axis=-1, keepdims=True)
            inverse = inv_ref[0, rows, 0:1]
            conv_grad = inverse * (scaled - first - q * second)
            chan_sum[0:8, :] += jnp.sum(conv_grad.reshape(-1, 8, C), axis=0)
            mid[rows, :] = conv_grad
        operand = mid[...].astype(bf16)
        for tap in range(2):
            rows = slice(tap * C, (tap + 1) * C)
            audio_grad = nt(operand, conv_ref[rows, :])
            for c in range(C // LANES):
                wide[c, pl.ds(tap, T, stride=2), :] = audio_grad[:, c * LANES : (c + 1) * LANES]
            conv_sum[rows, :] += tn(pair_ref[0, :, rows], operand)
        for c in range(C // LANES):
            audio_grad_ref[0, :, c * LANES : (c + 1) * LANES] = wide[c].astype(bf16)
        proj_sum[...] += tn(normed[...], feat_grad[...])

    @pl.when(jnp.logical_not(living))
    def _():
        audio_grad_ref[...] = jnp.zeros_like(audio_grad_ref)

    @pl.when(slot == SLOTS - 1)
    def _():
        first_core = place.core == 0
        columns[...] = jnp.zeros_like(columns)
        for n in range(5):
            columns[GC + n : GC + n + 1, :] = jnp.sum(
                chan_sum[8 * n : 8 * n + 8, :], axis=0, keepdims=True
            )
        proj_sum[...] += columns[...].T
        for x in range(X):
            lanes = slice(x * LANES, (x + 1) * LANES)
            for cell in range(CELLS):
                at = 2 * cell * 32
                even = conv_sum[at : at + 32, lanes]
                odd = conv_sum[at + 32 : at + 64, lanes]
                rows = slice(cell * 32, (cell + 1) * 32)
                keep_ref[x, rows, :] = (jnp.where(first_core, even, odd) * scale).astype(bf16)
                send_ref[x, rows, :] = (jnp.where(first_core, odd, even) * scale).astype(bf16)
            for four in range(CELLS // 4):
                even, odd = [
                    jnp.concatenate(
                        [
                            proj_sum[at : at + SPARE, :]
                            for at in (
                                (2 * cell + odd) * 16 + x * SPARE
                                for cell in range(4 * four, 4 * four + 4)
                            )
                        ],
                        axis=0,
                    )
                    for odd in range(2)
                ]
                rows = slice(CONV_ROWS + four * 16, CONV_ROWS + (four + 1) * 16)
                keep_ref[x, rows, :] = (jnp.where(first_core, even, odd) * scale).astype(bf16)
                send_ref[x, rows, :] = (jnp.where(first_core, odd, even) * scale).astype(bf16)


def backward(
    scale, place, pieces, edge, cotangent, received, weight, stored, conv_weight, channels, proj
):
    shape = jax.ShapeDtypeStruct((X, REST, LANES), bf16)
    return pl.pallas_call(
        functools.partial(backward_body, scale),
        grid=(SLOTS,),
        out_shape=(jax.ShapeDtypeStruct((SLOTS, 2 * T, C), bf16), shape, shape),
        in_specs=[SMEM] * 3
        + [
            all_x(PIECE),
            by_slot(REACH, LANES),
            by_slot(GC, T),
            by_slot(GC, T),
            once(*weight.shape),
            by_slot(T, 2 * C),
            by_slot(T, C),
            by_slot(T, C),
            by_slot(T, C),
            by_slot(T, 2 * LANES),
            once(2 * C, C),
            whole(5, C),
            whole(GC, C),
        ],
        out_specs=(by_slot(2 * T, C), whole(*shape.shape), whole(*shape.shape)),
        scratch_shapes=[
            pltpu.VMEM((EXT, LANES), f32),
            pltpu.VMEM((T + NEAR * (K // NEAR - 1), NEAR * LANES), bf16),
            pltpu.VMEM((LANES, T), f32),
            pltpu.VMEM((LANES, C), bf16),
            pltpu.VMEM((T, LANES), bf16),
            pltpu.VMEM((T, C), bf16),
            pltpu.VMEM((T, C), f32),
            pltpu.VMEM((C // LANES, 2 * T, LANES), f32),
            pltpu.VMEM((2 * C, C), f32),
            pltpu.VMEM((C, LANES), f32),
            pltpu.VMEM((40, C), f32),
            pltpu.VMEM((LANES, C), f32),
        ],
        compiler_params=params(56),
        cost_estimate=cost(
            2 * SLOTS * (SPAN * K * LANES * LANES + T * C * (4 * C + 2 * LANES)), 14 << 20
        ),
        name="backward",
    )(
        *place,
        pieces,
        edge,
        cotangent,
        received,
        weight,
        *stored,
        conv_weight,
        channels,
        proj,
    )


def join_body(dev_ref, keep_ref, recv_ref, *out_refs):
    x = lax.rem(dev_ref[0], X)
    for step, out_ref in enumerate(out_refs):
        at = lax.rem(x + step, X)
        out_ref[...] = (keep_ref[at].astype(f32) + recv_ref[at].astype(f32)).astype(bf16)


def join(dev, keep, received):
    shape = jax.ShapeDtypeStruct((REST, LANES), bf16)
    return pl.pallas_call(
        join_body,
        out_shape=(shape,) * X,
        in_specs=[SMEM] + [VMEM] * 2,
        out_specs=(VMEM,) * X,
        compiler_params=params(8),
        cost_estimate=cost(0, 2 << 20),
        name="join",
    )(dev, keep, received)


def cells_body(*refs):
    pos_refs, rest_refs, out_ref, rows = refs[:4], refs[4:8], refs[8], refs[9]

    def summed(parts, *at):
        result = parts[0][at].astype(f32)
        for part in parts[1:]:
            result += part[at].astype(f32)
        return result

    for four in range(CELLS // 4):
        at = CONV_ROWS + four * 16
        small = summed(rest_refs, slice(at, at + 16), slice(None))
        for n in range(4):
            cell = 4 * four + n
            rows[...] = summed(pos_refs, cell)
            rows[HALF:, :] = small[n * SPARE : (n + 1) * SPARE, :]
            out_ref[cell, :REACH, :] = rows[...].astype(bf16)
            conv = summed(rest_refs, slice(cell * 32, cell * 32 + 32), slice(None))
            out_ref[cell, REACH:, :] = conv.astype(bf16)


def make_cells(pos_parts, rest_parts):
    return pl.pallas_call(
        cells_body,
        out_shape=jax.ShapeDtypeStruct((CELLS, REACH + 32, LANES), bf16),
        in_specs=[VMEM] * 8,
        out_specs=VMEM,
        scratch_shapes=[pltpu.VMEM((REACH, LANES), f32)],
        compiler_params=params(8),
        cost_estimate=cost(0, 2 << 20),
        name="cells",
    )(*pos_parts, *rest_parts)


def total_body(in_ref, out_ref):
    total = in_ref[0].astype(f32)
    for n in range(1, in_ref.shape[0]):
        total += in_ref[n].astype(f32)
    for copy in range(MP):
        out_ref[copy] = total.astype(bf16)


def total(parts):
    return pl.pallas_call(
        total_body,
        out_shape=jax.ShapeDtypeStruct((MP,) + parts.shape[1:], bf16),
        in_specs=[VMEM],
        out_specs=VMEM,
        compiler_params=params(10),
        cost_estimate=cost(0, 2 * parts.size),
        name="total",
    )(parts)


def finish_body(
    dev_ref,
    len_ref,
    mov_ref,
    in_ref,
    states_ref,
    other_ref,
    hidden_ref,
    pos_ref,
    conv_ref,
    proj_ref,
    chan_ref,
):
    place = Place(dev_ref, len_ref, mov_ref)
    for slot in range(SLOTS):
        hidden_ref[slot] = jnp.where(
            place.chosen == slot, other_ref[...].astype(f32), states_ref[slot].astype(f32)
        ).astype(bf16)
    small = []
    for x in range(X):
        low, high = in_ref[x].astype(f32), in_ref[X + x].astype(f32)
        block = jnp.concatenate(
            [low[:HALF, :], high[:HALF, :], jnp.zeros((LANES - GC, LANES), f32)], axis=0
        ).T
        pos_ref[x] = block[:GC, :GC]
        both = low[HALF:, :] + high[HALF:, :]
        small.append(both[:SPARE, :])
        conv_ref[:, x * LANES : (x + 1) * LANES] = both[SPARE:, :]
    small = jnp.concatenate(small, axis=0)
    proj_ref[...] = small[:, :GC]
    chan_ref[...] = jnp.concatenate([small] * 8, axis=0).T[GC : GC + 5, :16]


def finish(place, cells, states, other):
    return pl.pallas_call(
        finish_body,
        out_shape=(
            jax.ShapeDtypeStruct((SLOTS, GC, T), bf16),
            jax.ShapeDtypeStruct((4, GC, GC), f32),
            jax.ShapeDtypeStruct((32, C), f32),
            jax.ShapeDtypeStruct((16, GC), f32),
            jax.ShapeDtypeStruct((5, 16), f32),
        ),
        in_specs=[SMEM] * 3 + [VMEM] * 3,
        out_specs=(VMEM,) * 5,
        compiler_params=params(8),
        name="finish",
    )(*place, cells, states, other)


def per_device(
    audio, lengths, moved_slots, conv_weight, channel_params, proj_weight, pos_weight, cotangent
):
    data_index = lax.axis_index("dp")
    model_index = lax.axis_index("mp")
    scale = (SLOTS * DP * T * MP) ** -0.5
    dev = (data_index * MP + model_index).astype(jnp.int32).reshape(1)
    place = (dev, lengths, moved_slots.reshape(-1))
    swap = [(i, i ^ (DP // 2)) for i in range(DP)]
    core_swap = [(i, i ^ 1) for i in range(DP)]
    channels = channel_params.T
    proj = proj_weight.T
    cot = cotangent.transpose(0, 2, 1)

    rows = [list(range(X)), list(range(X, 2 * X))]
    seam = [(X - 1, X), (X, X - 1)]

    def over_x(copies):
        return lax.all_to_all(copies, "mp", 0, 0, axis_index_groups=rows, tiled=True)

    received = lax.ppermute(cot, "dp", swap)
    features, edge, *stored = encode(place, audio, conv_weight, channels, proj)
    features = over_x(features)
    edge = lax.ppermute(edge, "mp", seam)
    ahead = turn(pos_weight.transpose(1, 2, 0))
    states, sent, pieces, edge = mix(place, features, edge, ahead, cot, received)
    pieces, ahead = lax.optimization_barrier((pieces, ahead))
    pieces = over_x(pieces)
    edge = lax.ppermute(edge, "mp", seam)
    other = lax.ppermute(sent, "dp", swap)
    behind = flip(ahead)
    own, to_core, to_low, to_both = taps(scale, place, features, pieces)
    to_core, to_low, to_both, edge = lax.optimization_barrier((to_core, to_low, to_both, edge))
    low_swap = [(i, i ^ X) for i in range(MP)]
    both_swap = [(i, i ^ MP ^ X) for i in range(DP * MP)]
    pos_parts = (
        own,
        lax.ppermute(to_core, "dp", core_swap),
        lax.ppermute(to_low, "mp", low_swap),
        lax.ppermute(to_both, ("dp", "mp"), both_swap),
    )
    audio_grad, keep, send = backward(
        scale,
        place,
        pieces,
        edge,
        cot,
        received,
        behind,
        stored,
        conv_weight,
        channels,
        proj,
    )
    send, pos_parts = lax.optimization_barrier((send, pos_parts))
    chunks = join(dev, keep, lax.ppermute(send, "dp", core_swap))
    rest_parts = [chunks[0]]
    for step in (2, 1, 3):
        route = [(X * y + x, X * y + (x + step) % X) for y in range(2) for x in range(X)]
        rest_parts.append(lax.ppermute(chunks[step], "mp", route))
    cells = make_cells(pos_parts, rest_parts)
    groups = [list(range(bit, DP, 2)) for bit in range(2)]
    cells = lax.all_to_all(cells, "dp", 0, 0, axis_index_groups=groups, tiled=True)
    cells, other = lax.optimization_barrier((cells, other))
    cells = lax.all_to_all(total(cells), "mp", 0, 0, tiled=True)
    hidden, grad_pos, grad_conv, grad_proj, grad_channels = finish(place, cells, states, other)
    return (
        hidden.transpose(0, 2, 1),
        audio_grad,
        grad_pos,
        grad_conv,
        grad_proj,
        grad_channels.T,
    )


def solution(mesh):
    return jax.shard_map(
        per_device,
        mesh=mesh,
        in_specs=(P("dp", "mp", None), P(), P(), P(), P(), P(), P(), P("dp", "mp", None)),
        out_specs=(
            P("dp", "mp", None),
            P("dp", "mp", None),
            P("dp", None, None),
            P("dp", None),
            P("dp", None),
            P("dp", None),
        ),
        check_vma=False,
    )
```

```python
import functools

import jax
import jax.numpy as jnp
from jax import lax
from jax.experimental import pallas as pl
from jax.experimental.pallas import tpu as pltpu
from jax.sharding import PartitionSpec as P

epsilon = 1e-05
root_half = 0.7071067811865476
density = 0.3989422804014327

SLOTS = 2
T = 256
C = 512
GC = 120
LANES = 128
K = 128
REACH = 64
EXT = T + 2 * REACH
NEAR = 16
GROUPS = 2
PER_GROUP = 4
SPAN = T + NEAR * (PER_GROUP - 1)
CHUNK = 32
MP = 8
DP = 32
X = 4
CELLS = 16
PIECE = 2 * T + REACH
HALF = GC // 2
SPARE = REACH - HALF
CONV_ROWS = CELLS * 32
REST = CONV_ROWS + CELLS * SPARE

f32 = jnp.float32
bf16 = jnp.bfloat16

VMEM = pl.BlockSpec(memory_space=pltpu.VMEM)
SMEM = pl.BlockSpec(memory_space=pltpu.SMEM)


def params(mebibytes):
    return pltpu.CompilerParams(vmem_limit_bytes=mebibytes << 20)


def cost(flops, moved, trans=0):
    return pl.CostEstimate(flops=flops, bytes_accessed=moved, transcendentals=trans)


def phi(values):
    return 0.5 * (1.0 + lax.erf(values * root_half))


def bell(values):
    return jnp.exp(-0.5 * values * values) * density


def nt(a, b):
    return lax.dot_general(a, b, (((1,), (1,)), ((), ())), preferred_element_type=f32)


def tn(a, b):
    return lax.dot_general(a, b, (((0,), (0,)), ((), ())), preferred_element_type=f32)


def nn(a, b):
    return jnp.dot(a, b, preferred_element_type=f32)


class Place:
    def __init__(self, dev_ref, len_ref, mov_ref):
        self.data = dev_ref[0] // MP
        self.model = lax.rem(dev_ref[0], MP)
        self.x = lax.rem(self.model, X)
        self.y = self.model // X
        self.core = lax.rem(self.data, 2)
        self.cell = self.data // 2
        self.first = self.model * T
        self.lengths = len_ref
        self.chosen = mov_ref[lax.rem(self.data, DP // 2)]

    def length(self, slot):
        return self.lengths[self.data * SLOTS + slot]

    def alive(self, slot):
        return self.first < self.length(slot)

    def mask(self, slot):
        ids = self.first + lax.broadcasted_iota(jnp.int32, (T, 1), 0)
        return ids < self.length(slot)


def by_slot(*dims):
    return pl.BlockSpec((1,) + dims, lambda s: (s,) + (0,) * len(dims))


def whole(*dims):
    return pl.BlockSpec(dims, lambda s: (0,) * len(dims))


def once(*dims):
    return pl.BlockSpec(dims, lambda s: (0,) * len(dims), pipeline_mode=pl.Buffered(1))


def turn_body(in_ref, ahead_ref, behind_ref, rows):
    block = pl.program_id(0)
    blocks = pl.num_programs(0)
    for n in range(NEAR):
        tile = jnp.concatenate(
            [in_ref[n].astype(f32), jnp.zeros((LANES - GC, K), f32)], axis=0
        ).T
        if n >= GC % NEAR:
            tile = jnp.where(block == blocks - 1, 0.0, tile)
        rows[pl.ds(n, K, stride=NEAR), :] = tile
    far = K // NEAR
    for q in range(far):
        for r in range(NEAR):
            at = (q * NEAR + r) * NEAR
            tile = rows[at : at + NEAR, :].astype(bf16)
            ahead_ref[r, :, q * LANES : (q + 1) * LANES] = tile
            r_back = NEAR - 1 - r
            behind_ref[far - 1 - q, :, r_back * LANES : (r_back + 1) * LANES] = tile


def turn(pos):
    far = K // NEAR
    ahead, behind = pl.pallas_call(
        turn_body,
        grid=(LANES // NEAR,),
        out_shape=(
            jax.ShapeDtypeStruct((NEAR, LANES, far * LANES), bf16),
            jax.ShapeDtypeStruct((far, LANES, NEAR * LANES), bf16),
        ),
        in_specs=[pl.BlockSpec((NEAR, GC, K), lambda b: (b, 0, 0))],
        out_specs=(
            pl.BlockSpec((NEAR, NEAR, far * LANES), lambda b: (0, b, 0)),
            pl.BlockSpec((far, NEAR, NEAR * LANES), lambda b: (0, b, 0)),
        ),
        scratch_shapes=[pltpu.VMEM((K * NEAR, LANES), f32)],
        compiler_params=params(56),
        cost_estimate=cost(0, 12 << 20),
        name="turn",
    )(pos)
    return ahead.reshape(NEAR * LANES, -1), behind.reshape(far * LANES, -1)


def encode_body(
    dev_ref,
    len_ref,
    mov_ref,
    audio_ref,
    conv_ref,
    chan_ref,
    proj_ref,
    feat_ref,
    tail_ref,
    head_ref,
    pair_ref,
    q_ref,
    slope_ref,
    m_ref,
    inv_ref,
    wide,
    proj,
    mid,
    normed,
):
    place = Place(dev_ref, len_ref, mov_ref)
    slot = pl.program_id(0)

    @pl.when(slot == 0)
    def _():
        proj[...] = jnp.zeros_like(proj)
        proj[:GC, :] = proj_ref[...]

    living = place.alive(slot)

    @pl.when(living)
    def _():
        for c in range(C // LANES):
            wide[c] = audio_ref[0, :, c * LANES : (c + 1) * LANES].astype(f32)
            for tap in range(2):
                at = tap * C + c * LANES
                pair_ref[0, :, at : at + LANES] = wide[c, pl.ds(tap, T, stride=2), :].astype(bf16)
        mid[...] = nn(pair_ref[0], conv_ref[...])
        bias, gain, shift = chan_ref[0:1, :], chan_ref[1:2, :], chan_ref[2:3, :]
        gain_two, shift_two = chan_ref[3:4, :], chan_ref[4:5, :]
        for at in range(0, T, CHUNK):
            rows = slice(at, at + CHUNK)
            conv = mid[rows, :] + bias
            offset = conv - jnp.mean(conv, axis=-1, keepdims=True)
            inverse = lax.rsqrt(jnp.mean(offset * offset, axis=-1, keepdims=True) + epsilon)
            q = offset * inverse
            pre = q * gain + shift
            below = phi(pre)
            encoded = (pre * below).astype(bf16).astype(f32)
            slope_ref[0, rows, :] = (below + pre * bell(pre)).astype(bf16)
            q_ref[0, rows, :] = q.astype(bf16)
            offset = encoded - jnp.mean(encoded, axis=-1, keepdims=True)
            inverse_two = lax.rsqrt(jnp.mean(offset * offset, axis=-1, keepdims=True) + epsilon)
            m = offset * inverse_two
            m_ref[0, rows, :] = m.astype(bf16)
            inv_ref[0, rows, :] = jnp.concatenate(
                [
                    jnp.broadcast_to(inverse, (CHUNK, LANES)),
                    jnp.broadcast_to(inverse_two, (CHUNK, LANES)),
                ],
                axis=1,
            )
            normed[rows, :] = (m * gain_two + shift_two).astype(bf16)
        projected = nt(normed[...], proj[...])
        feat_ref[0] = jnp.where(place.mask(slot), projected, 0.0).astype(bf16)

    @pl.when(jnp.logical_not(living))
    def _():
        feat_ref[...] = jnp.zeros_like(feat_ref)

    tail_ref[0] = feat_ref[0, T - REACH :, :]
    head_ref[0] = feat_ref[0, :REACH, :]


def encode(place, audio, conv_weight, channels, proj):
    return pl.pallas_call(
        encode_body,
        grid=(SLOTS,),
        out_shape=(
            jax.ShapeDtypeStruct((SLOTS, T, LANES), bf16),
            jax.ShapeDtypeStruct((SLOTS, REACH, LANES), bf16),
            jax.ShapeDtypeStruct((SLOTS, REACH, LANES), bf16),
            jax.ShapeDtypeStruct((SLOTS, T, 2 * C), bf16),
            jax.ShapeDtypeStruct((SLOTS, T, C), bf16),
            jax.ShapeDtypeStruct((SLOTS, T, C), bf16),
            jax.ShapeDtypeStruct((SLOTS, T, C), bf16),
            jax.ShapeDtypeStruct((SLOTS, T, 2 * LANES), f32),
        ),
        in_specs=[SMEM] * 3
        + [
            by_slot(2 * T, C),
            once(2 * C, C),
            whole(5, C),
            whole(GC, C),
        ],
        out_specs=(
            by_slot(T, LANES),
            by_slot(REACH, LANES),
            by_slot(REACH, LANES),
            by_slot(T, 2 * C),
            by_slot(T, C),
            by_slot(T, C),
            by_slot(T, C),
            by_slot(T, 2 * LANES),
        ),
        scratch_shapes=[
            pltpu.VMEM((C // LANES, 2 * T, LANES), f32),
            pltpu.VMEM((LANES, C), bf16),
            pltpu.VMEM((T, C), f32),
            pltpu.VMEM((T, C), bf16),
        ],
        compiler_params=params(56),
        cost_estimate=cost(2 * SLOTS * T * C * (2 * C + LANES), 8 << 20, SLOTS * T * C * 2),
        name="encode",
    )(*place, audio, conv_weight, channels, proj)


def fill_ext(ext, low, own, high):
    ext[:REACH, :] = low.astype(f32)
    ext[REACH : REACH + T, :] = own.astype(f32)
    ext[REACH + T :, :] = high.astype(f32)


def fill_windows(windows, ext, first):
    rows = T + NEAR * (K // NEAR - 1)
    for r in range(NEAR):
        windows[:, r * LANES : (r + 1) * LANES] = ext[first + r : first + r + rows, :].astype(bf16)


def gathered(group):
    total = group[:T, :LANES]
    for p in range(1, PER_GROUP):
        total += group[NEAR * p : NEAR * p + T, p * LANES : (p + 1) * LANES]
    return total


def fill_back(turned, place, slot, cot_ref, recv_ref):
    turned[GC:, :] = jnp.zeros((LANES - GC, T), f32)
    turned[:GC, :] = jnp.where(
        place.chosen == slot, recv_ref[0].astype(f32), cot_ref[0].astype(f32)
    )


def mix_body(
    dev_ref,
    len_ref,
    mov_ref,
    feat_ref,
    low_ref,
    high_ref,
    weight,
    cot_ref,
    recv_ref,
    states_ref,
    sent_ref,
    slopes_ref,
    tail_ref,
    head_ref,
    piece_ref,
    ext,
    windows,
    turned,
):
    place = Place(dev_ref, len_ref, mov_ref)
    slot = pl.program_id(0)
    living = place.alive(slot)
    wide = PER_GROUP * LANES

    @pl.when(living)
    def _():
        own = feat_ref[0].astype(f32)
        fill_ext(ext, low_ref[0], own, high_ref[0])
        fill_windows(windows, ext, 0)
        fill_back(turned, place, slot, cot_ref, recv_ref)
        back = turned[...].T
        group = jnp.zeros((SPAN, wide), f32)
        for g in range(GROUPS):
            at = g * NEAR * PER_GROUP
            group += nn(windows[at : at + SPAN, :], weight[:, g * wide : (g + 1) * wide])
        mixed = gathered(group)
        below = phi(mixed)
        mask = place.mask(slot)
        states = jnp.where(mask, own + mixed * below, 0.0)
        states_ref[0] = states.T[:GC, :].astype(bf16)
        slopes = jnp.where(mask, back * (below + mixed * bell(mixed)), 0.0)
        slopes_ref[0] = slopes.astype(bf16)
        edge = jnp.where(place.x < X // 2, low_ref[0].astype(f32), high_ref[0].astype(f32))
        piece_ref[0, :T, :] = feat_ref[0]
        piece_ref[0, T : T + REACH, :] = edge.astype(bf16)
        piece_ref[0, T + REACH :, :] = slopes.astype(bf16)

    @pl.when(jnp.logical_not(living))
    def _():
        states_ref[...] = jnp.zeros_like(states_ref)
        slopes_ref[...] = jnp.zeros_like(slopes_ref)
        piece_ref[...] = jnp.zeros_like(piece_ref)

    tail_ref[0] = slopes_ref[0, T - REACH :, :]
    head_ref[0] = slopes_ref[0, :REACH, :]

    @pl.when(place.chosen == slot)
    def _():
        sent_ref[...] = states_ref[0]


def mix(place, features, low, high, weight, cotangent, received):
    return pl.pallas_call(
        mix_body,
        grid=(SLOTS,),
        out_shape=(
            jax.ShapeDtypeStruct((SLOTS, GC, T), bf16),
            jax.ShapeDtypeStruct((GC, T), bf16),
            jax.ShapeDtypeStruct((SLOTS, T, LANES), bf16),
            jax.ShapeDtypeStruct((SLOTS, REACH, LANES), bf16),
            jax.ShapeDtypeStruct((SLOTS, REACH, LANES), bf16),
            jax.ShapeDtypeStruct((SLOTS, PIECE, LANES), bf16),
        ),
        in_specs=[SMEM] * 3
        + [
            by_slot(T, LANES),
            by_slot(REACH, LANES),
            by_slot(REACH, LANES),
            once(*weight.shape),
            by_slot(GC, T),
            by_slot(GC, T),
        ],
        out_specs=(
            by_slot(GC, T),
            whole(GC, T),
            by_slot(T, LANES),
            by_slot(REACH, LANES),
            by_slot(REACH, LANES),
            by_slot(PIECE, LANES),
        ),
        scratch_shapes=[
            pltpu.VMEM((EXT, LANES), f32),
            pltpu.VMEM((T + NEAR * (K // NEAR - 1), NEAR * LANES), bf16),
            pltpu.VMEM((LANES, T), f32),
        ],
        compiler_params=params(20),
        cost_estimate=cost(2 * SLOTS * SPAN * K * LANES * LANES, 7 << 20, SLOTS * T * LANES * 2),
        name="mix",
    )(*place, features, low, high, weight, cotangent, received)


def taps_body(scale, dev_ref, len_ref, mov_ref, *refs):
    piece_refs, (keep_ref, send_ref) = refs[:X], refs[X : X + 2]
    ext, windows, turned, sums = refs[X + 2 :]
    place = Place(dev_ref, len_ref, mov_ref)
    slot = pl.program_id(0)
    spread = X * T
    rows = spread + NEAR * (K // NEAR - 1)

    @pl.when(slot == 0)
    def _():
        sums[...] = jnp.zeros_like(sums)

    @pl.when(place.y * spread < place.length(slot))
    def _():
        for step, piece_ref in enumerate(piece_refs):
            x = lax.rem(place.x + (X - step), X)
            at = pl.multiple_of(x * T, T)
            ext[pl.ds(REACH + at, T), :] = piece_ref[0, :T, :].astype(f32)
            turned[:, pl.ds(at, T)] = piece_ref[0, T + REACH :, :].astype(f32).T.astype(bf16)

            @pl.when(x == 0)
            def _():
                ext[:REACH, :] = piece_ref[0, T : T + REACH, :].astype(f32)

            @pl.when(x == X - 1)
            def _():
                ext[REACH + spread :, :] = piece_ref[0, T : T + REACH, :].astype(f32)

        for j in range(4):
            windows[:, j * LANES : (j + 1) * LANES] = ext[
                pl.ds(place.x + 4 * j, rows), :
            ].astype(bf16)
        for q in range(K // NEAR):
            sums[q] += nn(turned[...], windows[q * NEAR : q * NEAR + spread, :])

    @pl.when(slot == SLOTS - 1)
    def _():
        first_core = place.core == 0
        for q in range(K // NEAR):
            for far in range(2):
                at = 2 * far * LANES
                even = sums[q, :, at : at + LANES] * scale
                odd = sums[q, :, at + LANES : at + 2 * LANES] * scale
                keep = jnp.where(first_core, even, odd)
                send = jnp.where(first_core, odd, even)
                for y in range(2):
                    rows = slice(y * HALF, y * HALF + REACH)
                    keep_ref[y, 2 * q + far] = keep[rows, :].astype(bf16)
                    send_ref[y, 2 * q + far] = send[rows, :].astype(bf16)


def taps(scale, place, pieces):
    shape = jax.ShapeDtypeStruct((2, CELLS, REACH, LANES), bf16)
    spread = X * T
    return pl.pallas_call(
        functools.partial(taps_body, scale),
        grid=(SLOTS,),
        out_shape=(shape,) * 2,
        in_specs=[SMEM] * 3 + [by_slot(PIECE, LANES)] * X,
        out_specs=(whole(*shape.shape),) * 2,
        scratch_shapes=[
            pltpu.VMEM((spread + 2 * REACH, LANES), f32),
            pltpu.VMEM((spread + NEAR * (K // NEAR - 1), 4 * LANES), bf16),
            pltpu.VMEM((LANES, spread), bf16),
            pltpu.VMEM((K // NEAR, LANES, 4 * LANES), f32),
        ],
        compiler_params=params(16),
        cost_estimate=cost(2 * SLOTS * SPAN * K * LANES * LANES, 4 << 20),
        name="taps",
    )(*place, *pieces)


def backward_body(
    scale,
    dev_ref,
    len_ref,
    mov_ref,
    slopes_ref,
    low_ref,
    high_ref,
    cot_ref,
    recv_ref,
    weight,
    pair_ref,
    q_ref,
    slope_ref,
    m_ref,
    inv_ref,
    conv_ref,
    chan_ref,
    proj_ref,
    audio_grad_ref,
    keep_ref,
    send_ref,
    ext,
    windows,
    turned,
    proj,
    feat_grad,
    normed,
    mid,
    wide,
    conv_sum,
    proj_sum,
    chan_sum,
    columns,
):
    place = Place(dev_ref, len_ref, mov_ref)
    slot = pl.program_id(0)
    living = place.alive(slot)
    span = PER_GROUP * LANES

    @pl.when(slot == 0)
    def _():
        proj[...] = jnp.zeros_like(proj)
        proj[:GC, :] = proj_ref[...]
        conv_sum[...] = jnp.zeros_like(conv_sum)
        proj_sum[...] = jnp.zeros_like(proj_sum)
        chan_sum[...] = jnp.zeros_like(chan_sum)

    @pl.when(living)
    def _():
        fill_ext(ext, low_ref[0], slopes_ref[0], high_ref[0])
        fill_windows(windows, ext, 1)
        fill_back(turned, place, slot, cot_ref, recv_ref)
        group = jnp.zeros((SPAN, span), f32)
        for g in range(GROUPS):
            at = g * NEAR * PER_GROUP
            group += nt(windows[at : at + SPAN, :], weight[g * span : (g + 1) * span, :])
        spread = gathered(group)
        feat_grad[...] = jnp.where(place.mask(slot), turned[...].T + spread, 0.0).astype(bf16)
        gain = chan_ref[1:2, :]
        gain_two, shift_two = chan_ref[3:4, :], chan_ref[4:5, :]
        mid[...] = nn(feat_grad[...], proj[...])
        for at in range(0, T, CHUNK):
            rows = slice(at, at + CHUNK)
            m = m_ref[0, rows, :].astype(f32)
            normed[rows, :] = (m * gain_two + shift_two).astype(bf16)
            normed_grad = mid[rows, :]
            chan_sum[24:32, :] += jnp.sum((normed_grad * m).reshape(-1, 8, C), axis=0)
            chan_sum[32:40, :] += jnp.sum(normed_grad.reshape(-1, 8, C), axis=0)
            scaled = normed_grad * gain_two
            first = jnp.mean(scaled, axis=-1, keepdims=True)
            second = jnp.mean(scaled * m, axis=-1, keepdims=True)
            inverse_two = inv_ref[0, rows, LANES : LANES + 1]
            pre_grad = inverse_two * (scaled - first - m * second) * slope_ref[
                0, rows, :
            ].astype(f32)
            q = q_ref[0, rows, :].astype(f32)
            chan_sum[8:16, :] += jnp.sum((pre_grad * q).reshape(-1, 8, C), axis=0)
            chan_sum[16:24, :] += jnp.sum(pre_grad.reshape(-1, 8, C), axis=0)
            scaled = pre_grad * gain
            first = jnp.mean(scaled, axis=-1, keepdims=True)
            second = jnp.mean(scaled * q, axis=-1, keepdims=True)
            inverse = inv_ref[0, rows, 0:1]
            conv_grad = inverse * (scaled - first - q * second)
            chan_sum[0:8, :] += jnp.sum(conv_grad.reshape(-1, 8, C), axis=0)
            mid[rows, :] = conv_grad
        operand = mid[...].astype(bf16)
        for tap in range(2):
            rows = slice(tap * C, (tap + 1) * C)
            audio_grad = nt(operand, conv_ref[rows, :])
            for c in range(C // LANES):
                wide[c, pl.ds(tap, T, stride=2), :] = audio_grad[:, c * LANES : (c + 1) * LANES]
            conv_sum[rows, :] += tn(pair_ref[0, :, rows], operand)
        for c in range(C // LANES):
            audio_grad_ref[0, :, c * LANES : (c + 1) * LANES] = wide[c].astype(bf16)
        proj_sum[...] += tn(normed[...], feat_grad[...])

    @pl.when(jnp.logical_not(living))
    def _():
        audio_grad_ref[...] = jnp.zeros_like(audio_grad_ref)

    @pl.when(slot == SLOTS - 1)
    def _():
        first_core = place.core == 0
        columns[...] = jnp.zeros_like(columns)
        for n in range(5):
            columns[GC + n : GC + n + 1, :] = jnp.sum(
                chan_sum[8 * n : 8 * n + 8, :], axis=0, keepdims=True
            )
        proj_sum[...] += columns[...].T
        for x in range(X):
            lanes = slice(x * LANES, (x + 1) * LANES)
            for cell in range(CELLS):
                at = 2 * cell * 32
                even = conv_sum[at : at + 32, lanes]
                odd = conv_sum[at + 32 : at + 64, lanes]
                rows = slice(cell * 32, (cell + 1) * 32)
                keep_ref[x, rows, :] = (jnp.where(first_core, even, odd) * scale).astype(bf16)
                send_ref[x, rows, :] = (jnp.where(first_core, odd, even) * scale).astype(bf16)
            for four in range(CELLS // 4):
                even, odd = [
                    jnp.concatenate(
                        [
                            proj_sum[at : at + SPARE, :]
                            for at in (
                                (2 * cell + odd) * 16 + x * SPARE
                                for cell in range(4 * four, 4 * four + 4)
                            )
                        ],
                        axis=0,
                    )
                    for odd in range(2)
                ]
                rows = slice(CONV_ROWS + four * 16, CONV_ROWS + (four + 1) * 16)
                keep_ref[x, rows, :] = (jnp.where(first_core, even, odd) * scale).astype(bf16)
                send_ref[x, rows, :] = (jnp.where(first_core, odd, even) * scale).astype(bf16)


def backward(
    scale, place, slopes, low, high, cotangent, received, weight, stored, conv_weight, channels, proj
):
    shape = jax.ShapeDtypeStruct((X, REST, LANES), bf16)
    return pl.pallas_call(
        functools.partial(backward_body, scale),
        grid=(SLOTS,),
        out_shape=(jax.ShapeDtypeStruct((SLOTS, 2 * T, C), bf16), shape, shape),
        in_specs=[SMEM] * 3
        + [
            by_slot(T, LANES),
            by_slot(REACH, LANES),
            by_slot(REACH, LANES),
            by_slot(GC, T),
            by_slot(GC, T),
            once(*weight.shape),
            by_slot(T, 2 * C),
            by_slot(T, C),
            by_slot(T, C),
            by_slot(T, C),
            by_slot(T, 2 * LANES),
            once(2 * C, C),
            whole(5, C),
            whole(GC, C),
        ],
        out_specs=(by_slot(2 * T, C), whole(*shape.shape), whole(*shape.shape)),
        scratch_shapes=[
            pltpu.VMEM((EXT, LANES), f32),
            pltpu.VMEM((T + NEAR * (K // NEAR - 1), NEAR * LANES), bf16),
            pltpu.VMEM((LANES, T), f32),
            pltpu.VMEM((LANES, C), bf16),
            pltpu.VMEM((T, LANES), bf16),
            pltpu.VMEM((T, C), bf16),
            pltpu.VMEM((T, C), f32),
            pltpu.VMEM((C // LANES, 2 * T, LANES), f32),
            pltpu.VMEM((2 * C, C), f32),
            pltpu.VMEM((C, LANES), f32),
            pltpu.VMEM((40, C), f32),
            pltpu.VMEM((LANES, C), f32),
        ],
        compiler_params=params(56),
        cost_estimate=cost(
            2 * SLOTS * (SPAN * K * LANES * LANES + T * C * (4 * C + 2 * LANES)), 14 << 20
        ),
        name="backward",
    )(
        *place,
        slopes,
        low,
        high,
        cotangent,
        received,
        weight,
        *stored,
        conv_weight,
        channels,
        proj,
    )


def halve_body(dev_ref, keep_ref, recv_ref, stay_ref, leave_ref):
    y = lax.rem(dev_ref[0], MP) // X
    for out_ref, at in ((stay_ref, y), (leave_ref, 1 - y)):
        out_ref[...] = (keep_ref[at].astype(f32) + recv_ref[at].astype(f32)).astype(bf16)


def halve(dev, keep, received):
    shape = jax.ShapeDtypeStruct(keep.shape[1:], bf16)
    return pl.pallas_call(
        halve_body,
        out_shape=(shape,) * 2,
        in_specs=[SMEM] + [VMEM] * 2,
        out_specs=(VMEM,) * 2,
        compiler_params=params(8),
        cost_estimate=cost(0, 2 << 20),
        name="halve",
    )(dev, keep, received)


def join_body(dev_ref, keep_ref, recv_ref, *out_refs):
    x = lax.rem(dev_ref[0], X)
    for step, out_ref in enumerate(out_refs):
        at = lax.rem(x + step, X)
        out_ref[...] = (keep_ref[at].astype(f32) + recv_ref[at].astype(f32)).astype(bf16)


def join(dev, keep, received):
    shape = jax.ShapeDtypeStruct((REST, LANES), bf16)
    return pl.pallas_call(
        join_body,
        out_shape=(shape,) * X,
        in_specs=[SMEM] + [VMEM] * 2,
        out_specs=(VMEM,) * X,
        compiler_params=params(8),
        cost_estimate=cost(0, 2 << 20),
        name="join",
    )(dev, keep, received)


def cells_body(*refs):
    pos_refs, rest_refs, out_ref, rows = refs[:2], refs[2:6], refs[6], refs[7]

    def summed(parts, *at):
        result = parts[0][at].astype(f32)
        for part in parts[1:]:
            result += part[at].astype(f32)
        return result

    for four in range(CELLS // 4):
        at = CONV_ROWS + four * 16
        small = summed(rest_refs, slice(at, at + 16), slice(None))
        for n in range(4):
            cell = 4 * four + n
            rows[...] = summed(pos_refs, cell)
            rows[HALF:, :] = small[n * SPARE : (n + 1) * SPARE, :]
            out_ref[cell, :REACH, :] = rows[...].astype(bf16)
            conv = summed(rest_refs, slice(cell * 32, cell * 32 + 32), slice(None))
            out_ref[cell, REACH:, :] = conv.astype(bf16)


def make_cells(pos_parts, rest_parts):
    return pl.pallas_call(
        cells_body,
        out_shape=jax.ShapeDtypeStruct((CELLS, REACH + 32, LANES), bf16),
        in_specs=[VMEM] * 6,
        out_specs=VMEM,
        scratch_shapes=[pltpu.VMEM((REACH, LANES), f32)],
        compiler_params=params(8),
        cost_estimate=cost(0, 2 << 20),
        name="cells",
    )(*pos_parts, *rest_parts)


def total_body(in_ref, out_ref):
    total = in_ref[0].astype(f32)
    for n in range(1, in_ref.shape[0]):
        total += in_ref[n].astype(f32)
    for copy in range(MP):
        out_ref[copy] = total.astype(bf16)


def total(parts):
    return pl.pallas_call(
        total_body,
        out_shape=jax.ShapeDtypeStruct((MP,) + parts.shape[1:], bf16),
        in_specs=[VMEM],
        out_specs=VMEM,
        compiler_params=params(10),
        cost_estimate=cost(0, 2 * parts.size),
        name="total",
    )(parts)


def finish_body(
    dev_ref,
    len_ref,
    mov_ref,
    in_ref,
    states_ref,
    other_ref,
    hidden_ref,
    pos_ref,
    conv_ref,
    proj_ref,
    chan_ref,
):
    place = Place(dev_ref, len_ref, mov_ref)
    for slot in range(SLOTS):
        hidden_ref[slot] = jnp.where(
            place.chosen == slot, other_ref[...].astype(f32), states_ref[slot].astype(f32)
        ).astype(bf16)
    small = []
    for x in range(X):
        low, high = in_ref[x].astype(f32), in_ref[X + x].astype(f32)
        block = jnp.concatenate(
            [low[:HALF, :], high[:HALF, :], jnp.zeros((LANES - GC, LANES), f32)], axis=0
        ).T
        pos_ref[x] = block[:GC, :GC]
        both = low[HALF:, :] + high[HALF:, :]
        small.append(both[:SPARE, :])
        conv_ref[:, x * LANES : (x + 1) * LANES] = both[SPARE:, :]
    small = jnp.concatenate(small, axis=0)
    proj_ref[...] = small[:, :GC]
    chan_ref[...] = jnp.concatenate([small] * 8, axis=0).T[GC : GC + 5, :16]


def finish(place, cells, states, other):
    return pl.pallas_call(
        finish_body,
        out_shape=(
            jax.ShapeDtypeStruct((SLOTS, GC, T), bf16),
            jax.ShapeDtypeStruct((4, GC, GC), f32),
            jax.ShapeDtypeStruct((32, C), f32),
            jax.ShapeDtypeStruct((16, GC), f32),
            jax.ShapeDtypeStruct((5, 16), f32),
        ),
        in_specs=[SMEM] * 3 + [VMEM] * 3,
        out_specs=(VMEM,) * 5,
        compiler_params=params(8),
        name="finish",
    )(*place, cells, states, other)


def neighbours(tail, head):
    forward = [(i, i + 1) for i in range(MP - 1)]
    backward_route = [(i + 1, i) for i in range(MP - 1)]
    return lax.ppermute(tail, "mp", forward), lax.ppermute(head, "mp", backward_route)


def along_x(block, step):
    route = [(X * y + x, X * y + (x + step) % X) for y in range(2) for x in range(X)]
    return lax.ppermute(block, "mp", route)


def per_device(
    audio, lengths, moved_slots, conv_weight, channel_params, proj_weight, pos_weight, cotangent
):
    data_index = lax.axis_index("dp")
    model_index = lax.axis_index("mp")
    scale = (SLOTS * DP * T * MP) ** -0.5
    dev = (data_index * MP + model_index).astype(jnp.int32).reshape(1)
    place = (dev, lengths, moved_slots.reshape(-1))
    swap = [(i, i ^ (DP // 2)) for i in range(DP)]
    core_swap = [(i, i ^ 1) for i in range(DP)]
    channels = channel_params.T
    proj = proj_weight.T
    cot = cotangent.transpose(0, 2, 1)

    received = lax.ppermute(cot, "dp", swap)
    features, tail, head, *stored = encode(place, audio, conv_weight, channels, proj)
    low, high = neighbours(tail, head)
    ahead, behind = turn(pos_weight.transpose(1, 2, 0))
    states, sent, slopes, tail, head, piece = mix(
        place, features, low, high, ahead, cot, received
    )
    low, high = neighbours(tail, head)
    other = lax.ppermute(sent, "dp", swap)
    piece, low, high = lax.optimization_barrier((piece, low, high))
    far = along_x(piece, 2)
    pieces = (piece, along_x(piece, 1), far, along_x(piece, 3))
    audio_grad, keep, send = backward(
        scale,
        place,
        slopes,
        low,
        high,
        cot,
        received,
        behind,
        stored,
        conv_weight,
        channels,
        proj,
    )
    send, pieces, other = lax.optimization_barrier((send, pieces, other))
    recv, pieces = lax.optimization_barrier((lax.ppermute(send, "dp", core_swap), pieces))
    chunks = join(dev, keep, recv)
    rest_parts = [chunks[0]] + [along_x(chunks[step], step) for step in (2, 1, 3)]
    pos_keep, pos_send = taps(scale, place, pieces)
    stay, leave = halve(dev, pos_keep, lax.ppermute(pos_send, "dp", core_swap))
    pos_parts = (stay, lax.ppermute(leave, "mp", [(i, i ^ X) for i in range(MP)]))
    cells = make_cells(pos_parts, rest_parts)
    groups = [list(range(bit, DP, 2)) for bit in range(2)]
    cells = lax.all_to_all(cells, "dp", 0, 0, axis_index_groups=groups, tiled=True)
    cells = lax.all_to_all(total(cells), "mp", 0, 0, tiled=True)
    hidden, grad_pos, grad_conv, grad_proj, grad_channels = finish(place, cells, states, other)
    return (
        hidden.transpose(0, 2, 1),
        audio_grad,
        grad_pos,
        grad_conv,
        grad_proj,
        grad_channels.T,
    )


def solution(mesh):
    return jax.shard_map(
        per_device,
        mesh=mesh,
        in_specs=(P("dp", "mp", None), P(), P(), P(), P(), P(), P(), P("dp", "mp", None)),
        out_specs=(
            P("dp", "mp", None),
            P("dp", "mp", None),
            P("dp", None, None),
            P("dp", None),
            P("dp", None),
            P("dp", None),
        ),
        check_vma=False,
    )
```

```python
import functools

import jax
import jax.numpy as jnp
from jax import lax
from jax.experimental import pallas as pl
from jax.experimental.pallas import tpu as pltpu
from jax.sharding import PartitionSpec as P

epsilon = 1e-05
root_half = 0.7071067811865476
density = 0.3989422804014327

SLOTS = 2
T = 256
C = 512
GC = 120
LANES = 128
K = 128
REACH = 64
EXT = T + 2 * REACH
NEAR = 16
GROUPS = 2
PER_GROUP = 4
SPAN = T + NEAR * (PER_GROUP - 1)
CHUNK = 32
MP = 8
DP = 32
X = 4
CELLS = 16
PIECE = T + REACH
HALF = GC // 2
SPARE = REACH - HALF
CONV_ROWS = CELLS * 32
REST = CONV_ROWS + CELLS * SPARE

f32 = jnp.float32
bf16 = jnp.bfloat16

VMEM = pl.BlockSpec(memory_space=pltpu.VMEM)
SMEM = pl.BlockSpec(memory_space=pltpu.SMEM)
HBM = pl.BlockSpec(memory_space=pltpu.HBM)


def params(mebibytes):
    return pltpu.CompilerParams(vmem_limit_bytes=mebibytes << 20)


def cost(flops, moved, trans=0):
    return pl.CostEstimate(flops=flops, bytes_accessed=moved, transcendentals=trans)


def phi(values):
    return 0.5 * (1.0 + lax.erf(values * root_half))


def bell(values):
    return jnp.exp(-0.5 * values * values) * density


def nt(a, b):
    return lax.dot_general(a, b, (((1,), (1,)), ((), ())), preferred_element_type=f32)


def tn(a, b):
    return lax.dot_general(a, b, (((0,), (0,)), ((), ())), preferred_element_type=f32)


def nn(a, b):
    return jnp.dot(a, b, preferred_element_type=f32)


class Place:
    def __init__(self, dev_ref, len_ref, mov_ref=None):
        self.data = dev_ref[0] // MP
        self.model = lax.rem(dev_ref[0], MP)
        self.x = lax.rem(self.model, X)
        self.y = self.model // X
        self.core = lax.rem(self.data, 2)
        self.cell = self.data // 2
        self.first = self.model * T
        self.lengths = len_ref
        if mov_ref is not None:
            self.chosen = mov_ref[lax.rem(self.data, DP // 2)]

    def length(self, slot):
        return self.lengths[self.data * SLOTS + slot]

    def alive(self, slot):
        return self.first < self.length(slot)

    def mask(self, slot):
        ids = self.first + lax.broadcasted_iota(jnp.int32, (T, 1), 0)
        return ids < self.length(slot)


def by_slot(*dims):
    return pl.BlockSpec((1,) + dims, lambda s: (s,) + (0,) * len(dims))


def whole(*dims):
    return pl.BlockSpec(dims, lambda s: (0,) * len(dims))


def once(*dims):
    return pl.BlockSpec(dims, lambda s: (0,) * len(dims), pipeline_mode=pl.Buffered(1))


def turn_body(in_ref, ahead_ref, behind_ref, rows, held, sems):
    block = pl.program_id(0)
    blocks = LANES // NEAR

    def fetch(n):
        count = min(NEAR, GC - n * NEAR)
        part = pl.ds(n * NEAR, count)
        return pltpu.make_async_copy(in_ref.at[part], held.at[part], sems.at[n])

    @pl.when(block == 0)
    def _():
        for n in range(blocks):
            fetch(n).start()

    for n in range(blocks):

        @pl.when(block == n)
        def _():
            fetch(n).wait()

    for n in range(NEAR):
        tile = jnp.concatenate(
            [held[block * NEAR + n].astype(f32), jnp.zeros((LANES - GC, K), f32)], axis=0
        ).T
        if n >= GC % NEAR:
            tile = jnp.where(block == blocks - 1, 0.0, tile)
        rows[pl.ds(n, K, stride=NEAR), :] = tile
    far = K // NEAR
    for q in range(far):
        for r in range(NEAR):
            at = (q * NEAR + r) * NEAR
            tile = rows[at : at + NEAR, :].astype(bf16)
            ahead_ref[r, :, q * LANES : (q + 1) * LANES] = tile
            r_back = NEAR - 1 - r
            behind_ref[far - 1 - q, :, r_back * LANES : (r_back + 1) * LANES] = tile


def turn(pos):
    far = K // NEAR
    ahead, behind = pl.pallas_call(
        turn_body,
        grid=(LANES // NEAR,),
        out_shape=(
            jax.ShapeDtypeStruct((NEAR, LANES, far * LANES), bf16),
            jax.ShapeDtypeStruct((far, LANES, NEAR * LANES), bf16),
        ),
        in_specs=[HBM],
        out_specs=(
            pl.BlockSpec((NEAR, NEAR, far * LANES), lambda b: (0, b, 0)),
            pl.BlockSpec((far, NEAR, NEAR * LANES), lambda b: (0, b, 0)),
        ),
        scratch_shapes=[
            pltpu.VMEM((K * NEAR, LANES), f32),
            pltpu.VMEM((LANES, GC, K), bf16),
            pltpu.SemaphoreType.DMA((LANES // NEAR,)),
        ],
        compiler_params=params(16),
        cost_estimate=cost(0, 12 << 20),
        name="turn",
    )(pos)
    return ahead.reshape(NEAR * LANES, -1), behind.reshape(far * LANES, -1)


def encode_body(
    dev_ref,
    len_hbm,
    audio_hbm,
    conv_hbm,
    chan_hbm,
    proj_hbm,
    feat_ref,
    tail_ref,
    head_ref,
    pair_ref,
    q_ref,
    slope_ref,
    m_ref,
    inv_ref,
    wide,
    proj,
    mid,
    normed,
    len_ref,
    audio_ref,
    conv_ref,
    chan_ref,
    sems,
):
    slot = pl.program_id(0)
    copies = [
        pltpu.make_async_copy(source, target, sems.at[n])
        for n, (source, target) in enumerate(
            (
                (len_hbm, len_ref),
                (audio_hbm.at[0], audio_ref.at[0]),
                (conv_hbm, conv_ref),
                (chan_hbm, chan_ref),
                (proj_hbm, proj.at[pl.ds(0, GC)]),
                (audio_hbm.at[1], audio_ref.at[1]),
            )
        )
    ]

    @pl.when(slot == 0)
    def _():
        proj[GC - 8 :, :] = jnp.zeros((LANES - GC + 8, C), bf16)
        for copy in copies:
            copy.start()
        for copy in copies[:-1]:
            copy.wait()

    @pl.when(slot == SLOTS - 1)
    def _():
        copies[-1].wait()

    place = Place(dev_ref, len_ref)
    living = place.alive(slot)

    @pl.when(living)
    def _():
        for c in range(C // LANES):
            wide[c] = audio_ref[slot, :, c * LANES : (c + 1) * LANES].astype(f32)
            for tap in range(2):
                at = tap * C + c * LANES
                pair_ref[0, :, at : at + LANES] = wide[c, pl.ds(tap, T, stride=2), :].astype(bf16)
        mid[...] = nn(pair_ref[0], conv_ref[...])
        bias, gain, shift = chan_ref[0:1, :], chan_ref[1:2, :], chan_ref[2:3, :]
        gain_two, shift_two = chan_ref[3:4, :], chan_ref[4:5, :]
        for at in range(0, T, CHUNK):
            rows = slice(at, at + CHUNK)
            conv = mid[rows, :] + bias
            offset = conv - jnp.mean(conv, axis=-1, keepdims=True)
            inverse = lax.rsqrt(jnp.mean(offset * offset, axis=-1, keepdims=True) + epsilon)
            q = offset * inverse
            pre = q * gain + shift
            below = phi(pre)
            encoded = (pre * below).astype(bf16).astype(f32)
            slope_ref[0, rows, :] = (below + pre * bell(pre)).astype(bf16)
            q_ref[0, rows, :] = q.astype(bf16)
            offset = encoded - jnp.mean(encoded, axis=-1, keepdims=True)
            inverse_two = lax.rsqrt(jnp.mean(offset * offset, axis=-1, keepdims=True) + epsilon)
            m = offset * inverse_two
            m_ref[0, rows, :] = m.astype(bf16)
            inv_ref[0, rows, :] = jnp.concatenate(
                [
                    jnp.broadcast_to(inverse, (CHUNK, LANES)),
                    jnp.broadcast_to(inverse_two, (CHUNK, LANES)),
                ],
                axis=1,
            )
            normed[rows, :] = (m * gain_two + shift_two).astype(bf16)
        projected = nt(normed[...], proj[...])
        feat_ref[0] = jnp.where(place.mask(slot), projected, 0.0).astype(bf16)

    @pl.when(jnp.logical_not(living))
    def _():
        feat_ref[...] = jnp.zeros_like(feat_ref)

    tail_ref[0] = feat_ref[0, T - REACH :, :]
    head_ref[0] = feat_ref[0, :REACH, :]


def encode(place, audio, conv_weight, channels, proj):
    return pl.pallas_call(
        encode_body,
        grid=(SLOTS,),
        out_shape=(
            jax.ShapeDtypeStruct((SLOTS, T, LANES), bf16),
            jax.ShapeDtypeStruct((SLOTS, REACH, LANES), bf16),
            jax.ShapeDtypeStruct((SLOTS, REACH, LANES), bf16),
            jax.ShapeDtypeStruct((SLOTS, T, 2 * C), bf16),
            jax.ShapeDtypeStruct((SLOTS, T, C), bf16),
            jax.ShapeDtypeStruct((SLOTS, T, C), bf16),
            jax.ShapeDtypeStruct((SLOTS, T, C), bf16),
            jax.ShapeDtypeStruct((SLOTS, T, 2 * LANES), f32),
        ),
        in_specs=[SMEM] + [HBM] * 5,
        out_specs=(
            by_slot(T, LANES),
            by_slot(REACH, LANES),
            by_slot(REACH, LANES),
            by_slot(T, 2 * C),
            by_slot(T, C),
            by_slot(T, C),
            by_slot(T, C),
            by_slot(T, 2 * LANES),
        ),
        scratch_shapes=[
            pltpu.VMEM((C // LANES, 2 * T, LANES), f32),
            pltpu.VMEM((LANES, C), bf16),
            pltpu.VMEM((T, C), f32),
            pltpu.VMEM((T, C), bf16),
            pltpu.SMEM((DP * SLOTS,), jnp.int32),
            pltpu.VMEM((SLOTS, 2 * T, C), bf16),
            pltpu.VMEM((2 * C, C), bf16),
            pltpu.VMEM((5, C), f32),
            pltpu.SemaphoreType.DMA((6,)),
        ],
        compiler_params=params(50),
        cost_estimate=cost(2 * SLOTS * T * C * (2 * C + LANES), 8 << 20, SLOTS * T * C * 2),
        name="encode",
    )(*place[:2], audio, conv_weight, channels, proj)


def fill_ext(ext, low, own, high):
    ext[:REACH, :] = low.astype(f32)
    ext[REACH : REACH + T, :] = own.astype(f32)
    ext[REACH + T :, :] = high.astype(f32)


def fill_windows(windows, ext, first):
    rows = T + NEAR * (K // NEAR - 1)
    for r in range(NEAR):
        windows[:, r * LANES : (r + 1) * LANES] = ext[first + r : first + r + rows, :].astype(bf16)


def gathered(group):
    total = group[:T, :LANES]
    for p in range(1, PER_GROUP):
        total += group[NEAR * p : NEAR * p + T, p * LANES : (p + 1) * LANES]
    return total


def fill_back(turned, place, slot, cot_ref, recv_ref):
    turned[GC:, :] = jnp.zeros((LANES - GC, T), f32)
    turned[:GC, :] = jnp.where(
        place.chosen == slot, recv_ref[0].astype(f32), cot_ref[0].astype(f32)
    )


def mix_body(
    dev_ref,
    len_ref,
    mov_ref,
    feat_ref,
    low_ref,
    high_ref,
    weight,
    cot_ref,
    recv_ref,
    states_ref,
    sent_ref,
    slopes_ref,
    tail_ref,
    head_ref,
    piece_ref,
    ext,
    windows,
    turned,
):
    place = Place(dev_ref, len_ref, mov_ref)
    slot = pl.program_id(0)
    living = place.alive(slot)
    wide = PER_GROUP * LANES

    @pl.when(living)
    def _():
        own = feat_ref[0].astype(f32)
        fill_ext(ext, low_ref[0], own, high_ref[0])
        fill_windows(windows, ext, 0)
        fill_back(turned, place, slot, cot_ref, recv_ref)
        back = turned[...].T
        group = jnp.zeros((SPAN, wide), f32)
        for g in range(GROUPS):
            at = g * NEAR * PER_GROUP
            group += nn(windows[at : at + SPAN, :], weight[:, g * wide : (g + 1) * wide])
        mixed = gathered(group)
        below = phi(mixed)
        mask = place.mask(slot)
        states = jnp.where(mask, own + mixed * below, 0.0)
        states_ref[0] = states.T[:GC, :].astype(bf16)
        slopes = jnp.where(mask, back * (below + mixed * bell(mixed)), 0.0)
        slopes_ref[0] = slopes.astype(bf16)
        edge = jnp.where(place.x < X // 2, low_ref[0].astype(f32), high_ref[0].astype(f32))
        piece_ref[0, :T, :] = slopes.astype(bf16)
        piece_ref[0, T:, :] = edge.astype(bf16)

    @pl.when(jnp.logical_not(living))
    def _():
        states_ref[...] = jnp.zeros_like(states_ref)
        slopes_ref[...] = jnp.zeros_like(slopes_ref)
        piece_ref[...] = jnp.zeros_like(piece_ref)

    tail_ref[0] = slopes_ref[0, T - REACH :, :]
    head_ref[0] = slopes_ref[0, :REACH, :]

    @pl.when(place.chosen == slot)
    def _():
        sent_ref[...] = states_ref[0]


def mix(place, features, low, high, weight, cotangent, received):
    return pl.pallas_call(
        mix_body,
        grid=(SLOTS,),
        out_shape=(
            jax.ShapeDtypeStruct((SLOTS, GC, T), bf16),
            jax.ShapeDtypeStruct((GC, T), bf16),
            jax.ShapeDtypeStruct((SLOTS, T, LANES), bf16),
            jax.ShapeDtypeStruct((SLOTS, REACH, LANES), bf16),
            jax.ShapeDtypeStruct((SLOTS, REACH, LANES), bf16),
            jax.ShapeDtypeStruct((SLOTS, PIECE, LANES), bf16),
        ),
        in_specs=[SMEM] * 3
        + [
            by_slot(T, LANES),
            by_slot(REACH, LANES),
            by_slot(REACH, LANES),
            once(*weight.shape),
            by_slot(GC, T),
            by_slot(GC, T),
        ],
        out_specs=(
            by_slot(GC, T),
            whole(GC, T),
            by_slot(T, LANES),
            by_slot(REACH, LANES),
            by_slot(REACH, LANES),
            by_slot(PIECE, LANES),
        ),
        scratch_shapes=[
            pltpu.VMEM((EXT, LANES), f32),
            pltpu.VMEM((T + NEAR * (K // NEAR - 1), NEAR * LANES), bf16),
            pltpu.VMEM((LANES, T), f32),
        ],
        compiler_params=params(20),
        cost_estimate=cost(2 * SLOTS * SPAN * K * LANES * LANES, 7 << 20, SLOTS * T * LANES * 2),
        name="mix",
    )(*place, features, low, high, weight, cotangent, received)


def taps_body(scale, dev_ref, len_ref, mov_ref, *refs):
    feat_refs, piece_refs, (keep_ref, send_ref) = refs[:X], refs[X : 2 * X], refs[2 * X : 2 * X + 2]
    ext, windows, turned, sums = refs[2 * X + 2 :]
    place = Place(dev_ref, len_ref, mov_ref)
    slot = pl.program_id(0)
    spread = X * T
    rows = spread + NEAR * (K // NEAR - 1)

    @pl.when(slot == 0)
    def _():
        sums[...] = jnp.zeros_like(sums)

    @pl.when(place.y * spread < place.length(slot))
    def _():
        for step, (feat_ref, piece_ref) in enumerate(zip(feat_refs, piece_refs)):
            x = lax.rem(place.x + (X - step), X)
            at = pl.multiple_of(x * T, T)
            ext[pl.ds(REACH + at, T), :] = feat_ref[0].astype(f32)
            turned[:, pl.ds(at, T)] = piece_ref[0, :T, :].astype(f32).T.astype(bf16)

            @pl.when(x == 0)
            def _():
                ext[:REACH, :] = piece_ref[0, T:, :].astype(f32)

            @pl.when(x == X - 1)
            def _():
                ext[REACH + spread :, :] = piece_ref[0, T:, :].astype(f32)

        for j in range(4):
            windows[:, j * LANES : (j + 1) * LANES] = ext[
                pl.ds(place.x + 4 * j, rows), :
            ].astype(bf16)
        for q in range(K // NEAR):
            sums[q] += nn(turned[...], windows[q * NEAR : q * NEAR + spread, :])

    @pl.when(slot == SLOTS - 1)
    def _():
        first_core = place.core == 0
        for q in range(K // NEAR):
            for far in range(2):
                at = 2 * far * LANES
                even = sums[q, :, at : at + LANES] * scale
                odd = sums[q, :, at + LANES : at + 2 * LANES] * scale
                keep = jnp.where(first_core, even, odd)
                send = jnp.where(first_core, odd, even)
                for y in range(2):
                    rows = slice(y * HALF, y * HALF + REACH)
                    keep_ref[y, 2 * q + far] = keep[rows, :].astype(bf16)
                    send_ref[y, 2 * q + far] = send[rows, :].astype(bf16)


def taps(scale, place, features, pieces):
    shape = jax.ShapeDtypeStruct((2, CELLS, REACH, LANES), bf16)
    spread = X * T
    return pl.pallas_call(
        functools.partial(taps_body, scale),
        grid=(SLOTS,),
        out_shape=(shape,) * 2,
        in_specs=[SMEM] * 3 + [by_slot(T, LANES)] * X + [by_slot(PIECE, LANES)] * X,
        out_specs=(whole(*shape.shape),) * 2,
        scratch_shapes=[
            pltpu.VMEM((spread + 2 * REACH, LANES), f32),
            pltpu.VMEM((spread + NEAR * (K // NEAR - 1), 4 * LANES), bf16),
            pltpu.VMEM((LANES, spread), bf16),
            pltpu.VMEM((K // NEAR, LANES, 4 * LANES), f32),
        ],
        compiler_params=params(16),
        cost_estimate=cost(2 * SLOTS * SPAN * K * LANES * LANES, 4 << 20),
        name="taps",
    )(*place, *features, *pieces)


def backward_body(
    scale,
    dev_ref,
    len_ref,
    mov_ref,
    slopes_ref,
    low_ref,
    high_ref,
    cot_ref,
    recv_ref,
    weight,
    pair_ref,
    q_ref,
    slope_ref,
    m_ref,
    inv_ref,
    conv_ref,
    chan_ref,
    proj_ref,
    audio_grad_ref,
    keep_ref,
    send_ref,
    ext,
    windows,
    turned,
    proj,
    feat_grad,
    normed,
    mid,
    wide,
    conv_sum,
    proj_sum,
    chan_sum,
    columns,
):
    place = Place(dev_ref, len_ref, mov_ref)
    slot = pl.program_id(0)
    living = place.alive(slot)
    span = PER_GROUP * LANES

    @pl.when(slot == 0)
    def _():
        proj[...] = jnp.zeros_like(proj)
        proj[:GC, :] = proj_ref[...]
        conv_sum[...] = jnp.zeros_like(conv_sum)
        proj_sum[...] = jnp.zeros_like(proj_sum)
        chan_sum[...] = jnp.zeros_like(chan_sum)

    @pl.when(living)
    def _():
        fill_ext(ext, low_ref[0], slopes_ref[0], high_ref[0])
        fill_windows(windows, ext, 1)
        fill_back(turned, place, slot, cot_ref, recv_ref)
        group = jnp.zeros((SPAN, span), f32)
        for g in range(GROUPS):
            at = g * NEAR * PER_GROUP
            group += nt(windows[at : at + SPAN, :], weight[g * span : (g + 1) * span, :])
        spread = gathered(group)
        feat_grad[...] = jnp.where(place.mask(slot), turned[...].T + spread, 0.0).astype(bf16)
        gain = chan_ref[1:2, :]
        gain_two, shift_two = chan_ref[3:4, :], chan_ref[4:5, :]
        mid[...] = nn(feat_grad[...], proj[...])
        for at in range(0, T, CHUNK):
            rows = slice(at, at + CHUNK)
            m = m_ref[0, rows, :].astype(f32)
            normed[rows, :] = (m * gain_two + shift_two).astype(bf16)
            normed_grad = mid[rows, :]
            chan_sum[24:32, :] += jnp.sum((normed_grad * m).reshape(-1, 8, C), axis=0)
            chan_sum[32:40, :] += jnp.sum(normed_grad.reshape(-1, 8, C), axis=0)
            scaled = normed_grad * gain_two
            first = jnp.mean(scaled, axis=-1, keepdims=True)
            second = jnp.mean(scaled * m, axis=-1, keepdims=True)
            inverse_two = inv_ref[0, rows, LANES : LANES + 1]
            pre_grad = inverse_two * (scaled - first - m * second) * slope_ref[
                0, rows, :
            ].astype(f32)
            q = q_ref[0, rows, :].astype(f32)
            chan_sum[8:16, :] += jnp.sum((pre_grad * q).reshape(-1, 8, C), axis=0)
            chan_sum[16:24, :] += jnp.sum(pre_grad.reshape(-1, 8, C), axis=0)
            scaled = pre_grad * gain
            first = jnp.mean(scaled, axis=-1, keepdims=True)
            second = jnp.mean(scaled * q, axis=-1, keepdims=True)
            inverse = inv_ref[0, rows, 0:1]
            conv_grad = inverse * (scaled - first - q * second)
            chan_sum[0:8, :] += jnp.sum(conv_grad.reshape(-1, 8, C), axis=0)
            mid[rows, :] = conv_grad
        operand = mid[...].astype(bf16)
        for tap in range(2):
            rows = slice(tap * C, (tap + 1) * C)
            audio_grad = nt(operand, conv_ref[rows, :])
            for c in range(C // LANES):
                wide[c, pl.ds(tap, T, stride=2), :] = audio_grad[:, c * LANES : (c + 1) * LANES]
            conv_sum[rows, :] += tn(pair_ref[0, :, rows], operand)
        for c in range(C // LANES):
            audio_grad_ref[0, :, c * LANES : (c + 1) * LANES] = wide[c].astype(bf16)
        proj_sum[...] += tn(normed[...], feat_grad[...])

    @pl.when(jnp.logical_not(living))
    def _():
        audio_grad_ref[...] = jnp.zeros_like(audio_grad_ref)

    @pl.when(slot == SLOTS - 1)
    def _():
        first_core = place.core == 0
        columns[...] = jnp.zeros_like(columns)
        for n in range(5):
            columns[GC + n : GC + n + 1, :] = jnp.sum(
                chan_sum[8 * n : 8 * n + 8, :], axis=0, keepdims=True
            )
        proj_sum[...] += columns[...].T
        for x in range(X):
            lanes = slice(x * LANES, (x + 1) * LANES)
            for cell in range(CELLS):
                at = 2 * cell * 32
                even = conv_sum[at : at + 32, lanes]
                odd = conv_sum[at + 32 : at + 64, lanes]
                rows = slice(cell * 32, (cell + 1) * 32)
                keep_ref[x, rows, :] = (jnp.where(first_core, even, odd) * scale).astype(bf16)
                send_ref[x, rows, :] = (jnp.where(first_core, odd, even) * scale).astype(bf16)
            for four in range(CELLS // 4):
                even, odd = [
                    jnp.concatenate(
                        [
                            proj_sum[at : at + SPARE, :]
                            for at in (
                                (2 * cell + odd) * 16 + x * SPARE
                                for cell in range(4 * four, 4 * four + 4)
                            )
                        ],
                        axis=0,
                    )
                    for odd in range(2)
                ]
                rows = slice(CONV_ROWS + four * 16, CONV_ROWS + (four + 1) * 16)
                keep_ref[x, rows, :] = (jnp.where(first_core, even, odd) * scale).astype(bf16)
                send_ref[x, rows, :] = (jnp.where(first_core, odd, even) * scale).astype(bf16)


def backward(
    scale, place, slopes, low, high, cotangent, received, weight, stored, conv_weight, channels, proj
):
    shape = jax.ShapeDtypeStruct((X, REST, LANES), bf16)
    return pl.pallas_call(
        functools.partial(backward_body, scale),
        grid=(SLOTS,),
        out_shape=(jax.ShapeDtypeStruct((SLOTS, 2 * T, C), bf16), shape, shape),
        in_specs=[SMEM] * 3
        + [
            by_slot(T, LANES),
            by_slot(REACH, LANES),
            by_slot(REACH, LANES),
            by_slot(GC, T),
            by_slot(GC, T),
            once(*weight.shape),
            by_slot(T, 2 * C),
            by_slot(T, C),
            by_slot(T, C),
            by_slot(T, C),
            by_slot(T, 2 * LANES),
            once(2 * C, C),
            whole(5, C),
            whole(GC, C),
        ],
        out_specs=(by_slot(2 * T, C), whole(*shape.shape), whole(*shape.shape)),
        scratch_shapes=[
            pltpu.VMEM((EXT, LANES), f32),
            pltpu.VMEM((T + NEAR * (K // NEAR - 1), NEAR * LANES), bf16),
            pltpu.VMEM((LANES, T), f32),
            pltpu.VMEM((LANES, C), bf16),
            pltpu.VMEM((T, LANES), bf16),
            pltpu.VMEM((T, C), bf16),
            pltpu.VMEM((T, C), f32),
            pltpu.VMEM((C // LANES, 2 * T, LANES), f32),
            pltpu.VMEM((2 * C, C), f32),
            pltpu.VMEM((C, LANES), f32),
            pltpu.VMEM((40, C), f32),
            pltpu.VMEM((LANES, C), f32),
        ],
        compiler_params=params(30),
        cost_estimate=cost(
            2 * SLOTS * (SPAN * K * LANES * LANES + T * C * (4 * C + 2 * LANES)), 14 << 20
        ),
        name="backward",
    )(
        *place,
        slopes,
        low,
        high,
        cotangent,
        received,
        weight,
        *stored,
        conv_weight,
        channels,
        proj,
    )


def halve_body(dev_ref, keep_ref, recv_ref, stay_ref, leave_ref):
    y = lax.rem(dev_ref[0], MP) // X
    for out_ref, at in ((stay_ref, y), (leave_ref, 1 - y)):
        out_ref[...] = (keep_ref[at].astype(f32) + recv_ref[at].astype(f32)).astype(bf16)


def halve(dev, keep, received):
    shape = jax.ShapeDtypeStruct(keep.shape[1:], bf16)
    return pl.pallas_call(
        halve_body,
        out_shape=(shape,) * 2,
        in_specs=[SMEM] + [VMEM] * 2,
        out_specs=(VMEM,) * 2,
        compiler_params=params(8),
        cost_estimate=cost(0, 2 << 20),
        name="halve",
    )(dev, keep, received)


def join_body(dev_ref, keep_ref, recv_ref, *out_refs):
    x = lax.rem(dev_ref[0], X)
    for step, out_ref in enumerate(out_refs):
        at = lax.rem(x + step, X)
        out_ref[...] = (keep_ref[at].astype(f32) + recv_ref[at].astype(f32)).astype(bf16)


def join(dev, keep, received):
    shape = jax.ShapeDtypeStruct((REST, LANES), bf16)
    return pl.pallas_call(
        join_body,
        out_shape=(shape,) * X,
        in_specs=[SMEM] + [VMEM] * 2,
        out_specs=(VMEM,) * X,
        compiler_params=params(8),
        cost_estimate=cost(0, 2 << 20),
        name="join",
    )(dev, keep, received)


def cells_body(*refs):
    pos_refs, rest_refs, out_ref, rows = refs[:2], refs[2:6], refs[6], refs[7]

    def summed(parts, *at):
        result = parts[0][at].astype(f32)
        for part in parts[1:]:
            result += part[at].astype(f32)
        return result

    for four in range(CELLS // 4):
        at = CONV_ROWS + four * 16
        small = summed(rest_refs, slice(at, at + 16), slice(None))
        for n in range(4):
            cell = 4 * four + n
            rows[...] = summed(pos_refs, cell)
            rows[HALF:, :] = small[n * SPARE : (n + 1) * SPARE, :]
            out_ref[cell, :REACH, :] = rows[...].astype(bf16)
            conv = summed(rest_refs, slice(cell * 32, cell * 32 + 32), slice(None))
            out_ref[cell, REACH:, :] = conv.astype(bf16)


def make_cells(pos_parts, rest_parts):
    return pl.pallas_call(
        cells_body,
        out_shape=jax.ShapeDtypeStruct((CELLS, REACH + 32, LANES), bf16),
        in_specs=[VMEM] * 6,
        out_specs=VMEM,
        scratch_shapes=[pltpu.VMEM((REACH, LANES), f32)],
        compiler_params=params(8),
        cost_estimate=cost(0, 2 << 20),
        name="cells",
    )(*pos_parts, *rest_parts)


def total_body(in_ref, out_ref):
    total = in_ref[0].astype(f32)
    for n in range(1, in_ref.shape[0]):
        total += in_ref[n].astype(f32)
    for copy in range(MP):
        out_ref[copy] = total.astype(bf16)


def total(parts):
    return pl.pallas_call(
        total_body,
        out_shape=jax.ShapeDtypeStruct((MP,) + parts.shape[1:], bf16),
        in_specs=[VMEM],
        out_specs=VMEM,
        compiler_params=params(10),
        cost_estimate=cost(0, 2 * parts.size),
        name="total",
    )(parts)


def finish_body(
    dev_ref,
    len_ref,
    mov_ref,
    in_ref,
    states_ref,
    other_ref,
    hidden_ref,
    pos_ref,
    conv_ref,
    proj_ref,
    chan_ref,
):
    place = Place(dev_ref, len_ref, mov_ref)
    for slot in range(SLOTS):
        hidden_ref[slot] = jnp.where(
            place.chosen == slot, other_ref[...].astype(f32), states_ref[slot].astype(f32)
        ).astype(bf16)
    small = []
    for x in range(X):
        low, high = in_ref[x].astype(f32), in_ref[X + x].astype(f32)
        block = jnp.concatenate(
            [low[:HALF, :], high[:HALF, :], jnp.zeros((LANES - GC, LANES), f32)], axis=0
        ).T
        pos_ref[x] = block[:GC, :GC]
        both = low[HALF:, :] + high[HALF:, :]
        small.append(both[:SPARE, :])
        conv_ref[:, x * LANES : (x + 1) * LANES] = both[SPARE:, :]
    small = jnp.concatenate(small, axis=0)
    proj_ref[...] = small[:, :GC]
    chan_ref[...] = jnp.concatenate([small] * 8, axis=0).T[GC : GC + 5, :16]


def finish(place, cells, states, other):
    return pl.pallas_call(
        finish_body,
        out_shape=(
            jax.ShapeDtypeStruct((SLOTS, GC, T), bf16),
            jax.ShapeDtypeStruct((4, GC, GC), f32),
            jax.ShapeDtypeStruct((32, C), f32),
            jax.ShapeDtypeStruct((16, GC), f32),
            jax.ShapeDtypeStruct((5, 16), f32),
        ),
        in_specs=[SMEM] * 3 + [VMEM] * 3,
        out_specs=(VMEM,) * 5,
        compiler_params=params(8),
        name="finish",
    )(*place, cells, states, other)


def neighbours(tail, head):
    forward = [(i, i + 1) for i in range(MP - 1)]
    backward_route = [(i + 1, i) for i in range(MP - 1)]
    return lax.ppermute(tail, "mp", forward), lax.ppermute(head, "mp", backward_route)


def along_x(block, step):
    route = [(X * y + x, X * y + (x + step) % X) for y in range(2) for x in range(X)]
    return lax.ppermute(block, "mp", route)


def around_x(block):
    far = along_x(block, 2)
    return (block, along_x(block, 1), far, along_x(block, 3))


def per_device(
    audio, lengths, moved_slots, conv_weight, channel_params, proj_weight, pos_weight, cotangent
):
    data_index = lax.axis_index("dp")
    model_index = lax.axis_index("mp")
    scale = (SLOTS * DP * T * MP) ** -0.5
    dev = (data_index * MP + model_index).astype(jnp.int32).reshape(1)
    place = (dev, lengths, moved_slots.reshape(-1))
    swap = [(i, i ^ (DP // 2)) for i in range(DP)]
    core_swap = [(i, i ^ 1) for i in range(DP)]
    channels = channel_params.T
    proj = proj_weight.T
    cot = cotangent.transpose(0, 2, 1)

    received = lax.ppermute(cot, "dp", swap)
    features, tail, head, *stored = encode(place, audio, conv_weight, channels, proj)
    low, high = neighbours(tail, head)
    all_features = around_x(features)
    ahead, behind = turn(pos_weight.transpose(1, 2, 0))
    states, sent, slopes, tail, head, piece = mix(
        place, features, low, high, ahead, cot, received
    )
    low, high = neighbours(tail, head)
    other = lax.ppermute(sent, "dp", swap)
    piece, low, high, all_features = lax.optimization_barrier(
        (piece, low, high, all_features)
    )
    pieces = around_x(piece)
    audio_grad, keep, send = backward(
        scale,
        place,
        slopes,
        low,
        high,
        cot,
        received,
        behind,
        stored,
        conv_weight,
        channels,
        proj,
    )
    send, other, pieces = lax.optimization_barrier((send, other, pieces))
    chunks = join(dev, keep, lax.ppermute(send, "dp", core_swap))
    chunks, pieces = lax.optimization_barrier((chunks, pieces))
    rest_parts = [chunks[0]] + [along_x(chunks[step], step) for step in (2, 1, 3)]
    pos_keep, pos_send = taps(scale, place, all_features, pieces)
    stay, leave = halve(dev, pos_keep, lax.ppermute(pos_send, "dp", core_swap))
    pos_parts = (stay, lax.ppermute(leave, "mp", [(i, i ^ X) for i in range(MP)]))
    cells = make_cells(pos_parts, rest_parts)
    groups = [list(range(bit, DP, 2)) for bit in range(2)]
    cells = lax.all_to_all(cells, "dp", 0, 0, axis_index_groups=groups, tiled=True)
    cells = lax.all_to_all(total(cells), "mp", 0, 0, tiled=True)
    hidden, grad_pos, grad_conv, grad_proj, grad_channels = finish(place, cells, states, other)
    return (
        hidden.transpose(0, 2, 1),
        audio_grad,
        grad_pos,
        grad_conv,
        grad_proj,
        grad_channels.T,
    )


def solution(mesh):
    return jax.shard_map(
        per_device,
        mesh=mesh,
        in_specs=(P("dp", "mp", None), P(), P(), P(), P(), P(), P(), P("dp", "mp", None)),
        out_specs=(
            P("dp", "mp", None),
            P("dp", "mp", None),
            P("dp", None, None),
            P("dp", None),
            P("dp", None),
            P("dp", None),
        ),
        check_vma=False,
    )
```

```python
import functools

import jax
import jax.numpy as jnp
from jax import lax
from jax.experimental import pallas as pl
from jax.experimental.pallas import tpu as pltpu
from jax.sharding import PartitionSpec as P

epsilon = 1e-05
root_half = 0.7071067811865476
density = 0.3989422804014327

SLOTS = 2
T = 256
C = 512
GC = 120
LANES = 128
K = 128
REACH = 64
EXT = T + 2 * REACH
NEAR = 16
GROUPS = 2
PER_GROUP = 4
SPAN = T + NEAR * (PER_GROUP - 1)
CHUNK = 32
MP = 8
DP = 32
X = 4
CELLS = 16
PIECE = T + REACH
HALF = GC // 2
SPARE = REACH - HALF
CONV_ROWS = CELLS * 32
REST = CONV_ROWS + CELLS * SPARE

f32 = jnp.float32
bf16 = jnp.bfloat16

VMEM = pl.BlockSpec(memory_space=pltpu.VMEM)
SMEM = pl.BlockSpec(memory_space=pltpu.SMEM)
HBM = pl.BlockSpec(memory_space=pltpu.HBM)


def params(mebibytes):
    return pltpu.CompilerParams(vmem_limit_bytes=mebibytes << 20)


def cost(flops, moved, trans=0):
    return pl.CostEstimate(flops=flops, bytes_accessed=moved, transcendentals=trans)


def phi(values):
    return 0.5 * (1.0 + lax.erf(values * root_half))


def bell(values):
    return jnp.exp(-0.5 * values * values) * density


def nt(a, b):
    return lax.dot_general(a, b, (((1,), (1,)), ((), ())), preferred_element_type=f32)


def tn(a, b):
    return lax.dot_general(a, b, (((0,), (0,)), ((), ())), preferred_element_type=f32)


def nn(a, b):
    return jnp.dot(a, b, preferred_element_type=f32)


class Place:
    def __init__(self, dev_ref, len_ref, mov_ref=None):
        self.data = dev_ref[0] // MP
        self.model = lax.rem(dev_ref[0], MP)
        self.x = lax.rem(self.model, X)
        self.y = self.model // X
        self.core = lax.rem(self.data, 2)
        self.cell = self.data // 2
        self.first = self.model * T
        self.lengths = len_ref
        if mov_ref is not None:
            self.chosen = mov_ref[lax.rem(self.data, DP // 2)]

    def length(self, slot):
        return self.lengths[self.data * SLOTS + slot]

    def alive(self, slot):
        return self.first < self.length(slot)

    def seam(self, rows):
        return jnp.where(self.x == 0, rows[:REACH, :], rows[T - REACH :, :]).astype(bf16)

    def extended(self, ext, edge, pieces):
        own = pieces[self.x, 0, :T, :].astype(f32)
        before = pieces[jnp.maximum(self.x - 1, 0), 0, T - REACH : T, :].astype(f32)
        after = pieces[jnp.minimum(self.x + 1, X - 1), 0, :REACH, :].astype(f32)
        ext[:REACH, :] = jnp.where(self.x == 0, edge, before)
        ext[REACH : REACH + T, :] = own
        ext[REACH + T :, :] = jnp.where(self.x == X - 1, edge, after)
        return own

    def mask(self, slot):
        ids = self.first + lax.broadcasted_iota(jnp.int32, (T, 1), 0)
        return ids < self.length(slot)


def by_slot(*dims):
    return pl.BlockSpec((1,) + dims, lambda s: (s,) + (0,) * len(dims))


def whole(*dims):
    return pl.BlockSpec(dims, lambda s: (0,) * len(dims))


def all_x(rows):
    return pl.BlockSpec((X, 1, rows, LANES), lambda s: (0, s, 0, 0))


def once(*dims):
    return pl.BlockSpec(dims, lambda s: (0,) * len(dims), pipeline_mode=pl.Buffered(1))


def turn_body(forward, in_ref, out_ref, rows):
    block = pl.program_id(0)
    blocks = pl.num_programs(0)
    for n in range(NEAR):
        tile = jnp.concatenate(
            [in_ref[n].astype(f32), jnp.zeros((LANES - GC, K), f32)], axis=0
        ).T
        if n >= GC % NEAR:
            tile = jnp.where(block == blocks - 1, 0.0, tile)
        rows[pl.ds(n, K, stride=NEAR), :] = tile
    far = K // NEAR
    for q in range(far):
        for r in range(NEAR):
            at = (q * NEAR + r) * NEAR
            tile = rows[at : at + NEAR, :].astype(bf16)
            if forward:
                out_ref[r, :, q * LANES : (q + 1) * LANES] = tile
            else:
                back = NEAR - 1 - r
                out_ref[far - 1 - q, :, back * LANES : (back + 1) * LANES] = tile


def turn(pos, forward):
    outer, inner = (NEAR, K // NEAR) if forward else (K // NEAR, NEAR)
    weight = pl.pallas_call(
        functools.partial(turn_body, forward),
        grid=(LANES // NEAR,),
        out_shape=jax.ShapeDtypeStruct((outer, LANES, inner * LANES), bf16),
        in_specs=[pl.BlockSpec((NEAR, GC, K), lambda b: (b, 0, 0))],
        out_specs=pl.BlockSpec((outer, NEAR, inner * LANES), lambda b: (0, b, 0)),
        scratch_shapes=[pltpu.VMEM((K * NEAR, LANES), f32)],
        compiler_params=params(56),
        cost_estimate=cost(0, 8 << 20),
        name="ahead" if forward else "behind",
    )(pos)
    return weight.reshape(outer * LANES, -1)


def encode_body(
    dev_ref,
    len_hbm,
    audio_hbm,
    conv_hbm,
    chan_hbm,
    proj_hbm,
    feat_ref,
    edge_ref,
    pair_ref,
    q_ref,
    slope_ref,
    m_ref,
    inv_ref,
    wide,
    proj,
    mid,
    normed,
    len_ref,
    audio_ref,
    conv_ref,
    chan_ref,
    sems,
):
    slot = pl.program_id(0)
    copies = [
        pltpu.make_async_copy(source, target, sems.at[n])
        for n, (source, target) in enumerate(
            (
                (len_hbm, len_ref),
                (audio_hbm.at[0], audio_ref.at[0]),
                (conv_hbm, conv_ref),
                (chan_hbm, chan_ref),
                (proj_hbm, proj.at[pl.ds(0, GC)]),
                (audio_hbm.at[1], audio_ref.at[1]),
            )
        )
    ]

    @pl.when(slot == 0)
    def _():
        proj[GC - 8 :, :] = jnp.zeros((LANES - GC + 8, C), bf16)
        for copy in copies:
            copy.start()
        for copy in copies[:-1]:
            copy.wait()

    @pl.when(slot == SLOTS - 1)
    def _():
        copies[-1].wait()

    place = Place(dev_ref, len_ref)
    living = place.alive(slot)

    @pl.when(living)
    def _():
        for c in range(C // LANES):
            wide[c] = audio_ref[slot, :, c * LANES : (c + 1) * LANES].astype(f32)
            for tap in range(2):
                at = tap * C + c * LANES
                pair_ref[0, :, at : at + LANES] = wide[c, pl.ds(tap, T, stride=2), :].astype(bf16)
        mid[...] = nn(pair_ref[0], conv_ref[...])
        bias, gain, shift = chan_ref[0:1, :], chan_ref[1:2, :], chan_ref[2:3, :]
        gain_two, shift_two = chan_ref[3:4, :], chan_ref[4:5, :]
        for at in range(0, T, CHUNK):
            rows = slice(at, at + CHUNK)
            conv = mid[rows, :] + bias
            offset = conv - jnp.mean(conv, axis=-1, keepdims=True)
            inverse = lax.rsqrt(jnp.mean(offset * offset, axis=-1, keepdims=True) + epsilon)
            q = offset * inverse
            pre = q * gain + shift
            below = phi(pre)
            encoded = (pre * below).astype(bf16).astype(f32)
            slope_ref[0, rows, :] = (below + pre * bell(pre)).astype(bf16)
            q_ref[0, rows, :] = q.astype(bf16)
            offset = encoded - jnp.mean(encoded, axis=-1, keepdims=True)
            inverse_two = lax.rsqrt(jnp.mean(offset * offset, axis=-1, keepdims=True) + epsilon)
            m = offset * inverse_two
            m_ref[0, rows, :] = m.astype(bf16)
            inv_ref[0, rows, :] = jnp.concatenate(
                [
                    jnp.broadcast_to(inverse, (CHUNK, LANES // 2)),
                    jnp.broadcast_to(inverse_two, (CHUNK, LANES // 2)),
                ],
                axis=1,
            )
            normed[rows, :] = (m * gain_two + shift_two).astype(bf16)
        projected = nt(normed[...], proj[...])
        features = jnp.where(place.mask(slot), projected, 0.0)
        for copy in range(X):
            feat_ref[copy, 0] = features.astype(bf16)
        edge_ref[0] = place.seam(features)

    @pl.when(jnp.logical_not(living))
    def _():
        feat_ref[...] = jnp.zeros_like(feat_ref)
        edge_ref[...] = jnp.zeros_like(edge_ref)


def encode(place, audio, conv_weight, channels, proj):
    return pl.pallas_call(
        encode_body,
        grid=(SLOTS,),
        out_shape=(
            jax.ShapeDtypeStruct((X, SLOTS, T, LANES), bf16),
            jax.ShapeDtypeStruct((SLOTS, REACH, LANES), bf16),
            jax.ShapeDtypeStruct((SLOTS, T, 2 * C), bf16),
            jax.ShapeDtypeStruct((SLOTS, T, C), bf16),
            jax.ShapeDtypeStruct((SLOTS, T, C), bf16),
            jax.ShapeDtypeStruct((SLOTS, T, C), bf16),
            jax.ShapeDtypeStruct((SLOTS, T, LANES), f32),
        ),
        in_specs=[SMEM] + [HBM] * 5,
        out_specs=(
            all_x(T),
            by_slot(REACH, LANES),
            by_slot(T, 2 * C),
            by_slot(T, C),
            by_slot(T, C),
            by_slot(T, C),
            by_slot(T, LANES),
        ),
        scratch_shapes=[
            pltpu.VMEM((C // LANES, 2 * T, LANES), f32),
            pltpu.VMEM((LANES, C), bf16),
            pltpu.VMEM((T, C), f32),
            pltpu.VMEM((T, C), bf16),
            pltpu.SMEM((DP * SLOTS,), jnp.int32),
            pltpu.VMEM((SLOTS, 2 * T, C), bf16),
            pltpu.VMEM((2 * C, C), bf16),
            pltpu.VMEM((5, C), f32),
            pltpu.SemaphoreType.DMA((6,)),
        ],
        compiler_params=params(52),
        cost_estimate=cost(2 * SLOTS * T * C * (2 * C + LANES), 8 << 20, SLOTS * T * C * 2),
        name="encode",
    )(*place[:2], audio, conv_weight, channels, proj)


def fill_windows(windows, ext, first):
    rows = T + NEAR * (K // NEAR - 1)
    for r in range(NEAR):
        windows[:, r * LANES : (r + 1) * LANES] = ext[first + r : first + r + rows, :].astype(bf16)


def gathered(group):
    total = group[:T, :LANES]
    for p in range(1, PER_GROUP):
        total += group[NEAR * p : NEAR * p + T, p * LANES : (p + 1) * LANES]
    return total


def fill_back(turned, place, slot, cot_ref, recv_ref):
    turned[GC:, :] = jnp.zeros((LANES - GC, T), f32)
    turned[:GC, :] = jnp.where(
        place.chosen == slot, recv_ref[0].astype(f32), cot_ref[0].astype(f32)
    )


def mix_body(
    dev_ref,
    len_ref,
    mov_ref,
    feat_ref,
    edge_ref,
    weight,
    cot_ref,
    recv_ref,
    states_ref,
    sent_ref,
    piece_ref,
    seam_ref,
    ext,
    windows,
    turned,
):
    place = Place(dev_ref, len_ref, mov_ref)
    slot = pl.program_id(0)
    living = place.alive(slot)
    wide = PER_GROUP * LANES

    @pl.when(living)
    def _():
        edge = edge_ref[0].astype(f32)
        own = place.extended(ext, edge, feat_ref)
        fill_windows(windows, ext, 0)
        fill_back(turned, place, slot, cot_ref, recv_ref)
        back = turned[...].T
        group = jnp.zeros((SPAN, wide), f32)
        for g in range(GROUPS):
            at = g * NEAR * PER_GROUP
            group += nn(windows[at : at + SPAN, :], weight[:, g * wide : (g + 1) * wide])
        mixed = gathered(group)
        below = phi(mixed)
        mask = place.mask(slot)
        states = jnp.where(mask, own + mixed * below, 0.0)
        states_ref[0] = states.T[:GC, :].astype(bf16)
        slopes = jnp.where(mask, back * (below + mixed * bell(mixed)), 0.0)
        for copy in range(X):
            piece_ref[copy, 0, :T, :] = slopes.astype(bf16)
            piece_ref[copy, 0, T:, :] = edge.astype(bf16)
        seam_ref[0] = place.seam(slopes)

    @pl.when(jnp.logical_not(living))
    def _():
        states_ref[...] = jnp.zeros_like(states_ref)
        piece_ref[...] = jnp.zeros_like(piece_ref)
        seam_ref[...] = jnp.zeros_like(seam_ref)

    @pl.when(place.chosen == slot)
    def _():
        sent_ref[...] = states_ref[0]


def mix(place, features, edge, weight, cotangent, received):
    return pl.pallas_call(
        mix_body,
        grid=(SLOTS,),
        out_shape=(
            jax.ShapeDtypeStruct((SLOTS, GC, T), bf16),
            jax.ShapeDtypeStruct((GC, T), bf16),
            jax.ShapeDtypeStruct((X, SLOTS, PIECE, LANES), bf16),
            jax.ShapeDtypeStruct((SLOTS, REACH, LANES), bf16),
        ),
        in_specs=[SMEM] * 3
        + [
            all_x(T),
            by_slot(REACH, LANES),
            once(*weight.shape),
            by_slot(GC, T),
            by_slot(GC, T),
        ],
        out_specs=(
            by_slot(GC, T),
            whole(GC, T),
            all_x(PIECE),
            by_slot(REACH, LANES),
        ),
        scratch_shapes=[
            pltpu.VMEM((EXT, LANES), f32),
            pltpu.VMEM((T + NEAR * (K // NEAR - 1), NEAR * LANES), bf16),
            pltpu.VMEM((LANES, T), f32),
        ],
        compiler_params=params(50),
        cost_estimate=cost(2 * SLOTS * SPAN * K * LANES * LANES, 7 << 20, SLOTS * T * LANES * 2),
        name="mix",
    )(*place, features, edge, weight, cotangent, received)


def taps_body(
    scale, dev_ref, len_ref, mov_ref, feat_ref, piece_ref, keep_ref, send_ref, ext, windows, turned, sums
):
    place = Place(dev_ref, len_ref, mov_ref)
    slot = pl.program_id(0)
    spread = X * T
    rows = spread + NEAR * (K // NEAR - 1)

    @pl.when(slot == 0)
    def _():
        sums[...] = jnp.zeros_like(sums)

    @pl.when(place.y * spread < place.length(slot))
    def _():
        ext[:REACH, :] = piece_ref[0, 0, T:, :].astype(f32)
        ext[REACH + spread :, :] = piece_ref[X - 1, 0, T:, :].astype(f32)
        for x in range(X):
            ext[REACH + x * T : REACH + (x + 1) * T, :] = feat_ref[x, 0].astype(f32)
            turned[:, x * T : (x + 1) * T] = (
                piece_ref[x, 0, :T, :].astype(f32).T.astype(bf16)
            )
        for j in range(4):
            windows[:, j * LANES : (j + 1) * LANES] = ext[
                pl.ds(place.x + 4 * j, rows), :
            ].astype(bf16)
        for q in range(K // NEAR):
            sums[q] += nn(turned[...], windows[q * NEAR : q * NEAR + spread, :])

    @pl.when(slot == SLOTS - 1)
    def _():
        first_core = place.core == 0
        for q in range(K // NEAR):
            for far in range(2):
                at = 2 * far * LANES
                even = sums[q, :, at : at + LANES] * scale
                odd = sums[q, :, at + LANES : at + 2 * LANES] * scale
                keep = jnp.where(first_core, even, odd)
                send = jnp.where(first_core, odd, even)
                for y in range(2):
                    rows = slice(y * HALF, y * HALF + REACH)
                    keep_ref[y, 2 * q + far] = keep[rows, :].astype(bf16)
                    send_ref[y, 2 * q + far] = send[rows, :].astype(bf16)


def taps(scale, place, features, pieces):
    shape = jax.ShapeDtypeStruct((2, CELLS, REACH, LANES), bf16)
    spread = X * T
    return pl.pallas_call(
        functools.partial(taps_body, scale),
        grid=(SLOTS,),
        out_shape=(shape,) * 2,
        in_specs=[SMEM] * 3 + [all_x(T), all_x(PIECE)],
        out_specs=(whole(*shape.shape),) * 2,
        scratch_shapes=[
            pltpu.VMEM((spread + 2 * REACH, LANES), f32),
            pltpu.VMEM((spread + NEAR * (K // NEAR - 1), 4 * LANES), bf16),
            pltpu.VMEM((LANES, spread), bf16),
            pltpu.VMEM((K // NEAR, LANES, 4 * LANES), f32),
        ],
        compiler_params=params(16),
        cost_estimate=cost(2 * SLOTS * SPAN * K * LANES * LANES, 4 << 20),
        name="taps",
    )(*place, features, pieces)


def backward_body(
    scale,
    dev_ref,
    len_ref,
    mov_ref,
    piece_ref,
    edge_ref,
    cot_ref,
    recv_ref,
    weight,
    pair_ref,
    q_ref,
    slope_ref,
    m_ref,
    inv_ref,
    conv_ref,
    chan_ref,
    proj_ref,
    audio_grad_ref,
    keep_ref,
    send_ref,
    ext,
    windows,
    turned,
    proj,
    feat_grad,
    normed,
    mid,
    wide,
    conv_sum,
    proj_sum,
    chan_sum,
    columns,
):
    place = Place(dev_ref, len_ref, mov_ref)
    slot = pl.program_id(0)
    living = place.alive(slot)
    span = PER_GROUP * LANES

    @pl.when(slot == 0)
    def _():
        proj[...] = jnp.zeros_like(proj)
        proj[:GC, :] = proj_ref[...]
        conv_sum[...] = jnp.zeros_like(conv_sum)
        proj_sum[...] = jnp.zeros_like(proj_sum)
        chan_sum[...] = jnp.zeros_like(chan_sum)

    @pl.when(living)
    def _():
        place.extended(ext, edge_ref[0].astype(f32), piece_ref)
        fill_windows(windows, ext, 1)
        fill_back(turned, place, slot, cot_ref, recv_ref)
        group = jnp.zeros((SPAN, span), f32)
        for g in range(GROUPS):
            at = g * NEAR * PER_GROUP
            group += nt(windows[at : at + SPAN, :], weight[g * span : (g + 1) * span, :])
        spread = gathered(group)
        feat_grad[...] = jnp.where(place.mask(slot), turned[...].T + spread, 0.0).astype(bf16)
        gain = chan_ref[1:2, :]
        gain_two, shift_two = chan_ref[3:4, :], chan_ref[4:5, :]
        mid[...] = nn(feat_grad[...], proj[...])
        for at in range(0, T, CHUNK):
            rows = slice(at, at + CHUNK)
            m = m_ref[0, rows, :].astype(f32)
            normed[rows, :] = (m * gain_two + shift_two).astype(bf16)
            normed_grad = mid[rows, :]
            chan_sum[24:32, :] += jnp.sum((normed_grad * m).reshape(-1, 8, C), axis=0)
            chan_sum[32:40, :] += jnp.sum(normed_grad.reshape(-1, 8, C), axis=0)
            scaled = normed_grad * gain_two
            first = jnp.mean(scaled, axis=-1, keepdims=True)
            second = jnp.mean(scaled * m, axis=-1, keepdims=True)
            inverse_two = inv_ref[0, rows, LANES // 2 : LANES // 2 + 1]
            pre_grad = inverse_two * (scaled - first - m * second) * slope_ref[
                0, rows, :
            ].astype(f32)
            q = q_ref[0, rows, :].astype(f32)
            chan_sum[8:16, :] += jnp.sum((pre_grad * q).reshape(-1, 8, C), axis=0)
            chan_sum[16:24, :] += jnp.sum(pre_grad.reshape(-1, 8, C), axis=0)
            scaled = pre_grad * gain
            first = jnp.mean(scaled, axis=-1, keepdims=True)
            second = jnp.mean(scaled * q, axis=-1, keepdims=True)
            inverse = inv_ref[0, rows, 0:1]
            conv_grad = inverse * (scaled - first - q * second)
            chan_sum[0:8, :] += jnp.sum(conv_grad.reshape(-1, 8, C), axis=0)
            mid[rows, :] = conv_grad
        operand = mid[...].astype(bf16)
        for tap in range(2):
            rows = slice(tap * C, (tap + 1) * C)
            audio_grad = nt(operand, conv_ref[rows, :])
            for c in range(C // LANES):
                wide[c, pl.ds(tap, T, stride=2), :] = audio_grad[:, c * LANES : (c + 1) * LANES]
            conv_sum[rows, :] += tn(pair_ref[0, :, rows], operand)
        for c in range(C // LANES):
            audio_grad_ref[0, :, c * LANES : (c + 1) * LANES] = wide[c].astype(bf16)
        proj_sum[...] += tn(normed[...], feat_grad[...])

    @pl.when(jnp.logical_not(living))
    def _():
        audio_grad_ref[...] = jnp.zeros_like(audio_grad_ref)

    @pl.when(slot == SLOTS - 1)
    def _():
        first_core = place.core == 0
        columns[...] = jnp.zeros_like(columns)
        for n in range(5):
            columns[GC + n : GC + n + 1, :] = jnp.sum(
                chan_sum[8 * n : 8 * n + 8, :], axis=0, keepdims=True
            )
        proj_sum[...] += columns[...].T
        for x in range(X):
            lanes = slice(x * LANES, (x + 1) * LANES)
            for cell in range(CELLS):
                at = 2 * cell * 32
                even = conv_sum[at : at + 32, lanes]
                odd = conv_sum[at + 32 : at + 64, lanes]
                rows = slice(cell * 32, (cell + 1) * 32)
                keep_ref[x, rows, :] = (jnp.where(first_core, even, odd) * scale).astype(bf16)
                send_ref[x, rows, :] = (jnp.where(first_core, odd, even) * scale).astype(bf16)
            for four in range(CELLS // 4):
                even, odd = [
                    jnp.concatenate(
                        [
                            proj_sum[at : at + SPARE, :]
                            for at in (
                                (2 * cell + odd) * 16 + x * SPARE
                                for cell in range(4 * four, 4 * four + 4)
                            )
                        ],
                        axis=0,
                    )
                    for odd in range(2)
                ]
                rows = slice(CONV_ROWS + four * 16, CONV_ROWS + (four + 1) * 16)
                keep_ref[x, rows, :] = (jnp.where(first_core, even, odd) * scale).astype(bf16)
                send_ref[x, rows, :] = (jnp.where(first_core, odd, even) * scale).astype(bf16)


def backward(
    scale, place, pieces, edge, cotangent, received, weight, stored, conv_weight, channels, proj
):
    shape = jax.ShapeDtypeStruct((X, REST, LANES), bf16)
    return pl.pallas_call(
        functools.partial(backward_body, scale),
        grid=(SLOTS,),
        out_shape=(jax.ShapeDtypeStruct((SLOTS, 2 * T, C), bf16), shape, shape),
        in_specs=[SMEM] * 3
        + [
            all_x(PIECE),
            by_slot(REACH, LANES),
            by_slot(GC, T),
            by_slot(GC, T),
            once(*weight.shape),
            by_slot(T, 2 * C),
            by_slot(T, C),
            by_slot(T, C),
            by_slot(T, C),
            by_slot(T, LANES),
            once(2 * C, C),
            whole(5, C),
            whole(GC, C),
        ],
        out_specs=(by_slot(2 * T, C), whole(*shape.shape), whole(*shape.shape)),
        scratch_shapes=[
            pltpu.VMEM((EXT, LANES), f32),
            pltpu.VMEM((T + NEAR * (K // NEAR - 1), NEAR * LANES), bf16),
            pltpu.VMEM((LANES, T), f32),
            pltpu.VMEM((LANES, C), bf16),
            pltpu.VMEM((T, LANES), bf16),
            pltpu.VMEM((T, C), bf16),
            pltpu.VMEM((T, C), f32),
            pltpu.VMEM((C // LANES, 2 * T, LANES), f32),
            pltpu.VMEM((2 * C, C), f32),
            pltpu.VMEM((C, LANES), f32),
            pltpu.VMEM((40, C), f32),
            pltpu.VMEM((LANES, C), f32),
        ],
        compiler_params=params(50),
        cost_estimate=cost(
            2 * SLOTS * (SPAN * K * LANES * LANES + T * C * (4 * C + 2 * LANES)), 14 << 20
        ),
        name="backward",
    )(
        *place,
        pieces,
        edge,
        cotangent,
        received,
        weight,
        *stored,
        conv_weight,
        channels,
        proj,
    )


def halve_body(dev_ref, keep_ref, recv_ref, stay_ref, leave_ref):
    y = lax.rem(dev_ref[0], MP) // X
    for out_ref, at in ((stay_ref, y), (leave_ref, 1 - y)):
        out_ref[...] = (keep_ref[at].astype(f32) + recv_ref[at].astype(f32)).astype(bf16)


def halve(dev, keep, received):
    shape = jax.ShapeDtypeStruct(keep.shape[1:], bf16)
    return pl.pallas_call(
        halve_body,
        out_shape=(shape,) * 2,
        in_specs=[SMEM] + [VMEM] * 2,
        out_specs=(VMEM,) * 2,
        compiler_params=params(8),
        cost_estimate=cost(0, 2 << 20),
        name="halve",
    )(dev, keep, received)


def join_body(dev_ref, keep_ref, recv_ref, *out_refs):
    x = lax.rem(dev_ref[0], X)
    for step, out_ref in enumerate(out_refs):
        at = lax.rem(x + step, X)
        out_ref[...] = (keep_ref[at].astype(f32) + recv_ref[at].astype(f32)).astype(bf16)


def join(dev, keep, received):
    shape = jax.ShapeDtypeStruct((REST, LANES), bf16)
    return pl.pallas_call(
        join_body,
        out_shape=(shape,) * X,
        in_specs=[SMEM] + [VMEM] * 2,
        out_specs=(VMEM,) * X,
        compiler_params=params(8),
        cost_estimate=cost(0, 2 << 20),
        name="join",
    )(dev, keep, received)


def cells_body(*refs):
    pos_refs, rest_refs, out_ref, rows = refs[:2], refs[2:6], refs[6], refs[7]

    def summed(parts, *at):
        result = parts[0][at].astype(f32)
        for part in parts[1:]:
            result += part[at].astype(f32)
        return result

    for four in range(CELLS // 4):
        at = CONV_ROWS + four * 16
        small = summed(rest_refs, slice(at, at + 16), slice(None))
        for n in range(4):
            cell = 4 * four + n
            rows[...] = summed(pos_refs, cell)
            rows[HALF:, :] = small[n * SPARE : (n + 1) * SPARE, :]
            out_ref[cell, :REACH, :] = rows[...].astype(bf16)
            conv = summed(rest_refs, slice(cell * 32, cell * 32 + 32), slice(None))
            out_ref[cell, REACH:, :] = conv.astype(bf16)


def make_cells(pos_parts, rest_parts):
    return pl.pallas_call(
        cells_body,
        out_shape=jax.ShapeDtypeStruct((CELLS, REACH + 32, LANES), bf16),
        in_specs=[VMEM] * 6,
        out_specs=VMEM,
        scratch_shapes=[pltpu.VMEM((REACH, LANES), f32)],
        compiler_params=params(8),
        cost_estimate=cost(0, 2 << 20),
        name="cells",
    )(*pos_parts, *rest_parts)


def total_body(in_ref, out_ref):
    total = in_ref[0].astype(f32)
    for n in range(1, in_ref.shape[0]):
        total += in_ref[n].astype(f32)
    for copy in range(MP):
        out_ref[copy] = total.astype(bf16)


def total(parts):
    return pl.pallas_call(
        total_body,
        out_shape=jax.ShapeDtypeStruct((MP,) + parts.shape[1:], bf16),
        in_specs=[VMEM],
        out_specs=VMEM,
        compiler_params=params(10),
        cost_estimate=cost(0, 2 * parts.size),
        name="total",
    )(parts)


def finish_body(
    dev_ref,
    len_ref,
    mov_ref,
    in_ref,
    states_ref,
    other_ref,
    hidden_ref,
    pos_ref,
    conv_ref,
    proj_ref,
    chan_ref,
):
    place = Place(dev_ref, len_ref, mov_ref)
    for slot in range(SLOTS):
        hidden_ref[slot] = jnp.where(
            place.chosen == slot, other_ref[...].astype(f32), states_ref[slot].astype(f32)
        ).astype(bf16)
    small = []
    for x in range(X):
        low, high = in_ref[x].astype(f32), in_ref[X + x].astype(f32)
        block = jnp.concatenate(
            [low[:HALF, :], high[:HALF, :], jnp.zeros((LANES - GC, LANES), f32)], axis=0
        ).T
        pos_ref[x] = block[:GC, :GC]
        both = low[HALF:, :] + high[HALF:, :]
        small.append(both[:SPARE, :])
        conv_ref[:, x * LANES : (x + 1) * LANES] = both[SPARE:, :]
    small = jnp.concatenate(small, axis=0)
    proj_ref[...] = small[:, :GC]
    chan_ref[...] = jnp.concatenate([small] * 8, axis=0).T[GC : GC + 5, :16]


def finish(place, cells, states, other):
    return pl.pallas_call(
        finish_body,
        out_shape=(
            jax.ShapeDtypeStruct((SLOTS, GC, T), bf16),
            jax.ShapeDtypeStruct((4, GC, GC), f32),
            jax.ShapeDtypeStruct((32, C), f32),
            jax.ShapeDtypeStruct((16, GC), f32),
            jax.ShapeDtypeStruct((5, 16), f32),
        ),
        in_specs=[SMEM] * 3 + [VMEM] * 3,
        out_specs=(VMEM,) * 5,
        compiler_params=params(8),
        name="finish",
    )(*place, cells, states, other)


def along_x(block, step):
    route = [(X * y + x, X * y + (x + step) % X) for y in range(2) for x in range(X)]
    return lax.ppermute(block, "mp", route)


def per_device(
    audio, lengths, moved_slots, conv_weight, channel_params, proj_weight, pos_weight, cotangent
):
    data_index = lax.axis_index("dp")
    model_index = lax.axis_index("mp")
    scale = (SLOTS * DP * T * MP) ** -0.5
    dev = (data_index * MP + model_index).astype(jnp.int32).reshape(1)
    place = (dev, lengths, moved_slots.reshape(-1))
    swap = [(i, i ^ (DP // 2)) for i in range(DP)]
    core_swap = [(i, i ^ 1) for i in range(DP)]
    channels = channel_params.T
    proj = proj_weight.T
    cot = cotangent.transpose(0, 2, 1)

    rows = [list(range(X)), list(range(X, 2 * X))]
    seam = [(X - 1, X), (X, X - 1)]
    natural = pos_weight.transpose(1, 2, 0)

    def over_x(copies):
        return lax.all_to_all(copies, "mp", 0, 0, axis_index_groups=rows, tiled=True)

    received = lax.ppermute(cot, "dp", swap)
    features, edge, *stored = encode(place, audio, conv_weight, channels, proj)
    features = over_x(features)
    edge = lax.ppermute(edge, "mp", seam)
    ahead = turn(natural, True)
    states, sent, pieces, edge = mix(place, features, edge, ahead, cot, received)
    pieces, natural = lax.optimization_barrier((pieces, natural))
    pieces = over_x(pieces)
    edge = lax.ppermute(edge, "mp", seam)
    other = lax.ppermute(sent, "dp", swap)
    behind = turn(natural, False)
    pieces, other, behind = lax.optimization_barrier((pieces, other, behind))
    pos_keep, pos_send = taps(scale, place, features, pieces)
    pos_send, edge = lax.optimization_barrier((pos_send, edge))
    pos_recv = lax.ppermute(pos_send, "dp", core_swap)
    audio_grad, keep, send = backward(
        scale,
        place,
        pieces,
        edge,
        cot,
        received,
        behind,
        stored,
        conv_weight,
        channels,
        proj,
    )
    send, pos_recv = lax.optimization_barrier((send, pos_recv))
    chunks = join(dev, keep, lax.ppermute(send, "dp", core_swap))
    rest_parts = [chunks[0]] + [along_x(chunks[step], step) for step in (2, 1, 3)]
    stay, leave = halve(dev, pos_keep, pos_recv)
    pos_parts = (stay, lax.ppermute(leave, "mp", [(i, i ^ X) for i in range(MP)]))
    cells = make_cells(pos_parts, rest_parts)
    groups = [list(range(bit, DP, 2)) for bit in range(2)]
    cells = lax.all_to_all(cells, "dp", 0, 0, axis_index_groups=groups, tiled=True)
    cells = lax.all_to_all(total(cells), "mp", 0, 0, tiled=True)
    hidden, grad_pos, grad_conv, grad_proj, grad_channels = finish(place, cells, states, other)
    return (
        hidden.transpose(0, 2, 1),
        audio_grad,
        grad_pos,
        grad_conv,
        grad_proj,
        grad_channels.T,
    )


def solution(mesh):
    return jax.shard_map(
        per_device,
        mesh=mesh,
        in_specs=(P("dp", "mp", None), P(), P(), P(), P(), P(), P(), P("dp", "mp", None)),
        out_specs=(
            P("dp", "mp", None),
            P("dp", "mp", None),
            P("dp", None, None),
            P("dp", None),
            P("dp", None),
            P("dp", None),
        ),
        check_vma=False,
    )
```

```python
import functools

import jax
import jax.numpy as jnp
from jax import lax
from jax.experimental import pallas as pl
from jax.experimental.pallas import tpu as pltpu
from jax.sharding import PartitionSpec as P

epsilon = 1e-05
root_half = 0.7071067811865476
density = 0.3989422804014327

SLOTS = 2
T = 256
C = 512
GC = 120
LANES = 128
K = 128
REACH = 64
EXT = T + 2 * REACH
NEAR = 16
GROUPS = 2
PER_GROUP = 4
SPAN = T + NEAR * (PER_GROUP - 1)
CHUNK = 32
MP = 8
DP = 32
X = 4
CELLS = 16
PIECE = T + REACH
HALF = GC // 2
SPARE = REACH - HALF
CONV_ROWS = CELLS * 32
REST = CONV_ROWS + CELLS * SPARE

f32 = jnp.float32
bf16 = jnp.bfloat16

VMEM = pl.BlockSpec(memory_space=pltpu.VMEM)
SMEM = pl.BlockSpec(memory_space=pltpu.SMEM)
HBM = pl.BlockSpec(memory_space=pltpu.HBM)


def params(mebibytes):
    return pltpu.CompilerParams(vmem_limit_bytes=mebibytes << 20)


def cost(flops, moved, trans=0):
    return pl.CostEstimate(flops=flops, bytes_accessed=moved, transcendentals=trans)


def phi(values):
    return 0.5 * (1.0 + lax.erf(values * root_half))


def bell(values):
    return jnp.exp(-0.5 * values * values) * density


def nt(a, b):
    return lax.dot_general(a, b, (((1,), (1,)), ((), ())), preferred_element_type=f32)


def tn(a, b):
    return lax.dot_general(a, b, (((0,), (0,)), ((), ())), preferred_element_type=f32)


def nn(a, b):
    return jnp.dot(a, b, preferred_element_type=f32)


class Place:
    def __init__(self, dev_ref, len_ref, mov_ref=None):
        self.data = dev_ref[0] // MP
        self.model = lax.rem(dev_ref[0], MP)
        self.x = lax.rem(self.model, X)
        self.y = self.model // X
        self.core = lax.rem(self.data, 2)
        self.cell = self.data // 2
        self.first = self.model * T
        self.lengths = len_ref
        if mov_ref is not None:
            self.chosen = mov_ref[lax.rem(self.data, DP // 2)]

    def length(self, slot):
        return self.lengths[self.data * SLOTS + slot]

    def alive(self, slot):
        return self.first < self.length(slot)

    def mask(self, slot):
        ids = self.first + lax.broadcasted_iota(jnp.int32, (T, 1), 0)
        return ids < self.length(slot)


def by_slot(*dims):
    return pl.BlockSpec((1,) + dims, lambda s: (s,) + (0,) * len(dims))


def whole(*dims):
    return pl.BlockSpec(dims, lambda s: (0,) * len(dims))


def once(*dims):
    return pl.BlockSpec(dims, lambda s: (0,) * len(dims), pipeline_mode=pl.Buffered(1))


def turn_body(in_ref, ahead_ref, behind_ref, rows):
    block = pl.program_id(0)
    blocks = pl.num_programs(0)
    for n in range(NEAR):
        tile = jnp.concatenate(
            [in_ref[n].astype(f32), jnp.zeros((LANES - GC, K), f32)], axis=0
        ).T
        if n >= GC % NEAR:
            tile = jnp.where(block == blocks - 1, 0.0, tile)
        rows[pl.ds(n, K, stride=NEAR), :] = tile
    far = K // NEAR
    for q in range(far):
        for r in range(NEAR):
            at = (q * NEAR + r) * NEAR
            tile = rows[at : at + NEAR, :].astype(bf16)
            ahead_ref[r, :, q * LANES : (q + 1) * LANES] = tile
            r_back = NEAR - 1 - r
            behind_ref[far - 1 - q, :, r_back * LANES : (r_back + 1) * LANES] = tile


def turn(pos):
    far = K // NEAR
    ahead, behind = pl.pallas_call(
        turn_body,
        grid=(LANES // NEAR,),
        out_shape=(
            jax.ShapeDtypeStruct((NEAR, LANES, far * LANES), bf16),
            jax.ShapeDtypeStruct((far, LANES, NEAR * LANES), bf16),
        ),
        in_specs=[pl.BlockSpec((NEAR, GC, K), lambda b: (b, 0, 0))],
        out_specs=(
            pl.BlockSpec((NEAR, NEAR, far * LANES), lambda b: (0, b, 0)),
            pl.BlockSpec((far, NEAR, NEAR * LANES), lambda b: (0, b, 0)),
        ),
        scratch_shapes=[pltpu.VMEM((K * NEAR, LANES), f32)],
        compiler_params=params(16),
        cost_estimate=cost(0, 12 << 20),
        name="turn",
    )(pos)
    return ahead.reshape(NEAR * LANES, -1), behind.reshape(far * LANES, -1)


def encode_body(
    dev_ref,
    len_hbm,
    audio_hbm,
    conv_hbm,
    chan_hbm,
    proj_hbm,
    feat_ref,
    tail_ref,
    head_ref,
    pair_ref,
    q_ref,
    slope_ref,
    m_ref,
    inv_ref,
    wide,
    proj,
    mid,
    normed,
    len_ref,
    audio_ref,
    conv_ref,
    chan_ref,
    sems,
):
    slot = pl.program_id(0)
    copies = [
        pltpu.make_async_copy(source, target, sems.at[n])
        for n, (source, target) in enumerate(
            (
                (len_hbm, len_ref),
                (audio_hbm.at[0], audio_ref.at[0]),
                (conv_hbm, conv_ref),
                (chan_hbm, chan_ref),
                (proj_hbm, proj.at[pl.ds(0, GC)]),
                (audio_hbm.at[1], audio_ref.at[1]),
            )
        )
    ]

    @pl.when(slot == 0)
    def _():
        proj[GC - 8 :, :] = jnp.zeros((LANES - GC + 8, C), bf16)
        for copy in copies:
            copy.start()
        for copy in copies[:-1]:
            copy.wait()

    @pl.when(slot == SLOTS - 1)
    def _():
        copies[-1].wait()

    place = Place(dev_ref, len_ref)
    living = place.alive(slot)

    @pl.when(living)
    def _():
        for c in range(C // LANES):
            wide[c] = audio_ref[slot, :, c * LANES : (c + 1) * LANES].astype(f32)
            for tap in range(2):
                at = tap * C + c * LANES
                pair_ref[0, :, at : at + LANES] = wide[c, pl.ds(tap, T, stride=2), :].astype(bf16)
        mid[...] = nn(pair_ref[0], conv_ref[...])
        bias, gain, shift = chan_ref[0:1, :], chan_ref[1:2, :], chan_ref[2:3, :]
        gain_two, shift_two = chan_ref[3:4, :], chan_ref[4:5, :]
        for at in range(0, T, CHUNK):
            rows = slice(at, at + CHUNK)
            conv = mid[rows, :] + bias
            offset = conv - jnp.mean(conv, axis=-1, keepdims=True)
            inverse = lax.rsqrt(jnp.mean(offset * offset, axis=-1, keepdims=True) + epsilon)
            q = offset * inverse
            pre = q * gain + shift
            below = phi(pre)
            encoded = (pre * below).astype(bf16).astype(f32)
            slope_ref[0, rows, :] = (below + pre * bell(pre)).astype(bf16)
            q_ref[0, rows, :] = q.astype(bf16)
            offset = encoded - jnp.mean(encoded, axis=-1, keepdims=True)
            inverse_two = lax.rsqrt(jnp.mean(offset * offset, axis=-1, keepdims=True) + epsilon)
            m = offset * inverse_two
            m_ref[0, rows, :] = m.astype(bf16)
            inv_ref[0, rows, :] = jnp.concatenate(
                [
                    jnp.broadcast_to(inverse, (CHUNK, LANES // 2)),
                    jnp.broadcast_to(inverse_two, (CHUNK, LANES // 2)),
                ],
                axis=1,
            )
            normed[rows, :] = (m * gain_two + shift_two).astype(bf16)
        projected = nt(normed[...], proj[...])
        feat_ref[0] = jnp.where(place.mask(slot), projected, 0.0).astype(bf16)

    @pl.when(jnp.logical_not(living))
    def _():
        feat_ref[...] = jnp.zeros_like(feat_ref)

    tail_ref[0] = feat_ref[0, T - REACH :, :]
    head_ref[0] = feat_ref[0, :REACH, :]


def encode(place, audio, conv_weight, channels, proj):
    return pl.pallas_call(
        encode_body,
        grid=(SLOTS,),
        out_shape=(
            jax.ShapeDtypeStruct((SLOTS, T, LANES), bf16),
            jax.ShapeDtypeStruct((SLOTS, REACH, LANES), bf16),
            jax.ShapeDtypeStruct((SLOTS, REACH, LANES), bf16),
            jax.ShapeDtypeStruct((SLOTS, T, 2 * C), bf16),
            jax.ShapeDtypeStruct((SLOTS, T, C), bf16),
            jax.ShapeDtypeStruct((SLOTS, T, C), bf16),
            jax.ShapeDtypeStruct((SLOTS, T, C), bf16),
            jax.ShapeDtypeStruct((SLOTS, T, LANES), f32),
        ),
        in_specs=[SMEM] + [HBM] * 5,
        out_specs=(
            by_slot(T, LANES),
            by_slot(REACH, LANES),
            by_slot(REACH, LANES),
            by_slot(T, 2 * C),
            by_slot(T, C),
            by_slot(T, C),
            by_slot(T, C),
            by_slot(T, LANES),
        ),
        scratch_shapes=[
            pltpu.VMEM((C // LANES, 2 * T, LANES), f32),
            pltpu.VMEM((LANES, C), bf16),
            pltpu.VMEM((T, C), f32),
            pltpu.VMEM((T, C), bf16),
            pltpu.SMEM((DP * SLOTS,), jnp.int32),
            pltpu.VMEM((SLOTS, 2 * T, C), bf16),
            pltpu.VMEM((2 * C, C), bf16),
            pltpu.VMEM((5, C), f32),
            pltpu.SemaphoreType.DMA((6,)),
        ],
        compiler_params=params(50),
        cost_estimate=cost(2 * SLOTS * T * C * (2 * C + LANES), 8 << 20, SLOTS * T * C * 2),
        name="encode",
    )(*place[:2], audio, conv_weight, channels, proj)


def fill_ext(ext, low, own, high):
    ext[:REACH, :] = low.astype(f32)
    ext[REACH : REACH + T, :] = own.astype(f32)
    ext[REACH + T :, :] = high.astype(f32)


def fill_windows(windows, ext, first):
    rows = T + NEAR * (K // NEAR - 1)
    for r in range(NEAR):
        windows[:, r * LANES : (r + 1) * LANES] = ext[first + r : first + r + rows, :].astype(bf16)


def gathered(group):
    total = group[:T, :LANES]
    for p in range(1, PER_GROUP):
        total += group[NEAR * p : NEAR * p + T, p * LANES : (p + 1) * LANES]
    return total


def fill_back(turned, place, slot, cot_ref, recv_ref):
    turned[GC:, :] = jnp.zeros((LANES - GC, T), f32)
    turned[:GC, :] = jnp.where(
        place.chosen == slot, recv_ref[0].astype(f32), cot_ref[0].astype(f32)
    )


def mix_body(
    dev_ref,
    len_ref,
    mov_ref,
    feat_ref,
    low_ref,
    high_ref,
    weight,
    cot_ref,
    recv_ref,
    states_ref,
    sent_ref,
    slopes_ref,
    tail_ref,
    head_ref,
    piece_ref,
    ext,
    windows,
    turned,
):
    place = Place(dev_ref, len_ref, mov_ref)
    slot = pl.program_id(0)
    living = place.alive(slot)
    wide = PER_GROUP * LANES

    @pl.when(living)
    def _():
        own = feat_ref[0].astype(f32)
        fill_ext(ext, low_ref[0], own, high_ref[0])
        fill_windows(windows, ext, 0)
        fill_back(turned, place, slot, cot_ref, recv_ref)
        back = turned[...].T
        group = jnp.zeros((SPAN, wide), f32)
        for g in range(GROUPS):
            at = g * NEAR * PER_GROUP
            group += nn(windows[at : at + SPAN, :], weight[:, g * wide : (g + 1) * wide])
        mixed = gathered(group)
        below = phi(mixed)
        mask = place.mask(slot)
        states = jnp.where(mask, own + mixed * below, 0.0)
        states_ref[0] = states.T[:GC, :].astype(bf16)
        slopes = jnp.where(mask, back * (below + mixed * bell(mixed)), 0.0)
        slopes_ref[0] = slopes.astype(bf16)
        edge = jnp.where(place.x < X // 2, low_ref[0].astype(f32), high_ref[0].astype(f32))
        piece_ref[0, :T, :] = slopes.astype(bf16)
        piece_ref[0, T:, :] = edge.astype(bf16)

    @pl.when(jnp.logical_not(living))
    def _():
        states_ref[...] = jnp.zeros_like(states_ref)
        slopes_ref[...] = jnp.zeros_like(slopes_ref)
        piece_ref[...] = jnp.zeros_like(piece_ref)

    tail_ref[0] = slopes_ref[0, T - REACH :, :]
    head_ref[0] = slopes_ref[0, :REACH, :]

    @pl.when(place.chosen == slot)
    def _():
        sent_ref[...] = states_ref[0]


def mix(place, features, low, high, weight, cotangent, received):
    return pl.pallas_call(
        mix_body,
        grid=(SLOTS,),
        out_shape=(
            jax.ShapeDtypeStruct((SLOTS, GC, T), bf16),
            jax.ShapeDtypeStruct((GC, T), bf16),
            jax.ShapeDtypeStruct((SLOTS, T, LANES), bf16),
            jax.ShapeDtypeStruct((SLOTS, REACH, LANES), bf16),
            jax.ShapeDtypeStruct((SLOTS, REACH, LANES), bf16),
            jax.ShapeDtypeStruct((SLOTS, PIECE, LANES), bf16),
        ),
        in_specs=[SMEM] * 3
        + [
            by_slot(T, LANES),
            by_slot(REACH, LANES),
            by_slot(REACH, LANES),
            once(*weight.shape),
            by_slot(GC, T),
            by_slot(GC, T),
        ],
        out_specs=(
            by_slot(GC, T),
            whole(GC, T),
            by_slot(T, LANES),
            by_slot(REACH, LANES),
            by_slot(REACH, LANES),
            by_slot(PIECE, LANES),
        ),
        scratch_shapes=[
            pltpu.VMEM((EXT, LANES), f32),
            pltpu.VMEM((T + NEAR * (K // NEAR - 1), NEAR * LANES), bf16),
            pltpu.VMEM((LANES, T), f32),
        ],
        compiler_params=params(20),
        cost_estimate=cost(2 * SLOTS * SPAN * K * LANES * LANES, 7 << 20, SLOTS * T * LANES * 2),
        name="mix",
    )(*place, features, low, high, weight, cotangent, received)


def taps_body(scale, dev_ref, len_ref, mov_ref, *refs):
    feat_refs, piece_refs, (keep_ref, send_ref) = refs[:X], refs[X : 2 * X], refs[2 * X : 2 * X + 2]
    ext, windows, turned, sums = refs[2 * X + 2 :]
    place = Place(dev_ref, len_ref, mov_ref)
    slot = pl.program_id(0)
    spread = X * T
    rows = spread + NEAR * (K // NEAR - 1)

    @pl.when(slot == 0)
    def _():
        sums[...] = jnp.zeros_like(sums)

    @pl.when(place.y * spread < place.length(slot))
    def _():
        for step, (feat_ref, piece_ref) in enumerate(zip(feat_refs, piece_refs)):
            x = lax.rem(place.x + (X - step), X)
            at = pl.multiple_of(x * T, T)
            ext[pl.ds(REACH + at, T), :] = feat_ref[0].astype(f32)
            turned[:, pl.ds(at, T)] = piece_ref[0, :T, :].astype(f32).T.astype(bf16)

            @pl.when(x == 0)
            def _():
                ext[:REACH, :] = piece_ref[0, T:, :].astype(f32)

            @pl.when(x == X - 1)
            def _():
                ext[REACH + spread :, :] = piece_ref[0, T:, :].astype(f32)

        for j in range(4):
            windows[:, j * LANES : (j + 1) * LANES] = ext[
                pl.ds(place.x + 4 * j, rows), :
            ].astype(bf16)
        for q in range(K // NEAR):
            sums[q] += nn(turned[...], windows[q * NEAR : q * NEAR + spread, :])

    @pl.when(slot == SLOTS - 1)
    def _():
        first_core = place.core == 0
        for q in range(K // NEAR):
            for far in range(2):
                at = 2 * far * LANES
                even = sums[q, :, at : at + LANES] * scale
                odd = sums[q, :, at + LANES : at + 2 * LANES] * scale
                keep = jnp.where(first_core, even, odd)
                send = jnp.where(first_core, odd, even)
                for y in range(2):
                    rows = slice(y * HALF, y * HALF + REACH)
                    keep_ref[y, 2 * q + far] = keep[rows, :].astype(bf16)
                    send_ref[y, 2 * q + far] = send[rows, :].astype(bf16)


def taps(scale, place, features, pieces):
    shape = jax.ShapeDtypeStruct((2, CELLS, REACH, LANES), bf16)
    spread = X * T
    return pl.pallas_call(
        functools.partial(taps_body, scale),
        grid=(SLOTS,),
        out_shape=(shape,) * 2,
        in_specs=[SMEM] * 3 + [by_slot(T, LANES)] * X + [by_slot(PIECE, LANES)] * X,
        out_specs=(whole(*shape.shape),) * 2,
        scratch_shapes=[
            pltpu.VMEM((spread + 2 * REACH, LANES), f32),
            pltpu.VMEM((spread + NEAR * (K // NEAR - 1), 4 * LANES), bf16),
            pltpu.VMEM((LANES, spread), bf16),
            pltpu.VMEM((K // NEAR, LANES, 4 * LANES), f32),
        ],
        compiler_params=params(16),
        cost_estimate=cost(2 * SLOTS * SPAN * K * LANES * LANES, 4 << 20),
        name="taps",
    )(*place, *features, *pieces)


def backward_body(
    scale,
    dev_ref,
    len_ref,
    mov_ref,
    slopes_ref,
    low_ref,
    high_ref,
    cot_ref,
    recv_ref,
    weight,
    pair_ref,
    q_ref,
    slope_ref,
    m_ref,
    inv_ref,
    conv_ref,
    chan_ref,
    proj_ref,
    audio_grad_ref,
    keep_ref,
    send_ref,
    ext,
    windows,
    turned,
    proj,
    feat_grad,
    normed,
    mid,
    wide,
    conv_sum,
    proj_sum,
    chan_sum,
    columns,
):
    place = Place(dev_ref, len_ref, mov_ref)
    slot = pl.program_id(0)
    living = place.alive(slot)
    span = PER_GROUP * LANES

    @pl.when(slot == 0)
    def _():
        proj[...] = jnp.zeros_like(proj)
        proj[:GC, :] = proj_ref[...]
        conv_sum[...] = jnp.zeros_like(conv_sum)
        proj_sum[...] = jnp.zeros_like(proj_sum)
        chan_sum[...] = jnp.zeros_like(chan_sum)

    @pl.when(living)
    def _():
        fill_ext(ext, low_ref[0], slopes_ref[0], high_ref[0])
        fill_windows(windows, ext, 1)
        fill_back(turned, place, slot, cot_ref, recv_ref)
        group = jnp.zeros((SPAN, span), f32)
        for g in range(GROUPS):
            at = g * NEAR * PER_GROUP
            group += nt(windows[at : at + SPAN, :], weight[g * span : (g + 1) * span, :])
        spread = gathered(group)
        feat_grad[...] = jnp.where(place.mask(slot), turned[...].T + spread, 0.0).astype(bf16)
        gain = chan_ref[1:2, :]
        gain_two, shift_two = chan_ref[3:4, :], chan_ref[4:5, :]
        mid[...] = nn(feat_grad[...], proj[...])
        for at in range(0, T, CHUNK):
            rows = slice(at, at + CHUNK)
            m = m_ref[0, rows, :].astype(f32)
            normed[rows, :] = (m * gain_two + shift_two).astype(bf16)
            normed_grad = mid[rows, :]
            chan_sum[24:32, :] += jnp.sum((normed_grad * m).reshape(-1, 8, C), axis=0)
            chan_sum[32:40, :] += jnp.sum(normed_grad.reshape(-1, 8, C), axis=0)
            scaled = normed_grad * gain_two
            first = jnp.mean(scaled, axis=-1, keepdims=True)
            second = jnp.mean(scaled * m, axis=-1, keepdims=True)
            inverse_two = inv_ref[0, rows, LANES // 2 : LANES // 2 + 1]
            pre_grad = inverse_two * (scaled - first - m * second) * slope_ref[
                0, rows, :
            ].astype(f32)
            q = q_ref[0, rows, :].astype(f32)
            chan_sum[8:16, :] += jnp.sum((pre_grad * q).reshape(-1, 8, C), axis=0)
            chan_sum[16:24, :] += jnp.sum(pre_grad.reshape(-1, 8, C), axis=0)
            scaled = pre_grad * gain
            first = jnp.mean(scaled, axis=-1, keepdims=True)
            second = jnp.mean(scaled * q, axis=-1, keepdims=True)
            inverse = inv_ref[0, rows, 0:1]
            conv_grad = inverse * (scaled - first - q * second)
            chan_sum[0:8, :] += jnp.sum(conv_grad.reshape(-1, 8, C), axis=0)
            mid[rows, :] = conv_grad
        operand = mid[...].astype(bf16)
        for tap in range(2):
            rows = slice(tap * C, (tap + 1) * C)
            audio_grad = nt(operand, conv_ref[rows, :])
            for c in range(C // LANES):
                wide[c, pl.ds(tap, T, stride=2), :] = audio_grad[:, c * LANES : (c + 1) * LANES]
            conv_sum[rows, :] += tn(pair_ref[0, :, rows], operand)
        for c in range(C // LANES):
            audio_grad_ref[0, :, c * LANES : (c + 1) * LANES] = wide[c].astype(bf16)
        proj_sum[...] += tn(normed[...], feat_grad[...])

    @pl.when(jnp.logical_not(living))
    def _():
        audio_grad_ref[...] = jnp.zeros_like(audio_grad_ref)

    @pl.when(slot == SLOTS - 1)
    def _():
        first_core = place.core == 0
        columns[...] = jnp.zeros_like(columns)
        for n in range(5):
            columns[GC + n : GC + n + 1, :] = jnp.sum(
                chan_sum[8 * n : 8 * n + 8, :], axis=0, keepdims=True
            )
        proj_sum[...] += columns[...].T
        for x in range(X):
            lanes = slice(x * LANES, (x + 1) * LANES)
            for cell in range(CELLS):
                at = 2 * cell * 32
                even = conv_sum[at : at + 32, lanes]
                odd = conv_sum[at + 32 : at + 64, lanes]
                rows = slice(cell * 32, (cell + 1) * 32)
                keep_ref[x, rows, :] = (jnp.where(first_core, even, odd) * scale).astype(bf16)
                send_ref[x, rows, :] = (jnp.where(first_core, odd, even) * scale).astype(bf16)
            for four in range(CELLS // 4):
                even, odd = [
                    jnp.concatenate(
                        [
                            proj_sum[at : at + SPARE, :]
                            for at in (
                                (2 * cell + odd) * 16 + x * SPARE
                                for cell in range(4 * four, 4 * four + 4)
                            )
                        ],
                        axis=0,
                    )
                    for odd in range(2)
                ]
                rows = slice(CONV_ROWS + four * 16, CONV_ROWS + (four + 1) * 16)
                keep_ref[x, rows, :] = (jnp.where(first_core, even, odd) * scale).astype(bf16)
                send_ref[x, rows, :] = (jnp.where(first_core, odd, even) * scale).astype(bf16)


def backward(
    scale, place, slopes, low, high, cotangent, received, weight, stored, conv_weight, channels, proj
):
    shape = jax.ShapeDtypeStruct((X, REST, LANES), bf16)
    return pl.pallas_call(
        functools.partial(backward_body, scale),
        grid=(SLOTS,),
        out_shape=(jax.ShapeDtypeStruct((SLOTS, 2 * T, C), bf16), shape, shape),
        in_specs=[SMEM] * 3
        + [
            by_slot(T, LANES),
            by_slot(REACH, LANES),
            by_slot(REACH, LANES),
            by_slot(GC, T),
            by_slot(GC, T),
            once(*weight.shape),
            by_slot(T, 2 * C),
            by_slot(T, C),
            by_slot(T, C),
            by_slot(T, C),
            by_slot(T, LANES),
            once(2 * C, C),
            whole(5, C),
            whole(GC, C),
        ],
        out_specs=(by_slot(2 * T, C), whole(*shape.shape), whole(*shape.shape)),
        scratch_shapes=[
            pltpu.VMEM((EXT, LANES), f32),
            pltpu.VMEM((T + NEAR * (K // NEAR - 1), NEAR * LANES), bf16),
            pltpu.VMEM((LANES, T), f32),
            pltpu.VMEM((LANES, C), bf16),
            pltpu.VMEM((T, LANES), bf16),
            pltpu.VMEM((T, C), bf16),
            pltpu.VMEM((T, C), f32),
            pltpu.VMEM((C // LANES, 2 * T, LANES), f32),
            pltpu.VMEM((2 * C, C), f32),
            pltpu.VMEM((C, LANES), f32),
            pltpu.VMEM((40, C), f32),
            pltpu.VMEM((LANES, C), f32),
        ],
        compiler_params=params(30),
        cost_estimate=cost(
            2 * SLOTS * (SPAN * K * LANES * LANES + T * C * (4 * C + 2 * LANES)), 14 << 20
        ),
        name="backward",
    )(
        *place,
        slopes,
        low,
        high,
        cotangent,
        received,
        weight,
        *stored,
        conv_weight,
        channels,
        proj,
    )


def halve_body(dev_ref, keep_ref, recv_ref, stay_ref, leave_ref):
    y = lax.rem(dev_ref[0], MP) // X
    for out_ref, at in ((stay_ref, y), (leave_ref, 1 - y)):
        out_ref[...] = (keep_ref[at].astype(f32) + recv_ref[at].astype(f32)).astype(bf16)


def halve(dev, keep, received):
    shape = jax.ShapeDtypeStruct(keep.shape[1:], bf16)
    return pl.pallas_call(
        halve_body,
        out_shape=(shape,) * 2,
        in_specs=[SMEM] + [VMEM] * 2,
        out_specs=(VMEM,) * 2,
        compiler_params=params(8),
        cost_estimate=cost(0, 2 << 20),
        name="halve",
    )(dev, keep, received)


def join_body(dev_ref, keep_ref, recv_ref, *out_refs):
    x = lax.rem(dev_ref[0], X)
    for step, out_ref in enumerate(out_refs):
        at = lax.rem(x + step, X)
        out_ref[...] = (keep_ref[at].astype(f32) + recv_ref[at].astype(f32)).astype(bf16)


def join(dev, keep, received):
    shape = jax.ShapeDtypeStruct((REST, LANES), bf16)
    return pl.pallas_call(
        join_body,
        out_shape=(shape,) * X,
        in_specs=[SMEM] + [VMEM] * 2,
        out_specs=(VMEM,) * X,
        compiler_params=params(8),
        cost_estimate=cost(0, 2 << 20),
        name="join",
    )(dev, keep, received)


def cells_body(*refs):
    pos_refs, rest_refs, out_ref, rows = refs[:2], refs[2:6], refs[6], refs[7]

    def summed(parts, *at):
        result = parts[0][at].astype(f32)
        for part in parts[1:]:
            result += part[at].astype(f32)
        return result

    for four in range(CELLS // 4):
        at = CONV_ROWS + four * 16
        small = summed(rest_refs, slice(at, at + 16), slice(None))
        for n in range(4):
            cell = 4 * four + n
            rows[...] = summed(pos_refs, cell)
            rows[HALF:, :] = small[n * SPARE : (n + 1) * SPARE, :]
            out_ref[cell, :REACH, :] = rows[...].astype(bf16)
            conv = summed(rest_refs, slice(cell * 32, cell * 32 + 32), slice(None))
            out_ref[cell, REACH:, :] = conv.astype(bf16)


def make_cells(pos_parts, rest_parts):
    return pl.pallas_call(
        cells_body,
        out_shape=jax.ShapeDtypeStruct((CELLS, REACH + 32, LANES), bf16),
        in_specs=[VMEM] * 6,
        out_specs=VMEM,
        scratch_shapes=[pltpu.VMEM((REACH, LANES), f32)],
        compiler_params=params(8),
        cost_estimate=cost(0, 2 << 20),
        name="cells",
    )(*pos_parts, *rest_parts)


def total_body(in_ref, out_ref):
    total = in_ref[0].astype(f32)
    for n in range(1, in_ref.shape[0]):
        total += in_ref[n].astype(f32)
    for copy in range(MP):
        out_ref[copy] = total.astype(bf16)


def total(parts):
    return pl.pallas_call(
        total_body,
        out_shape=jax.ShapeDtypeStruct((MP,) + parts.shape[1:], bf16),
        in_specs=[VMEM],
        out_specs=VMEM,
        compiler_params=params(10),
        cost_estimate=cost(0, 2 * parts.size),
        name="total",
    )(parts)


def finish_body(
    dev_ref,
    len_ref,
    mov_ref,
    in_ref,
    states_ref,
    other_ref,
    hidden_ref,
    pos_ref,
    conv_ref,
    proj_ref,
    chan_ref,
):
    place = Place(dev_ref, len_ref, mov_ref)
    for slot in range(SLOTS):
        hidden_ref[slot] = jnp.where(
            place.chosen == slot, other_ref[...].astype(f32), states_ref[slot].astype(f32)
        ).astype(bf16)
    small = []
    for x in range(X):
        low, high = in_ref[x].astype(f32), in_ref[X + x].astype(f32)
        block = jnp.concatenate(
            [low[:HALF, :], high[:HALF, :], jnp.zeros((LANES - GC, LANES), f32)], axis=0
        ).T
        pos_ref[x] = block[:GC, :GC]
        both = low[HALF:, :] + high[HALF:, :]
        small.append(both[:SPARE, :])
        conv_ref[:, x * LANES : (x + 1) * LANES] = both[SPARE:, :]
    small = jnp.concatenate(small, axis=0)
    proj_ref[...] = small[:, :GC]
    chan_ref[...] = jnp.concatenate([small] * 8, axis=0).T[GC : GC + 5, :16]


def finish(place, cells, states, other):
    return pl.pallas_call(
        finish_body,
        out_shape=(
            jax.ShapeDtypeStruct((SLOTS, GC, T), bf16),
            jax.ShapeDtypeStruct((4, GC, GC), f32),
            jax.ShapeDtypeStruct((32, C), f32),
            jax.ShapeDtypeStruct((16, GC), f32),
            jax.ShapeDtypeStruct((5, 16), f32),
        ),
        in_specs=[SMEM] * 3 + [VMEM] * 3,
        out_specs=(VMEM,) * 5,
        compiler_params=params(8),
        name="finish",
    )(*place, cells, states, other)


def neighbours(tail, head):
    forward = [(i, i + 1) for i in range(MP - 1)]
    backward_route = [(i + 1, i) for i in range(MP - 1)]
    return lax.ppermute(tail, "mp", forward), lax.ppermute(head, "mp", backward_route)


def along_x(block, step):
    route = [(X * y + x, X * y + (x + step) % X) for y in range(2) for x in range(X)]
    return lax.ppermute(block, "mp", route)


def around_x(block):
    far = along_x(block, 2)
    return (block, along_x(block, 1), far, along_x(block, 3))


def per_device(
    audio, lengths, moved_slots, conv_weight, channel_params, proj_weight, pos_weight, cotangent
):
    data_index = lax.axis_index("dp")
    model_index = lax.axis_index("mp")
    scale = (SLOTS * DP * T * MP) ** -0.5
    dev = (data_index * MP + model_index).astype(jnp.int32).reshape(1)
    place = (dev, lengths, moved_slots.reshape(-1))
    swap = [(i, i ^ (DP // 2)) for i in range(DP)]
    core_swap = [(i, i ^ 1) for i in range(DP)]
    channels = channel_params.T
    proj = proj_weight.T
    cot = cotangent.transpose(0, 2, 1)

    received = lax.ppermute(cot, "dp", swap)
    features, tail, head, *stored = encode(place, audio, conv_weight, channels, proj)
    low, high = neighbours(tail, head)
    all_features = around_x(features)
    ahead, behind = turn(pos_weight.transpose(1, 2, 0))
    states, sent, slopes, tail, head, piece = mix(
        place, features, low, high, ahead, cot, received
    )
    low, high = neighbours(tail, head)
    piece, low, high, all_features = lax.optimization_barrier(
        (piece, low, high, all_features)
    )
    pieces = around_x(piece)
    audio_grad, keep, send = backward(
        scale,
        place,
        slopes,
        low,
        high,
        cot,
        received,
        behind,
        stored,
        conv_weight,
        channels,
        proj,
    )
    send, pieces, sent = lax.optimization_barrier((send, pieces, sent))
    chunks = join(dev, keep, lax.ppermute(send, "dp", core_swap))
    chunks, pieces = lax.optimization_barrier((chunks, pieces))
    rest_parts = [chunks[0]] + [along_x(chunks[step], step) for step in (2, 1, 3)]
    pos_keep, pos_send = taps(scale, place, all_features, pieces)
    stay, leave = halve(dev, pos_keep, lax.ppermute(pos_send, "dp", core_swap))
    pos_parts = (stay, lax.ppermute(leave, "mp", [(i, i ^ X) for i in range(MP)]))
    other = lax.ppermute(sent, "dp", swap)
    rest_parts, other = lax.optimization_barrier((rest_parts, other))
    cells = make_cells(pos_parts, rest_parts)
    groups = [list(range(bit, DP, 2)) for bit in range(2)]
    cells = lax.all_to_all(cells, "dp", 0, 0, axis_index_groups=groups, tiled=True)
    cells = lax.all_to_all(total(cells), "mp", 0, 0, tiled=True)
    hidden, grad_pos, grad_conv, grad_proj, grad_channels = finish(place, cells, states, other)
    return (
        hidden.transpose(0, 2, 1),
        audio_grad,
        grad_pos,
        grad_conv,
        grad_proj,
        grad_channels.T,
    )


def solution(mesh):
    return jax.shard_map(
        per_device,
        mesh=mesh,
        in_specs=(P("dp", "mp", None), P(), P(), P(), P(), P(), P(), P("dp", "mp", None)),
        out_specs=(
            P("dp", "mp", None),
            P("dp", "mp", None),
            P("dp", None, None),
            P("dp", None),
            P("dp", None),
            P("dp", None),
        ),
        check_vma=False,
    )
```

```python
import functools

import jax
import jax.numpy as jnp
from jax import lax
from jax.experimental import pallas as pl
from jax.experimental.pallas import tpu as pltpu
from jax.sharding import PartitionSpec as P

epsilon = 1e-05
root_half = 0.7071067811865476
density = 0.3989422804014327

SLOTS = 2
T = 256
C = 512
GC = 120
LANES = 128
K = 128
REACH = 64
EXT = T + 2 * REACH
NEAR = 16
GROUPS = 2
PER_GROUP = 4
SPAN = T + NEAR * (PER_GROUP - 1)
CHUNK = 32
MP = 8
DP = 32
X = 4
CELLS = 16
PIECE = T + REACH
HALF = GC // 2
SPARE = REACH - HALF
CONV_ROWS = CELLS * 32
REST = CONV_ROWS + CELLS * SPARE

f32 = jnp.float32
bf16 = jnp.bfloat16

VMEM = pl.BlockSpec(memory_space=pltpu.VMEM)
SMEM = pl.BlockSpec(memory_space=pltpu.SMEM)
HBM = pl.BlockSpec(memory_space=pltpu.HBM)


def params(mebibytes):
    return pltpu.CompilerParams(vmem_limit_bytes=mebibytes << 20)


def cost(flops, moved, trans=0):
    return pl.CostEstimate(flops=flops, bytes_accessed=moved, transcendentals=trans)


def phi(values):
    return 0.5 * (1.0 + lax.erf(values * root_half))


def bell(values):
    return jnp.exp(-0.5 * values * values) * density


def nt(a, b):
    return lax.dot_general(a, b, (((1,), (1,)), ((), ())), preferred_element_type=f32)


def tn(a, b):
    return lax.dot_general(a, b, (((0,), (0,)), ((), ())), preferred_element_type=f32)


def nn(a, b):
    return jnp.dot(a, b, preferred_element_type=f32)


class Place:
    def __init__(self, dev_ref, len_ref, mov_ref=None):
        self.data = dev_ref[0] // MP
        self.model = lax.rem(dev_ref[0], MP)
        self.x = lax.rem(self.model, X)
        self.y = self.model // X
        self.core = lax.rem(self.data, 2)
        self.cell = self.data // 2
        self.first = self.model * T
        self.lengths = len_ref
        if mov_ref is not None:
            self.chosen = mov_ref[lax.rem(self.data, DP // 2)]

    def length(self, slot):
        return self.lengths[self.data * SLOTS + slot]

    def alive(self, slot):
        return self.first < self.length(slot)

    def mask(self, slot):
        ids = self.first + lax.broadcasted_iota(jnp.int32, (T, 1), 0)
        return ids < self.length(slot)


def by_slot(*dims):
    return pl.BlockSpec((1,) + dims, lambda s: (s,) + (0,) * len(dims))


def whole(*dims):
    return pl.BlockSpec(dims, lambda s: (0,) * len(dims))


def once(*dims):
    return pl.BlockSpec(dims, lambda s: (0,) * len(dims), pipeline_mode=pl.Buffered(1))


def turn_body(in_ref, ahead_ref, behind_ref, rows):
    block = pl.program_id(0)
    blocks = pl.num_programs(0)
    for n in range(NEAR):
        tile = jnp.concatenate(
            [in_ref[n].astype(f32), jnp.zeros((LANES - GC, K), f32)], axis=0
        ).T
        if n >= GC % NEAR:
            tile = jnp.where(block == blocks - 1, 0.0, tile)
        rows[pl.ds(n, K, stride=NEAR), :] = tile
    far = K // NEAR
    for q in range(far):
        for r in range(NEAR):
            at = (q * NEAR + r) * NEAR
            tile = rows[at : at + NEAR, :].astype(bf16)
            ahead_ref[r, :, q * LANES : (q + 1) * LANES] = tile
            r_back = NEAR - 1 - r
            behind_ref[far - 1 - q, :, r_back * LANES : (r_back + 1) * LANES] = tile


def turn(pos):
    far = K // NEAR
    ahead, behind = pl.pallas_call(
        turn_body,
        grid=(LANES // NEAR,),
        out_shape=(
            jax.ShapeDtypeStruct((NEAR, LANES, far * LANES), bf16),
            jax.ShapeDtypeStruct((far, LANES, NEAR * LANES), bf16),
        ),
        in_specs=[pl.BlockSpec((NEAR, GC, K), lambda b: (b, 0, 0))],
        out_specs=(
            pl.BlockSpec((NEAR, NEAR, far * LANES), lambda b: (0, b, 0)),
            pl.BlockSpec((far, NEAR, NEAR * LANES), lambda b: (0, b, 0)),
        ),
        scratch_shapes=[pltpu.VMEM((K * NEAR, LANES), f32)],
        compiler_params=params(16),
        cost_estimate=cost(0, 12 << 20),
        name="turn",
    )(pos)
    return ahead.reshape(NEAR * LANES, -1), behind.reshape(far * LANES, -1)


def encode_body(
    dev_ref,
    len_hbm,
    audio_hbm,
    conv_hbm,
    chan_hbm,
    proj_hbm,
    feat_ref,
    tail_ref,
    head_ref,
    pair_ref,
    q_ref,
    slope_ref,
    m_ref,
    inv_ref,
    wide,
    proj,
    mid,
    normed,
    len_ref,
    audio_ref,
    conv_ref,
    chan_ref,
    sems,
):
    slot = pl.program_id(0)
    copies = [
        pltpu.make_async_copy(source, target, sems.at[n])
        for n, (source, target) in enumerate(
            (
                (len_hbm, len_ref),
                (audio_hbm.at[0], audio_ref.at[0]),
                (conv_hbm, conv_ref),
                (chan_hbm, chan_ref),
                (proj_hbm, proj.at[pl.ds(0, GC)]),
                (audio_hbm.at[1], audio_ref.at[1]),
            )
        )
    ]

    @pl.when(slot == 0)
    def _():
        proj[GC - 8 :, :] = jnp.zeros((LANES - GC + 8, C), bf16)
        for copy in copies:
            copy.start()
        for copy in copies[:-1]:
            copy.wait()

    @pl.when(slot == SLOTS - 1)
    def _():
        copies[-1].wait()

    place = Place(dev_ref, len_ref)
    living = place.alive(slot)

    @pl.when(living)
    def _():
        for c in range(C // LANES):
            wide[c] = audio_ref[slot, :, c * LANES : (c + 1) * LANES].astype(f32)
            for tap in range(2):
                at = tap * C + c * LANES
                pair_ref[0, :, at : at + LANES] = wide[c, pl.ds(tap, T, stride=2), :].astype(bf16)
        mid[...] = nn(pair_ref[0], conv_ref[...])
        bias, gain, shift = chan_ref[0:1, :], chan_ref[1:2, :], chan_ref[2:3, :]
        gain_two, shift_two = chan_ref[3:4, :], chan_ref[4:5, :]
        for at in range(0, T, CHUNK):
            rows = slice(at, at + CHUNK)
            conv = mid[rows, :] + bias
            offset = conv - jnp.mean(conv, axis=-1, keepdims=True)
            inverse = lax.rsqrt(jnp.mean(offset * offset, axis=-1, keepdims=True) + epsilon)
            q = offset * inverse
            pre = q * gain + shift
            below = phi(pre)
            encoded = (pre * below).astype(bf16).astype(f32)
            slope_ref[0, rows, :] = (below + pre * bell(pre)).astype(bf16)
            q_ref[0, rows, :] = q.astype(bf16)
            offset = encoded - jnp.mean(encoded, axis=-1, keepdims=True)
            inverse_two = lax.rsqrt(jnp.mean(offset * offset, axis=-1, keepdims=True) + epsilon)
            m = offset * inverse_two
            m_ref[0, rows, :] = m.astype(bf16)
            inv_ref[0, rows, :] = jnp.concatenate(
                [
                    jnp.broadcast_to(inverse, (CHUNK, LANES // 2)),
                    jnp.broadcast_to(inverse_two, (CHUNK, LANES // 2)),
                ],
                axis=1,
            )
            normed[rows, :] = (m * gain_two + shift_two).astype(bf16)
        projected = nt(normed[...], proj[...])
        feat_ref[0] = jnp.where(place.mask(slot), projected, 0.0).astype(bf16)

    @pl.when(jnp.logical_not(living))
    def _():
        feat_ref[...] = jnp.zeros_like(feat_ref)

    tail_ref[0] = feat_ref[0, T - REACH :, :]
    head_ref[0] = feat_ref[0, :REACH, :]


def encode(place, audio, conv_weight, channels, proj):
    return pl.pallas_call(
        encode_body,
        grid=(SLOTS,),
        out_shape=(
            jax.ShapeDtypeStruct((SLOTS, T, LANES), bf16),
            jax.ShapeDtypeStruct((SLOTS, REACH, LANES), bf16),
            jax.ShapeDtypeStruct((SLOTS, REACH, LANES), bf16),
            jax.ShapeDtypeStruct((SLOTS, T, 2 * C), bf16),
            jax.ShapeDtypeStruct((SLOTS, T, C), bf16),
            jax.ShapeDtypeStruct((SLOTS, T, C), bf16),
            jax.ShapeDtypeStruct((SLOTS, T, C), bf16),
            jax.ShapeDtypeStruct((SLOTS, T, LANES), f32),
        ),
        in_specs=[SMEM] + [HBM] * 5,
        out_specs=(
            by_slot(T, LANES),
            by_slot(REACH, LANES),
            by_slot(REACH, LANES),
            by_slot(T, 2 * C),
            by_slot(T, C),
            by_slot(T, C),
            by_slot(T, C),
            by_slot(T, LANES),
        ),
        scratch_shapes=[
            pltpu.VMEM((C // LANES, 2 * T, LANES), f32),
            pltpu.VMEM((LANES, C), bf16),
            pltpu.VMEM((T, C), f32),
            pltpu.VMEM((T, C), bf16),
            pltpu.SMEM((DP * SLOTS,), jnp.int32),
            pltpu.VMEM((SLOTS, 2 * T, C), bf16),
            pltpu.VMEM((2 * C, C), bf16),
            pltpu.VMEM((5, C), f32),
            pltpu.SemaphoreType.DMA((6,)),
        ],
        compiler_params=params(50),
        cost_estimate=cost(2 * SLOTS * T * C * (2 * C + LANES), 8 << 20, SLOTS * T * C * 2),
        name="encode",
    )(*place[:2], audio, conv_weight, channels, proj)


def fill_ext(ext, low, own, high):
    ext[:REACH, :] = low.astype(f32)
    ext[REACH : REACH + T, :] = own.astype(f32)
    ext[REACH + T :, :] = high.astype(f32)


def fill_windows(windows, ext, first):
    rows = T + NEAR * (K // NEAR - 1)
    for r in range(NEAR):
        windows[:, r * LANES : (r + 1) * LANES] = ext[first + r : first + r + rows, :].astype(bf16)


def gathered(group):
    total = group[:T, :LANES]
    for p in range(1, PER_GROUP):
        total += group[NEAR * p : NEAR * p + T, p * LANES : (p + 1) * LANES]
    return total


def fill_back(turned, place, slot, cot_ref, recv_ref):
    turned[GC:, :] = jnp.zeros((LANES - GC, T), f32)
    turned[:GC, :] = jnp.where(
        place.chosen == slot, recv_ref[0].astype(f32), cot_ref[0].astype(f32)
    )


def mix_body(
    dev_ref,
    len_ref,
    mov_ref,
    feat_ref,
    low_ref,
    high_ref,
    weight,
    cot_ref,
    recv_ref,
    states_ref,
    sent_ref,
    slopes_ref,
    tail_ref,
    head_ref,
    piece_ref,
    ext,
    windows,
    turned,
):
    place = Place(dev_ref, len_ref, mov_ref)
    slot = pl.program_id(0)
    living = place.alive(slot)
    wide = PER_GROUP * LANES

    @pl.when(living)
    def _():
        own = feat_ref[0].astype(f32)
        fill_ext(ext, low_ref[0], own, high_ref[0])
        fill_windows(windows, ext, 0)
        fill_back(turned, place, slot, cot_ref, recv_ref)
        back = turned[...].T
        group = jnp.zeros((SPAN, wide), f32)
        for g in range(GROUPS):
            at = g * NEAR * PER_GROUP
            group += nn(windows[at : at + SPAN, :], weight[:, g * wide : (g + 1) * wide])
        mixed = gathered(group)
        below = phi(mixed)
        mask = place.mask(slot)
        states = jnp.where(mask, own + mixed * below, 0.0)
        states_ref[0] = states.T[:GC, :].astype(bf16)
        slopes = jnp.where(mask, back * (below + mixed * bell(mixed)), 0.0)
        slopes_ref[0] = slopes.astype(bf16)
        edge = jnp.where(place.x < X // 2, low_ref[0].astype(f32), high_ref[0].astype(f32))
        piece_ref[0, :T, :] = slopes.astype(bf16)
        piece_ref[0, T:, :] = edge.astype(bf16)

    @pl.when(jnp.logical_not(living))
    def _():
        states_ref[...] = jnp.zeros_like(states_ref)
        slopes_ref[...] = jnp.zeros_like(slopes_ref)
        piece_ref[...] = jnp.zeros_like(piece_ref)

    tail_ref[0] = slopes_ref[0, T - REACH :, :]
    head_ref[0] = slopes_ref[0, :REACH, :]

    @pl.when(place.chosen == slot)
    def _():
        sent_ref[...] = states_ref[0]


def mix(place, features, low, high, weight, cotangent, received):
    return pl.pallas_call(
        mix_body,
        grid=(SLOTS,),
        out_shape=(
            jax.ShapeDtypeStruct((SLOTS, GC, T), bf16),
            jax.ShapeDtypeStruct((GC, T), bf16),
            jax.ShapeDtypeStruct((SLOTS, T, LANES), bf16),
            jax.ShapeDtypeStruct((SLOTS, REACH, LANES), bf16),
            jax.ShapeDtypeStruct((SLOTS, REACH, LANES), bf16),
            jax.ShapeDtypeStruct((SLOTS, PIECE, LANES), bf16),
        ),
        in_specs=[SMEM] * 3
        + [
            by_slot(T, LANES),
            by_slot(REACH, LANES),
            by_slot(REACH, LANES),
            once(*weight.shape),
            by_slot(GC, T),
            by_slot(GC, T),
        ],
        out_specs=(
            by_slot(GC, T),
            whole(GC, T),
            by_slot(T, LANES),
            by_slot(REACH, LANES),
            by_slot(REACH, LANES),
            by_slot(PIECE, LANES),
        ),
        scratch_shapes=[
            pltpu.VMEM((EXT, LANES), f32),
            pltpu.VMEM((T + NEAR * (K // NEAR - 1), NEAR * LANES), bf16),
            pltpu.VMEM((LANES, T), f32),
        ],
        compiler_params=params(20),
        cost_estimate=cost(2 * SLOTS * SPAN * K * LANES * LANES, 7 << 20, SLOTS * T * LANES * 2),
        name="mix",
    )(*place, features, low, high, weight, cotangent, received)


def taps_body(scale, dev_ref, len_ref, mov_ref, *refs):
    feat_refs, piece_refs, (keep_ref, send_ref) = refs[:X], refs[X : 2 * X], refs[2 * X : 2 * X + 2]
    ext, windows, turned, sums = refs[2 * X + 2 :]
    place = Place(dev_ref, len_ref, mov_ref)
    slot = pl.program_id(0)
    spread = X * T
    rows = spread + NEAR * (K // NEAR - 1)

    @pl.when(slot == 0)
    def _():
        sums[...] = jnp.zeros_like(sums)

    @pl.when(place.y * spread < place.length(slot))
    def _():
        for step, (feat_ref, piece_ref) in enumerate(zip(feat_refs, piece_refs)):
            x = lax.rem(place.x + (X - step), X)
            at = pl.multiple_of(x * T, T)
            ext[pl.ds(REACH + at, T), :] = feat_ref[0].astype(f32)
            turned[:, pl.ds(at, T)] = piece_ref[0, :T, :].astype(f32).T.astype(bf16)

            @pl.when(x == 0)
            def _():
                ext[:REACH, :] = piece_ref[0, T:, :].astype(f32)

            @pl.when(x == X - 1)
            def _():
                ext[REACH + spread :, :] = piece_ref[0, T:, :].astype(f32)

        for j in range(4):
            windows[:, j * LANES : (j + 1) * LANES] = ext[
                pl.ds(place.x + 4 * j, rows), :
            ].astype(bf16)
        for q in range(K // NEAR):
            sums[q] += nn(turned[...], windows[q * NEAR : q * NEAR + spread, :])

    @pl.when(slot == SLOTS - 1)
    def _():
        first_core = place.core == 0
        for q in range(K // NEAR):
            for far in range(2):
                at = 2 * far * LANES
                even = sums[q, :, at : at + LANES] * scale
                odd = sums[q, :, at + LANES : at + 2 * LANES] * scale
                keep = jnp.where(first_core, even, odd)
                send = jnp.where(first_core, odd, even)
                for y in range(2):
                    rows = slice(y * HALF, y * HALF + REACH)
                    keep_ref[y, 2 * q + far] = keep[rows, :].astype(bf16)
                    send_ref[y, 2 * q + far] = send[rows, :].astype(bf16)


def taps(scale, place, features, pieces):
    shape = jax.ShapeDtypeStruct((2, CELLS, REACH, LANES), bf16)
    spread = X * T
    return pl.pallas_call(
        functools.partial(taps_body, scale),
        grid=(SLOTS,),
        out_shape=(shape,) * 2,
        in_specs=[SMEM] * 3 + [by_slot(T, LANES)] * X + [by_slot(PIECE, LANES)] * X,
        out_specs=(whole(*shape.shape),) * 2,
        scratch_shapes=[
            pltpu.VMEM((spread + 2 * REACH, LANES), f32),
            pltpu.VMEM((spread + NEAR * (K // NEAR - 1), 4 * LANES), bf16),
            pltpu.VMEM((LANES, spread), bf16),
            pltpu.VMEM((K // NEAR, LANES, 4 * LANES), f32),
        ],
        compiler_params=params(16),
        cost_estimate=cost(2 * SLOTS * SPAN * K * LANES * LANES, 4 << 20),
        name="taps",
    )(*place, *features, *pieces)


def backward_body(
    scale,
    dev_ref,
    len_ref,
    mov_ref,
    slopes_ref,
    low_ref,
    high_ref,
    cot_ref,
    recv_ref,
    weight,
    pair_ref,
    q_ref,
    slope_ref,
    m_ref,
    inv_ref,
    conv_ref,
    chan_ref,
    proj_ref,
    audio_grad_ref,
    keep_ref,
    send_ref,
    ext,
    windows,
    turned,
    proj,
    feat_grad,
    normed,
    mid,
    wide,
    conv_sum,
    proj_sum,
    chan_sum,
    columns,
):
    place = Place(dev_ref, len_ref, mov_ref)
    slot = pl.program_id(0)
    living = place.alive(slot)
    span = PER_GROUP * LANES

    @pl.when(slot == 0)
    def _():
        proj[...] = jnp.zeros_like(proj)
        proj[:GC, :] = proj_ref[...]
        conv_sum[...] = jnp.zeros_like(conv_sum)
        proj_sum[...] = jnp.zeros_like(proj_sum)
        chan_sum[...] = jnp.zeros_like(chan_sum)

    @pl.when(living)
    def _():
        fill_ext(ext, low_ref[0], slopes_ref[0], high_ref[0])
        fill_windows(windows, ext, 1)
        fill_back(turned, place, slot, cot_ref, recv_ref)
        group = jnp.zeros((SPAN, span), f32)
        for g in range(GROUPS):
            at = g * NEAR * PER_GROUP
            group += nt(windows[at : at + SPAN, :], weight[g * span : (g + 1) * span, :])
        spread = gathered(group)
        feat_grad[...] = jnp.where(place.mask(slot), turned[...].T + spread, 0.0).astype(bf16)
        gain = chan_ref[1:2, :]
        gain_two, shift_two = chan_ref[3:4, :], chan_ref[4:5, :]
        mid[...] = nn(feat_grad[...], proj[...])
        for at in range(0, T, CHUNK):
            rows = slice(at, at + CHUNK)
            m = m_ref[0, rows, :].astype(f32)
            normed[rows, :] = (m * gain_two + shift_two).astype(bf16)
            normed_grad = mid[rows, :]
            chan_sum[24:32, :] += jnp.sum((normed_grad * m).reshape(-1, 8, C), axis=0)
            chan_sum[32:40, :] += jnp.sum(normed_grad.reshape(-1, 8, C), axis=0)
            scaled = normed_grad * gain_two
            first = jnp.mean(scaled, axis=-1, keepdims=True)
            second = jnp.mean(scaled * m, axis=-1, keepdims=True)
            inverse_two = inv_ref[0, rows, LANES // 2 : LANES // 2 + 1]
            pre_grad = inverse_two * (scaled - first - m * second) * slope_ref[
                0, rows, :
            ].astype(f32)
            q = q_ref[0, rows, :].astype(f32)
            chan_sum[8:16, :] += jnp.sum((pre_grad * q).reshape(-1, 8, C), axis=0)
            chan_sum[16:24, :] += jnp.sum(pre_grad.reshape(-1, 8, C), axis=0)
            scaled = pre_grad * gain
            first = jnp.mean(scaled, axis=-1, keepdims=True)
            second = jnp.mean(scaled * q, axis=-1, keepdims=True)
            inverse = inv_ref[0, rows, 0:1]
            conv_grad = inverse * (scaled - first - q * second)
            chan_sum[0:8, :] += jnp.sum(conv_grad.reshape(-1, 8, C), axis=0)
            mid[rows, :] = conv_grad
        operand = mid[...].astype(bf16)
        for tap in range(2):
            rows = slice(tap * C, (tap + 1) * C)
            audio_grad = nt(operand, conv_ref[rows, :])
            for c in range(C // LANES):
                wide[c, pl.ds(tap, T, stride=2), :] = audio_grad[:, c * LANES : (c + 1) * LANES]
            conv_sum[rows, :] += tn(pair_ref[0, :, rows], operand)
        for c in range(C // LANES):
            audio_grad_ref[0, :, c * LANES : (c + 1) * LANES] = wide[c].astype(bf16)
        proj_sum[...] += tn(normed[...], feat_grad[...])

    @pl.when(jnp.logical_not(living))
    def _():
        audio_grad_ref[...] = jnp.zeros_like(audio_grad_ref)

    @pl.when(slot == SLOTS - 1)
    def _():
        first_core = place.core == 0
        columns[...] = jnp.zeros_like(columns)
        for n in range(5):
            columns[GC + n : GC + n + 1, :] = jnp.sum(
                chan_sum[8 * n : 8 * n + 8, :], axis=0, keepdims=True
            )
        proj_sum[...] += columns[...].T
        for x in range(X):
            lanes = slice(x * LANES, (x + 1) * LANES)
            for cell in range(CELLS):
                at = 2 * cell * 32
                even = conv_sum[at : at + 32, lanes]
                odd = conv_sum[at + 32 : at + 64, lanes]
                rows = slice(cell * 32, (cell + 1) * 32)
                keep_ref[x, rows, :] = (jnp.where(first_core, even, odd) * scale).astype(bf16)
                send_ref[x, rows, :] = (jnp.where(first_core, odd, even) * scale).astype(bf16)
            for four in range(CELLS // 4):
                even, odd = [
                    jnp.concatenate(
                        [
                            proj_sum[at : at + SPARE, :]
                            for at in (
                                (2 * cell + odd) * 16 + x * SPARE
                                for cell in range(4 * four, 4 * four + 4)
                            )
                        ],
                        axis=0,
                    )
                    for odd in range(2)
                ]
                rows = slice(CONV_ROWS + four * 16, CONV_ROWS + (four + 1) * 16)
                keep_ref[x, rows, :] = (jnp.where(first_core, even, odd) * scale).astype(bf16)
                send_ref[x, rows, :] = (jnp.where(first_core, odd, even) * scale).astype(bf16)


def backward(
    scale, place, slopes, low, high, cotangent, received, weight, stored, conv_weight, channels, proj
):
    shape = jax.ShapeDtypeStruct((X, REST, LANES), bf16)
    return pl.pallas_call(
        functools.partial(backward_body, scale),
        grid=(SLOTS,),
        out_shape=(jax.ShapeDtypeStruct((SLOTS, 2 * T, C), bf16), shape, shape),
        in_specs=[SMEM] * 3
        + [
            by_slot(T, LANES),
            by_slot(REACH, LANES),
            by_slot(REACH, LANES),
            by_slot(GC, T),
            by_slot(GC, T),
            once(*weight.shape),
            by_slot(T, 2 * C),
            by_slot(T, C),
            by_slot(T, C),
            by_slot(T, C),
            by_slot(T, LANES),
            once(2 * C, C),
            whole(5, C),
            whole(GC, C),
        ],
        out_specs=(by_slot(2 * T, C), whole(*shape.shape), whole(*shape.shape)),
        scratch_shapes=[
            pltpu.VMEM((EXT, LANES), f32),
            pltpu.VMEM((T + NEAR * (K // NEAR - 1), NEAR * LANES), bf16),
            pltpu.VMEM((LANES, T), f32),
            pltpu.VMEM((LANES, C), bf16),
            pltpu.VMEM((T, LANES), bf16),
            pltpu.VMEM((T, C), bf16),
            pltpu.VMEM((T, C), f32),
            pltpu.VMEM((C // LANES, 2 * T, LANES), f32),
            pltpu.VMEM((2 * C, C), f32),
            pltpu.VMEM((C, LANES), f32),
            pltpu.VMEM((40, C), f32),
            pltpu.VMEM((LANES, C), f32),
        ],
        compiler_params=params(30),
        cost_estimate=cost(
            2 * SLOTS * (SPAN * K * LANES * LANES + T * C * (4 * C + 2 * LANES)), 14 << 20
        ),
        name="backward",
    )(
        *place,
        slopes,
        low,
        high,
        cotangent,
        received,
        weight,
        *stored,
        conv_weight,
        channels,
        proj,
    )


def halve_body(dev_ref, keep_ref, recv_ref, stay_ref, leave_ref):
    y = lax.rem(dev_ref[0], MP) // X
    for out_ref, at in ((stay_ref, y), (leave_ref, 1 - y)):
        out_ref[...] = (keep_ref[at].astype(f32) + recv_ref[at].astype(f32)).astype(bf16)


def halve(dev, keep, received):
    shape = jax.ShapeDtypeStruct(keep.shape[1:], bf16)
    return pl.pallas_call(
        halve_body,
        out_shape=(shape,) * 2,
        in_specs=[SMEM] + [VMEM] * 2,
        out_specs=(VMEM,) * 2,
        compiler_params=params(8),
        cost_estimate=cost(0, 2 << 20),
        name="halve",
    )(dev, keep, received)


def join_body(dev_ref, keep_ref, recv_ref, *out_refs):
    x = lax.rem(dev_ref[0], X)
    for step, out_ref in enumerate(out_refs):
        at = lax.rem(x + step, X)
        out_ref[...] = (keep_ref[at].astype(f32) + recv_ref[at].astype(f32)).astype(bf16)


def join(dev, keep, received):
    shape = jax.ShapeDtypeStruct((REST, LANES), bf16)
    return pl.pallas_call(
        join_body,
        out_shape=(shape,) * X,
        in_specs=[SMEM] + [VMEM] * 2,
        out_specs=(VMEM,) * X,
        compiler_params=params(8),
        cost_estimate=cost(0, 2 << 20),
        name="join",
    )(dev, keep, received)


def cells_body(*refs):
    pos_refs, rest_refs, out_ref, rows = refs[:2], refs[2:6], refs[6], refs[7]

    def summed(parts, *at):
        result = parts[0][at].astype(f32)
        for part in parts[1:]:
            result += part[at].astype(f32)
        return result

    for four in range(CELLS // 4):
        at = CONV_ROWS + four * 16
        small = summed(rest_refs, slice(at, at + 16), slice(None))
        for n in range(4):
            cell = 4 * four + n
            rows[...] = summed(pos_refs, cell)
            rows[HALF:, :] = small[n * SPARE : (n + 1) * SPARE, :]
            out_ref[cell, :REACH, :] = rows[...].astype(bf16)
            conv = summed(rest_refs, slice(cell * 32, cell * 32 + 32), slice(None))
            out_ref[cell, REACH:, :] = conv.astype(bf16)


def make_cells(pos_parts, rest_parts):
    return pl.pallas_call(
        cells_body,
        out_shape=jax.ShapeDtypeStruct((CELLS, REACH + 32, LANES), bf16),
        in_specs=[VMEM] * 6,
        out_specs=VMEM,
        scratch_shapes=[pltpu.VMEM((REACH, LANES), f32)],
        compiler_params=params(8),
        cost_estimate=cost(0, 2 << 20),
        name="cells",
    )(*pos_parts, *rest_parts)


def total_body(in_ref, out_ref):
    total = in_ref[0].astype(f32)
    for n in range(1, in_ref.shape[0]):
        total += in_ref[n].astype(f32)
    for copy in range(MP):
        out_ref[copy] = total.astype(bf16)


def total(parts):
    return pl.pallas_call(
        total_body,
        out_shape=jax.ShapeDtypeStruct((MP,) + parts.shape[1:], bf16),
        in_specs=[VMEM],
        out_specs=VMEM,
        compiler_params=params(10),
        cost_estimate=cost(0, 2 * parts.size),
        name="total",
    )(parts)


def finish_body(
    dev_ref,
    len_ref,
    mov_ref,
    in_ref,
    states_ref,
    other_ref,
    hidden_ref,
    pos_ref,
    conv_ref,
    proj_ref,
    chan_ref,
):
    place = Place(dev_ref, len_ref, mov_ref)
    for slot in range(SLOTS):
        hidden_ref[slot] = jnp.where(
            place.chosen == slot, other_ref[...].astype(f32), states_ref[slot].astype(f32)
        ).astype(bf16)
    small = []
    for x in range(X):
        low, high = in_ref[x].astype(f32), in_ref[X + x].astype(f32)
        block = jnp.concatenate(
            [low[:HALF, :], high[:HALF, :], jnp.zeros((LANES - GC, LANES), f32)], axis=0
        ).T
        pos_ref[x] = block[:GC, :GC]
        both = low[HALF:, :] + high[HALF:, :]
        small.append(both[:SPARE, :])
        conv_ref[:, x * LANES : (x + 1) * LANES] = both[SPARE:, :]
    small = jnp.concatenate(small, axis=0)
    proj_ref[...] = small[:, :GC]
    chan_ref[...] = jnp.concatenate([small] * 8, axis=0).T[GC : GC + 5, :16]


def finish(place, cells, states, other):
    return pl.pallas_call(
        finish_body,
        out_shape=(
            jax.ShapeDtypeStruct((SLOTS, GC, T), bf16),
            jax.ShapeDtypeStruct((4, GC, GC), f32),
            jax.ShapeDtypeStruct((32, C), f32),
            jax.ShapeDtypeStruct((16, GC), f32),
            jax.ShapeDtypeStruct((5, 16), f32),
        ),
        in_specs=[SMEM] * 3 + [VMEM] * 3,
        out_specs=(VMEM,) * 5,
        compiler_params=params(8),
        name="finish",
    )(*place, cells, states, other)


def neighbours(tail, head):
    forward = [(i, i + 1) for i in range(MP - 1)]
    backward_route = [(i + 1, i) for i in range(MP - 1)]
    return lax.ppermute(tail, "mp", forward), lax.ppermute(head, "mp", backward_route)


def along_x(block, step):
    route = [(X * y + x, X * y + (x + step) % X) for y in range(2) for x in range(X)]
    return lax.ppermute(block, "mp", route)


def around_x(block):
    far = along_x(block, 2)
    return (block, along_x(block, 1), far, along_x(block, 3))


def per_device(
    audio, lengths, moved_slots, conv_weight, channel_params, proj_weight, pos_weight, cotangent
):
    data_index = lax.axis_index("dp")
    model_index = lax.axis_index("mp")
    scale = (SLOTS * DP * T * MP) ** -0.5
    dev = (data_index * MP + model_index).astype(jnp.int32).reshape(1)
    place = (dev, lengths, moved_slots.reshape(-1))
    swap = [(i, i ^ (DP // 2)) for i in range(DP)]
    core_swap = [(i, i ^ 1) for i in range(DP)]
    channels = channel_params.T
    proj = proj_weight.T
    cot = cotangent.transpose(0, 2, 1)

    received = lax.ppermute(cot, "dp", swap)
    features, tail, head, *stored = encode(place, audio, conv_weight, channels, proj)
    low, high = neighbours(tail, head)
    all_features = around_x(features)
    ahead, behind = turn(pos_weight.transpose(1, 2, 0))
    states, sent, slopes, tail, head, piece = mix(
        place, features, low, high, ahead, cot, received
    )
    low, high = neighbours(tail, head)
    piece, all_features = lax.optimization_barrier((piece, all_features))
    pieces = around_x(piece)
    audio_grad, keep, send = backward(
        scale,
        place,
        slopes,
        low,
        high,
        cot,
        received,
        behind,
        stored,
        conv_weight,
        channels,
        proj,
    )
    send, pieces, sent = lax.optimization_barrier((send, pieces, sent))
    chunks = join(dev, keep, lax.ppermute(send, "dp", core_swap))
    chunks, pieces = lax.optimization_barrier((chunks, pieces))
    rest_parts = [chunks[0]] + [along_x(chunks[step], step) for step in (2, 1, 3)]
    pos_keep, pos_send = taps(scale, place, all_features, pieces)
    stay, leave = halve(dev, pos_keep, lax.ppermute(pos_send, "dp", core_swap))
    pos_parts = (stay, lax.ppermute(leave, "mp", [(i, i ^ X) for i in range(MP)]))
    other = lax.ppermute(sent, "dp", swap)
    cells = make_cells(pos_parts, rest_parts)
    groups = [list(range(bit, DP, 2)) for bit in range(2)]
    cells = lax.all_to_all(cells, "dp", 0, 0, axis_index_groups=groups, tiled=True)
    cells, other = lax.optimization_barrier((cells, other))
    cells = lax.all_to_all(total(cells), "mp", 0, 0, tiled=True)
    hidden, grad_pos, grad_conv, grad_proj, grad_channels = finish(place, cells, states, other)
    return (
        hidden.transpose(0, 2, 1),
        audio_grad,
        grad_pos,
        grad_conv,
        grad_proj,
        grad_channels.T,
    )


def solution(mesh):
    return jax.shard_map(
        per_device,
        mesh=mesh,
        in_specs=(P("dp", "mp", None), P(), P(), P(), P(), P(), P(), P("dp", "mp", None)),
        out_specs=(
            P("dp", "mp", None),
            P("dp", "mp", None),
            P("dp", None, None),
            P("dp", None),
            P("dp", None),
            P("dp", None),
        ),
        check_vma=False,
    )
```

```python
import functools

import jax
import jax.numpy as jnp
from jax import lax
from jax.experimental import pallas as pl
from jax.experimental.pallas import tpu as pltpu
from jax.sharding import PartitionSpec as P

epsilon = 1e-05
root_half = 0.7071067811865476
density = 0.3989422804014327

SLOTS = 2
T = 256
C = 512
GC = 120
LANES = 128
K = 128
REACH = 64
EXT = T + 2 * REACH
NEAR = 16
GROUPS = 2
PER_GROUP = 4
SPAN = T + NEAR * (PER_GROUP - 1)
CHUNK = 32
MP = 8
DP = 32
X = 4
CELLS = 16
PIECE = T + REACH
HALF = GC // 2
SPARE = REACH - HALF
CONV_ROWS = CELLS * 32
REST = CONV_ROWS + CELLS * SPARE

f32 = jnp.float32
bf16 = jnp.bfloat16

VMEM = pl.BlockSpec(memory_space=pltpu.VMEM)
SMEM = pl.BlockSpec(memory_space=pltpu.SMEM)
HBM = pl.BlockSpec(memory_space=pltpu.HBM)


def params(mebibytes):
    return pltpu.CompilerParams(vmem_limit_bytes=mebibytes << 20)


def cost(flops, moved, trans=0):
    return pl.CostEstimate(flops=flops, bytes_accessed=moved, transcendentals=trans)


def phi(values):
    return 0.5 * (1.0 + lax.erf(values * root_half))


def bell(values):
    return jnp.exp(-0.5 * values * values) * density


def nt(a, b):
    return lax.dot_general(a, b, (((1,), (1,)), ((), ())), preferred_element_type=f32)


def tn(a, b):
    return lax.dot_general(a, b, (((0,), (0,)), ((), ())), preferred_element_type=f32)


def nn(a, b):
    return jnp.dot(a, b, preferred_element_type=f32)


class Place:
    def __init__(self, dev_ref, len_ref, mov_ref=None):
        self.data = dev_ref[0] // MP
        self.model = lax.rem(dev_ref[0], MP)
        self.x = lax.rem(self.model, X)
        self.y = self.model // X
        self.core = lax.rem(self.data, 2)
        self.cell = self.data // 2
        self.first = self.model * T
        self.lengths = len_ref
        if mov_ref is not None:
            self.chosen = mov_ref[lax.rem(self.data, DP // 2)]

    def length(self, slot):
        return self.lengths[self.data * SLOTS + slot]

    def alive(self, slot):
        return self.first < self.length(slot)

    def mask(self, slot):
        ids = self.first + lax.broadcasted_iota(jnp.int32, (T, 1), 0)
        return ids < self.length(slot)


def by_slot(*dims):
    return pl.BlockSpec((1,) + dims, lambda s: (s,) + (0,) * len(dims))


def whole(*dims):
    return pl.BlockSpec(dims, lambda s: (0,) * len(dims))


def once(*dims):
    return pl.BlockSpec(dims, lambda s: (0,) * len(dims), pipeline_mode=pl.Buffered(1))


def turn_body(in_ref, ahead_ref, behind_ref, rows):
    block = pl.program_id(0)
    blocks = pl.num_programs(0)
    for n in range(NEAR):
        tile = jnp.concatenate(
            [in_ref[n].astype(f32), jnp.zeros((LANES - GC, K), f32)], axis=0
        ).T
        if n >= GC % NEAR:
            tile = jnp.where(block == blocks - 1, 0.0, tile)
        rows[pl.ds(n, K, stride=NEAR), :] = tile
    far = K // NEAR
    for q in range(far):
        for r in range(NEAR):
            at = (q * NEAR + r) * NEAR
            tile = rows[at : at + NEAR, :].astype(bf16)
            ahead_ref[r, :, q * LANES : (q + 1) * LANES] = tile
            r_back = NEAR - 1 - r
            behind_ref[far - 1 - q, :, r_back * LANES : (r_back + 1) * LANES] = tile


def turn(pos):
    far = K // NEAR
    ahead, behind = pl.pallas_call(
        turn_body,
        grid=(LANES // NEAR,),
        out_shape=(
            jax.ShapeDtypeStruct((NEAR, LANES, far * LANES), bf16),
            jax.ShapeDtypeStruct((far, LANES, NEAR * LANES), bf16),
        ),
        in_specs=[pl.BlockSpec((NEAR, GC, K), lambda b: (b, 0, 0))],
        out_specs=(
            pl.BlockSpec((NEAR, NEAR, far * LANES), lambda b: (0, b, 0)),
            pl.BlockSpec((far, NEAR, NEAR * LANES), lambda b: (0, b, 0)),
        ),
        scratch_shapes=[pltpu.VMEM((K * NEAR, LANES), f32)],
        compiler_params=params(16),
        cost_estimate=cost(0, 12 << 20),
        name="turn",
    )(pos)
    return ahead.reshape(NEAR * LANES, -1), behind.reshape(far * LANES, -1)


def encode_body(
    dev_ref,
    len_hbm,
    audio_hbm,
    conv_hbm,
    chan_hbm,
    proj_hbm,
    feat_ref,
    tail_ref,
    head_ref,
    pair_ref,
    q_ref,
    slope_ref,
    m_ref,
    inv_ref,
    wide,
    proj,
    mid,
    normed,
    len_ref,
    audio_ref,
    conv_ref,
    chan_ref,
    sems,
):
    slot = pl.program_id(0)
    copies = [
        pltpu.make_async_copy(source, target, sems.at[n])
        for n, (source, target) in enumerate(
            (
                (len_hbm, len_ref),
                (audio_hbm.at[0], audio_ref.at[0]),
                (conv_hbm, conv_ref),
                (chan_hbm, chan_ref),
                (proj_hbm, proj.at[pl.ds(0, GC)]),
                (audio_hbm.at[1], audio_ref.at[1]),
            )
        )
    ]

    @pl.when(slot == 0)
    def _():
        proj[GC - 8 :, :] = jnp.zeros((LANES - GC + 8, C), bf16)
        for copy in copies:
            copy.start()
        for copy in copies[:-1]:
            copy.wait()

    @pl.when(slot == SLOTS - 1)
    def _():
        copies[-1].wait()

    place = Place(dev_ref, len_ref)
    living = place.alive(slot)

    @pl.when(living)
    def _():
        for c in range(C // LANES):
            wide[c] = audio_ref[slot, :, c * LANES : (c + 1) * LANES].astype(f32)
            for tap in range(2):
                at = tap * C + c * LANES
                pair_ref[0, :, at : at + LANES] = wide[c, pl.ds(tap, T, stride=2), :].astype(bf16)
        mid[...] = nn(pair_ref[0], conv_ref[...])
        bias, gain, shift = chan_ref[0:1, :], chan_ref[1:2, :], chan_ref[2:3, :]
        gain_two, shift_two = chan_ref[3:4, :], chan_ref[4:5, :]
        for at in range(0, T, CHUNK):
            rows = slice(at, at + CHUNK)
            conv = mid[rows, :] + bias
            offset = conv - jnp.mean(conv, axis=-1, keepdims=True)
            inverse = lax.rsqrt(jnp.mean(offset * offset, axis=-1, keepdims=True) + epsilon)
            q = offset * inverse
            pre = q * gain + shift
            below = phi(pre)
            encoded = (pre * below).astype(bf16).astype(f32)
            slope_ref[0, rows, :] = (below + pre * bell(pre)).astype(bf16)
            q_ref[0, rows, :] = q.astype(bf16)
            offset = encoded - jnp.mean(encoded, axis=-1, keepdims=True)
            inverse_two = lax.rsqrt(jnp.mean(offset * offset, axis=-1, keepdims=True) + epsilon)
            m = offset * inverse_two
            m_ref[0, rows, :] = m.astype(bf16)
            inv_ref[0, rows, :] = jnp.concatenate(
                [
                    jnp.broadcast_to(inverse, (CHUNK, LANES // 2)),
                    jnp.broadcast_to(inverse_two, (CHUNK, LANES // 2)),
                ],
                axis=1,
            )
            normed[rows, :] = (m * gain_two + shift_two).astype(bf16)
        projected = nt(normed[...], proj[...])
        feat_ref[0] = jnp.where(place.mask(slot), projected, 0.0).astype(bf16)

    @pl.when(jnp.logical_not(living))
    def _():
        feat_ref[...] = jnp.zeros_like(feat_ref)

    tail_ref[0] = feat_ref[0, T - REACH :, :]
    head_ref[0] = feat_ref[0, :REACH, :]


def encode(place, audio, conv_weight, channels, proj):
    return pl.pallas_call(
        encode_body,
        grid=(SLOTS,),
        out_shape=(
            jax.ShapeDtypeStruct((SLOTS, T, LANES), bf16),
            jax.ShapeDtypeStruct((SLOTS, REACH, LANES), bf16),
            jax.ShapeDtypeStruct((SLOTS, REACH, LANES), bf16),
            jax.ShapeDtypeStruct((SLOTS, T, 2 * C), bf16),
            jax.ShapeDtypeStruct((SLOTS, T, C), bf16),
            jax.ShapeDtypeStruct((SLOTS, T, C), bf16),
            jax.ShapeDtypeStruct((SLOTS, T, C), bf16),
            jax.ShapeDtypeStruct((SLOTS, T, LANES), f32),
        ),
        in_specs=[SMEM] + [HBM] * 5,
        out_specs=(
            by_slot(T, LANES),
            by_slot(REACH, LANES),
            by_slot(REACH, LANES),
            by_slot(T, 2 * C),
            by_slot(T, C),
            by_slot(T, C),
            by_slot(T, C),
            by_slot(T, LANES),
        ),
        scratch_shapes=[
            pltpu.VMEM((C // LANES, 2 * T, LANES), f32),
            pltpu.VMEM((LANES, C), bf16),
            pltpu.VMEM((T, C), f32),
            pltpu.VMEM((T, C), bf16),
            pltpu.SMEM((DP * SLOTS,), jnp.int32),
            pltpu.VMEM((SLOTS, 2 * T, C), bf16),
            pltpu.VMEM((2 * C, C), bf16),
            pltpu.VMEM((5, C), f32),
            pltpu.SemaphoreType.DMA((6,)),
        ],
        compiler_params=params(50),
        cost_estimate=cost(2 * SLOTS * T * C * (2 * C + LANES), 8 << 20, SLOTS * T * C * 2),
        name="encode",
    )(*place[:2], audio, conv_weight, channels, proj)


def fill_ext(ext, low, own, high):
    ext[:REACH, :] = low.astype(f32)
    ext[REACH : REACH + T, :] = own.astype(f32)
    ext[REACH + T :, :] = high.astype(f32)


def fill_windows(windows, ext, first):
    rows = T + NEAR * (K // NEAR - 1)
    for r in range(NEAR):
        windows[:, r * LANES : (r + 1) * LANES] = ext[first + r : first + r + rows, :].astype(bf16)


def gathered(group):
    total = group[:T, :LANES]
    for p in range(1, PER_GROUP):
        total += group[NEAR * p : NEAR * p + T, p * LANES : (p + 1) * LANES]
    return total


def fill_back(turned, place, slot, cot_ref, recv_ref):
    turned[GC:, :] = jnp.zeros((LANES - GC, T), f32)
    turned[:GC, :] = jnp.where(
        place.chosen == slot, recv_ref[0].astype(f32), cot_ref[0].astype(f32)
    )


def mix_body(
    dev_ref,
    len_ref,
    mov_ref,
    feat_ref,
    low_ref,
    high_ref,
    weight,
    cot_ref,
    recv_ref,
    states_ref,
    sent_ref,
    slopes_ref,
    tail_ref,
    head_ref,
    piece_ref,
    ext,
    windows,
    turned,
):
    place = Place(dev_ref, len_ref, mov_ref)
    slot = pl.program_id(0)
    living = place.alive(slot)
    wide = PER_GROUP * LANES

    @pl.when(living)
    def _():
        own = feat_ref[0].astype(f32)
        fill_ext(ext, low_ref[0], own, high_ref[0])
        fill_windows(windows, ext, 0)
        fill_back(turned, place, slot, cot_ref, recv_ref)
        back = turned[...].T
        group = jnp.zeros((SPAN, wide), f32)
        for g in range(GROUPS):
            at = g * NEAR * PER_GROUP
            group += nn(windows[at : at + SPAN, :], weight[:, g * wide : (g + 1) * wide])
        mixed = gathered(group)
        below = phi(mixed)
        mask = place.mask(slot)
        states = jnp.where(mask, own + mixed * below, 0.0)
        states_ref[0] = states.T[:GC, :].astype(bf16)
        slopes = jnp.where(mask, back * (below + mixed * bell(mixed)), 0.0)
        slopes_ref[0] = slopes.astype(bf16)
        edge = jnp.where(place.x < X // 2, low_ref[0].astype(f32), high_ref[0].astype(f32))
        piece_ref[0, :T, :] = slopes.astype(bf16)
        piece_ref[0, T:, :] = edge.astype(bf16)

    @pl.when(jnp.logical_not(living))
    def _():
        states_ref[...] = jnp.zeros_like(states_ref)
        slopes_ref[...] = jnp.zeros_like(slopes_ref)
        piece_ref[...] = jnp.zeros_like(piece_ref)

    tail_ref[0] = slopes_ref[0, T - REACH :, :]
    head_ref[0] = slopes_ref[0, :REACH, :]

    @pl.when(place.chosen == slot)
    def _():
        sent_ref[...] = states_ref[0]


def mix(place, features, low, high, weight, cotangent, received):
    return pl.pallas_call(
        mix_body,
        grid=(SLOTS,),
        out_shape=(
            jax.ShapeDtypeStruct((SLOTS, GC, T), bf16),
            jax.ShapeDtypeStruct((GC, T), bf16),
            jax.ShapeDtypeStruct((SLOTS, T, LANES), bf16),
            jax.ShapeDtypeStruct((SLOTS, REACH, LANES), bf16),
            jax.ShapeDtypeStruct((SLOTS, REACH, LANES), bf16),
            jax.ShapeDtypeStruct((SLOTS, PIECE, LANES), bf16),
        ),
        in_specs=[SMEM] * 3
        + [
            by_slot(T, LANES),
            by_slot(REACH, LANES),
            by_slot(REACH, LANES),
            once(*weight.shape),
            by_slot(GC, T),
            by_slot(GC, T),
        ],
        out_specs=(
            by_slot(GC, T),
            whole(GC, T),
            by_slot(T, LANES),
            by_slot(REACH, LANES),
            by_slot(REACH, LANES),
            by_slot(PIECE, LANES),
        ),
        scratch_shapes=[
            pltpu.VMEM((EXT, LANES), f32),
            pltpu.VMEM((T + NEAR * (K // NEAR - 1), NEAR * LANES), bf16),
            pltpu.VMEM((LANES, T), f32),
        ],
        compiler_params=params(20),
        cost_estimate=cost(2 * SLOTS * SPAN * K * LANES * LANES, 7 << 20, SLOTS * T * LANES * 2),
        name="mix",
    )(*place, features, low, high, weight, cotangent, received)


def taps_body(scale, dev_ref, len_ref, mov_ref, *refs):
    feat_refs, piece_refs, (keep_ref, send_ref) = refs[:X], refs[X : 2 * X], refs[2 * X : 2 * X + 2]
    ext, windows, turned, sums = refs[2 * X + 2 :]
    place = Place(dev_ref, len_ref, mov_ref)
    slot = pl.program_id(0)
    spread = X * T
    rows = spread + NEAR * (K // NEAR - 1)

    @pl.when(slot == 0)
    def _():
        sums[...] = jnp.zeros_like(sums)

    @pl.when(place.y * spread < place.length(slot))
    def _():
        for step, (feat_ref, piece_ref) in enumerate(zip(feat_refs, piece_refs)):
            x = lax.rem(place.x + (X - step), X)
            at = pl.multiple_of(x * T, T)
            ext[pl.ds(REACH + at, T), :] = feat_ref[0].astype(f32)
            turned[:, pl.ds(at, T)] = piece_ref[0, :T, :].astype(f32).T.astype(bf16)

            @pl.when(x == 0)
            def _():
                ext[:REACH, :] = piece_ref[0, T:, :].astype(f32)

            @pl.when(x == X - 1)
            def _():
                ext[REACH + spread :, :] = piece_ref[0, T:, :].astype(f32)

        for j in range(4):
            windows[:, j * LANES : (j + 1) * LANES] = ext[
                pl.ds(place.x + 4 * j, rows), :
            ].astype(bf16)
        for q in range(K // NEAR):
            sums[q] += nn(turned[...], windows[q * NEAR : q * NEAR + spread, :])

    @pl.when(slot == SLOTS - 1)
    def _():
        first_core = place.core == 0
        for q in range(K // NEAR):
            for far in range(2):
                at = 2 * far * LANES
                even = sums[q, :, at : at + LANES] * scale
                odd = sums[q, :, at + LANES : at + 2 * LANES] * scale
                keep = jnp.where(first_core, even, odd)
                send = jnp.where(first_core, odd, even)
                for y in range(2):
                    rows = slice(y * HALF, y * HALF + REACH)
                    keep_ref[y, 2 * q + far] = keep[rows, :].astype(bf16)
                    send_ref[y, 2 * q + far] = send[rows, :].astype(bf16)


def taps(scale, place, features, pieces):
    shape = jax.ShapeDtypeStruct((2, CELLS, REACH, LANES), bf16)
    spread = X * T
    return pl.pallas_call(
        functools.partial(taps_body, scale),
        grid=(SLOTS,),
        out_shape=(shape,) * 2,
        in_specs=[SMEM] * 3 + [by_slot(T, LANES)] * X + [by_slot(PIECE, LANES)] * X,
        out_specs=(whole(*shape.shape),) * 2,
        scratch_shapes=[
            pltpu.VMEM((spread + 2 * REACH, LANES), f32),
            pltpu.VMEM((spread + NEAR * (K // NEAR - 1), 4 * LANES), bf16),
            pltpu.VMEM((LANES, spread), bf16),
            pltpu.VMEM((K // NEAR, LANES, 4 * LANES), f32),
        ],
        compiler_params=params(16),
        cost_estimate=cost(2 * SLOTS * SPAN * K * LANES * LANES, 4 << 20),
        name="taps",
    )(*place, *features, *pieces)


def backward_body(
    scale,
    dev_ref,
    len_ref,
    mov_ref,
    slopes_ref,
    low_ref,
    high_ref,
    cot_ref,
    recv_ref,
    weight,
    pair_ref,
    q_ref,
    slope_ref,
    m_ref,
    inv_ref,
    conv_ref,
    chan_ref,
    proj_ref,
    audio_grad_ref,
    keep_ref,
    send_ref,
    ext,
    windows,
    turned,
    proj,
    feat_grad,
    normed,
    mid,
    wide,
    conv_sum,
    proj_sum,
    chan_sum,
    columns,
):
    place = Place(dev_ref, len_ref, mov_ref)
    slot = pl.program_id(0)
    living = place.alive(slot)
    span = PER_GROUP * LANES

    @pl.when(slot == 0)
    def _():
        proj[...] = jnp.zeros_like(proj)
        proj[:GC, :] = proj_ref[...]
        conv_sum[...] = jnp.zeros_like(conv_sum)
        proj_sum[...] = jnp.zeros_like(proj_sum)
        chan_sum[...] = jnp.zeros_like(chan_sum)

    @pl.when(living)
    def _():
        fill_ext(ext, low_ref[0], slopes_ref[0], high_ref[0])
        fill_windows(windows, ext, 1)
        fill_back(turned, place, slot, cot_ref, recv_ref)
        group = jnp.zeros((SPAN, span), f32)
        for g in range(GROUPS):
            at = g * NEAR * PER_GROUP
            group += nt(windows[at : at + SPAN, :], weight[g * span : (g + 1) * span, :])
        spread = gathered(group)
        feat_grad[...] = jnp.where(place.mask(slot), turned[...].T + spread, 0.0).astype(bf16)
        gain = chan_ref[1:2, :]
        gain_two, shift_two = chan_ref[3:4, :], chan_ref[4:5, :]
        mid[...] = nn(feat_grad[...], proj[...])
        for at in range(0, T, CHUNK):
            rows = slice(at, at + CHUNK)
            m = m_ref[0, rows, :].astype(f32)
            normed[rows, :] = (m * gain_two + shift_two).astype(bf16)
            normed_grad = mid[rows, :]
            chan_sum[24:32, :] += jnp.sum((normed_grad * m).reshape(-1, 8, C), axis=0)
            chan_sum[32:40, :] += jnp.sum(normed_grad.reshape(-1, 8, C), axis=0)
            scaled = normed_grad * gain_two
            first = jnp.mean(scaled, axis=-1, keepdims=True)
            second = jnp.mean(scaled * m, axis=-1, keepdims=True)
            inverse_two = inv_ref[0, rows, LANES // 2 : LANES // 2 + 1]
            pre_grad = inverse_two * (scaled - first - m * second) * slope_ref[
                0, rows, :
            ].astype(f32)
            q = q_ref[0, rows, :].astype(f32)
            chan_sum[8:16, :] += jnp.sum((pre_grad * q).reshape(-1, 8, C), axis=0)
            chan_sum[16:24, :] += jnp.sum(pre_grad.reshape(-1, 8, C), axis=0)
            scaled = pre_grad * gain
            first = jnp.mean(scaled, axis=-1, keepdims=True)
            second = jnp.mean(scaled * q, axis=-1, keepdims=True)
            inverse = inv_ref[0, rows, 0:1]
            conv_grad = inverse * (scaled - first - q * second)
            chan_sum[0:8, :] += jnp.sum(conv_grad.reshape(-1, 8, C), axis=0)
            mid[rows, :] = conv_grad
        operand = mid[...].astype(bf16)
        for tap in range(2):
            rows = slice(tap * C, (tap + 1) * C)
            audio_grad = nt(operand, conv_ref[rows, :])
            for c in range(C // LANES):
                wide[c, pl.ds(tap, T, stride=2), :] = audio_grad[:, c * LANES : (c + 1) * LANES]
            conv_sum[rows, :] += tn(pair_ref[0, :, rows], operand)
        for c in range(C // LANES):
            audio_grad_ref[0, :, c * LANES : (c + 1) * LANES] = wide[c].astype(bf16)
        proj_sum[...] += tn(normed[...], feat_grad[...])

    @pl.when(jnp.logical_not(living))
    def _():
        audio_grad_ref[...] = jnp.zeros_like(audio_grad_ref)

    @pl.when(slot == SLOTS - 1)
    def _():
        first_core = place.core == 0
        columns[...] = jnp.zeros_like(columns)
        for n in range(5):
            columns[GC + n : GC + n + 1, :] = jnp.sum(
                chan_sum[8 * n : 8 * n + 8, :], axis=0, keepdims=True
            )
        proj_sum[...] += columns[...].T
        for x in range(X):
            lanes = slice(x * LANES, (x + 1) * LANES)
            for cell in range(CELLS):
                at = 2 * cell * 32
                even = conv_sum[at : at + 32, lanes]
                odd = conv_sum[at + 32 : at + 64, lanes]
                rows = slice(cell * 32, (cell + 1) * 32)
                keep_ref[x, rows, :] = (jnp.where(first_core, even, odd) * scale).astype(bf16)
                send_ref[x, rows, :] = (jnp.where(first_core, odd, even) * scale).astype(bf16)
            for four in range(CELLS // 4):
                even, odd = [
                    jnp.concatenate(
                        [
                            proj_sum[at : at + SPARE, :]
                            for at in (
                                (2 * cell + odd) * 16 + x * SPARE
                                for cell in range(4 * four, 4 * four + 4)
                            )
                        ],
                        axis=0,
                    )
                    for odd in range(2)
                ]
                rows = slice(CONV_ROWS + four * 16, CONV_ROWS + (four + 1) * 16)
                keep_ref[x, rows, :] = (jnp.where(first_core, even, odd) * scale).astype(bf16)
                send_ref[x, rows, :] = (jnp.where(first_core, odd, even) * scale).astype(bf16)


def backward(
    scale, place, slopes, low, high, cotangent, received, weight, stored, conv_weight, channels, proj
):
    shape = jax.ShapeDtypeStruct((X, REST, LANES), bf16)
    return pl.pallas_call(
        functools.partial(backward_body, scale),
        grid=(SLOTS,),
        out_shape=(jax.ShapeDtypeStruct((SLOTS, 2 * T, C), bf16), shape, shape),
        in_specs=[SMEM] * 3
        + [
            by_slot(T, LANES),
            by_slot(REACH, LANES),
            by_slot(REACH, LANES),
            by_slot(GC, T),
            by_slot(GC, T),
            once(*weight.shape),
            by_slot(T, 2 * C),
            by_slot(T, C),
            by_slot(T, C),
            by_slot(T, C),
            by_slot(T, LANES),
            once(2 * C, C),
            whole(5, C),
            whole(GC, C),
        ],
        out_specs=(by_slot(2 * T, C), whole(*shape.shape), whole(*shape.shape)),
        scratch_shapes=[
            pltpu.VMEM((EXT, LANES), f32),
            pltpu.VMEM((T + NEAR * (K // NEAR - 1), NEAR * LANES), bf16),
            pltpu.VMEM((LANES, T), f32),
            pltpu.VMEM((LANES, C), bf16),
            pltpu.VMEM((T, LANES), bf16),
            pltpu.VMEM((T, C), bf16),
            pltpu.VMEM((T, C), f32),
            pltpu.VMEM((C // LANES, 2 * T, LANES), f32),
            pltpu.VMEM((2 * C, C), f32),
            pltpu.VMEM((C, LANES), f32),
            pltpu.VMEM((40, C), f32),
            pltpu.VMEM((LANES, C), f32),
        ],
        compiler_params=params(30),
        cost_estimate=cost(
            2 * SLOTS * (SPAN * K * LANES * LANES + T * C * (4 * C + 2 * LANES)), 14 << 20
        ),
        name="backward",
    )(
        *place,
        slopes,
        low,
        high,
        cotangent,
        received,
        weight,
        *stored,
        conv_weight,
        channels,
        proj,
    )


def halve_body(dev_ref, keep_ref, recv_ref, stay_ref, leave_ref):
    y = lax.rem(dev_ref[0], MP) // X
    for out_ref, at in ((stay_ref, y), (leave_ref, 1 - y)):
        out_ref[...] = (keep_ref[at].astype(f32) + recv_ref[at].astype(f32)).astype(bf16)


def halve(dev, keep, received):
    shape = jax.ShapeDtypeStruct(keep.shape[1:], bf16)
    return pl.pallas_call(
        halve_body,
        out_shape=(shape,) * 2,
        in_specs=[SMEM] + [VMEM] * 2,
        out_specs=(VMEM,) * 2,
        compiler_params=params(8),
        cost_estimate=cost(0, 2 << 20),
        name="halve",
    )(dev, keep, received)


def join_body(dev_ref, keep_ref, recv_ref, *out_refs):
    x = lax.rem(dev_ref[0], X)
    for step, out_ref in enumerate(out_refs):
        at = lax.rem(x + step, X)
        out_ref[...] = (keep_ref[at].astype(f32) + recv_ref[at].astype(f32)).astype(bf16)


def join(dev, keep, received):
    shape = jax.ShapeDtypeStruct((REST, LANES), bf16)
    return pl.pallas_call(
        join_body,
        out_shape=(shape,) * X,
        in_specs=[SMEM] + [VMEM] * 2,
        out_specs=(VMEM,) * X,
        compiler_params=params(8),
        cost_estimate=cost(0, 2 << 20),
        name="join",
    )(dev, keep, received)


def cells_body(*refs):
    pos_refs, rest_refs, out_ref, rows = refs[:2], refs[2:6], refs[6], refs[7]

    def summed(parts, *at):
        result = parts[0][at].astype(f32)
        for part in parts[1:]:
            result += part[at].astype(f32)
        return result

    for four in range(CELLS // 4):
        at = CONV_ROWS + four * 16
        small = summed(rest_refs, slice(at, at + 16), slice(None))
        for n in range(4):
            cell = 4 * four + n
            rows[...] = summed(pos_refs, cell)
            rows[HALF:, :] = small[n * SPARE : (n + 1) * SPARE, :]
            out_ref[cell, :REACH, :] = rows[...].astype(bf16)
            conv = summed(rest_refs, slice(cell * 32, cell * 32 + 32), slice(None))
            out_ref[cell, REACH:, :] = conv.astype(bf16)


def make_cells(pos_parts, rest_parts):
    return pl.pallas_call(
        cells_body,
        out_shape=jax.ShapeDtypeStruct((CELLS, REACH + 32, LANES), bf16),
        in_specs=[VMEM] * 6,
        out_specs=VMEM,
        scratch_shapes=[pltpu.VMEM((REACH, LANES), f32)],
        compiler_params=params(8),
        cost_estimate=cost(0, 2 << 20),
        name="cells",
    )(*pos_parts, *rest_parts)


def total_body(in_ref, out_ref):
    total = in_ref[0].astype(f32)
    for n in range(1, in_ref.shape[0]):
        total += in_ref[n].astype(f32)
    for copy in range(MP):
        out_ref[copy] = total.astype(bf16)


def total(parts):
    return pl.pallas_call(
        total_body,
        out_shape=jax.ShapeDtypeStruct((MP,) + parts.shape[1:], bf16),
        in_specs=[VMEM],
        out_specs=VMEM,
        compiler_params=params(10),
        cost_estimate=cost(0, 2 * parts.size),
        name="total",
    )(parts)


def finish_body(
    dev_ref,
    len_ref,
    mov_ref,
    in_ref,
    states_ref,
    other_ref,
    hidden_ref,
    pos_ref,
    conv_ref,
    proj_ref,
    chan_ref,
):
    place = Place(dev_ref, len_ref, mov_ref)
    for slot in range(SLOTS):
        hidden_ref[slot] = jnp.where(
            place.chosen == slot, other_ref[...].astype(f32), states_ref[slot].astype(f32)
        ).astype(bf16)
    small = []
    for x in range(X):
        low, high = in_ref[x].astype(f32), in_ref[X + x].astype(f32)
        block = jnp.concatenate(
            [low[:HALF, :], high[:HALF, :], jnp.zeros((LANES - GC, LANES), f32)], axis=0
        ).T
        pos_ref[x] = block[:GC, :GC]
        both = low[HALF:, :] + high[HALF:, :]
        small.append(both[:SPARE, :])
        conv_ref[:, x * LANES : (x + 1) * LANES] = both[SPARE:, :]
    small = jnp.concatenate(small, axis=0)
    proj_ref[...] = small[:, :GC]
    chan_ref[...] = jnp.concatenate([small] * 8, axis=0).T[GC : GC + 5, :16]


def finish(place, cells, states, other):
    return pl.pallas_call(
        finish_body,
        out_shape=(
            jax.ShapeDtypeStruct((SLOTS, GC, T), bf16),
            jax.ShapeDtypeStruct((4, GC, GC), f32),
            jax.ShapeDtypeStruct((32, C), f32),
            jax.ShapeDtypeStruct((16, GC), f32),
            jax.ShapeDtypeStruct((5, 16), f32),
        ),
        in_specs=[SMEM] * 3 + [VMEM] * 3,
        out_specs=(VMEM,) * 5,
        compiler_params=params(8),
        name="finish",
    )(*place, cells, states, other)


def neighbours(tail, head):
    forward = [(i, i + 1) for i in range(MP - 1)]
    backward_route = [(i + 1, i) for i in range(MP - 1)]
    return lax.ppermute(tail, "mp", forward), lax.ppermute(head, "mp", backward_route)


def along_x(block, step):
    route = [(X * y + x, X * y + (x + step) % X) for y in range(2) for x in range(X)]
    return lax.ppermute(block, "mp", route)


def around_x(block):
    far = along_x(block, 2)
    return (block, along_x(block, 1), far, along_x(block, 3))


def per_device(
    audio, lengths, moved_slots, conv_weight, channel_params, proj_weight, pos_weight, cotangent
):
    data_index = lax.axis_index("dp")
    model_index = lax.axis_index("mp")
    scale = (SLOTS * DP * T * MP) ** -0.5
    dev = (data_index * MP + model_index).astype(jnp.int32).reshape(1)
    place = (dev, lengths, moved_slots.reshape(-1))
    swap = [(i, i ^ (DP // 2)) for i in range(DP)]
    core_swap = [(i, i ^ 1) for i in range(DP)]
    channels = channel_params.T
    proj = proj_weight.T
    cot = cotangent.transpose(0, 2, 1)

    received = lax.ppermute(cot, "dp", swap)
    features, tail, head, *stored = encode(place, audio, conv_weight, channels, proj)
    low, high = neighbours(tail, head)
    all_features = around_x(features)
    ahead, behind = turn(pos_weight.transpose(1, 2, 0))
    states, sent, slopes, tail, head, piece = mix(
        place, features, low, high, ahead, cot, received
    )
    low, high = neighbours(tail, head)
    piece, all_features = lax.optimization_barrier((piece, all_features))
    pieces = around_x(piece)
    audio_grad, keep, send = backward(
        scale,
        place,
        slopes,
        low,
        high,
        cot,
        received,
        behind,
        stored,
        conv_weight,
        channels,
        proj,
    )
    other = lax.ppermute(sent, "dp", swap)
    send, pieces, other = lax.optimization_barrier((send, pieces, other))
    chunks = join(dev, keep, lax.ppermute(send, "dp", core_swap))
    chunks, pieces = lax.optimization_barrier((chunks, pieces))
    rest_parts = [chunks[0]] + [along_x(chunks[step], step) for step in (2, 1, 3)]
    pos_keep, pos_send = taps(scale, place, all_features, pieces)
    stay, leave = halve(dev, pos_keep, lax.ppermute(pos_send, "dp", core_swap))
    pos_parts = (stay, lax.ppermute(leave, "mp", [(i, i ^ X) for i in range(MP)]))
    cells = make_cells(pos_parts, rest_parts)
    groups = [list(range(bit, DP, 2)) for bit in range(2)]
    cells = lax.all_to_all(cells, "dp", 0, 0, axis_index_groups=groups, tiled=True)
    cells = lax.all_to_all(total(cells), "mp", 0, 0, tiled=True)
    hidden, grad_pos, grad_conv, grad_proj, grad_channels = finish(place, cells, states, other)
    return (
        hidden.transpose(0, 2, 1),
        audio_grad,
        grad_pos,
        grad_conv,
        grad_proj,
        grad_channels.T,
    )


def solution(mesh):
    return jax.shard_map(
        per_device,
        mesh=mesh,
        in_specs=(P("dp", "mp", None), P(), P(), P(), P(), P(), P(), P("dp", "mp", None)),
        out_specs=(
            P("dp", "mp", None),
            P("dp", "mp", None),
            P("dp", None, None),
            P("dp", None),
            P("dp", None),
            P("dp", None),
        ),
        check_vma=False,
    )
```

```python
import functools

import jax
import jax.numpy as jnp
from jax import lax
from jax.experimental import pallas as pl
from jax.experimental.pallas import tpu as pltpu
from jax.sharding import PartitionSpec as P

epsilon = 1e-05
root_half = 0.7071067811865476
density = 0.3989422804014327

SLOTS = 2
T = 256
C = 512
GC = 120
LANES = 128
K = 128
REACH = 64
EXT = T + 2 * REACH
NEAR = 16
GROUPS = 2
PER_GROUP = 4
SPAN = T + NEAR * (PER_GROUP - 1)
CHUNK = 32
MP = 8
DP = 32
X = 4
CELLS = 16
PIECE = T + REACH
HALF = GC // 2
SPARE = REACH - HALF
CONV_ROWS = CELLS * 32
REST = CONV_ROWS + CELLS * SPARE

f32 = jnp.float32
bf16 = jnp.bfloat16

VMEM = pl.BlockSpec(memory_space=pltpu.VMEM)
SMEM = pl.BlockSpec(memory_space=pltpu.SMEM)
HBM = pl.BlockSpec(memory_space=pltpu.HBM)


def params(mebibytes):
    return pltpu.CompilerParams(vmem_limit_bytes=mebibytes << 20)


def cost(flops, moved, trans=0):
    return pl.CostEstimate(flops=flops, bytes_accessed=moved, transcendentals=trans)


def phi(values):
    return 0.5 * (1.0 + lax.erf(values * root_half))


def bell(values):
    return jnp.exp(-0.5 * values * values) * density


def nt(a, b):
    return lax.dot_general(a, b, (((1,), (1,)), ((), ())), preferred_element_type=f32)


def tn(a, b):
    return lax.dot_general(a, b, (((0,), (0,)), ((), ())), preferred_element_type=f32)


def nn(a, b):
    return jnp.dot(a, b, preferred_element_type=f32)


class Place:
    def __init__(self, dev_ref, len_ref, mov_ref=None):
        self.data = dev_ref[0] // MP
        self.model = lax.rem(dev_ref[0], MP)
        self.x = lax.rem(self.model, X)
        self.y = self.model // X
        self.core = lax.rem(self.data, 2)
        self.cell = self.data // 2
        self.first = self.model * T
        self.lengths = len_ref
        if mov_ref is not None:
            self.chosen = mov_ref[lax.rem(self.data, DP // 2)]

    def length(self, slot):
        return self.lengths[self.data * SLOTS + slot]

    def alive(self, slot):
        return self.first < self.length(slot)

    def mask(self, slot):
        ids = self.first + lax.broadcasted_iota(jnp.int32, (T, 1), 0)
        return ids < self.length(slot)


def by_slot(*dims):
    return pl.BlockSpec((1,) + dims, lambda s: (s,) + (0,) * len(dims))


def whole(*dims):
    return pl.BlockSpec(dims, lambda s: (0,) * len(dims))


def once(*dims):
    return pl.BlockSpec(dims, lambda s: (0,) * len(dims), pipeline_mode=pl.Buffered(1))


def turn_body(in_ref, ahead_ref, behind_ref, rows):
    block = pl.program_id(0)
    blocks = pl.num_programs(0)
    for n in range(NEAR):
        tile = jnp.concatenate(
            [in_ref[n].astype(f32), jnp.zeros((LANES - GC, K), f32)], axis=0
        ).T
        if n >= GC % NEAR:
            tile = jnp.where(block == blocks - 1, 0.0, tile)
        rows[pl.ds(n, K, stride=NEAR), :] = tile
    far = K // NEAR
    for q in range(far):
        for r in range(NEAR):
            at = (q * NEAR + r) * NEAR
            tile = rows[at : at + NEAR, :].astype(bf16)
            ahead_ref[r, :, q * LANES : (q + 1) * LANES] = tile
            r_back = NEAR - 1 - r
            behind_ref[far - 1 - q, :, r_back * LANES : (r_back + 1) * LANES] = tile


def turn(pos):
    far = K // NEAR
    ahead, behind = pl.pallas_call(
        turn_body,
        grid=(LANES // NEAR,),
        out_shape=(
            jax.ShapeDtypeStruct((NEAR, LANES, far * LANES), bf16),
            jax.ShapeDtypeStruct((far, LANES, NEAR * LANES), bf16),
        ),
        in_specs=[pl.BlockSpec((NEAR, GC, K), lambda b: (b, 0, 0))],
        out_specs=(
            pl.BlockSpec((NEAR, NEAR, far * LANES), lambda b: (0, b, 0)),
            pl.BlockSpec((far, NEAR, NEAR * LANES), lambda b: (0, b, 0)),
        ),
        scratch_shapes=[pltpu.VMEM((K * NEAR, LANES), f32)],
        compiler_params=params(16),
        cost_estimate=cost(0, 12 << 20),
        name="turn",
    )(pos)
    return ahead.reshape(NEAR * LANES, -1), behind.reshape(far * LANES, -1)


def encode_body(
    dev_ref,
    len_hbm,
    audio_hbm,
    conv_hbm,
    chan_hbm,
    proj_hbm,
    feat_ref,
    tail_ref,
    head_ref,
    pair_ref,
    q_ref,
    slope_ref,
    m_ref,
    inv_ref,
    wide,
    proj,
    mid,
    normed,
    len_ref,
    audio_ref,
    conv_ref,
    chan_ref,
    sems,
):
    slot = pl.program_id(0)
    copies = [
        pltpu.make_async_copy(source, target, sems.at[n])
        for n, (source, target) in enumerate(
            (
                (len_hbm, len_ref),
                (audio_hbm.at[0], audio_ref.at[0]),
                (conv_hbm, conv_ref),
                (chan_hbm, chan_ref),
                (proj_hbm, proj.at[pl.ds(0, GC)]),
                (audio_hbm.at[1], audio_ref.at[1]),
            )
        )
    ]

    @pl.when(slot == 0)
    def _():
        proj[GC - 8 :, :] = jnp.zeros((LANES - GC + 8, C), bf16)
        for copy in copies:
            copy.start()
        for copy in copies[:-1]:
            copy.wait()

    @pl.when(slot == SLOTS - 1)
    def _():
        copies[-1].wait()

    place = Place(dev_ref, len_ref)
    living = place.alive(slot)

    @pl.when(living)
    def _():
        for c in range(C // LANES):
            wide[c] = audio_ref[slot, :, c * LANES : (c + 1) * LANES].astype(f32)
            for tap in range(2):
                at = tap * C + c * LANES
                pair_ref[0, :, at : at + LANES] = wide[c, pl.ds(tap, T, stride=2), :].astype(bf16)
        mid[...] = nn(pair_ref[0], conv_ref[...])
        bias, gain, shift = chan_ref[0:1, :], chan_ref[1:2, :], chan_ref[2:3, :]
        gain_two, shift_two = chan_ref[3:4, :], chan_ref[4:5, :]
        for at in range(0, T, CHUNK):
            rows = slice(at, at + CHUNK)
            conv = mid[rows, :] + bias
            offset = conv - jnp.mean(conv, axis=-1, keepdims=True)
            inverse = lax.rsqrt(jnp.mean(offset * offset, axis=-1, keepdims=True) + epsilon)
            q = offset * inverse
            pre = q * gain + shift
            below = phi(pre)
            encoded = (pre * below).astype(bf16).astype(f32)
            slope_ref[0, rows, :] = (below + pre * bell(pre)).astype(bf16)
            q_ref[0, rows, :] = q.astype(bf16)
            offset = encoded - jnp.mean(encoded, axis=-1, keepdims=True)
            inverse_two = lax.rsqrt(jnp.mean(offset * offset, axis=-1, keepdims=True) + epsilon)
            m = offset * inverse_two
            m_ref[0, rows, :] = m.astype(bf16)
            inv_ref[0, rows, :] = jnp.concatenate(
                [
                    jnp.broadcast_to(inverse, (CHUNK, LANES // 2)),
                    jnp.broadcast_to(inverse_two, (CHUNK, LANES // 2)),
                ],
                axis=1,
            )
            normed[rows, :] = (m * gain_two + shift_two).astype(bf16)
        projected = nt(normed[...], proj[...])
        feat_ref[0] = jnp.where(place.mask(slot), projected, 0.0).astype(bf16)

    @pl.when(jnp.logical_not(living))
    def _():
        feat_ref[...] = jnp.zeros_like(feat_ref)

    tail_ref[0] = feat_ref[0, T - REACH :, :]
    head_ref[0] = feat_ref[0, :REACH, :]


def encode(place, audio, conv_weight, channels, proj):
    return pl.pallas_call(
        encode_body,
        grid=(SLOTS,),
        out_shape=(
            jax.ShapeDtypeStruct((SLOTS, T, LANES), bf16),
            jax.ShapeDtypeStruct((SLOTS, REACH, LANES), bf16),
            jax.ShapeDtypeStruct((SLOTS, REACH, LANES), bf16),
            jax.ShapeDtypeStruct((SLOTS, T, 2 * C), bf16),
            jax.ShapeDtypeStruct((SLOTS, T, C), bf16),
            jax.ShapeDtypeStruct((SLOTS, T, C), bf16),
            jax.ShapeDtypeStruct((SLOTS, T, C), bf16),
            jax.ShapeDtypeStruct((SLOTS, T, LANES), f32),
        ),
        in_specs=[SMEM] + [HBM] * 5,
        out_specs=(
            by_slot(T, LANES),
            by_slot(REACH, LANES),
            by_slot(REACH, LANES),
            by_slot(T, 2 * C),
            by_slot(T, C),
            by_slot(T, C),
            by_slot(T, C),
            by_slot(T, LANES),
        ),
        scratch_shapes=[
            pltpu.VMEM((C // LANES, 2 * T, LANES), f32),
            pltpu.VMEM((LANES, C), bf16),
            pltpu.VMEM((T, C), f32),
            pltpu.VMEM((T, C), bf16),
            pltpu.SMEM((DP * SLOTS,), jnp.int32),
            pltpu.VMEM((SLOTS, 2 * T, C), bf16),
            pltpu.VMEM((2 * C, C), bf16),
            pltpu.VMEM((5, C), f32),
            pltpu.SemaphoreType.DMA((6,)),
        ],
        compiler_params=params(50),
        cost_estimate=cost(2 * SLOTS * T * C * (2 * C + LANES), 8 << 20, SLOTS * T * C * 2),
        name="encode",
    )(*place[:2], audio, conv_weight, channels, proj)


def fill_ext(ext, low, own, high):
    ext[:REACH, :] = low.astype(f32)
    ext[REACH : REACH + T, :] = own.astype(f32)
    ext[REACH + T :, :] = high.astype(f32)


def fill_windows(windows, ext, first):
    rows = T + NEAR * (K // NEAR - 1)
    for r in range(NEAR):
        windows[:, r * LANES : (r + 1) * LANES] = ext[first + r : first + r + rows, :].astype(bf16)


def gathered(group):
    total = group[:T, :LANES]
    for p in range(1, PER_GROUP):
        total += group[NEAR * p : NEAR * p + T, p * LANES : (p + 1) * LANES]
    return total


def fill_back(turned, place, slot, cot_ref, recv_ref):
    turned[GC:, :] = jnp.zeros((LANES - GC, T), f32)
    turned[:GC, :] = jnp.where(
        place.chosen == slot, recv_ref[0].astype(f32), cot_ref[0].astype(f32)
    )


def mix_body(
    dev_ref,
    len_ref,
    mov_ref,
    feat_ref,
    low_ref,
    high_ref,
    weight,
    cot_ref,
    recv_ref,
    states_ref,
    sent_ref,
    slopes_ref,
    tail_ref,
    head_ref,
    piece_ref,
    ext,
    windows,
    turned,
):
    place = Place(dev_ref, len_ref, mov_ref)
    slot = pl.program_id(0)
    living = place.alive(slot)
    wide = PER_GROUP * LANES

    @pl.when(living)
    def _():
        own = feat_ref[0].astype(f32)
        fill_ext(ext, low_ref[0], own, high_ref[0])
        fill_windows(windows, ext, 0)
        fill_back(turned, place, slot, cot_ref, recv_ref)
        back = turned[...].T
        group = jnp.zeros((SPAN, wide), f32)
        for g in range(GROUPS):
            at = g * NEAR * PER_GROUP
            group += nn(windows[at : at + SPAN, :], weight[:, g * wide : (g + 1) * wide])
        mixed = gathered(group)
        below = phi(mixed)
        mask = place.mask(slot)
        states = jnp.where(mask, own + mixed * below, 0.0)
        states_ref[0] = states.T[:GC, :].astype(bf16)
        slopes = jnp.where(mask, back * (below + mixed * bell(mixed)), 0.0)
        slopes_ref[0] = slopes.astype(bf16)
        edge = jnp.where(place.x < X // 2, low_ref[0].astype(f32), high_ref[0].astype(f32))
        piece_ref[0, :T, :] = slopes.astype(bf16)
        piece_ref[0, T:, :] = edge.astype(bf16)

    @pl.when(jnp.logical_not(living))
    def _():
        states_ref[...] = jnp.zeros_like(states_ref)
        slopes_ref[...] = jnp.zeros_like(slopes_ref)
        piece_ref[...] = jnp.zeros_like(piece_ref)

    tail_ref[0] = slopes_ref[0, T - REACH :, :]
    head_ref[0] = slopes_ref[0, :REACH, :]

    @pl.when(place.chosen == slot)
    def _():
        sent_ref[...] = states_ref[0]


def mix(place, features, low, high, weight, cotangent, received):
    return pl.pallas_call(
        mix_body,
        grid=(SLOTS,),
        out_shape=(
            jax.ShapeDtypeStruct((SLOTS, GC, T), bf16),
            jax.ShapeDtypeStruct((GC, T), bf16),
            jax.ShapeDtypeStruct((SLOTS, T, LANES), bf16),
            jax.ShapeDtypeStruct((SLOTS, REACH, LANES), bf16),
            jax.ShapeDtypeStruct((SLOTS, REACH, LANES), bf16),
            jax.ShapeDtypeStruct((SLOTS, PIECE, LANES), bf16),
        ),
        in_specs=[SMEM] * 3
        + [
            by_slot(T, LANES),
            by_slot(REACH, LANES),
            by_slot(REACH, LANES),
            once(*weight.shape),
            by_slot(GC, T),
            by_slot(GC, T),
        ],
        out_specs=(
            by_slot(GC, T),
            whole(GC, T),
            by_slot(T, LANES),
            by_slot(REACH, LANES),
            by_slot(REACH, LANES),
            by_slot(PIECE, LANES),
        ),
        scratch_shapes=[
            pltpu.VMEM((EXT, LANES), f32),
            pltpu.VMEM((T + NEAR * (K // NEAR - 1), NEAR * LANES), bf16),
            pltpu.VMEM((LANES, T), f32),
        ],
        compiler_params=params(20),
        cost_estimate=cost(2 * SLOTS * SPAN * K * LANES * LANES, 7 << 20, SLOTS * T * LANES * 2),
        name="mix",
    )(*place, features, low, high, weight, cotangent, received)


def taps_body(scale, dev_ref, len_ref, mov_ref, *refs):
    feat_refs, piece_refs, (keep_ref, send_ref) = refs[:X], refs[X : 2 * X], refs[2 * X : 2 * X + 2]
    ext, windows, turned, sums, later = refs[2 * X + 2 :]
    place = Place(dev_ref, len_ref, mov_ref)
    slot = pl.program_id(0)
    spread = X * T
    rows = spread + NEAR * (K // NEAR - 1)

    @pl.when(slot == 0)
    def _():
        sums[...] = jnp.zeros_like(sums)

    @pl.when(place.y * spread < place.length(slot))
    def _():
        for step, (feat_ref, piece_ref) in enumerate(zip(feat_refs, piece_refs)):
            x = lax.rem(place.x + (X - step), X)
            at = pl.multiple_of(x * T, T)
            ext[pl.ds(REACH + at, T), :] = feat_ref[0].astype(f32)
            slopes = piece_ref[0, :T, :].astype(f32)
            turned[:LANES, pl.ds(at, T)] = slopes.T.astype(bf16)
            later[pl.ds(NEAR + at, T), :] = slopes

            @pl.when(x == 0)
            def _():
                ext[:REACH, :] = piece_ref[0, T:, :].astype(f32)

            @pl.when(x == X - 1)
            def _():
                ext[REACH + spread :, :] = piece_ref[0, T:, :].astype(f32)

        for j in range(4):
            windows[:, j * LANES : (j + 1) * LANES] = ext[
                pl.ds(place.x + 4 * j, rows), :
            ].astype(bf16)
        turned[:LANES, spread:] = jnp.zeros((LANES, LANES), bf16)
        later[:NEAR, :] = jnp.zeros((NEAR, LANES), f32)
        later[NEAR + spread :, :] = jnp.zeros((LANES - NEAR, LANES), f32)
        turned[LANES:, :] = later[...].T.astype(bf16)
        depth = spread + NEAR
        for q in range(0, K // NEAR, 2):
            pair = nn(turned[:, :depth], windows[q * NEAR : q * NEAR + depth, :])
            sums[q] += pair[:LANES, :]
            sums[q + 1] += pair[LANES:, :]

    @pl.when(slot == SLOTS - 1)
    def _():
        first_core = place.core == 0
        for q in range(K // NEAR):
            for far in range(2):
                at = 2 * far * LANES
                even = sums[q, :, at : at + LANES] * scale
                odd = sums[q, :, at + LANES : at + 2 * LANES] * scale
                keep = jnp.where(first_core, even, odd)
                send = jnp.where(first_core, odd, even)
                for y in range(2):
                    rows = slice(y * HALF, y * HALF + REACH)
                    keep_ref[y, 2 * q + far] = keep[rows, :].astype(bf16)
                    send_ref[y, 2 * q + far] = send[rows, :].astype(bf16)


def taps(scale, place, features, pieces):
    shape = jax.ShapeDtypeStruct((2, CELLS, REACH, LANES), bf16)
    spread = X * T
    return pl.pallas_call(
        functools.partial(taps_body, scale),
        grid=(SLOTS,),
        out_shape=(shape,) * 2,
        in_specs=[SMEM] * 3 + [by_slot(T, LANES)] * X + [by_slot(PIECE, LANES)] * X,
        out_specs=(whole(*shape.shape),) * 2,
        scratch_shapes=[
            pltpu.VMEM((spread + 2 * REACH, LANES), f32),
            pltpu.VMEM((spread + NEAR * (K // NEAR - 1), 4 * LANES), bf16),
            pltpu.VMEM((2 * LANES, spread + LANES), bf16),
            pltpu.VMEM((K // NEAR, LANES, 4 * LANES), f32),
            pltpu.VMEM((spread + LANES, LANES), f32),
        ],
        compiler_params=params(16),
        cost_estimate=cost(2 * SLOTS * SPAN * K * LANES * LANES, 4 << 20),
        name="taps",
    )(*place, *features, *pieces)


def backward_body(
    scale,
    dev_ref,
    len_ref,
    mov_ref,
    slopes_ref,
    low_ref,
    high_ref,
    cot_ref,
    recv_ref,
    weight,
    pair_ref,
    q_ref,
    slope_ref,
    m_ref,
    inv_ref,
    conv_ref,
    chan_ref,
    proj_ref,
    audio_grad_ref,
    keep_ref,
    send_ref,
    ext,
    windows,
    turned,
    proj,
    feat_grad,
    normed,
    mid,
    wide,
    conv_sum,
    proj_sum,
    chan_sum,
    columns,
):
    place = Place(dev_ref, len_ref, mov_ref)
    slot = pl.program_id(0)
    living = place.alive(slot)
    span = PER_GROUP * LANES

    @pl.when(slot == 0)
    def _():
        proj[...] = jnp.zeros_like(proj)
        proj[:GC, :] = proj_ref[...]
        conv_sum[...] = jnp.zeros_like(conv_sum)
        proj_sum[...] = jnp.zeros_like(proj_sum)
        chan_sum[...] = jnp.zeros_like(chan_sum)

    @pl.when(living)
    def _():
        fill_ext(ext, low_ref[0], slopes_ref[0], high_ref[0])
        fill_windows(windows, ext, 1)
        fill_back(turned, place, slot, cot_ref, recv_ref)
        group = jnp.zeros((SPAN, span), f32)
        for g in range(GROUPS):
            at = g * NEAR * PER_GROUP
            group += nt(windows[at : at + SPAN, :], weight[g * span : (g + 1) * span, :])
        spread = gathered(group)
        feat_grad[...] = jnp.where(place.mask(slot), turned[...].T + spread, 0.0).astype(bf16)
        gain = chan_ref[1:2, :]
        gain_two, shift_two = chan_ref[3:4, :], chan_ref[4:5, :]
        mid[...] = nn(feat_grad[...], proj[...])
        for at in range(0, T, CHUNK):
            rows = slice(at, at + CHUNK)
            m = m_ref[0, rows, :].astype(f32)
            normed[rows, :] = (m * gain_two + shift_two).astype(bf16)
            normed_grad = mid[rows, :]
            chan_sum[24:32, :] += jnp.sum((normed_grad * m).reshape(-1, 8, C), axis=0)
            chan_sum[32:40, :] += jnp.sum(normed_grad.reshape(-1, 8, C), axis=0)
            scaled = normed_grad * gain_two
            first = jnp.mean(scaled, axis=-1, keepdims=True)
            second = jnp.mean(scaled * m, axis=-1, keepdims=True)
            inverse_two = inv_ref[0, rows, LANES // 2 : LANES // 2 + 1]
            pre_grad = inverse_two * (scaled - first - m * second) * slope_ref[
                0, rows, :
            ].astype(f32)
            q = q_ref[0, rows, :].astype(f32)
            chan_sum[8:16, :] += jnp.sum((pre_grad * q).reshape(-1, 8, C), axis=0)
            chan_sum[16:24, :] += jnp.sum(pre_grad.reshape(-1, 8, C), axis=0)
            scaled = pre_grad * gain
            first = jnp.mean(scaled, axis=-1, keepdims=True)
            second = jnp.mean(scaled * q, axis=-1, keepdims=True)
            inverse = inv_ref[0, rows, 0:1]
            conv_grad = inverse * (scaled - first - q * second)
            chan_sum[0:8, :] += jnp.sum(conv_grad.reshape(-1, 8, C), axis=0)
            mid[rows, :] = conv_grad
        operand = mid[...].astype(bf16)
        for tap in range(2):
            rows = slice(tap * C, (tap + 1) * C)
            audio_grad = nt(operand, conv_ref[rows, :])
            for c in range(C // LANES):
                wide[c, pl.ds(tap, T, stride=2), :] = audio_grad[:, c * LANES : (c + 1) * LANES]
            conv_sum[rows, :] += tn(pair_ref[0, :, rows], operand)
        for c in range(C // LANES):
            audio_grad_ref[0, :, c * LANES : (c + 1) * LANES] = wide[c].astype(bf16)
        proj_sum[...] += tn(normed[...], feat_grad[...])

    @pl.when(jnp.logical_not(living))
    def _():
        audio_grad_ref[...] = jnp.zeros_like(audio_grad_ref)

    @pl.when(slot == SLOTS - 1)
    def _():
        first_core = place.core == 0
        columns[...] = jnp.zeros_like(columns)
        for n in range(5):
            columns[GC + n : GC + n + 1, :] = jnp.sum(
                chan_sum[8 * n : 8 * n + 8, :], axis=0, keepdims=True
            )
        proj_sum[...] += columns[...].T
        for x in range(X):
            lanes = slice(x * LANES, (x + 1) * LANES)
            for cell in range(CELLS):
                at = 2 * cell * 32
                even = conv_sum[at : at + 32, lanes]
                odd = conv_sum[at + 32 : at + 64, lanes]
                rows = slice(cell * 32, (cell + 1) * 32)
                keep_ref[x, rows, :] = (jnp.where(first_core, even, odd) * scale).astype(bf16)
                send_ref[x, rows, :] = (jnp.where(first_core, odd, even) * scale).astype(bf16)
            for four in range(CELLS // 4):
                even, odd = [
                    jnp.concatenate(
                        [
                            proj_sum[at : at + SPARE, :]
                            for at in (
                                (2 * cell + odd) * 16 + x * SPARE
                                for cell in range(4 * four, 4 * four + 4)
                            )
                        ],
                        axis=0,
                    )
                    for odd in range(2)
                ]
                rows = slice(CONV_ROWS + four * 16, CONV_ROWS + (four + 1) * 16)
                keep_ref[x, rows, :] = (jnp.where(first_core, even, odd) * scale).astype(bf16)
                send_ref[x, rows, :] = (jnp.where(first_core, odd, even) * scale).astype(bf16)


def backward(
    scale, place, slopes, low, high, cotangent, received, weight, stored, conv_weight, channels, proj
):
    shape = jax.ShapeDtypeStruct((X, REST, LANES), bf16)
    return pl.pallas_call(
        functools.partial(backward_body, scale),
        grid=(SLOTS,),
        out_shape=(jax.ShapeDtypeStruct((SLOTS, 2 * T, C), bf16), shape, shape),
        in_specs=[SMEM] * 3
        + [
            by_slot(T, LANES),
            by_slot(REACH, LANES),
            by_slot(REACH, LANES),
            by_slot(GC, T),
            by_slot(GC, T),
            once(*weight.shape),
            by_slot(T, 2 * C),
            by_slot(T, C),
            by_slot(T, C),
            by_slot(T, C),
            by_slot(T, LANES),
            once(2 * C, C),
            whole(5, C),
            whole(GC, C),
        ],
        out_specs=(by_slot(2 * T, C), whole(*shape.shape), whole(*shape.shape)),
        scratch_shapes=[
            pltpu.VMEM((EXT, LANES), f32),
            pltpu.VMEM((T + NEAR * (K // NEAR - 1), NEAR * LANES), bf16),
            pltpu.VMEM((LANES, T), f32),
            pltpu.VMEM((LANES, C), bf16),
            pltpu.VMEM((T, LANES), bf16),
            pltpu.VMEM((T, C), bf16),
            pltpu.VMEM((T, C), f32),
            pltpu.VMEM((C // LANES, 2 * T, LANES), f32),
            pltpu.VMEM((2 * C, C), f32),
            pltpu.VMEM((C, LANES), f32),
            pltpu.VMEM((40, C), f32),
            pltpu.VMEM((LANES, C), f32),
        ],
        compiler_params=params(30),
        cost_estimate=cost(
            2 * SLOTS * (SPAN * K * LANES * LANES + T * C * (4 * C + 2 * LANES)), 14 << 20
        ),
        name="backward",
    )(
        *place,
        slopes,
        low,
        high,
        cotangent,
        received,
        weight,
        *stored,
        conv_weight,
        channels,
        proj,
    )


def halve_body(dev_ref, keep_ref, recv_ref, stay_ref, leave_ref):
    y = lax.rem(dev_ref[0], MP) // X
    for out_ref, at in ((stay_ref, y), (leave_ref, 1 - y)):
        out_ref[...] = (keep_ref[at].astype(f32) + recv_ref[at].astype(f32)).astype(bf16)


def halve(dev, keep, received):
    shape = jax.ShapeDtypeStruct(keep.shape[1:], bf16)
    return pl.pallas_call(
        halve_body,
        out_shape=(shape,) * 2,
        in_specs=[SMEM] + [VMEM] * 2,
        out_specs=(VMEM,) * 2,
        compiler_params=params(8),
        cost_estimate=cost(0, 2 << 20),
        name="halve",
    )(dev, keep, received)


def join_body(dev_ref, keep_ref, recv_ref, *out_refs):
    x = lax.rem(dev_ref[0], X)
    for step, out_ref in enumerate(out_refs):
        at = lax.rem(x + step, X)
        out_ref[...] = (keep_ref[at].astype(f32) + recv_ref[at].astype(f32)).astype(bf16)


def join(dev, keep, received):
    shape = jax.ShapeDtypeStruct((REST, LANES), bf16)
    return pl.pallas_call(
        join_body,
        out_shape=(shape,) * X,
        in_specs=[SMEM] + [VMEM] * 2,
        out_specs=(VMEM,) * X,
        compiler_params=params(8),
        cost_estimate=cost(0, 2 << 20),
        name="join",
    )(dev, keep, received)


def cells_body(*refs):
    pos_refs, rest_refs, out_ref, rows = refs[:2], refs[2:6], refs[6], refs[7]

    def summed(parts, *at):
        result = parts[0][at].astype(f32)
        for part in parts[1:]:
            result += part[at].astype(f32)
        return result

    for four in range(CELLS // 4):
        at = CONV_ROWS + four * 16
        small = summed(rest_refs, slice(at, at + 16), slice(None))
        for n in range(4):
            cell = 4 * four + n
            rows[...] = summed(pos_refs, cell)
            rows[HALF:, :] = small[n * SPARE : (n + 1) * SPARE, :]
            out_ref[cell, :REACH, :] = rows[...].astype(bf16)
            conv = summed(rest_refs, slice(cell * 32, cell * 32 + 32), slice(None))
            out_ref[cell, REACH:, :] = conv.astype(bf16)


def make_cells(pos_parts, rest_parts):
    return pl.pallas_call(
        cells_body,
        out_shape=jax.ShapeDtypeStruct((CELLS, REACH + 32, LANES), bf16),
        in_specs=[VMEM] * 6,
        out_specs=VMEM,
        scratch_shapes=[pltpu.VMEM((REACH, LANES), f32)],
        compiler_params=params(8),
        cost_estimate=cost(0, 2 << 20),
        name="cells",
    )(*pos_parts, *rest_parts)


def total_body(in_ref, out_ref):
    total = in_ref[0].astype(f32)
    for n in range(1, in_ref.shape[0]):
        total += in_ref[n].astype(f32)
    for copy in range(MP):
        out_ref[copy] = total.astype(bf16)


def total(parts):
    return pl.pallas_call(
        total_body,
        out_shape=jax.ShapeDtypeStruct((MP,) + parts.shape[1:], bf16),
        in_specs=[VMEM],
        out_specs=VMEM,
        compiler_params=params(10),
        cost_estimate=cost(0, 2 * parts.size),
        name="total",
    )(parts)


def finish_body(
    dev_ref,
    len_ref,
    mov_ref,
    in_ref,
    states_ref,
    other_ref,
    hidden_ref,
    pos_ref,
    conv_ref,
    proj_ref,
    chan_ref,
):
    place = Place(dev_ref, len_ref, mov_ref)
    for slot in range(SLOTS):
        hidden_ref[slot] = jnp.where(
            place.chosen == slot, other_ref[...].astype(f32), states_ref[slot].astype(f32)
        ).astype(bf16)
    small = []
    for x in range(X):
        low, high = in_ref[x].astype(f32), in_ref[X + x].astype(f32)
        block = jnp.concatenate(
            [low[:HALF, :], high[:HALF, :], jnp.zeros((LANES - GC, LANES), f32)], axis=0
        ).T
        pos_ref[x] = block[:GC, :GC]
        both = low[HALF:, :] + high[HALF:, :]
        small.append(both[:SPARE, :])
        conv_ref[:, x * LANES : (x + 1) * LANES] = both[SPARE:, :]
    small = jnp.concatenate(small, axis=0)
    proj_ref[...] = small[:, :GC]
    chan_ref[...] = jnp.concatenate([small] * 8, axis=0).T[GC : GC + 5, :16]


def finish(place, cells, states, other):
    return pl.pallas_call(
        finish_body,
        out_shape=(
            jax.ShapeDtypeStruct((SLOTS, GC, T), bf16),
            jax.ShapeDtypeStruct((4, GC, GC), f32),
            jax.ShapeDtypeStruct((32, C), f32),
            jax.ShapeDtypeStruct((16, GC), f32),
            jax.ShapeDtypeStruct((5, 16), f32),
        ),
        in_specs=[SMEM] * 3 + [VMEM] * 3,
        out_specs=(VMEM,) * 5,
        compiler_params=params(8),
        name="finish",
    )(*place, cells, states, other)


def neighbours(tail, head):
    forward = [(i, i + 1) for i in range(MP - 1)]
    backward_route = [(i + 1, i) for i in range(MP - 1)]
    return lax.ppermute(tail, "mp", forward), lax.ppermute(head, "mp", backward_route)


def along_x(block, step):
    route = [(X * y + x, X * y + (x + step) % X) for y in range(2) for x in range(X)]
    return lax.ppermute(block, "mp", route)


def around_x(block):
    far = along_x(block, 2)
    return (block, along_x(block, 1), far, along_x(block, 3))


def per_device(
    audio, lengths, moved_slots, conv_weight, channel_params, proj_weight, pos_weight, cotangent
):
    data_index = lax.axis_index("dp")
    model_index = lax.axis_index("mp")
    scale = (SLOTS * DP * T * MP) ** -0.5
    dev = (data_index * MP + model_index).astype(jnp.int32).reshape(1)
    place = (dev, lengths, moved_slots.reshape(-1))
    swap = [(i, i ^ (DP // 2)) for i in range(DP)]
    core_swap = [(i, i ^ 1) for i in range(DP)]
    channels = channel_params.T
    proj = proj_weight.T
    cot = cotangent.transpose(0, 2, 1)

    received = lax.ppermute(cot, "dp", swap)
    features, tail, head, *stored = encode(place, audio, conv_weight, channels, proj)
    low, high = neighbours(tail, head)
    all_features = around_x(features)
    ahead, behind = turn(pos_weight.transpose(1, 2, 0))
    states, sent, slopes, tail, head, piece = mix(
        place, features, low, high, ahead, cot, received
    )
    low, high = neighbours(tail, head)
    piece, all_features = lax.optimization_barrier((piece, all_features))
    pieces = around_x(piece)
    audio_grad, keep, send = backward(
        scale,
        place,
        slopes,
        low,
        high,
        cot,
        received,
        behind,
        stored,
        conv_weight,
        channels,
        proj,
    )
    other = lax.ppermute(sent, "dp", swap)
    send, pieces, other = lax.optimization_barrier((send, pieces, other))
    chunks = join(dev, keep, lax.ppermute(send, "dp", core_swap))
    chunks, pieces = lax.optimization_barrier((chunks, pieces))
    rest_parts = [chunks[0]] + [along_x(chunks[step], step) for step in (2, 1, 3)]
    pos_keep, pos_send = taps(scale, place, all_features, pieces)
    stay, leave = halve(dev, pos_keep, lax.ppermute(pos_send, "dp", core_swap))
    pos_parts = (stay, lax.ppermute(leave, "mp", [(i, i ^ X) for i in range(MP)]))
    cells = make_cells(pos_parts, rest_parts)
    groups = [list(range(bit, DP, 2)) for bit in range(2)]
    cells = lax.all_to_all(cells, "dp", 0, 0, axis_index_groups=groups, tiled=True)
    cells = lax.all_to_all(total(cells), "mp", 0, 0, tiled=True)
    hidden, grad_pos, grad_conv, grad_proj, grad_channels = finish(place, cells, states, other)
    return (
        hidden.transpose(0, 2, 1),
        audio_grad,
        grad_pos,
        grad_conv,
        grad_proj,
        grad_channels.T,
    )


def solution(mesh):
    return jax.shard_map(
        per_device,
        mesh=mesh,
        in_specs=(P("dp", "mp", None), P(), P(), P(), P(), P(), P(), P("dp", "mp", None)),
        out_specs=(
            P("dp", "mp", None),
            P("dp", "mp", None),
            P("dp", None, None),
            P("dp", None),
            P("dp", None),
            P("dp", None),
        ),
        check_vma=False,
    )
```
